32 devices in a mesh: tok: 8 (over z, x), dim: 4 (over y, core).
Axes of the slice: x: 2, y: 2, z: 4, core: 2. Of those that a mesh axis runs over, the one named last changes fastest.
Arguments:
- inputs: bfloat16 [16384, 1024], P('tok', 'dim'), may hold values from -9 to 9
- cotangent: bfloat16 [16384, 1024], P('tok', 'dim'), may hold values from -6 to 6
- lengths: int32 [8, 3], P('tok'), may hold values from 1 to 1024, 2048 in all within a row
- pad_mask: int32 [16384], P('tok'), may hold values 0 or 1
- attention_weights: float32 [4, 1024, 1024], P(None, 'dim', 'tok'), may hold values from -5.8 to 5.8
- gated_weights: float32 [3, 4096, 1024], P(None, 'dim', 'tok'), may hold values from -5.8 to 5.8
- model_gains: float32 [3, 1024], P(None, 'dim'), may hold values from 0.1 to 1.8
- unit_gains: float32 [2, 4096], P(None, 'dim'), may hold values from 0.5 to 1.5
- attention_moment: float32 [4, 1024, 1024], P(None, 'dim', 'tok'), may hold values from -6 to 6
- attention_square: float32 [4, 1024, 1024], P(None, 'dim', 'tok'), may hold values from 1.44 to 5.76
- gated_moment: float32 [3, 4096, 1024], P(None, 'dim', 'tok'), may hold values from -6 to 6
- gated_square: float32 [3, 4096, 1024], P(None, 'dim', 'tok'), may hold values from 1.44 to 5.76
- model_moment: float32 [3, 1024], P(None, 'dim'), may hold values from -384 to 384
- model_square: float32 [3, 1024], P(None, 'dim'), may hold values from 4096 to 16384
- unit_moment: float32 [2, 4096], P(None, 'dim'), may hold values from -384 to 384
- unit_square: float32 [2, 4096], P(None, 'dim'), may hold values from 4096 to 16384
Outputs:
- layer_out: bfloat16 [16384, 1024], P('tok', 'dim')
- input_gradient: float32 [16384, 1024], P('tok', 'dim')
- attention_next: float32 [4, 1024, 1024], P(None, 'dim', 'tok')
- attention_copy: bfloat16 [4, 1024, 1024], P(None, 'dim', 'tok')
- moment_attention: float32 [4, 1024, 1024], P(None, 'dim', 'tok')
- square_attention: float32 [4, 1024, 1024], P(None, 'dim', 'tok')
- gated_next: float32 [3, 4096, 1024], P(None, 'dim', 'tok')
- gated_copy: bfloat16 [3, 4096, 1024], P(None, 'dim', 'tok')
- moment_gated: float32 [3, 4096, 1024], P(None, 'dim', 'tok')
- square_gated: float32 [3, 4096, 1024], P(None, 'dim', 'tok')
- model_next: float32 [3, 1024], P(None, 'dim')
- moment_model: float32 [3, 1024], P(None, 'dim')
- square_model: float32 [3, 1024], P(None, 'dim')
- unit_next: float32 [2, 4096], P(None, 'dim')
- moment_unit: float32 [2, 4096], P(None, 'dim')
- square_unit: float32 [2, 4096], P(None, 'dim')
- gradient_norm: float32 [1], replicated
- mean_alpha: float32 [2], replicated
The draws below stay inside these ranges and needn't reach their ends.
Inputs may be any that keep to these rules, and one draw needn't show every extreme that they name: Each pack's 3 lengths add up to 2048.
All inputs are finite; a program needn't handle non-finite values. No bound on the sum of `pad_mask` on one device may be relied on, other than what follows from the above.
Results may differ from the reference program's by a relative error of at most 0.01.
The reference program's roundings to bfloat16 on the way count: a program that leaves them out, or rounds other values in their place, can miss the bound.
Values may be sent and summed in bfloat16 or wider, within the bound.
No kernel may reach another device: no remote copies, remote signals or barrier semaphores. Data moves between devices by JAX's collectives and lax.ppermute only.
A program may use at most 192 MiB of HBM per device.

```python
import math
import jax
import jax.numpy as jnp
import numpy as np
from jax import lax

D = 1024
HEADS = 16
HEAD = 64
FF = 4096
TOK_DEV = 2048
SEQ_DEV = 3
STEP = 4
MAXLEN = 1024
QBLK = 512
GROUPS = 8
TOKENS = 16384


def column_scales(width):
    return 0.6 + 1.2 * jnp.arange(width, dtype=jnp.float32) / (width - 1)


def draw_inputs(key, part):
    key = jax.random.fold_in(key, 11)
    scales = column_scales(D)
    entries = jnp.clip(jax.random.normal(key, (TOKENS, D), jnp.float32), -5.0, 5.0)
    return (entries * scales).astype(jnp.bfloat16)


def scaled_entries(key, shape):
    scales = column_scales(D) / 1.25
    entries = jnp.clip(jax.random.normal(key, shape, jnp.float32), -4.0, 4.0)
    return entries * scales


def draw_attention_weights(key, part):
    key = jax.random.fold_in(key, 23)
    return scaled_entries(key, (4, D, D))


def draw_gated_weights(key, part):
    key = jax.random.fold_in(key, 37)
    return scaled_entries(key, (3, FF, D))


def draw_model_gains(key, part):
    key = jax.random.fold_in(key, 41)
    first_key, second_key = jax.random.split(key)
    scale_row = jax.random.uniform(first_key, (1, D), jnp.float32, 0.9, 1.8)
    alpha_rows = jnp.exp(jax.random.uniform(second_key, (2, D), jnp.float32, math.log(0.1), math.log(0.6)))
    return jnp.concatenate([scale_row, alpha_rows], axis=0)


def plant(drawn, key, least, largest):
    longest = drawn.shape.index(max(drawn.shape))
    spots = []
    for shift in (0, 1):
        where = [jax.random.randint(jax.random.fold_in(key, axis), (), 0, length) for axis, length in enumerate(drawn.shape)]
        where[longest] = (where[longest] + shift) % drawn.shape[longest]
        spots.append(tuple(where))
    return drawn.at[spots[0]].set(least).at[spots[1]].set(largest)


def level_of(own_key, shape, pieces, smallest, high):
    def one(position, shards_of):
        heights = jax.random.uniform(jax.random.fold_in(jax.random.fold_in(own_key, 6), position), (shards_of,), jnp.float32, smallest / len(pieces), high / len(pieces))
        return jnp.repeat(jnp.exp(heights), shape[position] // shards_of).reshape((-1,) + (1,) * (len(shape) - position - 1))

    loudness = one(*pieces[0])
    for cut in pieces[1:]:
        loudness = loudness * one(*cut)
    return loudness


def length_profile(number_of, total, reach, slope):
    weights = [(1 << 20) // math.isqrt(standing ** slope) + 1 for standing in range(2, number_of + 1)]
    surplus, counts = total - reach - (number_of - 1), [1] * (number_of - 1)
    while surplus > 0:
        candidates = [i for i in range(number_of - 1) if counts[i] < reach]
        mass, left = sum([weights[i] for i in candidates]), surplus
        for i in candidates:
            extra = min(reach - counts[i], max(1, left * weights[i] // mass), surplus)
            counts[i] = counts[i] + extra
            surplus = surplus - extra
    return np.array([reach] + counts)


def ragged_sizes(stream_key, count, total, bound, lean):
    if count == 2:
        one = jax.random.randint(stream_key, (), max(1, total - bound), min(bound, total - 1) + 1)
        return jnp.stack([one, total - one])
    tallies = jnp.asarray(length_profile(count, total, bound, lean), jnp.int32)
    twos = (count - 1) // 2
    giver, receiver = tallies[1:1 + 2 * twos:2], tallies[2:2 + 2 * twos:2]
    room = jnp.minimum(giver - 1, bound - receiver)
    moved = jax.random.randint(jax.random.fold_in(stream_key, 1), (twos,), 0, 1 << 20) % (room + 1)
    tallies = tallies.at[1:1 + 2 * twos:2].set(giver - moved).at[2:2 + 2 * twos:2].set(receiver + moved)
    return tallies[jax.random.permutation(jax.random.fold_in(stream_key, 2), count)]


def gaussian(stream_key, dims, scale, bound, cuts=(), kind=jnp.bfloat16):
    gain = level_of(stream_key, dims, cuts, -0.22, 0.18) if cuts else 1.0
    array = jax.random.normal(stream_key, dims, jnp.float32) * scale * gain
    return jnp.minimum(jnp.maximum(array, -bound), bound).astype(kind)


def setup_inputs(seed: int = 0) -> dict:
    keys = jax.random.split(jax.random.key(seed), 17)
    inputs = draw_inputs(jax.random.fold_in(keys[16], 71), 0)
    cotangent = gaussian(keys[1], (TOKENS, D), 1.0, 6.0, ((0, 8), (1, 4)))
    lengths = jax.vmap(lambda own: ragged_sizes(own, SEQ_DEV, TOK_DEV, MAXLEN, 2))(jax.random.split(keys[2], GROUPS)).reshape((GROUPS, SEQ_DEV)).astype(jnp.int32)
    pad_mask = plant((jax.random.randint(keys[3], (TOKENS,), 0, 8) < 7).astype(jnp.int32), jax.random.fold_in(keys[3], 1), 0, 1)
    attention_weights = draw_attention_weights(jax.random.fold_in(keys[16], 71), 0)
    gated_weights = draw_gated_weights(jax.random.fold_in(keys[16], 71), 0)
    model_gains = draw_model_gains(jax.random.fold_in(keys[16], 71), 0)
    unit_gains = jnp.clip(0.5 + 1.0 * jax.random.uniform(keys[7], (2, FF), jnp.float32) ** level_of(keys[7], (2, FF), ((1, 4),), -0.2, 0.2), 0.5, 1.5)
    attention_moment = gaussian(keys[8], (4, D, D), (0.3 * (TOKENS // D) ** 0.5), 6.0, ((1, 4), (2, 8)), jnp.float32)
    attention_square = jnp.clip(jnp.exp(math.log(5.76) - 1.3862944 * jax.random.uniform(keys[9], (4, D, D), jnp.float32) ** level_of(keys[9], (4, D, D), ((1, 4), (2, 8)), -0.2, 0.2)), 1.44, 5.76)
    gated_moment = gaussian(keys[10], (3, FF, D), (0.3 * (TOKENS // D) ** 0.5), 6.0, ((1, 4), (2, 8)), jnp.float32)
    gated_square = jnp.clip(jnp.exp(math.log(5.76) - 1.3862944 * jax.random.uniform(keys[11], (3, FF, D), jnp.float32) ** level_of(keys[11], (3, FF, D), ((1, 4), (2, 8)), -0.2, 0.2)), 1.44, 5.76)
    model_moment = gaussian(keys[12], (3, D), (0.5 * TOKENS ** 0.5), 384.0, ((1, 4),), jnp.float32)
    model_square = jnp.clip(jnp.exp(math.log(16384.0) - 1.3862944 * jax.random.uniform(keys[13], (3, D), jnp.float32) ** level_of(keys[13], (3, D), ((1, 4),), -0.2, 0.2)), 4096.0, 16384.0)
    unit_moment = gaussian(keys[14], (2, FF), (0.5 * TOKENS ** 0.5), 384.0, ((1, 4),), jnp.float32)
    unit_square = jnp.clip(jnp.exp(math.log(16384.0) - 1.3862944 * jax.random.uniform(keys[15], (2, FF), jnp.float32) ** level_of(keys[15], (2, FF), ((1, 4),), -0.2, 0.2)), 4096.0, 16384.0)
    return {"inputs": inputs, "cotangent": cotangent, "lengths": lengths, "pad_mask": pad_mask, "attention_weights": attention_weights, "gated_weights": gated_weights, "model_gains": model_gains, "unit_gains": unit_gains, "attention_moment": attention_moment, "attention_square": attention_square, "gated_moment": gated_moment, "gated_square": gated_square, "model_moment": model_moment, "model_square": model_square, "unit_moment": unit_moment, "unit_square": unit_square}


EPSILON = 1e-06
ADAM_EPSILON = 1e-08
BETA_ONE = 0.5
BETA_TWO = 0.5
LEARN_RATE = 1.5
MASKED_SCORE = -1e+30
HIGHEST = lax.Precision.HIGHEST

@jax.custom_vjp
def low(v):
    return lax.optimization_barrier(v.astype(jnp.bfloat16)).astype(jnp.float32)

@jax.custom_vjp
def low_back(v):
    return v

def low_keep(v):
    return (low(v), None)

def low_pass(kept, grad):
    return (grad,)

def back_keep(v):
    return (v, None)

def back_low(kept, grad):
    return (low(grad),)
low.defvjp(low_keep, low_pass)
low_back.defvjp(back_keep, back_low)

def matmul(left, right):
    return jnp.dot(left, right, precision=HIGHEST)

def sphere(values):
    return values * lax.rsqrt(lax.optimization_barrier(jnp.mean(values * values, axis=-1, keepdims=True)) + EPSILON)

def head_sphere(values):
    split_rows = values.reshape(values.shape[0], HEADS, HEAD)
    return sphere(split_rows).reshape(values.shape[0], D)

def segments(length_row):
    pack_starts = jnp.cumsum(length_row) - length_row
    places = jnp.arange(TOK_DEV, dtype=jnp.int32)
    return lax.optimization_barrier(jnp.sum((places[:, None] >= pack_starts[None, 1:]).astype(jnp.int32), axis=1)).astype(jnp.int32)

def visible(first_row, segment, padding):
    places = jnp.arange(TOK_DEV, dtype=jnp.int32)
    row_ids = first_row + jnp.arange(QBLK, dtype=jnp.int32)
    segment_rows = lax.dynamic_slice_in_dim(segment, first_row, QBLK, 0)
    same_seq = segment_rows[:, None] == segment[None, :]
    before = places[None, :] <= row_ids[:, None]
    live_key = (padding[None, :] == 1) | (places[None, :] == row_ids[:, None])
    return same_seq & before & live_key

def attend(query_low, key_low, value_low, segment, padding):
    query_heads = query_low.reshape(TOK_DEV, HEADS, HEAD)
    key_heads = key_low.reshape(TOK_DEV, HEADS, HEAD)
    value_heads = value_low.reshape(TOK_DEV, HEADS, HEAD)

    def one_block(first_row):
        query_rows = lax.dynamic_slice_in_dim(query_heads, first_row, QBLK, 0)
        raw_scores = jnp.einsum('qhe,khe->hqk', query_rows, key_heads, precision=HIGHEST) * HEAD ** (-0.5)
        raw_scores = low_back(raw_scores)
        scores = jnp.where(visible(first_row, segment, padding)[None], raw_scores, MASKED_SCORE)
        row_max = lax.optimization_barrier(jnp.max(scores, axis=2, keepdims=True))
        exponents = jnp.exp(scores - row_max)
        probs_rows = exponents / lax.optimization_barrier(jnp.sum(exponents, axis=2, keepdims=True))
        return jnp.einsum('hqk,khe->qhe', low(probs_rows), value_heads, precision=HIGHEST)
    first_rows = jnp.arange(TOK_DEV // QBLK, dtype=jnp.int32) * QBLK
    mixed_heads = lax.map(jax.checkpoint(one_block), first_rows)
    return mixed_heads.reshape(TOK_DEV, D)

def layer_forward(tokens, attention_low, gated_low, model_gains, unit_gains, segment, padding):
    scale_model = D ** (-0.5)
    queries = low_back(matmul(tokens, attention_low[0].T) * scale_model)
    keys_full = low_back(matmul(tokens, attention_low[1].T) * scale_model)
    values_full = low_back(matmul(tokens, attention_low[2].T) * scale_model)
    query_low = low(head_sphere(queries) * model_gains[0])
    key_low = low(head_sphere(keys_full) * model_gains[0])
    value_low = low(values_full)
    mixed = attend(query_low, key_low, value_low, segment, padding)
    mixed_low = low_back(low(mixed))
    branch_mixer = low_back(matmul(mixed_low, attention_low[3]) * scale_model)
    hidden_one = sphere(tokens + model_gains[1] * (sphere(branch_mixer) - tokens))
    hidden_low = low(hidden_one)
    upward = low_back(matmul(hidden_low, gated_low[0].T) * scale_model)
    gating = low_back(matmul(hidden_low, gated_low[1].T) * scale_model)
    middle_low = low(unit_gains[0] * upward * jax.nn.silu(unit_gains[1] * gating))
    branch_gated = low_back(matmul(middle_low, gated_low[2]) * FF ** (-0.5))
    return sphere(hidden_one + model_gains[2] * (sphere(branch_gated) - hidden_one))

def moment_update(weights, gradient, moment, square, fix_first, fix_second):
    moment_next = BETA_ONE * moment + (1.0 - BETA_ONE) * gradient
    square_next = BETA_TWO * square + (1.0 - BETA_TWO) * gradient * gradient
    stepped = weights - LEARN_RATE * (moment_next / fix_first) / (jnp.sqrt(square_next / fix_second) + ADAM_EPSILON)
    return (stepped, moment_next, square_next)

def renormed(stepped):
    return stepped * lax.rsqrt(lax.optimization_barrier(jnp.mean(stepped * stepped, axis=2, keepdims=True)) + EPSILON)

def reference(inputs, cotangent, lengths, pad_mask, attention_weights, gated_weights, model_gains, unit_gains, attention_moment, attention_square, gated_moment, gated_square, model_moment, model_square, unit_moment, unit_square):
    segment_ids = jax.vmap(segments)(lengths)
    padding = pad_mask.reshape(GROUPS, TOK_DEV)
    tokens = inputs.astype(jnp.float32).reshape(GROUPS, TOK_DEV, D)

    def whole(token_rows, attention, gated, gains_model, gains_unit):
        attention_low = low(attention)
        gated_low = low(gated)

        def group_pass(running, item):
            group_tokens, group_segment, group_padding = item
            return (running, layer_forward(group_tokens, attention_low, gated_low, gains_model, gains_unit, group_segment, group_padding))
        ignored, outputs = lax.scan(group_pass, jnp.zeros((), jnp.float32), (token_rows, segment_ids, padding))
        return outputs
    outputs, pullback = jax.vjp(whole, tokens, attention_weights, gated_weights, model_gains, unit_gains)
    seed_rows = cotangent.astype(jnp.float32).reshape(GROUPS, TOK_DEV, D) * padding.astype(jnp.float32)[:, :, None]
    delta_tokens, delta_attention, delta_gated, delta_model, delta_unit = pullback(seed_rows)
    fix_first = 1.0 - BETA_ONE ** STEP
    fix_second = 1.0 - BETA_TWO ** STEP
    attention_stepped, moment_attention, square_attention = moment_update(attention_weights, delta_attention, attention_moment, attention_square, fix_first, fix_second)
    gated_stepped, moment_gated, square_gated = moment_update(gated_weights, delta_gated, gated_moment, gated_square, fix_first, fix_second)
    model_next, moment_model, square_model = moment_update(model_gains, delta_model, model_moment, model_square, fix_first, fix_second)
    unit_next, moment_unit, square_unit = moment_update(unit_gains, delta_unit, unit_moment, unit_square, fix_first, fix_second)
    attention_next = renormed(attention_stepped)
    gated_next = renormed(gated_stepped)
    square_total = jnp.sum(delta_attention * delta_attention) + jnp.sum(delta_gated * delta_gated) + jnp.sum(delta_model * delta_model) + jnp.sum(delta_unit * delta_unit)
    gradient_norm = jnp.sqrt(square_total).reshape(1)
    mean_alpha = lax.optimization_barrier(jnp.mean(model_next[1:], axis=1))
    return (outputs.reshape(TOKENS, D).astype(jnp.bfloat16), delta_tokens.reshape(TOKENS, D), attention_next, attention_next.astype(jnp.bfloat16), moment_attention, square_attention, gated_next, gated_next.astype(jnp.bfloat16), moment_gated, square_gated, model_next, moment_model, square_model, unit_next, moment_unit, square_unit, gradient_norm, mean_alpha)
```

```python
import functools
import math

import jax
import jax.numpy as jnp
from jax import lax
from jax.experimental import pallas as pl
from jax.experimental.pallas import tpu as pltpu
from jax.sharding import PartitionSpec as P

D = 1024
HEAD = 64
FF = 4096
STEP = 4
BLK = 256

EPSILON = 1e-06
ADAM_EPSILON = 1e-08
BETA_ONE = 0.5
BETA_TWO = 0.5
LEARN_RATE = 1.5

F32 = jnp.float32
BF16 = jnp.bfloat16
SCALE_MODEL = D**-0.5
SCALE_HIDDEN = FF**-0.5
SCORE = HEAD**-0.5 * math.log2(math.e)
NEVER = 1 << 24


def dot_nt(left, right):
    return lax.dot_general(left, right, (((1,), (1,)), ((), ())), preferred_element_type=F32)


def dot_nn(left, right):
    return lax.dot_general(left, right, (((1,), (0,)), ((), ())), preferred_element_type=F32)


def split_low(values):
    high = values.astype(BF16)
    return high, (values - high.astype(F32)).astype(BF16)


def params():
    return pltpu.CompilerParams(vmem_limit_bytes=48 << 20)


def cost(flops, traffic, transcendentals=0):
    return pl.CostEstimate(
        flops=int(flops), bytes_accessed=int(traffic), transcendentals=int(transcendentals)
    )


def like(shape, dtype):
    return jax.ShapeDtypeStruct(shape, dtype)


def whole(*shape):
    return pl.BlockSpec(shape, lambda *_: (0,) * len(shape))


def rows(count, width):
    return pl.BlockSpec((count, width), lambda i, *_: (i, 0))


def head_matrix(width):
    row = lax.broadcasted_iota(jnp.int32, (width, width), 0)
    column = lax.broadcasted_iota(jnp.int32, (width, width), 1)
    return jnp.where(row // HEAD == column // HEAD, 1.0, 0.0).astype(BF16)


def head_mean(values, ones):
    high, low = split_low(values)
    return (dot_nn(high, ones) + dot_nn(low, ones)) * (1.0 / HEAD)


def project_kernel(
    pieces, me_ref, *refs
):
    piece_refs, (w_ref, gain_ref, all_ref, raw_ref, q_ref, k_ref, v_ref) = refs[:pieces], refs[pieces:]
    width = piece_refs[0].shape[1]
    for step, piece in enumerate(piece_refs):
        start = pl.multiple_of(jnp.bitwise_xor(me_ref[0], step) * width, width)
        all_ref[:, pl.ds(start, width)] = piece[...]
    projected = dot_nt(all_ref[...], w_ref[...]) * SCALE_MODEL
    raw_ref[...] = projected[:, : 2 * width]
    ones = head_matrix(width)
    for place, out in enumerate((q_ref, k_ref)):
        values = projected[:, place * width : (place + 1) * width]
        factor = lax.rsqrt(head_mean(values * values, ones) + EPSILON)
        out[...] = (values * factor * gain_ref[...]).astype(BF16)
    v_ref[...] = projected[:, 2 * width :].astype(BF16)


def project(me, pieces, weight, gain):
    count, width = pieces[0].shape
    depth = width * len(pieces)
    return pl.pallas_call(
        functools.partial(project_kernel, len(pieces)),
        grid_spec=pltpu.PrefetchScalarGridSpec(
            num_scalar_prefetch=1,
            grid=(count // BLK,),
            in_specs=[rows(BLK, width)] * len(pieces) + [whole(3 * width, depth), whole(1, width)],
            out_specs=[rows(BLK, depth), rows(BLK, 2 * width)] + [rows(BLK, width)] * 3,
        ),
        out_shape=[like((count, depth), BF16), like((count, 2 * width), F32)]
        + [like((count, width), BF16)] * 3,
        compiler_params=params(),
        cost_estimate=cost(6 * count * width * depth, count * (4 * depth + 14 * width)),
        name="project",
    )(me, *pieces, weight, gain)


def seq_start(place, starts):
    found = jnp.zeros_like(place)
    for start in starts:
        found = jnp.where(place >= start, start, found)
    return found


def later_starts(length_ref, count):
    starts, total = [], jnp.int32(0)
    for position in range(count - 1):
        total = total + length_ref[position]
        starts.append(total)
    return starts


def attend_kernel(count, length_ref, pad_ref, q_ref, k_ref, v_ref, o_ref, aux_ref, acc_ref):
    step = pl.program_id(0)
    first_row = step * BLK
    starts = later_starts(length_ref, count)
    first = seq_start(first_row, starts) // BLK
    lane = lax.broadcasted_iota(jnp.int32, (BLK, 128), 1)
    left = lane < HEAD
    heads = q_ref.shape[1] // HEAD
    zero = jnp.zeros((BLK, 128), BF16)
    one = jnp.ones((BLK, 128), BF16)
    sides = [left if head % 2 == 0 else ~left for head in range(heads)]
    columns = [slice(head // 2 * 128, (head // 2 + 1) * 128) for head in range(heads)]
    queries = [jnp.where(sides[h], q_ref[:, columns[h]], zero) for h in range(heads)]
    acc_ref[...] = jnp.zeros_like(acc_ref)
    row = first_row + lax.broadcasted_iota(jnp.int32, (BLK, 1), 0)
    row_start = seq_start(row, starts)

    def body(block, carry):
        key_rows = pl.ds(pl.multiple_of(block * BLK, BLK), BLK)
        key = block * BLK + lax.broadcasted_iota(jnp.int32, (1, BLK), 1)
        code = jnp.where(pad_ref[:, key_rows] == 1, key, NEVER)
        mask = ((code >= row_start) & (code <= row)) | (key == row)
        for h in range(heads):
            value = jnp.where(sides[h], v_ref[key_rows, columns[h]], one)
            scores = dot_nt(queries[h], k_ref[key_rows, columns[h]])
            powers = jnp.where(mask, jnp.exp2(scores * SCORE), 0.0).astype(BF16)
            acc_ref[h] += dot_nn(powers, value)
        return carry

    lax.fori_loop(first, step + 1, body, 0)
    for pair in range(heads // 2):
        even, odd = acc_ref[2 * pair], acc_ref[2 * pair + 1]
        total = jnp.where(left, odd, even)
        mixed = jnp.where(left, even, odd)
        o_ref[:, pair * 128 : (pair + 1) * 128] = (mixed / pltpu.roll(total, HEAD, 1)).astype(BF16)
        high, low = split_low(jnp.log2(total) * (-1.0 / SCORE))
        aux_ref[:, pair * 128 : (pair + 1) * 128] = jnp.where(
            lax.rem(lane, HEAD) < HEAD // 2, high, low
        )


def attend(lengths, pad_row, queries, keys, values):
    count, width = queries.shape
    heads = width // HEAD
    return pl.pallas_call(
        functools.partial(attend_kernel, lengths.shape[0]),
        grid_spec=pltpu.PrefetchScalarGridSpec(
            num_scalar_prefetch=1,
            grid=(count // BLK,),
            in_specs=[whole(1, count), rows(BLK, width), whole(count, width), whole(count, width)],
            out_specs=[rows(BLK, width)] * 2,
            scratch_shapes=[pltpu.VMEM((heads, BLK, 128), F32)],
        ),
        out_shape=[like((count, width), BF16)] * 2,
        compiler_params=params(),
        cost_estimate=cost(4 * count * count * width, 10 * count * width, count * count * heads // 3),
        name="attend",
    )(lengths, pad_row, queries, keys, values)


def attend_back_kernel(
    count, pieces, length_ref, me_ref, pad_ref, q_ref, aux_ref, k_ref, v_ref, o_ref, *refs
):
    piece_refs = refs[:pieces]
    dqt_ref, dk_ref, dv_ref, do_ref, inner_ref, key_acc, value_acc = refs[pieces:]
    step = pl.program_id(0)
    tokens, width = q_ref.shape
    heads = width // HEAD
    starts = later_starts(length_ref, count)
    lane = lax.broadcasted_iota(jnp.int32, (BLK, 128), 1)
    left = lane < HEAD
    zero = jnp.zeros((BLK, 128), BF16)
    one = jnp.ones((BLK, 128), BF16)
    sides = [left if head % 2 == 0 else ~left for head in range(heads)]
    columns = [slice(head // 2 * 128, (head // 2 + 1) * 128) for head in range(heads)]

    @pl.when(step == 0)
    def prepare():
        dqt_ref[...] = jnp.zeros_like(dqt_ref)
        part = tokens // pieces
        for place, piece in enumerate(piece_refs):
            start = pl.multiple_of(jnp.bitwise_xor(me_ref[0], place) * part, part)
            do_ref[pl.ds(start, part), :] = piece[...]
        row = lax.broadcasted_iota(jnp.int32, (128, 128), 0)
        column = lax.broadcasted_iota(jnp.int32, (128, 128), 1)
        other = jnp.where(row // HEAD != column // HEAD, 1.0, 0.0).astype(BF16)

        def inner(block, carry):
            here = pl.ds(pl.multiple_of(block * BLK, BLK), BLK)
            for pair in range(heads // 2):
                tile = slice(pair * 128, (pair + 1) * 128)
                high, low = split_low(do_ref[here, tile].astype(F32) * o_ref[here, tile].astype(F32))
                high, low = split_low(-(dot_nn(high, other) + dot_nn(low, other)))
                inner_ref[here, tile] = jnp.where(lax.rem(lane, HEAD) < HEAD // 2, high, low)
            return carry

        lax.fori_loop(0, tokens // BLK, inner, 0)

    key_rows = pl.ds(pl.multiple_of(step * BLK, BLK), BLK)
    last_key = step * BLK + BLK - 1
    end = jnp.int32(tokens)
    for start in reversed(starts):
        end = jnp.where(last_key < start, start, end)
    last = (end - 1) // BLK
    key_acc[...] = jnp.zeros_like(key_acc)
    value_acc[...] = jnp.zeros_like(value_acc)
    turned = jnp.transpose(k_ref[key_rows, :].astype(F32)).astype(BF16)
    keys, values = [], []
    for h in range(heads):
        hot = jnp.where((lax.rem(lane, HEAD // 2) == 0) & (~sides[h]), one, zero)
        for source, into in ((k_ref, keys), (v_ref, values)):
            tile = jnp.where(sides[h], source[key_rows, columns[h]], zero)
            into.append(jnp.concatenate([tile, hot], axis=1))
    key = step * BLK + lax.broadcasted_iota(jnp.int32, (BLK, 1), 0)
    code = jnp.where(pad_ref[key_rows, :] == 1, key, NEVER)

    def body(block, carry):
        here = pl.ds(pl.multiple_of(block * BLK, BLK), BLK)
        row = block * BLK + lax.broadcasted_iota(jnp.int32, (1, BLK), 1)
        mask = ((code >= seq_start(row, starts)) & (code <= row)) | (key == row)
        for h in range(heads):
            query, delta = q_ref[here, columns[h]], do_ref[here, columns[h]]
            scores = dot_nt(keys[h], jnp.concatenate([query, aux_ref[here, columns[h]]], axis=1))
            delta_probs = dot_nt(
                values[h], jnp.concatenate([delta, inner_ref[here, columns[h]]], axis=1)
            )
            probs = jnp.where(mask, jnp.exp2(scores * SCORE), 0.0)
            delta_scores = (probs * delta_probs).astype(BF16)
            value_acc[h] += dot_nn(probs.astype(BF16), delta)
            key_acc[h] += dot_nn(delta_scores, query)
            head_rows = slice(h * HEAD, (h + 1) * HEAD)
            dqt_ref[head_rows, here] += dot_nn(turned[head_rows, :], delta_scores)
        return carry

    lax.fori_loop(step, last + 1, body, 0)
    for pair in range(heads // 2):
        tile = slice(pair * 128, (pair + 1) * 128)
        dk_ref[:, tile] = jnp.where(left, key_acc[2 * pair], key_acc[2 * pair + 1])
        dv_ref[:, tile] = jnp.where(left, value_acc[2 * pair], value_acc[2 * pair + 1])


def attend_back(lengths, me, pad_column, queries, aux, keys, values, mixed, delta_pieces):
    count, width = queries.shape
    heads = width // HEAD
    pieces = len(delta_pieces)
    return pl.pallas_call(
        functools.partial(attend_back_kernel, lengths.shape[0], pieces),
        grid_spec=pltpu.PrefetchScalarGridSpec(
            num_scalar_prefetch=2,
            grid=(count // BLK,),
            in_specs=[whole(count, 1)]
            + [whole(count, width)] * 5
            + [whole(count // pieces, width)] * pieces,
            out_specs=[whole(width, count), rows(BLK, width), rows(BLK, width)],
            scratch_shapes=[
                pltpu.VMEM((count, width), BF16),
                pltpu.VMEM((count, width), BF16),
                pltpu.VMEM((heads, BLK, 128), F32),
                pltpu.VMEM((heads, BLK, 128), F32),
            ],
        ),
        out_shape=[like((width, count), F32), like((count, width), F32), like((count, width), F32)],
        compiler_params=params(),
        cost_estimate=cost(8 * count * count * width, 22 * count * width, count * count * heads // 3),
        name="attend_back",
    )(lengths, me, pad_column, queries, aux, keys, values, mixed, *delta_pieces)


def unit_of(values):
    factor = lax.rsqrt(jnp.mean(values * values, axis=1, keepdims=True) + EPSILON)
    return values * factor, factor


def unit_back(delta, unit, factor):
    return factor * (delta - unit * jnp.mean(delta * unit, axis=1, keepdims=True))


def mixer_kernel(pieces, *refs):
    mixed_refs, out_weights = refs[:pieces], refs[pieces : 2 * pieces]
    tokens_ref, alpha_ref, low_ref, one_ref, unit_ref, unit_factor, one_factor = refs[2 * pieces :]
    branch = dot_nn(mixed_refs[0][...], out_weights[0][...])
    for mixed, weight in zip(mixed_refs[1:], out_weights[1:]):
        branch += dot_nn(mixed[...], weight[...])
    unit, factor = unit_of(branch * SCALE_MODEL)
    unit_ref[...] = unit
    unit_factor[...] = jnp.broadcast_to(factor, unit_factor.shape)
    residual = tokens_ref[...].astype(F32)
    hidden, factor = unit_of(residual + alpha_ref[...] * (unit - residual))
    one_ref[...] = hidden
    one_factor[...] = jnp.broadcast_to(factor, one_factor.shape)
    low_ref[...] = hidden.astype(BF16)


def mixer(mixed_pieces, out_weights, me, tokens_all, alpha):
    count, width = mixed_pieces[0].shape
    pieces = len(mixed_pieces)
    depth = tokens_all.shape[1]
    blocks = count // BLK
    kernel = functools.partial(mixer_kernel, pieces)
    return pl.pallas_call(
        lambda me_ref, *refs: kernel(*refs),
        grid_spec=pltpu.PrefetchScalarGridSpec(
            num_scalar_prefetch=1,
            grid=(blocks,),
            in_specs=[rows(BLK, width)] * pieces
            + [whole(width, depth)] * pieces
            + [
                pl.BlockSpec((BLK, depth), lambda i, me_ref: (me_ref[0] * blocks + i, 0)),
                whole(1, depth),
            ],
            out_specs=[rows(BLK, depth)] * 3 + [rows(BLK, 128)] * 2,
        ),
        out_shape=[like((count, depth), BF16)]
        + [like((count, depth), F32)] * 2
        + [like((count, 128), F32)] * 2,
        compiler_params=params(),
        cost_estimate=cost(2 * count * depth * depth, 16 * count * depth + 2 * depth * depth),
        name="mixer",
    )(me, *mixed_pieces, *out_weights, tokens_all, alpha)


def turn_kernel(pieces, me_ref, *refs):
    own_ref, near_ref, far_ref, one_ref = refs[:4]
    seed_refs = refs[4 : 4 + pieces]
    pad_ref, alpha_ref = refs[4 + pieces : 6 + pieces]
    out_refs = refs[6 + pieces : 6 + 2 * pieces]
    low_ref, hidden_ref, alpha_sum, seed, layer = refs[6 + 2 * pieces :]
    width = seed_refs[0].shape[1]
    starts = [
        pl.multiple_of(jnp.bitwise_xor(me_ref[0], place) * width, width) for place in range(pieces)
    ]
    for start, piece in zip(starts, seed_refs):
        seed[:, pl.ds(start, width)] = piece[...]

    @pl.when(pl.program_id(0) == 0)
    def clear():
        alpha_sum[...] = jnp.zeros_like(alpha_sum)

    branch = (own_ref[...].astype(F32) + near_ref[...].astype(F32)) + far_ref[...].astype(F32)
    unit, unit_factor = unit_of(branch)
    hidden = one_ref[...]
    alpha = alpha_ref[...]
    layer_rows, layer_factor = unit_of(hidden + alpha * (unit - hidden))
    layer[...] = layer_rows.astype(BF16)
    for start, out in zip(starts, out_refs):
        out[...] = layer[:, pl.ds(start, width)]
    delta = unit_back(seed[...].astype(F32) * pad_ref[...], layer_rows, layer_factor)
    alpha_sum[...] += jnp.sum(delta * (unit - hidden), axis=0, keepdims=True)
    hidden_ref[...] = (1.0 - alpha) * delta
    low_ref[...] = unit_back(alpha * delta, unit, unit_factor).astype(BF16)


def turn(me, own, near, far, hidden_one, seed_pieces, pad_rows, alpha):
    count, depth = hidden_one.shape
    pieces = len(seed_pieces)
    width = depth // pieces
    return pl.pallas_call(
        functools.partial(turn_kernel, pieces),
        grid_spec=pltpu.PrefetchScalarGridSpec(
            num_scalar_prefetch=1,
            grid=(count // BLK,),
            in_specs=[rows(BLK, depth)] * 4
            + [rows(BLK, width)] * pieces
            + [rows(BLK, 1), whole(1, depth)],
            out_specs=[rows(BLK, width)] * pieces
            + [rows(BLK, depth), rows(BLK, depth), whole(1, depth)],
            scratch_shapes=[pltpu.VMEM((BLK, depth), BF16)] * 2,
        ),
        out_shape=[like((count, width), BF16)] * pieces
        + [like((count, depth), BF16), like((count, depth), F32), like((1, depth), F32)],
        compiler_params=params(),
        cost_estimate=cost(40 * count * depth, 20 * count * depth),
        name="turn",
    )(me, own, near, far, hidden_one, *seed_pieces, pad_rows, alpha)


def mixer_back_kernel(pieces, *refs):
    hidden_ref, own_ref, near_ref, far_ref, one_ref, unit_ref = refs[:6]
    one_factor, unit_factor, tokens_ref, alpha_ref = refs[6:10]
    out_weights = refs[10 : 10 + pieces]
    delta_refs = refs[10 + pieces : 10 + 2 * pieces]
    low_ref, direct_ref, alpha_sum = refs[10 + 2 * pieces :]

    @pl.when(pl.program_id(0) == 0)
    def clear():
        alpha_sum[...] = jnp.zeros_like(alpha_sum)

    delta = hidden_ref[...] + (
        (own_ref[...].astype(F32) + near_ref[...].astype(F32)) + far_ref[...].astype(F32)
    )
    unit = unit_ref[...]
    alpha = alpha_ref[...]
    delta = unit_back(delta, one_ref[...], one_factor[:, :1])
    alpha_sum[...] += jnp.sum(delta * (unit - tokens_ref[...].astype(F32)), axis=0, keepdims=True)
    direct_ref[...] = (1.0 - alpha) * delta
    low = unit_back(alpha * delta, unit, unit_factor[:, :1]).astype(BF16)
    low_ref[...] = low
    for weight, out in zip(out_weights, delta_refs):
        out[...] = (dot_nt(low, weight[...]) * SCALE_MODEL).astype(BF16)


def mixer_back(
    me, hidden, own, near, far, one, unit, one_factor, unit_factor, tokens_all, alpha, out_weights
):
    count, depth = one.shape
    pieces = len(out_weights)
    width = depth // pieces
    blocks = count // BLK
    kernel = functools.partial(mixer_back_kernel, pieces)
    return pl.pallas_call(
        lambda me_ref, *refs: kernel(*refs),
        grid_spec=pltpu.PrefetchScalarGridSpec(
            num_scalar_prefetch=1,
            grid=(blocks,),
            in_specs=[rows(BLK, depth)] * 6
            + [rows(BLK, 128)] * 2
            + [
                pl.BlockSpec((BLK, depth), lambda i, me_ref: (me_ref[0] * blocks + i, 0)),
                whole(1, depth),
            ]
            + [whole(width, depth)] * pieces,
            out_specs=[rows(BLK, width)] * pieces
            + [rows(BLK, depth), rows(BLK, depth), whole(1, depth)],
        ),
        out_shape=[like((count, width), BF16)] * pieces
        + [like((count, depth), BF16), like((count, depth), F32), like((1, depth), F32)],
        compiler_params=params(),
        cost_estimate=cost(2 * count * depth * depth, 28 * count * depth + 2 * depth * depth),
        name="mixer_back",
    )(me, hidden, own, near, far, one, unit, one_factor, unit_factor, tokens_all, alpha, *out_weights)


def gated_kernel(
    half, first_ref, second_ref, up_w, gate_w, down_w, gain_ref, all_ref, up_ref, gate_ref, mid_ref, out_ref
):
    step = pl.program_id(0)

    @pl.when(step < half)
    def from_first():
        all_ref[...] = first_ref[...]

    @pl.when(step >= half)
    def from_second():
        all_ref[...] = second_ref[...]

    hidden = all_ref[...]
    up = dot_nt(hidden, up_w[...]) * SCALE_MODEL
    gate = dot_nt(hidden, gate_w[...]) * SCALE_MODEL
    up_ref[...] = up.astype(BF16)
    gate_ref[...] = gate.astype(BF16)
    scaled = gain_ref[1:2, :] * gate
    middle = (gain_ref[0:1, :] * up * scaled * jax.nn.sigmoid(scaled)).astype(BF16)
    mid_ref[...] = middle
    out_ref[...] = (dot_nn(middle, down_w[...]) * SCALE_HIDDEN).astype(BF16)


def two_halves(block, half, depth):
    return [
        pl.BlockSpec((block, depth), lambda i: (jnp.minimum(i, half - 1), 0)),
        pl.BlockSpec((block, depth), lambda i: (jnp.maximum(i - half, 0), 0)),
    ]


def gated(first, second, up_w, gate_w, down_w, gains):
    count, depth = first.shape
    hidden = up_w.shape[0]
    half = count // BLK
    return pl.pallas_call(
        functools.partial(gated_kernel, half),
        grid=(2 * half,),
        in_specs=two_halves(BLK, half, depth) + [whole(hidden, depth)] * 3 + [whole(2, hidden)],
        out_specs=[rows(BLK, depth)] + [rows(BLK, hidden)] * 3 + [rows(BLK, depth)],
        out_shape=[like((2 * count, depth), BF16)]
        + [like((2 * count, hidden), BF16)] * 3
        + [like((2 * count, depth), BF16)],
        compiler_params=params(),
        cost_estimate=cost(
            12 * count * depth * hidden,
            12 * count * (depth + hidden) + 6 * depth * hidden,
            2 * count * hidden,
        ),
        name="gated",
    )(first, second, up_w, gate_w, down_w, gains)


def gated_back_kernel(
    half,
    first_ref,
    second_ref,
    up_ref,
    gate_ref,
    up_w,
    gate_w,
    down_w,
    gain_ref,
    all_ref,
    du_ref,
    dg_ref,
    out_ref,
    unit_ref,
):
    step = pl.program_id(0)

    @pl.when(step < half)
    def from_first():
        all_ref[...] = first_ref[...]

    @pl.when(step >= half)
    def from_second():
        all_ref[...] = second_ref[...]

    @pl.when(step == 0)
    def clear():
        unit_ref[...] = jnp.zeros_like(unit_ref)

    delta_middle = dot_nt(all_ref[...], down_w[...]) * SCALE_HIDDEN
    up = up_ref[...].astype(F32)
    gate = gate_ref[...].astype(F32)
    scaled = gain_ref[1:2, :] * gate
    sigmoid = jax.nn.sigmoid(scaled)
    shared = delta_middle * sigmoid
    delta_up = shared * scaled
    delta_gate = shared * (gain_ref[0:1, :] * up) * (1.0 + scaled * (1.0 - sigmoid))
    unit_ref[0:1, :] += jnp.sum(delta_up * up, axis=0, keepdims=True)
    unit_ref[1:2, :] += jnp.sum(delta_gate * gate, axis=0, keepdims=True)
    up_low = (gain_ref[0:1, :] * delta_up).astype(BF16)
    gate_low = (gain_ref[1:2, :] * delta_gate).astype(BF16)
    du_ref[...] = up_low
    dg_ref[...] = gate_low
    out_ref[...] = (
        (dot_nn(up_low, up_w[...]) + dot_nn(gate_low, gate_w[...])) * SCALE_MODEL
    ).astype(BF16)


def gated_back(first, second, up, gate, up_w, gate_w, down_w, gains):
    count, depth = first.shape
    hidden = up_w.shape[0]
    half = count // BLK
    return pl.pallas_call(
        functools.partial(gated_back_kernel, half),
        grid=(2 * half,),
        in_specs=two_halves(BLK, half, depth)
        + [rows(BLK, hidden)] * 2
        + [whole(hidden, depth)] * 3
        + [whole(2, hidden)],
        out_specs=[rows(BLK, depth)] + [rows(BLK, hidden)] * 2 + [rows(BLK, depth), whole(2, hidden)],
        out_shape=[like((2 * count, depth), BF16)]
        + [like((2 * count, hidden), BF16)] * 2
        + [like((2 * count, depth), BF16), like((2, hidden), F32)],
        compiler_params=params(),
        cost_estimate=cost(
            12 * count * depth * hidden,
            12 * count * (depth + hidden) + 6 * depth * hidden,
            2 * count * hidden,
        ),
        name="gated_back",
    )(first, second, up, gate, up_w, gate_w, down_w, gains)


def project_back_kernel(pieces, me_ref, dqt_ref, dk_ref, dv_ref, raw_ref, gain_ref, w_ref, direct_ref, *refs):
    low_ref, scale_sum, total = refs[0], refs[1 + pieces], refs[2 + pieces]
    part_refs = refs[1 : 1 + pieces]
    step = pl.program_id(0)
    width = dk_ref.shape[1]
    scale_head = HEAD**-0.5

    @pl.when(step == 0)
    def clear():
        scale_sum[...] = jnp.zeros_like(scale_sum)

    ones = head_matrix(width)
    gain = gain_ref[...]
    for place, delta in enumerate((jnp.transpose(dqt_ref[...]), dk_ref[...])):
        here = slice(place * width, (place + 1) * width)
        values = raw_ref[:, here]
        factor = lax.rsqrt(head_mean(values * values, ones) + EPSILON)
        unit = values * factor
        delta = delta * scale_head
        scale_sum[...] += jnp.sum(delta * unit, axis=0, keepdims=True)
        delta = gain * delta
        low_ref[:, here] = (factor * (delta - unit * head_mean(delta * unit, ones))).astype(BF16)
    low_ref[:, 2 * width :] = dv_ref[...].astype(BF16)
    total[...] = dot_nn(low_ref[...], w_ref[...]) * SCALE_MODEL
    own_blocks = direct_ref.shape[0] // BLK

    @pl.when(step // own_blocks == me_ref[0])
    def add_direct():
        start = pl.multiple_of(lax.rem(step, own_blocks) * BLK, BLK)
        total[...] += direct_ref[pl.ds(start, BLK), :]

    part = total.shape[1] // pieces
    for place, out in enumerate(part_refs):
        start = pl.multiple_of(jnp.bitwise_xor(me_ref[0], place) * part, part)
        out[...] = total[:, pl.ds(start, part)].astype(BF16)


def project_back(me, pieces, dqt, dk, dv, raw, gain, weight, direct):
    count, width = dk.shape
    depth = weight.shape[1]
    part = depth // pieces
    return pl.pallas_call(
        functools.partial(project_back_kernel, pieces),
        grid_spec=pltpu.PrefetchScalarGridSpec(
            num_scalar_prefetch=1,
            grid=(count // BLK,),
            in_specs=[
                pl.BlockSpec((width, BLK), lambda i, *_: (0, i)),
                rows(BLK, width),
                rows(BLK, width),
                rows(BLK, 2 * width),
                whole(1, width),
                whole(3 * width, depth),
                whole(*direct.shape),
            ],
            out_specs=[rows(BLK, 3 * width)] + [rows(BLK, part)] * pieces + [whole(1, width)],
            scratch_shapes=[pltpu.VMEM((BLK, depth), F32)],
        ),
        out_shape=[like((count, 3 * width), BF16)]
        + [like((count, part), BF16)] * pieces
        + [like((1, width), F32)],
        compiler_params=params(),
        cost_estimate=cost(6 * count * width * depth, count * (26 * width + 2 * depth)),
        name="project_back",
    )(me, dqt, dk, dv, raw, gain, weight, direct)


def trade(value, axis, offset):
    size = lax.axis_size(axis)
    return lax.ppermute(value, axis, [(i, i ^ offset) for i in range(size)])


def sum_over(value, axis):
    offset = 1
    while offset < lax.axis_size(axis):
        value = value + trade(value, axis, offset)
        offset *= 2
    return value


def gather_pieces(value):
    near = trade(value, "dim", 1)
    far = trade(value, "dim", 2)
    return [value, near, far, trade(far, "dim", 1)]


def scatter_sum(near, far):
    own, pair = near
    across, corner = far
    corner = trade(corner, "dim", 1)
    across = (across.astype(F32) + corner.astype(F32)).astype(BF16)
    return own, trade(pair, "dim", 1), trade(across, "dim", 2)


def grad_of(left_pieces, right_pieces, scale):
    total = None
    for left, right in zip(left_pieces, right_pieces):
        term = jnp.einsum("tr,td->rd", left, right, preferred_element_type=F32)
        total = term if total is None else total + term
    return (total * scale).astype(BF16)


def moment_update(weights, gradient, moment, square, fix_first, fix_second):
    moment_next = BETA_ONE * moment + (1.0 - BETA_ONE) * gradient
    square_next = BETA_TWO * square + (1.0 - BETA_TWO) * gradient * gradient
    stepped = weights - LEARN_RATE * (moment_next / fix_first) / (
        jnp.sqrt(square_next / fix_second) + ADAM_EPSILON
    )
    return (stepped, moment_next, square_next)


def local(
    inputs,
    cotangent,
    lengths,
    pad_mask,
    attention_weights,
    gated_weights,
    model_gains,
    unit_gains,
    attention_moment,
    attention_square,
    gated_moment,
    gated_square,
    model_moment,
    model_square,
    unit_moment,
    unit_square,
):
    token_count, width = inputs.shape
    parts = lax.axis_size("dim")
    hidden_here = gated_weights.shape[1]
    own_count = token_count // parts
    place = lax.axis_index("dim")
    me = place.astype(jnp.int32).reshape(1)
    length_row = lengths[0]

    def token_rows(value, offset):
        return lax.dynamic_slice_in_dim(value, (place ^ offset) * own_count, own_count, 0)

    def to_tokens(value):
        return [token_rows(value, 0)] + [
            trade(token_rows(value, r), "dim", r) for r in range(1, parts)
        ]

    token_pieces = gather_pieces(inputs)
    attention_low = lax.all_gather(attention_weights.astype(BF16), "tok", axis=2, tiled=True)
    weight_in = attention_low[:3].reshape(3 * width, D)
    out_weights = gather_pieces(attention_low[3])
    expand_low = lax.all_gather(gated_weights[:2].astype(BF16), "tok", axis=2, tiled=True)
    down_low = lax.all_gather(gated_weights[2].astype(BF16), "tok", axis=1, tiled=True)
    up_low, gate_low = expand_low[0], expand_low[1]
    alphas = sum_over(
        lax.dynamic_update_slice(jnp.zeros((2, D), F32), model_gains[1:], (0, place * width)), "dim"
    )
    alpha_mixer, alpha_gated = alphas[:1], alphas[1:]
    score_gain = model_gains[:1]

    tokens_all, raw, queries, keys, values = project(me, token_pieces, weight_in, score_gain)
    mixed, aux = attend(length_row, pad_mask[None, :], queries, keys, values)
    mixed_pieces = to_tokens(mixed)
    seed_pieces = to_tokens(cotangent)
    hidden_low, hidden_one, mixer_unit, mixer_factor, one_factor = mixer(
        mixed_pieces, out_weights, me, tokens_all, alpha_mixer
    )

    h_own, h_near, h_far, h_corner = gather_pieces(hidden_low)
    h_one, up_one, gate_one, mid_one, part_one = gated(
        h_own, h_near, up_low, gate_low, down_low, unit_gains
    )
    h_two, up_two, gate_two, mid_two, part_two = gated(
        h_far, h_corner, up_low, gate_low, down_low, unit_gains
    )
    own, near, far = scatter_sum(
        (part_one[:own_count], part_one[own_count:]), (part_two[:own_count], part_two[own_count:])
    )
    pad_rows = token_rows(pad_mask, 0).astype(F32)[:, None]
    *layer_pieces, delta_branch, delta_hidden, sum_gated = turn(
        me, own, near, far, hidden_one, seed_pieces, pad_rows, alpha_gated
    )
    layer_out = jnp.zeros((token_count, width), BF16)
    for r, piece in enumerate(layer_pieces):
        piece = piece if r == 0 else trade(piece, "dim", r)
        layer_out = lax.dynamic_update_slice(layer_out, piece, ((place ^ r) * own_count, 0))

    b_own, b_near, b_far, b_corner = gather_pieces(delta_branch)
    b_one, du_one, dg_one, back_one, unit_sum_one = gated_back(
        b_own, b_near, up_one, gate_one, up_low, gate_low, down_low, unit_gains
    )
    b_two, du_two, dg_two, back_two, unit_sum_two = gated_back(
        b_far, b_corner, up_two, gate_two, up_low, gate_low, down_low, unit_gains
    )
    own, near, far = scatter_sum(
        (back_one[:own_count], back_one[own_count:]), (back_two[:own_count], back_two[own_count:])
    )
    delta_down = grad_of((mid_one, mid_two), (b_one, b_two), SCALE_HIDDEN)
    delta_up = grad_of((du_one, du_two), (h_one, h_two), SCALE_MODEL)
    delta_gate = grad_of((dg_one, dg_two), (h_one, h_two), SCALE_MODEL)
    down_grad = lax.psum_scatter(delta_down, "tok", scatter_dimension=1, tiled=True)
    up_grad = lax.psum_scatter(delta_up, "tok", scatter_dimension=1, tiled=True)
    gate_grad = lax.psum_scatter(delta_gate, "tok", scatter_dimension=1, tiled=True)

    *delta_pieces, mixer_low, delta_direct, sum_mixer = mixer_back(
        me,
        delta_hidden,
        own,
        near,
        far,
        hidden_one,
        mixer_unit,
        one_factor,
        mixer_factor,
        tokens_all,
        alpha_mixer,
        out_weights,
    )
    delta_pieces = [delta_pieces[0]] + [
        trade(piece, "dim", r) for r, piece in enumerate(delta_pieces) if r
    ]
    delta_out = [grad_of((piece,), (mixer_low,), SCALE_MODEL) for piece in mixed_pieces]
    own, near, far = scatter_sum(delta_out[:2], delta_out[2:])
    delta_out = ((own.astype(F32) + near.astype(F32)) + far.astype(F32)).astype(BF16)
    dqt, dk, dv = attend_back(
        length_row, me, pad_mask[:, None], queries, aux, keys, values, mixed, delta_pieces
    )
    delta_project, *input_parts, scale_sum = project_back(
        me, parts, dqt, dk, dv, raw, score_gain, weight_in, delta_direct
    )
    delta_in = grad_of((delta_project,), (tokens_all,), SCALE_MODEL)
    own, near, far = scatter_sum(input_parts[:2], input_parts[2:])
    input_gradient = (own.astype(F32) + near.astype(F32)) + far.astype(F32)
    attention_grad = lax.psum_scatter(
        jnp.concatenate([delta_in, delta_out], axis=0), "tok", scatter_dimension=1, tiled=True
    )
    attention_grad = attention_grad.astype(F32).reshape(4, width, -1)
    gated_grad = jnp.stack([up_grad, gate_grad, down_grad]).astype(F32)

    alpha_sums = lax.dynamic_slice_in_dim(
        sum_over(jnp.concatenate([sum_mixer, sum_gated], axis=0), "dim"), place * width, width, 1
    )
    gains_sum = sum_over(
        jnp.concatenate(
            [scale_sum.reshape(-1), alpha_sums.reshape(-1), (unit_sum_one + unit_sum_two).reshape(-1)]
        ),
        "tok",
    )
    model_grad = gains_sum[: 3 * width].reshape(3, width)
    unit_grad = gains_sum[3 * width :].reshape(2, hidden_here)

    fix_first = 1.0 - BETA_ONE**STEP
    fix_second = 1.0 - BETA_TWO**STEP
    attention_stepped, moment_attention, square_attention = moment_update(
        attention_weights, attention_grad, attention_moment, attention_square, fix_first, fix_second
    )
    gated_stepped, moment_gated, square_gated = moment_update(
        gated_weights, gated_grad, gated_moment, gated_square, fix_first, fix_second
    )
    model_next, moment_model, square_model = moment_update(
        model_gains, model_grad, model_moment, model_square, fix_first, fix_second
    )
    unit_next, moment_unit, square_unit = moment_update(
        unit_gains, unit_grad, unit_moment, unit_square, fix_first, fix_second
    )
    token_groups = lax.axis_size("tok")
    local_square = (
        jnp.sum(attention_grad * attention_grad)
        + jnp.sum(gated_grad * gated_grad)
        + (jnp.sum(model_grad * model_grad) + jnp.sum(unit_grad * unit_grad)) / token_groups
    )
    row_sums = sum_over(
        jnp.concatenate(
            [
                jnp.sum(attention_stepped * attention_stepped, axis=2).reshape(-1),
                jnp.sum(gated_stepped * gated_stepped, axis=2).reshape(-1),
                local_square.reshape(1),
            ]
        ),
        "tok",
    )
    attention_rows = row_sums[: 4 * width].reshape(4, width, 1)
    gated_rows = row_sums[4 * width : -1].reshape(3, hidden_here, 1)
    attention_next = attention_stepped * lax.rsqrt(attention_rows / D + EPSILON)
    gated_next = gated_stepped * lax.rsqrt(gated_rows / D + EPSILON)
    totals = sum_over(jnp.concatenate([row_sums[-1:], jnp.sum(model_next[1:], axis=1)]), "dim")
    gradient_norm = jnp.sqrt(totals[:1])
    mean_alpha = totals[1:] / D
    return (
        layer_out,
        input_gradient,
        attention_next,
        attention_next.astype(BF16),
        moment_attention,
        square_attention,
        gated_next,
        gated_next.astype(BF16),
        moment_gated,
        square_gated,
        model_next,
        moment_model,
        square_model,
        unit_next,
        moment_unit,
        square_unit,
        gradient_norm,
        mean_alpha,
    )


def solution(mesh):
    tokens = P("tok", "dim")
    weights = P(None, "dim", "tok")
    gains = P(None, "dim")
    in_specs = (tokens, tokens, P("tok", None), P("tok"), weights, weights, gains, gains)
    in_specs += (weights,) * 4 + (gains,) * 4
    out_specs = (tokens, tokens) + (weights,) * 8 + (gains,) * 6 + (P(), P())
    return jax.shard_map(local, mesh=mesh, in_specs=in_specs, out_specs=out_specs, check_vma=False)
```

```python
import functools
import math

import jax
import jax.numpy as jnp
from jax import lax
from jax.experimental import pallas as pl
from jax.experimental.pallas import tpu as pltpu
from jax.sharding import PartitionSpec as P

D = 1024
HEAD = 64
FF = 4096
STEP = 4
BLK = 256

EPSILON = 1e-06
ADAM_EPSILON = 1e-08
BETA_ONE = 0.5
BETA_TWO = 0.5
LEARN_RATE = 1.5

F32 = jnp.float32
BF16 = jnp.bfloat16
SCALE_MODEL = D**-0.5
SCALE_HIDDEN = FF**-0.5
SCORE = HEAD**-0.5 * math.log2(math.e)
NEVER = 1 << 24


def dot_nt(left, right):
    return lax.dot_general(left, right, (((1,), (1,)), ((), ())), preferred_element_type=F32)


def dot_nn(left, right):
    return lax.dot_general(left, right, (((1,), (0,)), ((), ())), preferred_element_type=F32)


def split_low(values):
    high = values.astype(BF16)
    return high, (values - high.astype(F32)).astype(BF16)


def params():
    return pltpu.CompilerParams(vmem_limit_bytes=60 << 20)


def cost(flops, traffic, transcendentals=0):
    return pl.CostEstimate(
        flops=int(flops) // 64, bytes_accessed=int(traffic) // 64, transcendentals=int(transcendentals) // 64
    )


def like(shape, dtype):
    return jax.ShapeDtypeStruct(shape, dtype)


def whole(*shape):
    return pl.BlockSpec(shape, lambda *_: (0,) * len(shape))


def rows(count, width):
    return pl.BlockSpec((count, width), lambda i, *_: (i, 0))


def head_matrix(width):
    row = lax.broadcasted_iota(jnp.int32, (width, width), 0)
    column = lax.broadcasted_iota(jnp.int32, (width, width), 1)
    return jnp.where(row // HEAD == column // HEAD, 1.0, 0.0).astype(BF16)


def head_mean(values, ones):
    high, low = split_low(values)
    return (dot_nn(high, ones) + dot_nn(low, ones)) * (1.0 / HEAD)


def project_kernel(pieces, me_ref, tok_ref, *refs):
    piece_refs = refs[:pieces]
    weight_refs = refs[pieces:-7]
    gain_ref, all_ref, raw_ref, q_ref, k_ref, v_ref, w_ref = refs[-7:]
    width = piece_refs[0].shape[1]
    if len(weight_refs) == 1:
        weight = weight_refs[0]
    else:
        weight = w_ref

        @pl.when(pl.program_id(0) == 0)
        def assemble_weight():
            place_columns(tok_ref[0], weight_refs, w_ref)

    place_columns(me_ref[0], piece_refs, all_ref)
    projected = dot_nt(all_ref[...], weight[...]) * SCALE_MODEL
    if weight is not w_ref:
        w_ref[...] = weight[...]
    raw_ref[...] = projected[:, : 2 * width]
    ones = head_matrix(width)
    for place, out in enumerate((q_ref, k_ref)):
        values = projected[:, place * width : (place + 1) * width]
        factor = lax.rsqrt(head_mean(values * values, ones) + EPSILON)
        out[...] = (values * factor * gain_ref[...]).astype(BF16)
    v_ref[...] = projected[:, 2 * width :].astype(BF16)


def place_columns(index, piece_refs, out_ref):
    width = piece_refs[0].shape[1]
    for offset, piece in enumerate(piece_refs):
        start = pl.multiple_of(jnp.bitwise_xor(index, offset) * width, width)
        out_ref[:, pl.ds(start, width)] = piece[...]


def piece_spec(piece, height, step):
    array, lead, block = piece
    width = array.shape[-1]
    if lead is None:
        return pl.BlockSpec((height, width), lambda i, *_: (block + step * i, 0))
    return pl.BlockSpec((None, height, width), lambda i, *_: (lead, block + step * i, 0))


def project(me, tok, pieces, weights, gain):
    count, width = pieces[0].shape
    depth = width * len(pieces)
    return pl.pallas_call(
        functools.partial(project_kernel, len(pieces)),
        grid_spec=pltpu.PrefetchScalarGridSpec(
            num_scalar_prefetch=2,
            grid=(count // BLK,),
            in_specs=[rows(BLK, width)] * len(pieces)
            + [piece_spec(weight, 3 * width, 0) for weight in weights]
            + [whole(1, width)],
            out_specs=[rows(BLK, depth), rows(BLK, 2 * width)]
            + [rows(BLK, width)] * 3
            + [whole(3 * width, depth)],
        ),
        out_shape=[like((count, depth), BF16), like((count, 2 * width), F32)]
        + [like((count, width), BF16)] * 3
        + [like((3 * width, depth), BF16)],
        compiler_params=params(),
        cost_estimate=cost(6 * count * width * depth, count * (4 * depth + 14 * width)),
        name="project",
    )(me, tok, *pieces, *[weight[0] for weight in weights], gain)


def assemble_kernel(tok_ref, *refs):
    place_columns(tok_ref[0], refs[:-1], refs[-1])


def assemble(tok, pieces, count):
    width = pieces[0][0].shape[-1]
    depth = width * len(pieces)
    return pl.pallas_call(
        assemble_kernel,
        grid_spec=pltpu.PrefetchScalarGridSpec(
            num_scalar_prefetch=1,
            grid=(count // BLK,),
            in_specs=[piece_spec(piece, BLK, 1) for piece in pieces],
            out_specs=rows(BLK, depth),
        ),
        out_shape=like((count, depth), BF16),
        compiler_params=params(),
        cost_estimate=cost(0, 4 * count * depth),
        name="assemble",
    )(tok, *[piece[0] for piece in pieces])


def seq_start(place, starts):
    found = jnp.zeros_like(place)
    for start in starts:
        found = jnp.where(place >= start, start, found)
    return found


def later_starts(length_ref, count):
    starts, total = [], jnp.int32(0)
    for position in range(count - 1):
        total = total + length_ref[position]
        starts.append(total)
    return starts


def attend_kernel(count, order, blocks, length_ref, me_ref, pad_ref, q_ref, k_ref, v_ref, *refs):
    mixed_ref, aux_ref, acc_ref = refs
    grid_step = pl.program_id(0)
    step = block_of(order, blocks, grid_step, me_ref)
    first_row = step * BLK
    starts = later_starts(length_ref, count)
    first = seq_start(first_row, starts) // BLK
    lane = lax.broadcasted_iota(jnp.int32, (BLK, 128), 1)
    left = lane < HEAD
    heads = q_ref.shape[1] // HEAD
    zero = jnp.zeros((BLK, 128), BF16)
    one = jnp.ones((BLK, 128), BF16)
    sides = [left if head % 2 == 0 else ~left for head in range(heads)]
    columns = [slice(head // 2 * 128, (head // 2 + 1) * 128) for head in range(heads)]
    queries = [jnp.where(sides[h], q_ref[:, columns[h]], zero) for h in range(heads)]
    acc_ref[...] = jnp.zeros_like(acc_ref)
    row = first_row + lax.broadcasted_iota(jnp.int32, (BLK, 1), 0)
    row_start = seq_start(row, starts)

    def body(block, carry):
        key_rows = pl.ds(pl.multiple_of(block * BLK, BLK), BLK)
        key = block * BLK + lax.broadcasted_iota(jnp.int32, (1, BLK), 1)
        code = jnp.where(pad_ref[:, key_rows] == 1, key, NEVER)
        mask = ((code >= row_start) & (code <= row)) | (key == row)
        for h in range(heads):
            value = jnp.where(sides[h], v_ref[key_rows, columns[h]], one)
            scores = dot_nt(queries[h], k_ref[key_rows, columns[h]])
            powers = jnp.where(mask, jnp.exp2(scores * SCORE), 0.0).astype(BF16)
            acc_ref[h] += dot_nn(powers, value)
        return carry

    lax.fori_loop(first, step + 1, body, 0)
    for pair in range(heads // 2):
        tile = slice(pair * 128, (pair + 1) * 128)
        even, odd = acc_ref[2 * pair], acc_ref[2 * pair + 1]
        total = jnp.where(left, odd, even)
        mixed = jnp.where(left, even, odd)
        mixed_ref[:, tile] = (mixed / pltpu.roll(total, HEAD, 1)).astype(BF16)
        high, low = split_low(jnp.log2(total) * (-1.0 / SCORE))
        aux_ref[:, tile] = jnp.where(lax.rem(lane, HEAD) < HEAD // 2, high, low)


def block_of(order, blocks, grid_step, me_ref):
    offset = order[0] + grid_step // blocks
    return jnp.bitwise_xor(me_ref[0], offset) * blocks + lax.rem(grid_step, blocks)


def piece_rows(blocks, place, width):
    return pl.BlockSpec(
        (BLK, width), lambda i, *_: (jnp.clip(i - place * blocks, 0, blocks - 1), 0)
    )


def attend(lengths, me, order, blocks, pad_row, queries, keys, values):
    count, width = queries.shape
    heads = width // HEAD
    return pl.pallas_call(
        functools.partial(attend_kernel, lengths.shape[0], order, blocks),
        grid_spec=pltpu.PrefetchScalarGridSpec(
            num_scalar_prefetch=2,
            grid=(blocks * len(order),),
            in_specs=[
                whole(1, count),
                pl.BlockSpec(
                    (BLK, width), lambda i, l_ref, me_ref: (block_of(order, blocks, i, me_ref), 0)
                ),
                whole(count, width),
                whole(count, width),
            ],
            out_specs=[rows(BLK, width)] * 2,
            scratch_shapes=[pltpu.VMEM((heads, BLK, 128), F32)],
        ),
        out_shape=[like((len(order) * blocks * BLK, width), BF16)] * 2,
        compiler_params=params(),
        cost_estimate=cost(2 * count * count * width, 6 * count * width, count * count * heads // 6),
        name="attend",
    )(lengths, me, pad_row, queries, keys, values)


def attend_back_kernel(
    count, pieces, length_ref, me_ref, pad_ref, q_ref, k_ref, v_ref, *refs
):
    pairs = pieces // 2
    aux_refs, mixed_refs, delta_refs = (
        refs[:pairs],
        refs[pairs : 2 * pairs],
        refs[2 * pairs : 2 * pairs + pieces],
    )
    dqt_ref, dk_ref, dv_ref, do_ref, inner_ref, aux_ref, key_acc, value_acc = refs[
        2 * pairs + pieces :
    ]
    step = pl.program_id(0)
    tokens, width = q_ref.shape
    heads = width // HEAD
    starts = later_starts(length_ref, count)
    lane = lax.broadcasted_iota(jnp.int32, (BLK, 128), 1)
    left = lane < HEAD
    zero = jnp.zeros((BLK, 128), BF16)
    one = jnp.ones((BLK, 128), BF16)
    sides = [left if head % 2 == 0 else ~left for head in range(heads)]
    columns = [slice(head // 2 * 128, (head // 2 + 1) * 128) for head in range(heads)]

    @pl.when(step == 0)
    def prepare():
        dqt_ref[...] = jnp.zeros_like(dqt_ref)
        part = tokens // pieces
        row = lax.broadcasted_iota(jnp.int32, (128, 128), 0)
        column = lax.broadcasted_iota(jnp.int32, (128, 128), 1)
        other = jnp.where(row // HEAD != column // HEAD, 1.0, 0.0).astype(BF16)
        for place in range(pieces):
            first = jnp.bitwise_xor(me_ref[0], place) * part
            do_ref[pl.ds(pl.multiple_of(first, part), part), :] = delta_refs[place][...]
            base = place % 2 * part
            aux_ref[pl.ds(pl.multiple_of(first, part), part), :] = aux_refs[place // 2][
                base : base + part, :
            ]
            for block in range(part // BLK):
                source = slice(block * BLK, (block + 1) * BLK)
                here = pl.ds(pl.multiple_of(first + block * BLK, BLK), BLK)
                for pair in range(heads // 2):
                    tile = slice(pair * 128, (pair + 1) * 128)
                    high, low = split_low(
                        delta_refs[place][source, tile].astype(F32)
                        * mixed_refs[place // 2][
                            base + block * BLK : base + (block + 1) * BLK, tile
                        ].astype(F32)
                    )
                    high, low = split_low(-(dot_nn(high, other) + dot_nn(low, other)))
                    inner_ref[here, tile] = jnp.where(lax.rem(lane, HEAD) < HEAD // 2, high, low)

    key_rows = pl.ds(pl.multiple_of(step * BLK, BLK), BLK)
    last_key = step * BLK + BLK - 1
    end = jnp.int32(tokens)
    for start in reversed(starts):
        end = jnp.where(last_key < start, start, end)
    last = (end - 1) // BLK
    key_acc[...] = jnp.zeros_like(key_acc)
    value_acc[...] = jnp.zeros_like(value_acc)
    turned = jnp.transpose(k_ref[key_rows, :].astype(F32)).astype(BF16)
    keys, values = [], []
    for h in range(heads):
        hot = jnp.where((lax.rem(lane, HEAD // 2) == 0) & (~sides[h]), one, zero)
        for source, into in ((k_ref, keys), (v_ref, values)):
            tile = jnp.where(sides[h], source[key_rows, columns[h]], zero)
            into.append(jnp.concatenate([tile, hot], axis=1))
    key = step * BLK + lax.broadcasted_iota(jnp.int32, (BLK, 1), 0)
    code = jnp.where(pad_ref[key_rows, :] == 1, key, NEVER)

    def body(block, carry):
        here = pl.ds(pl.multiple_of(block * BLK, BLK), BLK)
        row = block * BLK + lax.broadcasted_iota(jnp.int32, (1, BLK), 1)
        mask = ((code >= seq_start(row, starts)) & (code <= row)) | (key == row)
        for h in range(heads):
            query, delta = q_ref[here, columns[h]], do_ref[here, columns[h]]
            scores = dot_nt(keys[h], jnp.concatenate([query, aux_ref[here, columns[h]]], axis=1))
            delta_probs = dot_nt(
                values[h], jnp.concatenate([delta, inner_ref[here, columns[h]]], axis=1)
            )
            probs = jnp.where(mask, jnp.exp2(scores * SCORE), 0.0)
            delta_scores = (probs * delta_probs).astype(BF16)
            value_acc[h] += dot_nn(probs.astype(BF16), delta)
            key_acc[h] += dot_nn(delta_scores, query)
            head_rows = slice(h * HEAD, (h + 1) * HEAD)
            dqt_ref[head_rows, here] += dot_nn(turned[head_rows, :], delta_scores)
        return carry

    lax.fori_loop(step, last + 1, body, 0)
    for pair in range(heads // 2):
        tile = slice(pair * 128, (pair + 1) * 128)
        dk_ref[:, tile] = jnp.where(left, key_acc[2 * pair], key_acc[2 * pair + 1])
        dv_ref[:, tile] = jnp.where(left, value_acc[2 * pair], value_acc[2 * pair + 1])


def attend_back(lengths, me, pad_column, queries, keys, values, aux_pieces, mixed_pieces, delta_pieces):
    count, width = queries.shape
    heads = width // HEAD
    pieces = len(delta_pieces)
    return pl.pallas_call(
        functools.partial(attend_back_kernel, lengths.shape[0], pieces),
        grid_spec=pltpu.PrefetchScalarGridSpec(
            num_scalar_prefetch=2,
            grid=(count // BLK,),
            in_specs=[whole(count, 1)]
            + [whole(count, width)] * 3
            + [whole(2 * count // pieces, width)] * pieces
            + [piece_spec((array, lead, 0), count // pieces, 0) for array, lead in delta_pieces],
            out_specs=[whole(width, count), rows(BLK, width), rows(BLK, width)],
            scratch_shapes=[
                pltpu.VMEM((count, width), BF16),
                pltpu.VMEM((count, width), BF16),
                pltpu.VMEM((count, width), BF16),
                pltpu.VMEM((heads, BLK, 128), F32),
                pltpu.VMEM((heads, BLK, 128), F32),
            ],
        ),
        out_shape=[like((width, count), F32), like((count, width), F32), like((count, width), F32)],
        compiler_params=params(),
        cost_estimate=cost(8 * count * count * width, 22 * count * width, count * count * heads // 3),
        name="attend_back",
    )(lengths, me, pad_column, queries, keys, values, *aux_pieces, *mixed_pieces, *[array for array, lead in delta_pieces])


def unit_of(values):
    factor = lax.rsqrt(jnp.mean(values * values, axis=1, keepdims=True) + EPSILON)
    return values * factor, factor


def unit_back(delta, unit, factor):
    return factor * (delta - unit * jnp.mean(delta * unit, axis=1, keepdims=True))


def mixer_kernel(pieces, *refs):
    mixed_refs, out_weights = refs[:pieces], refs[pieces : 2 * pieces]
    tokens_ref, alpha_ref, low_ref, one_ref, unit_ref, unit_factor, one_factor = refs[2 * pieces :]
    branch = dot_nn(mixed_refs[0][...], out_weights[0][...])
    for mixed, weight in zip(mixed_refs[1:], out_weights[1:]):
        branch += dot_nn(mixed[...], weight[...])
    unit, factor = unit_of(branch * SCALE_MODEL)
    unit_ref[...] = unit
    unit_factor[...] = jnp.broadcast_to(factor, unit_factor.shape)
    residual = tokens_ref[...].astype(F32)
    hidden, factor = unit_of(residual + alpha_ref[...] * (unit - residual))
    one_ref[...] = hidden
    one_factor[...] = jnp.broadcast_to(factor, one_factor.shape)
    low_ref[...] = hidden.astype(BF16)


def mixer(mixed_pieces, out_weights, me, tokens_all, alpha):
    width = mixed_pieces[0][0].shape[-1]
    pieces = len(mixed_pieces)
    count = tokens_all.shape[0] // pieces
    depth = tokens_all.shape[1]
    blocks = count // BLK
    kernel = functools.partial(mixer_kernel, pieces)
    return pl.pallas_call(
        lambda me_ref, *refs: kernel(*refs),
        grid_spec=pltpu.PrefetchScalarGridSpec(
            num_scalar_prefetch=1,
            grid=(blocks,),
            in_specs=[piece_spec((array, lead, 0), BLK, 1) for array, lead in mixed_pieces]
            + [piece_spec((array, lead, 0), width, 0) for array, lead in out_weights]
            + [
                pl.BlockSpec((BLK, depth), lambda i, me_ref: (me_ref[0] * blocks + i, 0)),
                whole(1, depth),
            ],
            out_specs=[rows(BLK, depth)] * 3 + [rows(BLK, 128)] * 2,
        ),
        out_shape=[like((count, depth), BF16)]
        + [like((count, depth), F32)] * 2
        + [like((count, 128), F32)] * 2,
        compiler_params=params(),
        cost_estimate=cost(2 * count * depth * depth, 16 * count * depth + 2 * depth * depth),
        name="mixer",
    )(me, *[p[0] for p in mixed_pieces], *[w[0] for w in out_weights], tokens_all, alpha)


def turn_kernel(pieces, me_ref, *refs):
    own_ref, near_ref, far_ref, one_ref = refs[:4]
    seed_refs = refs[4 : 4 + pieces]
    pad_ref, alpha_ref = refs[4 + pieces : 6 + pieces]
    pair_refs = refs[6 + pieces : 6 + pieces + pieces // 2]
    low_ref, hidden_ref, alpha_sum, seed, layer = refs[6 + pieces + pieces // 2 :]
    width = seed_refs[0].shape[-1]
    starts = [
        pl.multiple_of(jnp.bitwise_xor(me_ref[0], place) * width, width) for place in range(pieces)
    ]
    for start, piece in zip(starts, seed_refs):
        seed[:, pl.ds(start, width)] = piece[...]

    @pl.when(pl.program_id(0) == 0)
    def clear():
        alpha_sum[...] = jnp.zeros_like(alpha_sum)

    branch = (own_ref[...].astype(F32) + near_ref[...].astype(F32)) + far_ref[...].astype(F32)
    unit, unit_factor = unit_of(branch)
    hidden = one_ref[...]
    alpha = alpha_ref[...]
    layer_rows, layer_factor = unit_of(hidden + alpha * (unit - hidden))
    layer[...] = layer_rows.astype(BF16)
    for offset, start in enumerate(starts):
        pair_refs[offset // 2][offset % 2] = layer[:, pl.ds(start, width)]
    delta = unit_back(seed[...].astype(F32) * pad_ref[...], layer_rows, layer_factor)
    alpha_sum[...] += jnp.sum(delta * (unit - hidden), axis=0, keepdims=True)
    hidden_ref[...] = (1.0 - alpha) * delta
    low_ref[...] = unit_back(alpha * delta, unit, unit_factor).astype(BF16)


def turn(me, own, near, far, hidden_one, seed_pieces, pad_rows, alpha):
    count, depth = hidden_one.shape
    pieces = len(seed_pieces)
    width = depth // pieces
    return pl.pallas_call(
        functools.partial(turn_kernel, pieces),
        grid_spec=pltpu.PrefetchScalarGridSpec(
            num_scalar_prefetch=1,
            grid=(count // BLK,),
            in_specs=[rows(BLK, depth)] * 4
            + [piece_spec((array, lead, 0), BLK, 1) for array, lead in seed_pieces]
            + [rows(BLK, 1), whole(1, depth)],
            out_specs=[pl.BlockSpec((2, BLK, width), lambda i, *_: (0, i, 0))] * (pieces // 2)
            + [rows(BLK, depth), rows(BLK, depth), whole(1, depth)],
            scratch_shapes=[pltpu.VMEM((BLK, depth), BF16)] * 2,
        ),
        out_shape=[like((2, count, width), BF16)] * (pieces // 2)
        + [like((count, depth), BF16), like((count, depth), F32), like((1, depth), F32)],
        compiler_params=params(),
        cost_estimate=cost(40 * count * depth, 20 * count * depth),
        name="turn",
    )(me, own, near, far, hidden_one, *[p[0] for p in seed_pieces], pad_rows, alpha)


def mixer_back_kernel(pieces, *refs):
    hidden_ref, own_ref, near_ref, far_ref, one_ref, unit_ref = refs[:6]
    one_factor, unit_factor, tokens_ref, alpha_ref = refs[6:10]
    out_weights = refs[10 : 10 + pieces]
    pair_refs = refs[10 + pieces : 10 + pieces + pieces // 2]
    low_ref, direct_ref, alpha_sum = refs[10 + pieces + pieces // 2 :]

    @pl.when(pl.program_id(0) == 0)
    def clear():
        alpha_sum[...] = jnp.zeros_like(alpha_sum)

    delta = hidden_ref[...] + (
        (own_ref[...].astype(F32) + near_ref[...].astype(F32)) + far_ref[...].astype(F32)
    )
    unit = unit_ref[...]
    alpha = alpha_ref[...]
    delta = unit_back(delta, one_ref[...], one_factor[:, :1])
    alpha_sum[...] += jnp.sum(delta * (unit - tokens_ref[...].astype(F32)), axis=0, keepdims=True)
    direct_ref[...] = (1.0 - alpha) * delta
    low = unit_back(alpha * delta, unit, unit_factor[:, :1]).astype(BF16)
    low_ref[...] = low
    for offset, weight in enumerate(out_weights):
        pair_refs[offset // 2][offset % 2] = (dot_nt(low, weight[...]) * SCALE_MODEL).astype(BF16)


def mixer_back(
    me, hidden, own, near, far, one, unit, one_factor, unit_factor, tokens_all, alpha, out_weights
):
    count, depth = one.shape
    pieces = len(out_weights)
    width = depth // pieces
    blocks = count // BLK
    kernel = functools.partial(mixer_back_kernel, pieces)
    return pl.pallas_call(
        lambda me_ref, *refs: kernel(*refs),
        grid_spec=pltpu.PrefetchScalarGridSpec(
            num_scalar_prefetch=1,
            grid=(blocks,),
            in_specs=[rows(BLK, depth)] * 6
            + [rows(BLK, 128)] * 2
            + [
                pl.BlockSpec((BLK, depth), lambda i, me_ref: (me_ref[0] * blocks + i, 0)),
                whole(1, depth),
            ]
            + [piece_spec((array, lead, 0), width, 0) for array, lead in out_weights],
            out_specs=[pl.BlockSpec((2, BLK, width), lambda i, *_: (0, i, 0))] * (pieces // 2)
            + [rows(BLK, depth), rows(BLK, depth), whole(1, depth)],
        ),
        out_shape=[like((2, count, width), BF16)] * (pieces // 2)
        + [like((count, depth), BF16), like((count, depth), F32), like((1, depth), F32)],
        compiler_params=params(),
        cost_estimate=cost(2 * count * depth * depth, 28 * count * depth + 2 * depth * depth),
        name="mixer_back",
    )(me, hidden, own, near, far, one, unit, one_factor, unit_factor, tokens_all, alpha, *[w[0] for w in out_weights])


def pick(half, first_ref, second_ref, out_ref):
    step = pl.program_id(0)

    @pl.when(step < half)
    def from_first():
        out_ref[...] = first_ref[...]

    @pl.when(step >= half)
    def from_second():
        out_ref[...] = second_ref[...]


def put(half, value, first_ref, second_ref):
    step = pl.program_id(0)

    @pl.when(step < half)
    def to_first():
        first_ref[...] = value

    @pl.when(step >= half)
    def to_second():
        second_ref[...] = value


def expand_kernel(
    half, first_ref, second_ref, up_w, gate_w, gain_ref, up_ref, gate_ref, mid_ref, hidden_ref
):
    pick(half, first_ref, second_ref, hidden_ref)
    hidden = hidden_ref[...]
    up = dot_nt(hidden, up_w[...]) * SCALE_MODEL
    gate = dot_nt(hidden, gate_w[...]) * SCALE_MODEL
    up_ref[...] = up.astype(BF16)
    gate_ref[...] = gate.astype(BF16)
    scaled = gain_ref[1:2, :] * gate
    mid_ref[...] = (gain_ref[0:1, :] * up * scaled * jax.nn.sigmoid(scaled)).astype(BF16)


def expand(first, second, up_w, gate_w, gains):
    count, depth = first.shape
    hidden = up_w.shape[0]
    half = count // BLK
    return pl.pallas_call(
        functools.partial(expand_kernel, half),
        grid=(2 * half,),
        in_specs=[piece_rows(half, 0, depth), piece_rows(half, 1, depth)]
        + [whole(hidden, depth)] * 2
        + [whole(2, hidden)],
        out_specs=[rows(BLK, hidden)] * 3,
        scratch_shapes=[pltpu.VMEM((BLK, depth), BF16)],
        out_shape=[like((2 * count, hidden), BF16)] * 3,
        compiler_params=params(),
        cost_estimate=cost(
            8 * count * depth * hidden,
            4 * count * (depth + 3 * hidden) + 4 * depth * hidden,
            2 * count * hidden,
        ),
        name="expand",
    )(first, second, up_w, gate_w, gains)


def contract_kernel(half, mid_ref, down_w, first_ref, second_ref):
    put(half, (dot_nn(mid_ref[...], down_w[...]) * SCALE_HIDDEN).astype(BF16), first_ref, second_ref)


def contract(middle, down_w):
    count, hidden = middle.shape
    depth = down_w.shape[1]
    half = count // 2 // BLK
    return pl.pallas_call(
        functools.partial(contract_kernel, half),
        grid=(2 * half,),
        in_specs=[rows(BLK, hidden), whole(hidden, depth)],
        out_specs=[piece_rows(half, 0, depth), piece_rows(half, 1, depth)],
        out_shape=[like((count // 2, depth), BF16)] * 2,
        compiler_params=params(),
        cost_estimate=cost(
            2 * count * depth * hidden, 2 * count * (depth + hidden) + 2 * depth * hidden
        ),
        name="contract",
    )(middle, down_w)


def gated_back_kernel(
    half,
    first_ref,
    second_ref,
    up_ref,
    gate_ref,
    up_w,
    gate_w,
    down_w,
    gain_ref,
    both_ref,
    first_out,
    second_out,
    unit_ref,
    delta_ref,
):
    @pl.when(pl.program_id(0) == 0)
    def clear():
        unit_ref[...] = jnp.zeros_like(unit_ref)

    pick(half, first_ref, second_ref, delta_ref)
    delta_middle = dot_nt(delta_ref[...], down_w[...]) * SCALE_HIDDEN
    up = up_ref[...].astype(F32)
    gate = gate_ref[...].astype(F32)
    scaled = gain_ref[1:2, :] * gate
    sigmoid = jax.nn.sigmoid(scaled)
    shared = delta_middle * sigmoid
    delta_up = shared * scaled
    delta_gate = shared * (gain_ref[0:1, :] * up) * (1.0 + scaled * (1.0 - sigmoid))
    unit_ref[0:1, :] += jnp.sum(delta_up * up, axis=0, keepdims=True)
    unit_ref[1:2, :] += jnp.sum(delta_gate * gate, axis=0, keepdims=True)
    up_low = (gain_ref[0:1, :] * delta_up).astype(BF16)
    gate_low = (gain_ref[1:2, :] * delta_gate).astype(BF16)
    both_ref[:, : up_low.shape[1]] = up_low
    both_ref[:, up_low.shape[1] :] = gate_low
    total = (dot_nn(up_low, up_w[...]) + dot_nn(gate_low, gate_w[...])) * SCALE_MODEL
    put(half, total.astype(BF16), first_out, second_out)


def gated_back(first, second, up, gate, up_w, gate_w, down_w, gains):
    count, depth = first.shape
    hidden = up_w.shape[0]
    half = count // BLK
    return pl.pallas_call(
        functools.partial(gated_back_kernel, half),
        grid=(2 * half,),
        in_specs=[piece_rows(half, 0, depth), piece_rows(half, 1, depth)]
        + [rows(BLK, hidden)] * 2
        + [whole(hidden, depth)] * 3
        + [whole(2, hidden)],
        out_specs=[rows(BLK, 2 * hidden)]
        + [piece_rows(half, 0, depth), piece_rows(half, 1, depth), whole(2, hidden)],
        scratch_shapes=[pltpu.VMEM((BLK, depth), BF16)],
        out_shape=[like((2 * count, 2 * hidden), BF16)]
        + [like((count, depth), BF16)] * 2
        + [like((2, hidden), F32)],
        compiler_params=params(),
        cost_estimate=cost(
            12 * count * depth * hidden,
            8 * count * (depth + hidden) + 6 * depth * hidden,
            2 * count * hidden,
        ),
        name="gated_back",
    )(first, second, up, gate, up_w, gate_w, down_w, gains)


def part_columns(tok_ref, total, keep_ref, send_ref):
    width = keep_ref.shape[2]
    for offset in range(2 * keep_ref.shape[0]):
        start = pl.multiple_of(jnp.bitwise_xor(tok_ref[0], offset) * width, width)
        into = send_ref if offset % 2 else keep_ref
        into[offset // 2] = total[:, pl.ds(start, width)].astype(BF16)


def weight_grad_kernel(lefts, scale, tok_ref, *refs):
    left_refs, right_refs, (keep_ref, send_ref, total) = refs[:lefts], refs[lefts:-3], refs[-3:]
    each = len(right_refs) // lefts
    acc = None
    for place, right in enumerate(right_refs):
        count = right.shape[0]
        left = left_refs[place // each][place % each * count : (place % each + 1) * count, :]
        term = lax.dot_general(
            left, right[...], (((0,), (0,)), ((), ())), preferred_element_type=F32
        )
        acc = term if acc is None else acc + term
    total[...] = acc * scale
    part_columns(tok_ref, total, keep_ref, send_ref)


def weight_grad(tok, groups, lefts, rights, scale):
    height = lefts[0].shape[1]
    depth = rights[0].shape[1]
    count = sum(left.shape[0] for left in lefts)
    part = depth // groups
    out = pl.BlockSpec((groups // 2, BLK, part), lambda i, *_: (0, i, 0))
    return pl.pallas_call(
        functools.partial(weight_grad_kernel, len(lefts), scale),
        grid_spec=pltpu.PrefetchScalarGridSpec(
            num_scalar_prefetch=1,
            grid=(height // BLK,),
            in_specs=[pl.BlockSpec((left.shape[0], BLK), lambda i, *_: (0, i)) for left in lefts]
            + [whole(*right.shape) for right in rights],
            out_specs=[out, out],
            scratch_shapes=[pltpu.VMEM((BLK, depth), F32)],
        ),
        out_shape=[like((groups // 2, height, part), BF16)] * 2,
        compiler_params=params(),
        cost_estimate=cost(
            2 * count * height * depth, 2 * count * (height + depth) + 2 * height * depth
        ),
        name="weight_grad",
    )(tok, *lefts, *rights)


def out_grad_kernel(pieces, *refs):
    right, pair_refs = refs[pieces], refs[pieces + 1 :]
    for offset, left in enumerate(refs[:pieces]):
        total = lax.dot_general(
            left[...], right[...], (((0,), (0,)), ((), ())), preferred_element_type=F32
        )
        pair_refs[offset // 2][offset % 2] = (total * SCALE_MODEL).astype(BF16)


def out_grad(lefts, right):
    width = lefts[0][0].shape[-1]
    count, depth = right.shape
    pieces = len(lefts)
    return pl.pallas_call(
        functools.partial(out_grad_kernel, pieces),
        grid=(1,),
        in_specs=[piece_spec((array, lead, 0), count, 0) for array, lead in lefts]
        + [whole(count, depth)],
        out_specs=[whole(2, width, depth)] * (pieces // 2),
        out_shape=[like((2, width, depth), BF16)] * (pieces // 2),
        compiler_params=params(),
        cost_estimate=cost(2 * count * depth * depth, 4 * count * depth + 2 * depth * depth),
        name="out_grad",
    )(*[p[0] for p in lefts], right)


def fold_kernel(tok_ref, own_ref, near_ref, far_ref, keep_ref, send_ref, total):
    total[...] = (own_ref[...].astype(F32) + near_ref[...].astype(F32)) + far_ref[...].astype(F32)
    part_columns(tok_ref, total, keep_ref, send_ref)


def fold(tok, groups, own, near, far):
    height, depth = own[0].shape[-2:]
    part = depth // groups
    return pl.pallas_call(
        fold_kernel,
        grid_spec=pltpu.PrefetchScalarGridSpec(
            num_scalar_prefetch=1,
            grid=(1,),
            in_specs=[piece_spec((array, lead, 0), height, 0) for array, lead in (own, near, far)],
            out_specs=[whole(groups // 2, height, part)] * 2,
            scratch_shapes=[pltpu.VMEM((height, depth), F32)],
        ),
        out_shape=[like((groups // 2, height, part), BF16)] * 2,
        compiler_params=params(),
        cost_estimate=cost(3 * height * depth, 8 * height * depth),
        name="fold",
    )(tok, own[0], near[0], far[0])


def project_back_kernel(pieces, me_ref, dqt_ref, dk_ref, dv_ref, raw_ref, gain_ref, w_ref, direct_ref, *refs):
    low_ref, scale_sum, total = refs[0], refs[1 + pieces], refs[2 + pieces]
    part_refs = refs[1 : 1 + pieces]
    step = pl.program_id(0)
    width = dk_ref.shape[1]
    scale_head = HEAD**-0.5

    @pl.when(step == 0)
    def clear():
        scale_sum[...] = jnp.zeros_like(scale_sum)

    ones = head_matrix(width)
    gain = gain_ref[...]
    for place, delta in enumerate((jnp.transpose(dqt_ref[...]), dk_ref[...])):
        here = slice(place * width, (place + 1) * width)
        values = raw_ref[:, here]
        factor = lax.rsqrt(head_mean(values * values, ones) + EPSILON)
        unit = values * factor
        delta = delta * scale_head
        scale_sum[...] += jnp.sum(delta * unit, axis=0, keepdims=True)
        delta = gain * delta
        low_ref[:, here] = (factor * (delta - unit * head_mean(delta * unit, ones))).astype(BF16)
    low_ref[:, 2 * width :] = dv_ref[...].astype(BF16)
    total[...] = dot_nn(low_ref[...], w_ref[...]) * SCALE_MODEL
    own_blocks = direct_ref.shape[0] // BLK

    @pl.when(step // own_blocks == me_ref[0])
    def add_direct():
        start = pl.multiple_of(lax.rem(step, own_blocks) * BLK, BLK)
        total[...] += direct_ref[pl.ds(start, BLK), :]

    part = total.shape[1] // pieces
    for place, out in enumerate(part_refs):
        start = pl.multiple_of(jnp.bitwise_xor(me_ref[0], place) * part, part)
        out[...] = total[:, pl.ds(start, part)].astype(BF16)


def project_back(me, pieces, dqt, dk, dv, raw, gain, weight, direct):
    count, width = dk.shape
    depth = weight.shape[1]
    part = depth // pieces
    return pl.pallas_call(
        functools.partial(project_back_kernel, pieces),
        grid_spec=pltpu.PrefetchScalarGridSpec(
            num_scalar_prefetch=1,
            grid=(count // BLK,),
            in_specs=[
                pl.BlockSpec((width, BLK), lambda i, *_: (0, i)),
                rows(BLK, width),
                rows(BLK, width),
                rows(BLK, 2 * width),
                whole(1, width),
                whole(3 * width, depth),
                whole(*direct.shape),
            ],
            out_specs=[rows(BLK, 3 * width)] + [rows(BLK, part)] * pieces + [whole(1, width)],
            scratch_shapes=[pltpu.VMEM((BLK, depth), F32)],
        ),
        out_shape=[like((count, 3 * width), BF16)]
        + [like((count, part), BF16)] * pieces
        + [like((1, width), F32)],
        compiler_params=params(),
        cost_estimate=cost(6 * count * width * depth, count * (26 * width + 2 * depth)),
        name="project_back",
    )(me, dqt, dk, dv, raw, gain, weight, direct)


def merge_kernel(keep_ref, came_ref, first_ref, later_ref, send_ref):
    sums = [keep_ref[r].astype(F32) + came_ref[r].astype(F32) for r in range(4)]
    first_ref[...] = sums[0]
    later_ref[...] = sums[2]
    send_ref[0] = sums[1].astype(BF16)
    send_ref[1] = sums[3].astype(BF16)


def merge(keep, came):
    parts, height, part = keep.shape
    block = pl.BlockSpec((parts, BLK, part), lambda i: (0, i, 0))
    return pl.pallas_call(
        merge_kernel,
        grid=(height // BLK,),
        in_specs=[block, block],
        out_specs=[rows(BLK, part)] * 2 + [pl.BlockSpec((2, BLK, part), lambda i: (0, i, 0))],
        out_shape=[like((height, part), F32)] * 2 + [like((2, height, part), BF16)],
        compiler_params=params(),
        cost_estimate=cost(4 * height * part, 28 * height * part),
        name="merge",
    )(keep, came)


def trade(value, axis, offset):
    size = lax.axis_size(axis)
    return lax.ppermute(value, axis, [(i, i ^ offset) for i in range(size)])


def sum_over(value, axis):
    offset = 1
    while offset < lax.axis_size(axis):
        value = value + trade(value, axis, offset)
        offset *= 2
    return value


def after(value, *others):
    return lax.optimization_barrier((value, others))[0]


def join(*values):
    return lax.optimization_barrier(values)


def stack(*values):
    return jnp.concatenate([v if v.ndim == 3 else v[None] for v in values], axis=0)


def by_offset(own, first, same, far, other, block):
    own, first, same, far, other = [
        value if isinstance(value, tuple) else (value, block) for value in (own, first, same, far, other)
    ]

    def at(source, lead=None):
        return (source[0], lead, source[1])

    return [
        at(own),
        at(first),
        at(same, 0),
        at(other, 1),
        at(far),
        at(other, 0),
        at(same, 1),
        at(other, 2),
    ]


def scatter_dim(pairs):
    near, far = pairs
    corner = trade(far[1], "dim", 1)
    across = (far[0].astype(F32) + corner.astype(F32)).astype(BF16)
    return near[0], trade(near[1], "dim", 1), trade(across, "dim", 2)


def plain_sum(left, right, scale):
    total = jnp.einsum("tr,td->rd", left, right, preferred_element_type=F32) * scale
    return lax.psum_scatter(total.astype(BF16), "tok", scatter_dimension=1, tiled=True).astype(F32)


def moment_update(weights, gradient, moment, square, fix_first, fix_second):
    moment_next = BETA_ONE * moment + (1.0 - BETA_ONE) * gradient
    square_next = BETA_TWO * square + (1.0 - BETA_TWO) * gradient * gradient
    stepped = weights - LEARN_RATE * (moment_next / fix_first) / (
        jnp.sqrt(square_next / fix_second) + ADAM_EPSILON
    )
    return (stepped, moment_next, square_next)


def local(
    inputs,
    cotangent,
    lengths,
    pad_mask,
    attention_weights,
    gated_weights,
    model_gains,
    unit_gains,
    attention_moment,
    attention_square,
    gated_moment,
    gated_square,
    model_moment,
    model_square,
    unit_moment,
    unit_square,
):
    token_count, width = inputs.shape
    parts = lax.axis_size("dim")
    hidden_here = gated_weights.shape[1]
    own_count = token_count // parts
    place = lax.axis_index("dim")
    me = place.astype(jnp.int32).reshape(1)
    tok = lax.axis_index("tok").astype(jnp.int32).reshape(1)
    groups = lax.axis_size("tok")
    by_pieces = groups == 8 and (D // groups) % 128 == 0
    blocks = own_count // BLK
    length_row = lengths[0]

    def token_rows(value, offset):
        return lax.dynamic_slice_in_dim(value, (place ^ offset) * own_count, own_count, 0)

    ao = attention_weights.reshape(4 * width, -1).astype(BF16)
    up_own, gate_own, down_own = [gated_weights[k].astype(BF16) for k in range(3)]
    score_gain = model_gains[:1]
    pad_row = pad_mask[None, :]
    pad_column = pad_mask[:, None]
    pad_rows = token_rows(pad_mask, 0).astype(F32)[:, None]
    alpha_start = lax.dynamic_update_slice(
        jnp.zeros((2, D), F32), model_gains[1:], (0, place * width)
    )

    x_far = trade(inputs, "dim", 2)
    if by_pieces:
        ao_far = trade(ao, "tok", 4)
        ao_first = trade(ao, "tok", 1)
        ao_same = trade(stack(ao, ao_far), "tok", 2)
        gated_first = trade(
            after(gated_weights.reshape(3 * hidden_here, -1).astype(BF16), ao), "tok", 1
        )
        x_far, ao_far, ao_same, ao_first = join(x_far, ao_far, ao_same, ao_first)
        in_other = trade(stack(ao_far[: 3 * width], ao_same[:, : 3 * width]), "tok", 1)
        up_far = trade(after(up_own, x_far), "tok", 4)
    x_near = trade(after(inputs, x_far), "dim", 1)
    x_corner = trade(x_far, "dim", 1)
    token_pieces = [inputs, x_near, x_far, x_corner]
    if by_pieces:
        token_pieces, in_other, up_far = join(token_pieces, in_other, up_far)
        in_pieces = by_offset(ao, ao_first, ao_same, ao_far, in_other, 0)
        out_other = trade(
            stack(after(ao_far, in_other)[3 * width :], ao_same[:, 3 * width :]), "tok", 1
        )
        up_same = trade(stack(up_own, up_far), "tok", 2)
    else:
        gather = functools.partial(lax.all_gather, axis_name="tok", axis=1, tiled=True)
        in_pieces = [(gather(ao[: 3 * width]), None, 0)]
        out_weight, up_w, gate_w, down_w = [
            gather(shard) for shard in (ao[3 * width :], up_own, gate_own, down_own)
        ]
    tokens_all, raw, queries, keys, values, weight_in = project(
        me, tok, token_pieces, in_pieces, score_gain
    )

    if by_pieces:
        queries, out_other, gated_first = join(queries, out_other, gated_first)
        out_weight = assemble(
            tok, by_offset(ao, ao_first, ao_same, ao_far, (out_other, 0), 3 * width // BLK), width
        )
        gate_far = trade(after(gate_own, queries), "tok", 4)
    out_far = trade(out_weight, "dim", 2)
    far_mixed, far_aux = attend(
        length_row, me, (2, 3), blocks, pad_row, after(queries, out_weight), keys, values
    )
    if by_pieces:
        far_mixed, up_same = join(far_mixed, up_same)
        up_other = trade(stack(up_far, up_same), "tok", 1)
    far_came = trade(far_mixed, "dim", 2)
    near_mixed, near_aux = attend(
        length_row, me, (0, 1), blocks, pad_row, after(queries, far_mixed), keys, values
    )
    near_mixed, far_came, out_far = join(near_mixed, far_came, out_far)
    if by_pieces:
        near_mixed, gate_far = join(near_mixed, gate_far)
        gate_same = trade(stack(gate_own, gate_far), "tok", 2)
        down_far = trade(after(down_own, gate_far), "tok", 4)
    pair_came = trade(stack(near_mixed[own_count:], far_came[own_count:]), "dim", 1)
    out_pair = trade(stack(out_weight, out_far), "dim", 1)
    alphas = sum_over(after(alpha_start, near_mixed), "dim")
    alpha_mixer, alpha_gated = alphas[:1], alphas[1:]
    out_weights = [(out_weight, None), (out_pair, 0), (out_far, None), (out_pair, 1)]
    mixed_pieces = [(near_mixed, None), (pair_came, 0), (far_came, None), (pair_came, 1)]
    hidden_low, hidden_one, mixer_unit, mixer_factor, one_factor = mixer(
        mixed_pieces, out_weights, me, tokens_all, alpha_mixer
    )

    h_far = trade(hidden_low, "dim", 2)
    if by_pieces:
        hidden_low, gate_same, up_other, down_far = join(hidden_low, gate_same, up_other, down_far)
        gate_other = trade(stack(gate_far, gate_same), "tok", 1)
        down_same = trade(stack(down_own, down_far), "tok", 2)
    h_near = trade(hidden_low, "dim", 1)
    if by_pieces:
        each = hidden_here // BLK
        up_w = assemble(
            tok,
            by_offset(up_own, (gated_first, 0), up_same, up_far, after(up_other, hidden_low), 0),
            hidden_here,
        )
        up_w, gate_other, down_same = join(up_w, gate_other, down_same)
        down_other = trade(stack(down_far, down_same), "tok", 1)
        gate_w = assemble(
            tok,
            by_offset(gate_own, (gated_first, each), gate_same, gate_far, gate_other, 0),
            hidden_here,
        )
    up_one, gate_one, mid_one = expand(hidden_low, h_near, up_w, gate_w, unit_gains)
    mid_one, h_far = join(mid_one, h_far)
    h_corner = trade(h_far, "dim", 1)

    def swap_rows(own, near, across, corner):
        came = trade(stack(across, corner), "dim", 2)
        pair = trade(stack(near, came[1]), "dim", 1)
        return [(own, None), (pair, 0), (came, 0), (pair, 1)]

    seed_pieces = swap_rows(*[token_rows(after(cotangent, h_far), r) for r in range(parts)])
    up_two, gate_two, mid_two = expand(h_far, h_corner, up_w, gate_w, unit_gains)
    if by_pieces:
        mid_two, down_other = join(mid_two, down_other)
        down_w = assemble(
            tok,
            by_offset(down_own, (gated_first, 2 * each), down_same, down_far, down_other, 0),
            hidden_here,
        )
    far_parts = contract(mid_two, down_w)
    corner = trade(far_parts[1], "dim", 1)
    across = (far_parts[0].astype(F32) + corner.astype(F32)).astype(BF16)
    far = trade(across, "dim", 2)
    near_parts = contract(after(mid_one, corner), down_w)
    near = trade(near_parts[1], "dim", 1)
    own, near, far = join(near_parts[0], near, far)
    layer_near, layer_far, delta_branch, delta_hidden, sum_gated = turn(
        me, own, near, far, hidden_one, seed_pieces, pad_rows, alpha_gated
    )

    b_near = trade(delta_branch, "dim", 1)
    b_far = trade(delta_branch, "dim", 2)
    both_one, own, pair, unit_sum_one = gated_back(
        delta_branch, b_near, up_one, gate_one, up_w, gate_w, down_w, unit_gains
    )
    both_one, b_far = join(both_one, b_far)
    near = trade(pair, "dim", 1)
    b_corner = trade(b_far, "dim", 1)
    both_two, across, corner, unit_sum_two = gated_back(
        b_far, b_corner, up_two, gate_two, up_w, gate_w, down_w, unit_gains
    )
    corner = trade(corner, "dim", 1)
    across = (across.astype(F32) + corner.astype(F32)).astype(BF16)
    far = trade(across, "dim", 2)
    h_pieces = [hidden_low, h_near, h_far, h_corner]
    b_pieces = [delta_branch, b_near, b_far, b_corner]
    if by_pieces:
        down_keep, down_send = weight_grad(
            tok, groups, (after(mid_one, across), mid_two), b_pieces, SCALE_HIDDEN
        )
        down_came = trade(down_send, "tok", 1)
        both_keep, both_send = weight_grad(
            tok, groups, (after(both_one, down_send), both_two), h_pieces, SCALE_MODEL
        )
        own, near, far, both_send = join(own, near, far, both_send)
        both_came = trade(both_send, "tok", 1)
    else:
        down_grad = plain_sum(
            jnp.concatenate([mid_one, mid_two], axis=0),
            jnp.concatenate(b_pieces, axis=0),
            SCALE_HIDDEN,
        )
        both_grad = plain_sum(
            jnp.concatenate([both_one, both_two], axis=0),
            jnp.concatenate(h_pieces, axis=0),
            SCALE_MODEL,
        )

    delta_near, delta_far, mixer_low, delta_direct, sum_mixer = mixer_back(
        me,
        delta_hidden,
        own,
        near,
        far,
        hidden_one,
        mixer_unit,
        one_factor,
        mixer_factor,
        tokens_all,
        alpha_mixer,
        out_weights,
    )
    delta_came = trade(delta_far, "dim", 2)
    out_near_grad, out_far_grad = out_grad(mixed_pieces, mixer_low)
    out_corner = trade(out_far_grad[1], "dim", 1)
    if by_pieces:
        down_came, out_far_grad = join(down_came, out_far_grad)
        down_first, down_later, down_send = merge(down_keep, down_came)
        down_near = trade(down_send, "tok", 2)
        delta_came, down_send = join(delta_came, down_send)
    delta_pair = trade(stack(delta_near[1], delta_came[1]), "dim", 1)
    delta_pieces = [(delta_near, 0), (delta_pair, 0), (delta_came, 0), (delta_pair, 1)]
    out_across = (out_far_grad[0].astype(F32) + out_corner.astype(F32)).astype(BF16)
    delta_pair, out_across = join(delta_pair, out_across)
    delta_pieces = [(delta_near, 0), (delta_pair, 0), (delta_came, 0), (delta_pair, 1)]
    out_far_sum = trade(out_across, "dim", 2)
    layer_came = trade(after(layer_far, delta_pair), "dim", 2)
    dqt, dk, dv = attend_back(
        length_row,
        me,
        pad_column,
        queries,
        keys,
        values,
        [near_aux, far_aux],
        [near_mixed, far_mixed],
        delta_pieces,
    )
    dqt, out_far_sum, layer_came = join(dqt, out_far_sum, layer_came)
    out_near_sum = trade(after(out_near_grad[1], dqt), "dim", 1)
    if by_pieces:
        dqt, down_near, both_came = join(dqt, down_near, both_came)
        both_first, both_later, both_send = merge(both_keep, both_came)
        both_near = trade(both_send, "tok", 2)
        down_send = (down_later + down_near[1].astype(F32)).astype(BF16)
        down_last = trade(down_send, "tok", 4)
        out_keep, out_send = fold(
            tok, groups, (out_near_grad, 0), (out_near_sum, None), (out_far_sum, None)
        )
        out_came = trade(out_send, "tok", 1)
        dqt, both_send, down_send, out_send = join(dqt, both_send, down_send, out_send)
    delta_project, *input_parts, scale_sum = project_back(
        me, parts, dqt, dk, dv, raw, score_gain, weight_in, delta_direct
    )
    corner = trade(input_parts[3], "dim", 1)
    across = (input_parts[2].astype(F32) + corner.astype(F32)).astype(BF16)
    far = trade(across, "dim", 2)
    if by_pieces:
        in_keep, in_send = weight_grad(
            tok, groups, (after(delta_project, across),), (tokens_all,), SCALE_MODEL
        )
        in_send, out_came, both_near, down_last = join(in_send, out_came, both_near, down_last)
        in_came = trade(in_send, "tok", 1)
        both_send = (both_later + both_near[1].astype(F32)).astype(BF16)
        both_last = trade(both_send, "tok", 4)
        out_first, out_later, out_send = merge(out_keep, out_came)
        out_near = trade(out_send, "tok", 2)
    near = trade(input_parts[1], "dim", 1)
    layer_pair = trade(stack(layer_near[1], layer_came[1]), "dim", 1)
    layer_pieces = [layer_near[0], layer_pair[0], layer_came[0], layer_pair[1]]
    layer_out = jnp.zeros((token_count, width), BF16)
    for r, piece in enumerate(layer_pieces):
        layer_out = lax.dynamic_update_slice(layer_out, piece, ((place ^ r) * own_count, 0))
    if by_pieces:
        down_grad = (down_first + down_near[0].astype(F32)) + down_last.astype(F32)
        in_came, out_near, layer_out = join(in_came, out_near, layer_out)
        in_first, in_later, in_send = merge(in_keep, in_came)
        in_near = trade(in_send, "tok", 2)
        out_last = trade((out_later + out_near[1].astype(F32)).astype(BF16), "tok", 4)
        in_near, both_last, out_last = join(in_near, both_last, out_last)
        in_last = trade((in_later + in_near[1].astype(F32)).astype(BF16), "tok", 4)
        both_grad = (both_first + both_near[0].astype(F32)) + both_last.astype(F32)
        out_total = (out_first + out_near[0].astype(F32)) + out_last.astype(F32)
        in_total = (in_first + in_near[0].astype(F32)) + in_last.astype(F32)
    else:
        out_total = (out_near_grad[0].astype(F32) + out_near_sum.astype(F32)) + out_far_sum.astype(F32)
        out_total = lax.psum_scatter(
            out_total.astype(BF16), "tok", scatter_dimension=1, tiled=True
        ).astype(F32)
        in_total = plain_sum(delta_project, tokens_all, SCALE_MODEL)
    input_gradient = (input_parts[0].astype(F32) + near.astype(F32)) + far.astype(F32)
    attention_grad = jnp.concatenate([in_total, out_total], axis=0).reshape(4, width, -1)
    gated_grad = jnp.concatenate([both_grad, down_grad], axis=0).reshape(3, hidden_here, -1)

    alpha_sums = lax.dynamic_slice_in_dim(
        sum_over(jnp.concatenate([sum_mixer, sum_gated], axis=0), "dim"), place * width, width, 1
    )
    gains_sum = sum_over(
        jnp.concatenate(
            [scale_sum.reshape(-1), alpha_sums.reshape(-1), (unit_sum_one + unit_sum_two).reshape(-1)]
        ),
        "tok",
    )
    model_grad = gains_sum[: 3 * width].reshape(3, width)
    unit_grad = gains_sum[3 * width :].reshape(2, hidden_here)

    fix_first = 1.0 - BETA_ONE**STEP
    fix_second = 1.0 - BETA_TWO**STEP
    attention_stepped, moment_attention, square_attention = moment_update(
        attention_weights, attention_grad, attention_moment, attention_square, fix_first, fix_second
    )
    gated_stepped, moment_gated, square_gated = moment_update(
        gated_weights, gated_grad, gated_moment, gated_square, fix_first, fix_second
    )
    model_next, moment_model, square_model = moment_update(
        model_gains, model_grad, model_moment, model_square, fix_first, fix_second
    )
    unit_next, moment_unit, square_unit = moment_update(
        unit_gains, unit_grad, unit_moment, unit_square, fix_first, fix_second
    )
    token_groups = lax.axis_size("tok")
    gated_rows = sum_over(jnp.sum(gated_stepped * gated_stepped, axis=2), "tok")
    local_square = (
        jnp.sum(attention_grad * attention_grad)
        + jnp.sum(gated_grad * gated_grad)
        + (jnp.sum(model_grad * model_grad) + jnp.sum(unit_grad * unit_grad)) / token_groups
    )
    row_sums = sum_over(
        jnp.concatenate(
            [
                jnp.sum(attention_stepped * attention_stepped, axis=2).reshape(-1),
                local_square.reshape(1),
            ]
        ),
        "tok",
    )
    attention_rows = row_sums[:-1].reshape(4, width, 1)
    attention_next = attention_stepped * lax.rsqrt(attention_rows / D + EPSILON)
    gated_next = gated_stepped * lax.rsqrt(gated_rows[:, :, None] / D + EPSILON)
    totals = sum_over(jnp.concatenate([row_sums[-1:], jnp.sum(model_next[1:], axis=1)]), "dim")
    gradient_norm = jnp.sqrt(totals[:1])
    mean_alpha = totals[1:] / D
    return (
        layer_out,
        input_gradient,
        attention_next,
        attention_next.astype(BF16),
        moment_attention,
        square_attention,
        gated_next,
        gated_next.astype(BF16),
        moment_gated,
        square_gated,
        model_next,
        moment_model,
        square_model,
        unit_next,
        moment_unit,
        square_unit,
        gradient_norm,
        mean_alpha,
    )


def solution(mesh):
    tokens = P("tok", "dim")
    weights = P(None, "dim", "tok")
    gains = P(None, "dim")
    in_specs = (tokens, tokens, P("tok", None), P("tok"), weights, weights, gains, gains)
    in_specs += (weights,) * 4 + (gains,) * 4
    out_specs = (tokens, tokens) + (weights,) * 8 + (gains,) * 6 + (P(), P())
    return jax.shard_map(local, mesh=mesh, in_specs=in_specs, out_specs=out_specs, check_vma=False)
```

```python
import functools
import math

import jax
import jax.numpy as jnp
from jax import lax
from jax.experimental import pallas as pl
from jax.experimental.pallas import tpu as pltpu
from jax.sharding import PartitionSpec as P

D = 1024
HEAD = 64
FF = 4096
STEP = 4
BLK = 256

EPSILON = 1e-06
ADAM_EPSILON = 1e-08
BETA_ONE = 0.5
BETA_TWO = 0.5
LEARN_RATE = 1.5

F32 = jnp.float32
BF16 = jnp.bfloat16
SCALE_MODEL = D**-0.5
SCALE_HIDDEN = FF**-0.5
SCORE = HEAD**-0.5 * math.log2(math.e)
NEVER = 1 << 24


def dot_nt(left, right):
    return lax.dot_general(left, right, (((1,), (1,)), ((), ())), preferred_element_type=F32)


def dot_nn(left, right):
    return lax.dot_general(left, right, (((1,), (0,)), ((), ())), preferred_element_type=F32)


def split_low(values):
    high = values.astype(BF16)
    return high, (values - high.astype(F32)).astype(BF16)


def params():
    return pltpu.CompilerParams(vmem_limit_bytes=60 << 20)


def cost(flops, traffic, transcendentals=0):
    return pl.CostEstimate(
        flops=int(flops) // 64, bytes_accessed=int(traffic) // 64, transcendentals=int(transcendentals) // 64
    )


def like(shape, dtype):
    return jax.ShapeDtypeStruct(shape, dtype)


def whole(*shape):
    return pl.BlockSpec(shape, lambda *_: (0,) * len(shape))


def rows(count, width):
    return pl.BlockSpec((count, width), lambda i, *_: (i, 0))


def launch(kernel, needs, scalars, grid, in_specs, args, scratch_shapes=(), **options):
    taken = len(scalars) + len(args)

    def body(*refs):
        kernel(*refs[:taken], *refs[taken + len(needs) :])

    return pl.pallas_call(
        body,
        grid_spec=pltpu.PrefetchScalarGridSpec(
            num_scalar_prefetch=len(scalars),
            grid=grid,
            in_specs=[*in_specs] + [pl.BlockSpec(memory_space=pl.ANY)] * len(needs),
            out_specs=options.pop("out_specs"),
            scratch_shapes=scratch_shapes,
        ),
        compiler_params=params(),
        **options,
    )(*scalars, *args, *needs)


def head_matrix(width):
    row = lax.broadcasted_iota(jnp.int32, (width, width), 0)
    column = lax.broadcasted_iota(jnp.int32, (width, width), 1)
    return jnp.where(row // HEAD == column // HEAD, 1.0, 0.0).astype(BF16)


def head_mean(values, ones):
    high, low = split_low(values)
    return (dot_nn(high, ones) + dot_nn(low, ones)) * (1.0 / HEAD)


def project_kernel(pieces, me_ref, tok_ref, *refs):
    piece_refs = refs[:pieces]
    weight_refs = refs[pieces:-7]
    gain_ref, all_ref, raw_ref, q_ref, k_ref, v_ref, w_ref = refs[-7:]
    width = piece_refs[0].shape[1]
    if len(weight_refs) == 1:
        weight = weight_refs[0]
    else:
        weight = w_ref

        @pl.when(pl.program_id(0) == 0)
        def assemble_weight():
            place_columns(tok_ref[0], weight_refs, w_ref)

    place_columns(me_ref[0], piece_refs, all_ref)
    projected = dot_nt(all_ref[...], weight[...]) * SCALE_MODEL
    if weight is not w_ref:
        w_ref[...] = weight[...]
    raw_ref[...] = projected[:, : 2 * width]
    ones = head_matrix(width)
    for place, out in enumerate((q_ref, k_ref)):
        values = projected[:, place * width : (place + 1) * width]
        factor = lax.rsqrt(head_mean(values * values, ones) + EPSILON)
        out[...] = (values * factor * gain_ref[...]).astype(BF16)
    v_ref[...] = projected[:, 2 * width :].astype(BF16)


def place_columns(index, piece_refs, out_ref):
    width = piece_refs[0].shape[1]
    for offset, piece in enumerate(piece_refs):
        start = pl.multiple_of(jnp.bitwise_xor(index, offset) * width, width)
        out_ref[:, pl.ds(start, width)] = piece[...]


def piece_spec(piece, height, step):
    array, lead, block = piece
    width = array.shape[-1]
    if lead is None:
        return pl.BlockSpec((height, width), lambda i, *_: (block + step * i, 0))
    return pl.BlockSpec((None, height, width), lambda i, *_: (lead, block + step * i, 0))


def project(me, tok, pieces, weights, gain):
    count, width = pieces[0].shape
    depth = width * len(pieces)
    return pl.pallas_call(
        functools.partial(project_kernel, len(pieces)),
        grid_spec=pltpu.PrefetchScalarGridSpec(
            num_scalar_prefetch=2,
            grid=(count // BLK,),
            in_specs=[rows(BLK, width)] * len(pieces)
            + [piece_spec(weight, 3 * width, 0) for weight in weights]
            + [whole(1, width)],
            out_specs=[rows(BLK, depth), rows(BLK, 2 * width)]
            + [rows(BLK, width)] * 3
            + [whole(3 * width, depth)],
        ),
        out_shape=[like((count, depth), BF16), like((count, 2 * width), F32)]
        + [like((count, width), BF16)] * 3
        + [like((3 * width, depth), BF16)],
        compiler_params=params(),
        cost_estimate=cost(6 * count * width * depth, count * (4 * depth + 14 * width)),
        name="project",
    )(me, tok, *pieces, *[weight[0] for weight in weights], gain)


def assemble_kernel(tok_ref, *refs):
    place_columns(tok_ref[0], refs[:-1], refs[-1])


def assemble(tok, pieces, count, needs=()):
    width = pieces[0][0].shape[-1]
    depth = width * len(pieces)
    return launch(
        assemble_kernel,
        needs,
        (tok,),
        (count // BLK,),
        [piece_spec(piece, BLK, 1) for piece in pieces],
        (*[piece[0] for piece in pieces],),
        out_specs=rows(BLK, depth),
        out_shape=like((count, depth), BF16),
        cost_estimate=cost(0, 4 * count * depth),
        name="assemble",
    )


def seq_start(place, starts):
    found = jnp.zeros_like(place)
    for start in starts:
        found = jnp.where(place >= start, start, found)
    return found


def later_starts(length_ref, count):
    starts, total = [], jnp.int32(0)
    for position in range(count - 1):
        total = total + length_ref[position]
        starts.append(total)
    return starts


def attend_kernel(count, order, blocks, length_ref, me_ref, pad_ref, q_ref, k_ref, v_ref, *refs):
    mixed_ref, aux_ref, acc_ref = refs
    grid_step = pl.program_id(0)
    step = block_of(order, blocks, grid_step, me_ref)
    first_row = step * BLK
    starts = later_starts(length_ref, count)
    first = seq_start(first_row, starts) // BLK
    lane = lax.broadcasted_iota(jnp.int32, (BLK, 128), 1)
    left = lane < HEAD
    heads = q_ref.shape[1] // HEAD
    zero = jnp.zeros((BLK, 128), BF16)
    one = jnp.ones((BLK, 128), BF16)
    sides = [left if head % 2 == 0 else ~left for head in range(heads)]
    columns = [slice(head // 2 * 128, (head // 2 + 1) * 128) for head in range(heads)]
    queries = [jnp.where(sides[h], q_ref[:, columns[h]], zero) for h in range(heads)]
    acc_ref[...] = jnp.zeros_like(acc_ref)
    row = first_row + lax.broadcasted_iota(jnp.int32, (BLK, 1), 0)
    row_start = seq_start(row, starts)

    def body(block, carry):
        key_rows = pl.ds(pl.multiple_of(block * BLK, BLK), BLK)
        key = block * BLK + lax.broadcasted_iota(jnp.int32, (1, BLK), 1)
        code = jnp.where(pad_ref[:, key_rows] == 1, key, NEVER)
        mask = ((code >= row_start) & (code <= row)) | (key == row)
        for h in range(heads):
            value = jnp.where(sides[h], v_ref[key_rows, columns[h]], one)
            scores = dot_nt(queries[h], k_ref[key_rows, columns[h]])
            powers = jnp.where(mask, jnp.exp2(scores * SCORE), 0.0).astype(BF16)
            acc_ref[h] += dot_nn(powers, value)
        return carry

    lax.fori_loop(first, step + 1, body, 0)
    for pair in range(heads // 2):
        tile = slice(pair * 128, (pair + 1) * 128)
        even, odd = acc_ref[2 * pair], acc_ref[2 * pair + 1]
        total = jnp.where(left, odd, even)
        mixed = jnp.where(left, even, odd)
        mixed_ref[:, tile] = (mixed / pltpu.roll(total, HEAD, 1)).astype(BF16)
        high, low = split_low(jnp.log2(total) * (-1.0 / SCORE))
        aux_ref[:, tile] = jnp.where(lax.rem(lane, HEAD) < HEAD // 2, high, low)


def block_of(order, blocks, grid_step, me_ref):
    offset = order[0] + grid_step // blocks
    return jnp.bitwise_xor(me_ref[0], offset) * blocks + lax.rem(grid_step, blocks)


def piece_rows(blocks, place, width):
    return pl.BlockSpec(
        (BLK, width), lambda i, *_: (jnp.clip(i - place * blocks, 0, blocks - 1), 0)
    )


def attend(lengths, me, order, blocks, pad_row, queries, keys, values, needs=()):
    count, width = queries.shape
    heads = width // HEAD
    return launch(
        functools.partial(attend_kernel, lengths.shape[0], order, blocks),
        needs,
        (lengths, me,),
        (blocks * len(order),),
        [
                whole(1, count),
                pl.BlockSpec(
                    (BLK, width), lambda i, l_ref, me_ref: (block_of(order, blocks, i, me_ref), 0)
                ),
                whole(count, width),
                whole(count, width),
            ],
        (pad_row, queries, keys, values,),
        scratch_shapes=[pltpu.VMEM((heads, BLK, 128), F32)],
        out_specs=[rows(BLK, width)] * 2,
        out_shape=[like((len(order) * blocks * BLK, width), BF16)] * 2,
        cost_estimate=cost(2 * count * count * width, 6 * count * width, count * count * heads // 6),
        name="attend",
    )


def attend_back_kernel(
    count, pieces, length_ref, me_ref, pad_ref, q_ref, k_ref, v_ref, *refs
):
    pairs = pieces // 2
    aux_refs, mixed_refs, delta_refs = (
        refs[:pairs],
        refs[pairs : 2 * pairs],
        refs[2 * pairs : 2 * pairs + pieces],
    )
    dqt_ref, dk_ref, dv_ref, do_ref, inner_ref, aux_ref, key_acc, value_acc = refs[
        2 * pairs + pieces :
    ]
    step = pl.program_id(0)
    tokens, width = q_ref.shape
    heads = width // HEAD
    starts = later_starts(length_ref, count)
    lane = lax.broadcasted_iota(jnp.int32, (BLK, 128), 1)
    left = lane < HEAD
    zero = jnp.zeros((BLK, 128), BF16)
    one = jnp.ones((BLK, 128), BF16)
    sides = [left if head % 2 == 0 else ~left for head in range(heads)]
    columns = [slice(head // 2 * 128, (head // 2 + 1) * 128) for head in range(heads)]

    @pl.when(step == 0)
    def prepare():
        dqt_ref[...] = jnp.zeros_like(dqt_ref)
        part = tokens // pieces
        row = lax.broadcasted_iota(jnp.int32, (128, 128), 0)
        column = lax.broadcasted_iota(jnp.int32, (128, 128), 1)
        other = jnp.where(row // HEAD != column // HEAD, 1.0, 0.0).astype(BF16)
        for place in range(pieces):
            first = jnp.bitwise_xor(me_ref[0], place) * part
            do_ref[pl.ds(pl.multiple_of(first, part), part), :] = delta_refs[place][...]
            base = place % 2 * part
            aux_ref[pl.ds(pl.multiple_of(first, part), part), :] = aux_refs[place // 2][
                base : base + part, :
            ]
            for block in range(part // BLK):
                source = slice(block * BLK, (block + 1) * BLK)
                here = pl.ds(pl.multiple_of(first + block * BLK, BLK), BLK)
                for pair in range(heads // 2):
                    tile = slice(pair * 128, (pair + 1) * 128)
                    high, low = split_low(
                        delta_refs[place][source, tile].astype(F32)
                        * mixed_refs[place // 2][
                            base + block * BLK : base + (block + 1) * BLK, tile
                        ].astype(F32)
                    )
                    high, low = split_low(-(dot_nn(high, other) + dot_nn(low, other)))
                    inner_ref[here, tile] = jnp.where(lax.rem(lane, HEAD) < HEAD // 2, high, low)

    key_rows = pl.ds(pl.multiple_of(step * BLK, BLK), BLK)
    last_key = step * BLK + BLK - 1
    end = jnp.int32(tokens)
    for start in reversed(starts):
        end = jnp.where(last_key < start, start, end)
    last = (end - 1) // BLK
    key_acc[...] = jnp.zeros_like(key_acc)
    value_acc[...] = jnp.zeros_like(value_acc)
    turned = jnp.transpose(k_ref[key_rows, :].astype(F32)).astype(BF16)
    keys, values = [], []
    for h in range(heads):
        hot = jnp.where((lax.rem(lane, HEAD // 2) == 0) & (~sides[h]), one, zero)
        for source, into in ((k_ref, keys), (v_ref, values)):
            tile = jnp.where(sides[h], source[key_rows, columns[h]], zero)
            into.append(jnp.concatenate([tile, hot], axis=1))
    key = step * BLK + lax.broadcasted_iota(jnp.int32, (BLK, 1), 0)
    padding = jnp.transpose(
        jnp.broadcast_to(pad_ref[:, key_rows].astype(F32), (128, BLK))
    )[:, :1]
    code = jnp.where(padding > 0.5, key, NEVER)

    def body(block, carry):
        here = pl.ds(pl.multiple_of(block * BLK, BLK), BLK)
        row = block * BLK + lax.broadcasted_iota(jnp.int32, (1, BLK), 1)
        mask = ((code >= seq_start(row, starts)) & (code <= row)) | (key == row)
        for h in range(heads):
            query, delta = q_ref[here, columns[h]], do_ref[here, columns[h]]
            scores = dot_nt(keys[h], jnp.concatenate([query, aux_ref[here, columns[h]]], axis=1))
            delta_probs = dot_nt(
                values[h], jnp.concatenate([delta, inner_ref[here, columns[h]]], axis=1)
            )
            probs = jnp.where(mask, jnp.exp2(scores * SCORE), 0.0)
            delta_scores = (probs * delta_probs).astype(BF16)
            value_acc[h] += dot_nn(probs.astype(BF16), delta)
            key_acc[h] += dot_nn(delta_scores, query)
            head_rows = slice(h * HEAD, (h + 1) * HEAD)
            dqt_ref[head_rows, here] += dot_nn(turned[head_rows, :], delta_scores)
        return carry

    lax.fori_loop(step, last + 1, body, 0)
    for pair in range(heads // 2):
        tile = slice(pair * 128, (pair + 1) * 128)
        dk_ref[:, tile] = jnp.where(left, key_acc[2 * pair], key_acc[2 * pair + 1])
        dv_ref[:, tile] = jnp.where(left, value_acc[2 * pair], value_acc[2 * pair + 1])


def attend_back(lengths, me, pad_row, queries, keys, values, aux_pieces, mixed_pieces, delta_pieces):
    count, width = queries.shape
    heads = width // HEAD
    pieces = len(delta_pieces)
    return pl.pallas_call(
        functools.partial(attend_back_kernel, lengths.shape[0], pieces),
        grid_spec=pltpu.PrefetchScalarGridSpec(
            num_scalar_prefetch=2,
            grid=(count // BLK,),
            in_specs=[whole(1, count)]
            + [whole(count, width)] * 3
            + [whole(2 * count // pieces, width)] * pieces
            + [piece_spec((array, lead, 0), count // pieces, 0) for array, lead in delta_pieces],
            out_specs=[whole(width, count), rows(BLK, width), rows(BLK, width)],
            scratch_shapes=[
                pltpu.VMEM((count, width), BF16),
                pltpu.VMEM((count, width), BF16),
                pltpu.VMEM((count, width), BF16),
                pltpu.VMEM((heads, BLK, 128), F32),
                pltpu.VMEM((heads, BLK, 128), F32),
            ],
        ),
        out_shape=[like((width, count), F32), like((count, width), F32), like((count, width), F32)],
        compiler_params=params(),
        cost_estimate=cost(8 * count * count * width, 22 * count * width, count * count * heads // 3),
        name="attend_back",
    )(lengths, me, pad_row, queries, keys, values, *aux_pieces, *mixed_pieces, *[array for array, lead in delta_pieces])


def unit_of(values):
    factor = lax.rsqrt(jnp.mean(values * values, axis=1, keepdims=True) + EPSILON)
    return values * factor, factor


def unit_back(delta, unit, factor):
    return factor * (delta - unit * jnp.mean(delta * unit, axis=1, keepdims=True))


def mixer_kernel(pieces, *refs):
    mixed_refs, out_weights = refs[:pieces], refs[pieces : 2 * pieces]
    tokens_ref, alpha_ref, low_ref, one_ref, unit_ref, unit_factor, one_factor = refs[2 * pieces :]
    branch = dot_nn(mixed_refs[0][...], out_weights[0][...])
    for mixed, weight in zip(mixed_refs[1:], out_weights[1:]):
        branch += dot_nn(mixed[...], weight[...])
    unit, factor = unit_of(branch * SCALE_MODEL)
    unit_ref[...] = unit
    unit_factor[...] = jnp.broadcast_to(factor, unit_factor.shape)
    residual = tokens_ref[...].astype(F32)
    hidden, factor = unit_of(residual + alpha_ref[...] * (unit - residual))
    one_ref[...] = hidden
    one_factor[...] = jnp.broadcast_to(factor, one_factor.shape)
    low_ref[...] = hidden.astype(BF16)


def mixer(mixed_pieces, out_weights, me, tokens_all, alpha):
    width = mixed_pieces[0][0].shape[-1]
    pieces = len(mixed_pieces)
    count = tokens_all.shape[0] // pieces
    depth = tokens_all.shape[1]
    blocks = count // BLK
    kernel = functools.partial(mixer_kernel, pieces)
    return pl.pallas_call(
        lambda me_ref, *refs: kernel(*refs),
        grid_spec=pltpu.PrefetchScalarGridSpec(
            num_scalar_prefetch=1,
            grid=(blocks,),
            in_specs=[piece_spec((array, lead, 0), BLK, 1) for array, lead in mixed_pieces]
            + [piece_spec((array, lead, 0), width, 0) for array, lead in out_weights]
            + [
                pl.BlockSpec((BLK, depth), lambda i, me_ref: (me_ref[0] * blocks + i, 0)),
                whole(1, depth),
            ],
            out_specs=[rows(BLK, depth)] * 3 + [rows(BLK, 128)] * 2,
        ),
        out_shape=[like((count, depth), BF16)]
        + [like((count, depth), F32)] * 2
        + [like((count, 128), F32)] * 2,
        compiler_params=params(),
        cost_estimate=cost(2 * count * depth * depth, 16 * count * depth + 2 * depth * depth),
        name="mixer",
    )(me, *[p[0] for p in mixed_pieces], *[w[0] for w in out_weights], tokens_all, alpha)


def turn_kernel(pieces, me_ref, *refs):
    own_ref, near_ref, far_ref, one_ref = refs[:4]
    seed_refs = refs[4 : 4 + pieces]
    pad_ref, alpha_ref = refs[4 + pieces : 6 + pieces]
    pair_refs = refs[6 + pieces : 6 + pieces + pieces // 2]
    low_ref, hidden_ref, alpha_sum, seed, layer = refs[6 + pieces + pieces // 2 :]
    width = seed_refs[0].shape[-1]
    starts = [
        pl.multiple_of(jnp.bitwise_xor(me_ref[0], place) * width, width) for place in range(pieces)
    ]
    for start, piece in zip(starts, seed_refs):
        seed[:, pl.ds(start, width)] = piece[...]

    @pl.when(pl.program_id(0) == 0)
    def clear():
        alpha_sum[...] = jnp.zeros_like(alpha_sum)

    branch = (own_ref[...].astype(F32) + near_ref[...].astype(F32)) + far_ref[...].astype(F32)
    unit, unit_factor = unit_of(branch)
    hidden = one_ref[...]
    alpha = alpha_ref[...]
    layer_rows, layer_factor = unit_of(hidden + alpha * (unit - hidden))
    layer[...] = layer_rows.astype(BF16)
    for offset, start in enumerate(starts):
        pair_refs[offset // 2][offset % 2] = layer[:, pl.ds(start, width)]
    delta = unit_back(seed[...].astype(F32) * pad_ref[...], layer_rows, layer_factor)
    alpha_sum[...] += jnp.sum(delta * (unit - hidden), axis=0, keepdims=True)
    hidden_ref[...] = (1.0 - alpha) * delta
    low_ref[...] = unit_back(alpha * delta, unit, unit_factor).astype(BF16)


def turn(me, own, near, far, hidden_one, seed_pieces, pad_rows, alpha):
    count, depth = hidden_one.shape
    pieces = len(seed_pieces)
    width = depth // pieces
    return pl.pallas_call(
        functools.partial(turn_kernel, pieces),
        grid_spec=pltpu.PrefetchScalarGridSpec(
            num_scalar_prefetch=1,
            grid=(count // BLK,),
            in_specs=[rows(BLK, depth)] * 4
            + [piece_spec((array, lead, 0), BLK, 1) for array, lead in seed_pieces]
            + [rows(BLK, 1), whole(1, depth)],
            out_specs=[pl.BlockSpec((2, BLK, width), lambda i, *_: (0, i, 0))] * (pieces // 2)
            + [rows(BLK, depth), rows(BLK, depth), whole(1, depth)],
            scratch_shapes=[pltpu.VMEM((BLK, depth), BF16)] * 2,
        ),
        out_shape=[like((2, count, width), BF16)] * (pieces // 2)
        + [like((count, depth), BF16), like((count, depth), F32), like((1, depth), F32)],
        compiler_params=params(),
        cost_estimate=cost(40 * count * depth, 20 * count * depth),
        name="turn",
    )(me, own, near, far, hidden_one, *[p[0] for p in seed_pieces], pad_rows, alpha)


def mixer_back_kernel(pieces, *refs):
    hidden_ref, own_ref, near_ref, far_ref, one_ref, unit_ref = refs[:6]
    one_factor, unit_factor, tokens_ref, alpha_ref = refs[6:10]
    out_weights = refs[10 : 10 + pieces]
    pair_refs = refs[10 + pieces : 10 + pieces + pieces // 2]
    low_ref, direct_ref, alpha_sum = refs[10 + pieces + pieces // 2 :]

    @pl.when(pl.program_id(0) == 0)
    def clear():
        alpha_sum[...] = jnp.zeros_like(alpha_sum)

    delta = hidden_ref[...] + (
        (own_ref[...].astype(F32) + near_ref[...].astype(F32)) + far_ref[...].astype(F32)
    )
    unit = unit_ref[...]
    alpha = alpha_ref[...]
    delta = unit_back(delta, one_ref[...], one_factor[:, :1])
    alpha_sum[...] += jnp.sum(delta * (unit - tokens_ref[...].astype(F32)), axis=0, keepdims=True)
    direct_ref[...] = (1.0 - alpha) * delta
    low = unit_back(alpha * delta, unit, unit_factor[:, :1]).astype(BF16)
    low_ref[...] = low
    for offset, weight in enumerate(out_weights):
        pair_refs[offset // 2][offset % 2] = (dot_nt(low, weight[...]) * SCALE_MODEL).astype(BF16)


def mixer_back(
    me, hidden, own, near, far, one, unit, one_factor, unit_factor, tokens_all, alpha, out_weights
):
    count, depth = one.shape
    pieces = len(out_weights)
    width = depth // pieces
    blocks = count // BLK
    kernel = functools.partial(mixer_back_kernel, pieces)
    return pl.pallas_call(
        lambda me_ref, *refs: kernel(*refs),
        grid_spec=pltpu.PrefetchScalarGridSpec(
            num_scalar_prefetch=1,
            grid=(blocks,),
            in_specs=[rows(BLK, depth)] * 6
            + [rows(BLK, 128)] * 2
            + [
                pl.BlockSpec((BLK, depth), lambda i, me_ref: (me_ref[0] * blocks + i, 0)),
                whole(1, depth),
            ]
            + [piece_spec((array, lead, 0), width, 0) for array, lead in out_weights],
            out_specs=[pl.BlockSpec((2, BLK, width), lambda i, *_: (0, i, 0))] * (pieces // 2)
            + [rows(BLK, depth), rows(BLK, depth), whole(1, depth)],
        ),
        out_shape=[like((2, count, width), BF16)] * (pieces // 2)
        + [like((count, depth), BF16), like((count, depth), F32), like((1, depth), F32)],
        compiler_params=params(),
        cost_estimate=cost(2 * count * depth * depth, 28 * count * depth + 2 * depth * depth),
        name="mixer_back",
    )(me, hidden, own, near, far, one, unit, one_factor, unit_factor, tokens_all, alpha, *[w[0] for w in out_weights])


def pick(half, first_ref, second_ref, out_ref):
    step = pl.program_id(0)

    @pl.when(step < half)
    def from_first():
        out_ref[...] = first_ref[...]

    @pl.when(step >= half)
    def from_second():
        out_ref[...] = second_ref[...]


def put(half, value, first_ref, second_ref):
    step = pl.program_id(0)

    @pl.when(step < half)
    def to_first():
        first_ref[...] = value

    @pl.when(step >= half)
    def to_second():
        second_ref[...] = value


def whole_weight(tok_ref, piece_refs, out_ref):
    if out_ref is None:
        return piece_refs[0]

    @pl.when(pl.program_id(0) == 0)
    def assemble_weight():
        place_columns(tok_ref[0], piece_refs, out_ref)

    return out_ref


def expand_kernel(half, pieces, tok_ref, first_ref, second_ref, gain_ref, *refs):
    up_pieces, gate_pieces = refs[:pieces], refs[pieces : 2 * pieces]
    up_ref, gate_ref, mid_ref = refs[2 * pieces : 2 * pieces + 3]
    hidden_ref = refs[-1]
    outs = refs[2 * pieces + 3 : -1] or (None, None)
    up_w = whole_weight(tok_ref, up_pieces, outs[0])
    gate_w = whole_weight(tok_ref, gate_pieces, outs[1])
    pick(half, first_ref, second_ref, hidden_ref)
    hidden = hidden_ref[...]
    up = dot_nt(hidden, up_w[...]) * SCALE_MODEL
    gate = dot_nt(hidden, gate_w[...]) * SCALE_MODEL
    up_ref[...] = up.astype(BF16)
    gate_ref[...] = gate.astype(BF16)
    scaled = gain_ref[1:2, :] * gate
    mid_ref[...] = (gain_ref[0:1, :] * up * scaled * jax.nn.sigmoid(scaled)).astype(BF16)


def expand(tok, first, second, up_pieces, gate_pieces, gains):
    count, depth = first.shape
    hidden = gains.shape[1]
    half = count // BLK
    pieces = len(up_pieces)
    outs = 2 if pieces > 1 else 0
    return pl.pallas_call(
        functools.partial(expand_kernel, half, pieces),
        grid_spec=pltpu.PrefetchScalarGridSpec(
            num_scalar_prefetch=1,
            grid=(2 * half,),
            in_specs=[piece_rows(half, 0, depth), piece_rows(half, 1, depth), whole(2, hidden)]
            + [piece_spec(piece, hidden, 0) for piece in (*up_pieces, *gate_pieces)],
            out_specs=[rows(BLK, hidden)] * 3 + [whole(hidden, depth)] * outs,
            scratch_shapes=[pltpu.VMEM((BLK, depth), BF16)],
        ),
        out_shape=[like((2 * count, hidden), BF16)] * 3 + [like((hidden, depth), BF16)] * outs,
        compiler_params=params(),
        cost_estimate=cost(
            8 * count * depth * hidden,
            4 * count * (depth + 3 * hidden) + 4 * depth * hidden,
            2 * count * hidden,
        ),
        name="expand",
    )(tok, first, second, gains, *[piece[0] for piece in (*up_pieces, *gate_pieces)])


def contract_kernel(half, pieces, tok_ref, mid_ref, *refs):
    first_ref, second_ref = refs[pieces : pieces + 2]
    outs = refs[pieces + 2 :] or (None,)
    down_w = whole_weight(tok_ref, refs[:pieces], outs[0])
    put(half, (dot_nn(mid_ref[...], down_w[...]) * SCALE_HIDDEN).astype(BF16), first_ref, second_ref)


def contract(tok, middle, down_pieces, depth, needs=()):
    count, hidden = middle.shape
    half = count // 2 // BLK
    pieces = len(down_pieces)
    outs = 1 if pieces > 1 else 0
    return launch(
        functools.partial(contract_kernel, half, pieces),
        needs,
        (tok,),
        (2 * half,),
        [rows(BLK, hidden)] + [piece_spec(piece, hidden, 0) for piece in down_pieces],
        (middle, *[piece[0] for piece in down_pieces],),
        out_specs=[piece_rows(half, 0, depth), piece_rows(half, 1, depth)]
            + [whole(hidden, depth)] * outs,
        out_shape=[like((count // 2, depth), BF16)] * 2 + [like((hidden, depth), BF16)] * outs,
        cost_estimate=cost(
            2 * count * depth * hidden, 2 * count * (depth + hidden) + 2 * depth * hidden
        ),
        name="contract",
    )


def gated_back_kernel(
    half,
    first_ref,
    second_ref,
    up_ref,
    gate_ref,
    up_w,
    gate_w,
    down_w,
    gain_ref,
    both_ref,
    first_out,
    second_out,
    unit_ref,
    delta_ref,
):
    @pl.when(pl.program_id(0) == 0)
    def clear():
        unit_ref[...] = jnp.zeros_like(unit_ref)

    pick(half, first_ref, second_ref, delta_ref)
    delta_middle = dot_nt(delta_ref[...], down_w[...]) * SCALE_HIDDEN
    up = up_ref[...].astype(F32)
    gate = gate_ref[...].astype(F32)
    scaled = gain_ref[1:2, :] * gate
    sigmoid = jax.nn.sigmoid(scaled)
    shared = delta_middle * sigmoid
    delta_up = shared * scaled
    delta_gate = shared * (gain_ref[0:1, :] * up) * (1.0 + scaled * (1.0 - sigmoid))
    unit_ref[0:1, :] += jnp.sum(delta_up * up, axis=0, keepdims=True)
    unit_ref[1:2, :] += jnp.sum(delta_gate * gate, axis=0, keepdims=True)
    up_low = (gain_ref[0:1, :] * delta_up).astype(BF16)
    gate_low = (gain_ref[1:2, :] * delta_gate).astype(BF16)
    both_ref[:, : up_low.shape[1]] = up_low
    both_ref[:, up_low.shape[1] :] = gate_low
    total = (dot_nn(up_low, up_w[...]) + dot_nn(gate_low, gate_w[...])) * SCALE_MODEL
    put(half, total.astype(BF16), first_out, second_out)


def gated_back(first, second, up, gate, up_w, gate_w, down_w, gains):
    count, depth = first.shape
    hidden = up_w.shape[0]
    half = count // BLK
    return pl.pallas_call(
        functools.partial(gated_back_kernel, half),
        grid=(2 * half,),
        in_specs=[piece_rows(half, 0, depth), piece_rows(half, 1, depth)]
        + [rows(BLK, hidden)] * 2
        + [whole(hidden, depth)] * 3
        + [whole(2, hidden)],
        out_specs=[rows(BLK, 2 * hidden)]
        + [piece_rows(half, 0, depth), piece_rows(half, 1, depth), whole(2, hidden)],
        scratch_shapes=[pltpu.VMEM((BLK, depth), BF16)],
        out_shape=[like((2 * count, 2 * hidden), BF16)]
        + [like((count, depth), BF16)] * 2
        + [like((2, hidden), F32)],
        compiler_params=params(),
        cost_estimate=cost(
            12 * count * depth * hidden,
            8 * count * (depth + hidden) + 6 * depth * hidden,
            2 * count * hidden,
        ),
        name="gated_back",
    )(first, second, up, gate, up_w, gate_w, down_w, gains)


def part_columns(tok_ref, total, part_refs):
    width = part_refs[0].shape[2]
    for offset in range(8):
        start = pl.multiple_of(jnp.bitwise_xor(tok_ref[0], offset) * width, width)
        place = offset % 2 * 2 + offset // 2 % 2
        value = total[:, pl.ds(start, width)].astype(BF16)
        if place < 3 or len(part_refs) == 4:
            part_refs[place][offset // 4] = value
        else:
            half = pl.num_programs(0) // 2

            @pl.when(pl.program_id(0) < half)
            def first_half(value=value, lead=offset // 4):
                part_refs[3][lead] = value

            @pl.when(pl.program_id(0) >= half)
            def second_half(value=value, lead=offset // 4):
                part_refs[4][lead] = value


def weight_grad_kernel(lefts, rights, scale, steps, outs, tok_ref, *refs):
    left_refs, right_refs = refs[:lefts], refs[lefts : lefts + rights]
    fold_refs, part_refs = refs[lefts + rights : -outs - 1], refs[-outs - 1 : -1]
    total = refs[-1]

    @pl.when(pl.program_id(0) < steps)
    def product():
        acc, lefts_in = None, []
        for ref in left_refs:
            count = right_refs[0].shape[0]
            lefts_in += [ref[k * count : (k + 1) * count, :] for k in range(ref.shape[0] // count)]
        for left, right in zip(lefts_in, right_refs):
            term = lax.dot_general(
                left, right[...], (((0,), (0,)), ((), ())), preferred_element_type=F32
            )
            acc = term if acc is None else acc + term
        total[...] = acc * scale

    if fold_refs:

        @pl.when(pl.program_id(0) >= steps)
        def fold():
            own, near, far = [ref[...].astype(F32) for ref in fold_refs]
            total[...] = (own + near) + far

    part_columns(tok_ref, total, part_refs)


def weight_grad(tok, groups, lefts, rights, scale, folds=(), halves=False, needs=()):
    height = lefts[0].shape[1]
    depth = rights[0].shape[1]
    count = sum(left.shape[0] for left in lefts)
    part = depth // groups
    steps = height // BLK
    out = pl.BlockSpec((groups // 4, BLK, part), lambda i, *_: (0, i, 0))
    total_height = height + (BLK if folds else 0)
    outs, heights = [out] * 4, [total_height] * 4
    if halves:
        half = steps // 2
        outs[3:] = [
            pl.BlockSpec((groups // 4, BLK, part), lambda i, *_: (0, jnp.minimum(i, half - 1), 0)),
            pl.BlockSpec((groups // 4, BLK, part), lambda i, *_: (0, jnp.maximum(i - half, 0), 0)),
        ]
        heights[3:] = [height // 2] * 2
    return launch(
        functools.partial(
            weight_grad_kernel, len(lefts), len(rights), scale, steps, len(outs)
        ),
        needs,
        (tok,),
        (total_height // BLK,),
        [
                pl.BlockSpec((left.shape[0], BLK), lambda i, *_: (0, jnp.minimum(i, steps - 1)))
                for left in lefts
            ]
            + [whole(*right.shape) for right in rights]
            + [piece_spec((array, lead, 0), BLK, 0) for array, lead in folds],
        (*lefts, *rights, *[array for array, lead in folds],),
        scratch_shapes=[pltpu.VMEM((BLK, depth), F32)],
        out_specs=outs,
        out_shape=[like((groups // 4, tall, part), BF16) for tall in heights],
        cost_estimate=cost(
            2 * count * height * depth, 2 * count * (height + depth) + 2 * height * depth
        ),
        name="weight_grad",
    )


def out_grad_kernel(pieces, *refs):
    right, pair_refs = refs[pieces], refs[pieces + 1 :]
    for offset, left in enumerate(refs[:pieces]):
        total = lax.dot_general(
            left[...], right[...], (((0,), (0,)), ((), ())), preferred_element_type=F32
        )
        pair_refs[offset // 2][offset % 2] = (total * SCALE_MODEL).astype(BF16)


def out_grad(lefts, right):
    width = lefts[0][0].shape[-1]
    count, depth = right.shape
    pieces = len(lefts)
    return pl.pallas_call(
        functools.partial(out_grad_kernel, pieces),
        grid=(1,),
        in_specs=[piece_spec((array, lead, 0), count, 0) for array, lead in lefts]
        + [whole(count, depth)],
        out_specs=[whole(2, width, depth)] * (pieces // 2),
        out_shape=[like((2, width, depth), BF16)] * (pieces // 2),
        compiler_params=params(),
        cost_estimate=cost(2 * count * depth * depth, 4 * count * depth + 2 * depth * depth),
        name="out_grad",
    )(*[p[0] for p in lefts], right)


def project_back_kernel(pieces, me_ref, dqt_ref, dk_ref, dv_ref, raw_ref, gain_ref, w_ref, direct_ref, *refs):
    low_ref, scale_sum, total = refs[0], refs[1 + pieces], refs[2 + pieces]
    part_refs = refs[1 : 1 + pieces]
    step = pl.program_id(0)
    width = dk_ref.shape[1]
    scale_head = HEAD**-0.5

    @pl.when(step == 0)
    def clear():
        scale_sum[...] = jnp.zeros_like(scale_sum)

    ones = head_matrix(width)
    gain = gain_ref[...]
    for place, delta in enumerate((jnp.transpose(dqt_ref[...]), dk_ref[...])):
        here = slice(place * width, (place + 1) * width)
        values = raw_ref[:, here]
        factor = lax.rsqrt(head_mean(values * values, ones) + EPSILON)
        unit = values * factor
        delta = delta * scale_head
        scale_sum[...] += jnp.sum(delta * unit, axis=0, keepdims=True)
        delta = gain * delta
        low_ref[:, here] = (factor * (delta - unit * head_mean(delta * unit, ones))).astype(BF16)
    low_ref[:, 2 * width :] = dv_ref[...].astype(BF16)
    total[...] = dot_nn(low_ref[...], w_ref[...]) * SCALE_MODEL
    own_blocks = direct_ref.shape[0] // BLK

    @pl.when(step // own_blocks == me_ref[0])
    def add_direct():
        start = pl.multiple_of(lax.rem(step, own_blocks) * BLK, BLK)
        total[...] += direct_ref[pl.ds(start, BLK), :]

    part = total.shape[1] // pieces
    for place, out in enumerate(part_refs):
        start = pl.multiple_of(jnp.bitwise_xor(me_ref[0], place) * part, part)
        out[...] = total[:, pl.ds(start, part)].astype(BF16)


def project_back(me, pieces, dqt, dk, dv, raw, gain, weight, direct):
    count, width = dk.shape
    depth = weight.shape[1]
    part = depth // pieces
    return pl.pallas_call(
        functools.partial(project_back_kernel, pieces),
        grid_spec=pltpu.PrefetchScalarGridSpec(
            num_scalar_prefetch=1,
            grid=(count // BLK,),
            in_specs=[
                pl.BlockSpec((width, BLK), lambda i, *_: (0, i)),
                rows(BLK, width),
                rows(BLK, width),
                rows(BLK, 2 * width),
                whole(1, width),
                whole(3 * width, depth),
                whole(*direct.shape),
            ],
            out_specs=[rows(BLK, 3 * width)] + [rows(BLK, part)] * pieces + [whole(1, width)],
            scratch_shapes=[pltpu.VMEM((BLK, depth), F32)],
        ),
        out_shape=[like((count, 3 * width), BF16)]
        + [like((count, part), BF16)] * pieces
        + [like((1, width), F32)],
        compiler_params=params(),
        cost_estimate=cost(6 * count * width * depth, count * (26 * width + 2 * depth)),
        name="project_back",
    )(me, dqt, dk, dv, raw, gain, weight, direct)


def trade(value, axis, offset):
    size = lax.axis_size(axis)
    return lax.ppermute(value, axis, [(i, i ^ offset) for i in range(size)])


def sum_over(value, axis):
    offset = 1
    while offset < lax.axis_size(axis):
        value = value + trade(value, axis, offset)
        offset *= 2
    return value


def join(*values):
    return lax.optimization_barrier(values)


def stack(*values):
    return jnp.concatenate([v if v.ndim == 3 else v[None] for v in values], axis=0)


def add_low(*values):
    total = values[0].astype(F32)
    for value in values[1:]:
        total = total + value.astype(F32)
    return total


def plain_sum(left, right, scale):
    total = jnp.einsum("tr,td->rd", left, right, preferred_element_type=F32) * scale
    return lax.psum_scatter(total.astype(BF16), "tok", scatter_dimension=1, tiled=True).astype(F32)


def moment_update(weights, gradient, moment, square, fix_first, fix_second):
    moment_next = BETA_ONE * moment + (1.0 - BETA_ONE) * gradient
    square_next = BETA_TWO * square + (1.0 - BETA_TWO) * gradient * gradient
    stepped = weights - LEARN_RATE * (moment_next / fix_first) / (
        jnp.sqrt(square_next / fix_second) + ADAM_EPSILON
    )
    return (stepped, moment_next, square_next)


def local(
    inputs,
    cotangent,
    lengths,
    pad_mask,
    attention_weights,
    gated_weights,
    model_gains,
    unit_gains,
    attention_moment,
    attention_square,
    gated_moment,
    gated_square,
    model_moment,
    model_square,
    unit_moment,
    unit_square,
):
    token_count, width = inputs.shape
    parts = lax.axis_size("dim")
    hidden_here = gated_weights.shape[1]
    own_count = token_count // parts
    place = lax.axis_index("dim")
    me = place.astype(jnp.int32).reshape(1)
    tok = lax.axis_index("tok").astype(jnp.int32).reshape(1)
    groups = lax.axis_size("tok")
    by_pieces = groups == 8 and (D // groups) % 128 == 0
    blocks = own_count // BLK
    length_row = lengths[0]

    def token_rows(value, offset):
        return lax.dynamic_slice_in_dim(value, (place ^ offset) * own_count, own_count, 0)

    ao = attention_weights.reshape(4 * width, -1).astype(BF16)
    both_own = gated_weights[:2].reshape(2 * hidden_here, -1).astype(BF16)
    down_own = gated_weights[2].astype(BF16)
    score_gain = model_gains[:1]
    pad_row = pad_mask[None, :]
    pad_rows = token_rows(pad_mask, 0).astype(F32)[:, None]

    x_far = trade(inputs, "dim", 2)
    seed_rows = [token_rows(cotangent, r) for r in range(parts)]
    seed_send = stack(*seed_rows[2:])
    alphas = lax.dynamic_update_slice(
        jnp.zeros((2, D), F32), model_gains[1:], (0, place * width)
    )
    if by_pieces:
        ao_by = {0: ao, 4: trade(ao, "tok", 4), 2: trade(ao, "tok", 2), 1: trade(ao, "tok", 1)}
        ao_by[6] = trade(ao_by[4], "tok", 2)
        ao_by[5] = trade(ao_by[4], "tok", 1)
        ao_by[3] = trade(ao_by[2], "tok", 1)
        x_far, ao_by, both_own, seed_send, alphas = join(
            x_far, ao_by, both_own, seed_send, alphas
        )
        ao_by[7] = trade(ao_by[6], "tok", 1)
        by = {0: both_own, 2: trade(both_own, "tok", 2), 4: trade(both_own, "tok", 4)}
    else:
        gather = functools.partial(lax.all_gather, axis_name="tok", axis=1, tiled=True)
        in_pieces = [(gather(ao[: 3 * width]), None, 0)]
        out_weight, up_w, gate_w, down_w = [
            gather(shard)
            for shard in (ao[3 * width :], both_own[:hidden_here], both_own[hidden_here:], down_own)
        ]
        up_pieces, gate_pieces, down_pieces = [[(w, None, 0)] for w in (up_w, gate_w, down_w)]
    x_near = trade(inputs, "dim", 1)
    x_corner = trade(x_far, "dim", 1)
    token_pieces = [inputs, x_near, x_far, x_corner]
    if by_pieces:
        token_pieces, ao_by, both_own, down_own, seed_send, alphas = join(
            token_pieces, ao_by, both_own, down_own, seed_send, alphas
        )
        in_pieces = [(ao_by[offset], None, 0) for offset in range(8)]
        by[1] = trade(both_own, "tok", 1)
    seed_far = trade(seed_send, "dim", 2)
    alpha_near = trade(alphas, "dim", 1)
    tokens_all, raw, queries, keys, values, weight_in = project(
        me, tok, token_pieces, in_pieces, score_gain
    )
    queries, seed_far = join(queries, seed_far)

    queries, seed_far, alpha_near = join(queries, seed_far, alpha_near)
    alphas = alphas + alpha_near
    alpha_far = trade(alphas, "dim", 2)
    if by_pieces:
        queries, by[1], by[2], by[4], ao_by, down_own = join(
            queries, by[1], by[2], by[4], ao_by, down_own
        )
        by[3] = trade(by[2], "tok", 1)
        by[6] = trade(by[4], "tok", 2)
        out_weight = assemble(
            tok, [(ao_by[o], None, 3 * width // BLK) for o in range(8)], width, (queries,)
        )
    out_across = trade(out_weight, "dim", 2)
    far_mixed, far_aux = attend(
        length_row, me, (2, 3), blocks, pad_row, queries, keys, values, (out_weight,)
    )
    far_mixed, alpha_far, out_across = join(far_mixed, alpha_far, out_across)
    alphas = alphas + alpha_far
    alpha_mixer, alpha_gated = alphas[:1], alphas[1:]
    if by_pieces:
        far_mixed, by[3], by[6], down_own = join(far_mixed, by[3], by[6], down_own)
        by[5] = trade(by[4], "tok", 1)
        down_by = {0: down_own, 2: trade(down_own, "tok", 2), 4: trade(down_own, "tok", 4)}
    far_came = trade(far_mixed, "dim", 2)
    out_pair = trade(stack(out_weight, out_across), "dim", 1)
    near_mixed, near_aux = attend(
        length_row, me, (0, 1), blocks, pad_row, queries, keys, values, (far_mixed,)
    )
    near_mixed, far_came, out_pair = join(near_mixed, far_came, out_pair)
    if by_pieces:
        near_mixed, by[5], by[6], down_by = join(near_mixed, by[5], by[6], down_by)
    pair_came = trade(stack(near_mixed[own_count:], far_came[own_count:]), "dim", 1)
    out_weights = [(out_weight, None), (out_pair, 0), (out_across, None), (out_pair, 1)]
    mixed_pieces = [(near_mixed, None), (pair_came, 0), (far_came, None), (pair_came, 1)]
    hidden_low, hidden_one, mixer_unit, mixer_factor, one_factor = mixer(
        mixed_pieces, out_weights, me, tokens_all, alpha_mixer
    )

    h_far = trade(hidden_low, "dim", 2)
    h_near = trade(hidden_low, "dim", 1)
    if by_pieces:
        h_near, by[6], down_by = join(h_near, by[6], down_by)
        by[7] = trade(by[6], "tok", 1)
        down_by[1] = trade(down_by[0], "tok", 1)
        down_by[6] = trade(down_by[4], "tok", 2)
        h_near, by[7], down_by = join(h_near, by[7], down_by)
        down_by[3] = trade(down_by[2], "tok", 1)
        down_by[5] = trade(down_by[4], "tok", 1)
        up_pieces, gate_pieces = [[(by[o], None, k) for o in range(8)] for k in range(2)]
        up_one, gate_one, mid_one, up_w, gate_w = expand(
            tok, hidden_low, h_near, up_pieces, gate_pieces, unit_gains
        )
        up_pieces, gate_pieces = [(up_w, None, 0)], [(gate_w, None, 0)]
    else:
        up_one, gate_one, mid_one = expand(
            tok, hidden_low, h_near, up_pieces, gate_pieces, unit_gains
        )
    mid_one, h_far = join(mid_one, h_far)
    if by_pieces:
        mid_one, down_by = join(mid_one, down_by)
        down_by[7] = trade(down_by[6], "tok", 1)
    h_corner = trade(h_far, "dim", 1)
    seed_pair = trade(stack(seed_rows[1], seed_far[1]), "dim", 1)
    seed_pieces = [(seed_rows[0], None), (seed_pair, 0), (seed_far, 0), (seed_pair, 1)]
    up_two, gate_two, mid_two = expand(tok, h_far, h_corner, up_pieces, gate_pieces, unit_gains)
    if by_pieces:
        mid_two, down_by = join(mid_two, down_by)
        down_pieces = [(down_by[o], None, 0) for o in range(8)]
        *far_parts, down_w = contract(tok, mid_two, down_pieces, D)
        down_pieces = [(down_w, None, 0)]
    else:
        far_parts = contract(tok, mid_two, down_pieces, D)
    corner = trade(far_parts[1], "dim", 1)
    across = add_low(far_parts[0], corner).astype(BF16)
    far = trade(across, "dim", 2)
    own, pair = contract(tok, mid_one, down_pieces, D, (across,))
    own, pair, far = join(own, pair, far)
    near = trade(pair, "dim", 1)
    layer_near, layer_far, delta_branch, delta_hidden, sum_gated = turn(
        me, own, near, far, hidden_one, seed_pieces, pad_rows, alpha_gated
    )

    b_near = trade(delta_branch, "dim", 1)
    b_far = trade(delta_branch, "dim", 2)
    both_one, own, pair, unit_one = gated_back(
        delta_branch, b_near, up_one, gate_one, up_w, gate_w, down_w, unit_gains
    )
    both_one, b_far, pair = join(both_one, b_far, pair)
    near = trade(pair, "dim", 1)
    b_corner = trade(b_far, "dim", 1)
    both_two, across, corner, unit_two = gated_back(
        b_far, b_corner, up_two, gate_two, up_w, gate_w, down_w, unit_gains
    )
    corner = trade(corner, "dim", 1)
    across = add_low(across, corner).astype(BF16)
    far = trade(across, "dim", 2)
    both_pieces = [both_one, both_two]
    unit_sums = unit_one + unit_two
    h_pieces = [hidden_low, h_near, h_far, h_corner]
    b_pieces = [delta_branch, b_near, b_far, b_corner]
    if by_pieces:
        down_parts = weight_grad(
            tok, groups, (mid_one, mid_two), b_pieces, SCALE_HIDDEN, needs=(across,)
        )
        down_odd = trade(down_parts[3], "tok", 1)
        both_parts = weight_grad(
            tok,
            groups,
            both_pieces,
            h_pieces,
            SCALE_MODEL,
            halves=True,
            needs=(down_parts[0],),
        )
        own, near, far, both_parts, down_odd = join(own, near, far, both_parts, down_odd)
        up_odd = trade(both_parts[3], "tok", 1)
        down_low = add_low(down_parts[1], down_odd).astype(BF16)
        down_near = trade(down_low, "tok", 2)
    else:
        down_grad = plain_sum(
            jnp.concatenate([mid_one, mid_two], axis=0),
            jnp.concatenate(b_pieces, axis=0),
            SCALE_HIDDEN,
        )
        both_grad = plain_sum(
            jnp.concatenate(both_pieces, axis=0),
            jnp.concatenate(h_pieces, axis=0),
            SCALE_MODEL,
        )

    delta_near, delta_far, mixer_low, delta_direct, sum_mixer = mixer_back(
        me,
        delta_hidden,
        own,
        near,
        far,
        hidden_one,
        mixer_unit,
        one_factor,
        mixer_factor,
        tokens_all,
        alpha_mixer,
        out_weights,
    )
    if by_pieces:
        delta_far, mixer_low, up_odd, down_near = join(delta_far, mixer_low, up_odd, down_near)
        gate_odd = trade(both_parts[4], "tok", 1)
    delta_came = trade(delta_far, "dim", 2)
    out_near_grad, out_far_grad = out_grad(mixed_pieces, mixer_low)
    alpha_sums = jnp.concatenate([sum_mixer, sum_gated], axis=0)
    alpha_near = trade(alpha_sums, "dim", 1)
    delta_came, out_near_grad, out_far_grad, alpha_near = join(
        delta_came, out_near_grad, out_far_grad, alpha_near
    )
    if by_pieces:
        delta_came, gate_odd = join(delta_came, gate_odd)
        both_low = add_low(
            both_parts[1], jnp.concatenate([up_odd, gate_odd], axis=1)
        ).astype(BF16)
        both_near = trade(both_low, "tok", 2)
        both_even = trade(both_parts[2], "tok", 1)
        down_even = trade(down_parts[2], "tok", 1)
    delta_pair = trade(stack(delta_near[1], delta_came[1]), "dim", 1)
    alpha_sums = alpha_sums + alpha_near
    layer_came = trade(join(layer_far, delta_came)[0], "dim", 2)
    out_pair = trade(stack(out_near_grad[1], out_far_grad[1]), "dim", 1)
    delta_pieces = [(delta_near, 0), (delta_pair, 0), (delta_came, 0), (delta_pair, 1)]
    dqt, dk, dv = attend_back(
        length_row,
        me,
        pad_row,
        queries,
        keys,
        values,
        [near_aux, far_aux],
        [near_mixed, far_mixed],
        delta_pieces,
    )
    dqt, alpha_sums, out_pair, layer_came = join(dqt, alpha_sums, out_pair, layer_came)
    alpha_far = trade(alpha_sums, "dim", 2)
    if by_pieces:
        dqt, both_near, both_even, down_even = join(dqt, both_near, both_even, down_even)
        down_low = add_low(down_parts[0][1], down_even[1], down_near[1]).astype(BF16)
        down_last = trade(down_low, "tok", 4)
    out_far_sum = trade(add_low(out_far_grad[0], out_pair[1]).astype(BF16), "dim", 2)
    delta_project, *input_parts, scale_sum = project_back(
        me, parts, dqt, dk, dv, raw, score_gain, weight_in, delta_direct
    )
    input_parts, out_far_sum, alpha_far = join(input_parts, out_far_sum, alpha_far)
    alpha_sums = lax.dynamic_slice_in_dim(alpha_sums + alpha_far, place * width, width, 1)
    if by_pieces:
        input_parts, down_last = join(input_parts, down_last)
    corner = trade(input_parts[3], "dim", 1)
    across = add_low(input_parts[2], corner).astype(BF16)
    far = trade(across, "dim", 2)
    if by_pieces:
        both_low = add_low(both_parts[0][1], both_even[1], both_near[1]).astype(BF16)
        in_parts = weight_grad(
            tok,
            groups,
            (delta_project,),
            (tokens_all,),
            SCALE_MODEL,
            ((out_near_grad, 0), (out_pair, 0), (out_far_sum, None)),
            needs=(across,),
        )
        in_parts, input_parts, layer_near, both_low = join(
            in_parts, input_parts, layer_near, both_low
        )
        both_last = trade(both_low, "tok", 4)
        in_odd = trade(in_parts[3], "tok", 1)
    near = trade(input_parts[1], "dim", 1)
    gains_sum = jnp.concatenate(
        [scale_sum.reshape(-1), alpha_sums.reshape(-1), unit_sums.reshape(-1)]
    )
    if by_pieces:
        in_odd, near, in_parts = join(in_odd, near, in_parts)
        in_low = add_low(in_parts[1], in_odd).astype(BF16)
        in_near = trade(in_low, "tok", 2)
        in_even = trade(in_parts[2], "tok", 1)
        near, far, both_last, in_near, in_even = join(near, far, both_last, in_near, in_even)
        in_low = add_low(in_parts[0][1], in_even[1], in_near[1]).astype(BF16)
        in_last = trade(in_low, "tok", 4)
    layer_pair = trade(stack(layer_near[1], layer_came[1]), "dim", 1)
    layer_pieces = [layer_near[0], layer_pair[0], layer_came[0], layer_pair[1]]
    layer_out = jnp.zeros((token_count, width), BF16)
    for r, piece in enumerate(layer_pieces):
        layer_out = lax.dynamic_update_slice(layer_out, piece, ((place ^ r) * own_count, 0))
    input_gradient = add_low(input_parts[0], near, far)
    if by_pieces:
        down_grad = add_low(down_parts[0][0], down_even[0], down_near[0], down_last)
        both_grad = add_low(both_parts[0][0], both_even[0], both_near[0], both_last)
    gated_grad = jnp.concatenate([both_grad, down_grad], axis=0).reshape(3, hidden_here, -1)
    fix_first = 1.0 - BETA_ONE**STEP
    fix_second = 1.0 - BETA_TWO**STEP
    gated_stepped, moment_gated, square_gated = moment_update(
        gated_weights, gated_grad, gated_moment, gated_square, fix_first, fix_second
    )
    gated_row_sums = jnp.sum(gated_stepped * gated_stepped, axis=2)
    gated_square_sum = jnp.sum(gated_grad * gated_grad)
    if by_pieces:
        in_last, gated_row_sums, gated_square_sum, input_gradient, layer_out = join(
            in_last, gated_row_sums, gated_square_sum, input_gradient, layer_out
        )
        in_total = add_low(in_parts[0][0], in_even[0], in_near[0], in_last)
        attention_grad = in_total.reshape(4, width, -1)
    else:
        out_total = lax.psum_scatter(
            add_low(out_near_grad[0], out_pair[0], out_far_sum).astype(BF16),
            "tok",
            scatter_dimension=1,
            tiled=True,
        ).astype(F32)
        in_total = plain_sum(delta_project, tokens_all, SCALE_MODEL)
        attention_grad = jnp.concatenate([in_total, out_total], axis=0).reshape(4, width, -1)

    attention_stepped, moment_attention, square_attention = moment_update(
        attention_weights, attention_grad, attention_moment, attention_square, fix_first, fix_second
    )
    sums = sum_over(
        jnp.concatenate(
            [
                jnp.sum(attention_stepped * attention_stepped, axis=2).reshape(-1),
                gated_row_sums.reshape(-1),
                gains_sum,
                (jnp.sum(attention_grad * attention_grad) + gated_square_sum).reshape(1),
            ]
        ),
        "tok",
    )
    ends = [4 * width, 4 * width + 3 * hidden_here, 7 * width + 3 * hidden_here]
    model_grad = sums[ends[1] : ends[2]].reshape(3, width)
    unit_grad = sums[ends[2] : -1].reshape(2, hidden_here)
    model_next, moment_model, square_model = moment_update(
        model_gains, model_grad, model_moment, model_square, fix_first, fix_second
    )
    unit_next, moment_unit, square_unit = moment_update(
        unit_gains, unit_grad, unit_moment, unit_square, fix_first, fix_second
    )
    square_sum = sums[-1:] + jnp.sum(model_grad * model_grad) + jnp.sum(unit_grad * unit_grad)
    totals = sum_over(jnp.concatenate([square_sum, jnp.sum(model_next[1:], axis=1)]), "dim")
    attention_rows = sums[: ends[0]].reshape(4, width, 1)
    gated_rows = sums[ends[0] : ends[1]].reshape(3, hidden_here, 1)
    attention_next = attention_stepped * lax.rsqrt(attention_rows / D + EPSILON)
    gated_next = gated_stepped * lax.rsqrt(gated_rows / D + EPSILON)
    gradient_norm = jnp.sqrt(totals[:1])
    mean_alpha = totals[1:] / D
    return (
        layer_out,
        input_gradient,
        attention_next,
        attention_next.astype(BF16),
        moment_attention,
        square_attention,
        gated_next,
        gated_next.astype(BF16),
        moment_gated,
        square_gated,
        model_next,
        moment_model,
        square_model,
        unit_next,
        moment_unit,
        square_unit,
        gradient_norm,
        mean_alpha,
    )


def solution(mesh):
    tokens = P("tok", "dim")
    weights = P(None, "dim", "tok")
    gains = P(None, "dim")
    in_specs = (tokens, tokens, P("tok", None), P("tok"), weights, weights, gains, gains)
    in_specs += (weights,) * 4 + (gains,) * 4
    out_specs = (tokens, tokens) + (weights,) * 8 + (gains,) * 6 + (P(), P())
    return jax.shard_map(local, mesh=mesh, in_specs=in_specs, out_specs=out_specs, check_vma=False)
```

```python
import functools
import math

import jax
import jax.numpy as jnp
from jax import lax
from jax.experimental import pallas as pl
from jax.experimental.pallas import tpu as pltpu
from jax.sharding import PartitionSpec as P

D = 1024
HEAD = 64
FF = 4096
STEP = 4
BLK = 256

EPSILON = 1e-06
ADAM_EPSILON = 1e-08
BETA_ONE = 0.5
BETA_TWO = 0.5
LEARN_RATE = 1.5

F32 = jnp.float32
BF16 = jnp.bfloat16
SCALE_MODEL = D**-0.5
SCALE_HIDDEN = FF**-0.5
SCORE = HEAD**-0.5 * math.log2(math.e)
NEVER = 1 << 24


def dot_nt(left, right):
    return lax.dot_general(left, right, (((1,), (1,)), ((), ())), preferred_element_type=F32)


def dot_nn(left, right):
    return lax.dot_general(left, right, (((1,), (0,)), ((), ())), preferred_element_type=F32)


def split_low(values):
    high = values.astype(BF16)
    return high, (values - high.astype(F32)).astype(BF16)


def params():
    return pltpu.CompilerParams(vmem_limit_bytes=60 << 20)


def cost(flops, traffic, transcendentals=0):
    return pl.CostEstimate(
        flops=int(flops) // 64, bytes_accessed=int(traffic) // 64, transcendentals=int(transcendentals) // 64
    )


def like(shape, dtype):
    return jax.ShapeDtypeStruct(shape, dtype)


def whole(*shape):
    return pl.BlockSpec(shape, lambda *_: (0,) * len(shape))


def rows(count, width):
    return pl.BlockSpec((count, width), lambda i, *_: (i, 0))


def launch(kernel, needs, scalars, grid, in_specs, args, scratch_shapes=(), **options):
    taken = len(scalars) + len(args)

    def body(*refs):
        kernel(*refs[:taken], *refs[taken + len(needs) :])

    return pl.pallas_call(
        body,
        grid_spec=pltpu.PrefetchScalarGridSpec(
            num_scalar_prefetch=len(scalars),
            grid=grid,
            in_specs=[*in_specs] + [pl.BlockSpec(memory_space=pl.ANY)] * len(needs),
            out_specs=options.pop("out_specs"),
            scratch_shapes=scratch_shapes,
        ),
        compiler_params=params(),
        **options,
    )(*scalars, *args, *needs)


def head_matrix(width):
    row = lax.broadcasted_iota(jnp.int32, (width, width), 0)
    column = lax.broadcasted_iota(jnp.int32, (width, width), 1)
    return jnp.where(row // HEAD == column // HEAD, 1.0, 0.0).astype(BF16)


def head_mean(values, ones):
    return dot_nn(values.astype(BF16), ones) * (1.0 / HEAD)


def head_mean_fine(values, ones):
    high, low = split_low(values)
    return (dot_nn(high, ones) + dot_nn(low, ones)) * (1.0 / HEAD)


def project_kernel(pieces, me_ref, tok_ref, *refs):
    piece_refs = refs[:pieces]
    weight_refs = refs[pieces:-7]
    gain_ref, all_ref, raw_ref, q_ref, k_ref, v_ref, w_ref = refs[-7:]
    width = piece_refs[0].shape[1]
    if len(weight_refs) == 1:
        weight = weight_refs[0]
    else:
        weight = w_ref

        @pl.when(pl.program_id(0) == 0)
        def assemble_weight():
            place_columns(tok_ref[0], weight_refs, w_ref)

    place_columns(me_ref[0], piece_refs, all_ref)
    projected = dot_nt(all_ref[...], weight[...]) * SCALE_MODEL
    if weight is not w_ref:
        w_ref[...] = weight[...]
    raw_ref[...] = projected[:, : 2 * width]
    ones = head_matrix(width)
    for place, out in enumerate((q_ref, k_ref)):
        values = projected[:, place * width : (place + 1) * width]
        factor = lax.rsqrt(head_mean_fine(values * values, ones) + EPSILON)
        out[...] = (values * factor * gain_ref[...]).astype(BF16)
    v_ref[...] = projected[:, 2 * width :].astype(BF16)


def place_columns(index, piece_refs, out_ref):
    width = piece_refs[0].shape[1]
    for offset, piece in enumerate(piece_refs):
        start = pl.multiple_of(jnp.bitwise_xor(index, offset) * width, width)
        out_ref[:, pl.ds(start, width)] = piece[...]


def piece_spec(piece, height, step):
    array, lead, block = piece
    width = array.shape[-1]
    if lead is None:
        return pl.BlockSpec((height, width), lambda i, *_: (block + step * i, 0))
    return pl.BlockSpec((None, height, width), lambda i, *_: (lead, block + step * i, 0))


def project(me, tok, pieces, weights, gain):
    count, width = pieces[0].shape
    depth = width * len(pieces)
    return pl.pallas_call(
        functools.partial(project_kernel, len(pieces)),
        grid_spec=pltpu.PrefetchScalarGridSpec(
            num_scalar_prefetch=2,
            grid=(count // BLK,),
            in_specs=[rows(BLK, width)] * len(pieces)
            + [piece_spec(weight, 3 * width, 0) for weight in weights]
            + [whole(1, width)],
            out_specs=[rows(BLK, depth), rows(BLK, 2 * width)]
            + [rows(BLK, width)] * 3
            + [whole(3 * width, depth)],
        ),
        out_shape=[like((count, depth), BF16), like((count, 2 * width), F32)]
        + [like((count, width), BF16)] * 3
        + [like((3 * width, depth), BF16)],
        compiler_params=params(),
        cost_estimate=cost(6 * count * width * depth, count * (4 * depth + 14 * width)),
        name="project",
    )(me, tok, *pieces, *[weight[0] for weight in weights], gain)


def assemble_kernel(tok_ref, *refs):
    place_columns(tok_ref[0], refs[:-1], refs[-1])


def assemble(tok, pieces, count, needs=()):
    width = pieces[0][0].shape[-1]
    depth = width * len(pieces)
    return launch(
        assemble_kernel,
        needs,
        (tok,),
        (count // BLK,),
        [piece_spec(piece, BLK, 1) for piece in pieces],
        (*[piece[0] for piece in pieces],),
        out_specs=rows(BLK, depth),
        out_shape=like((count, depth), BF16),
        cost_estimate=cost(0, 4 * count * depth),
        name="assemble",
    )


def seq_start(place, starts):
    found = jnp.zeros_like(place)
    for start in starts:
        found = jnp.where(place >= start, start, found)
    return found


def later_starts(length_ref, count):
    starts, total = [], jnp.int32(0)
    for position in range(count - 1):
        total = total + length_ref[position]
        starts.append(total)
    return starts


def attend_kernel(count, order, blocks, length_ref, me_ref, pad_ref, q_ref, k_ref, v_ref, *refs):
    mixed_ref, aux_ref, acc_ref = refs
    grid_step = pl.program_id(0)
    step = block_of(order, blocks, grid_step, me_ref)
    first_row = step * BLK
    starts = later_starts(length_ref, count)
    first = seq_start(first_row, starts) // BLK
    lane = lax.broadcasted_iota(jnp.int32, (BLK, 128), 1)
    left = lane < HEAD
    heads = q_ref.shape[1] // HEAD
    zero = jnp.zeros((BLK, 128), BF16)
    one = jnp.ones((BLK, 128), BF16)
    sides = [left if head % 2 == 0 else ~left for head in range(heads)]
    columns = [slice(head // 2 * 128, (head // 2 + 1) * 128) for head in range(heads)]
    queries = [jnp.where(sides[h], q_ref[:, columns[h]], zero) for h in range(heads)]
    acc_ref[...] = jnp.zeros_like(acc_ref)
    row = first_row + lax.broadcasted_iota(jnp.int32, (BLK, 1), 0)
    row_start = seq_start(row, starts)

    def body(block, carry):
        key_rows = pl.ds(pl.multiple_of(block * BLK, BLK), BLK)
        key = block * BLK + lax.broadcasted_iota(jnp.int32, (1, BLK), 1)
        code = jnp.where(pad_ref[:, key_rows] == 1, key, NEVER)
        mask = ((code >= row_start) & (code <= row)) | (key == row)
        for h in range(heads):
            value = jnp.where(sides[h], v_ref[key_rows, columns[h]], one)
            scores = dot_nt(queries[h], k_ref[key_rows, columns[h]])
            powers = jnp.where(mask, jnp.exp2(scores * SCORE), 0.0).astype(BF16)
            acc_ref[h] += dot_nn(powers, value)
        return carry

    lax.fori_loop(first, step + 1, body, 0)
    for pair in range(heads // 2):
        tile = slice(pair * 128, (pair + 1) * 128)
        even, odd = acc_ref[2 * pair], acc_ref[2 * pair + 1]
        total = jnp.where(left, odd, even)
        mixed = jnp.where(left, even, odd)
        mixed_ref[:, tile] = (mixed / pltpu.roll(total, HEAD, 1)).astype(BF16)
        high, low = split_low(jnp.log2(total) * (-1.0 / SCORE))
        aux_ref[:, tile] = jnp.where(lax.rem(lane, HEAD) < HEAD // 2, high, low)


def block_of(order, blocks, grid_step, me_ref):
    offset = order[0] + grid_step // blocks
    return jnp.bitwise_xor(me_ref[0], offset) * blocks + lax.rem(grid_step, blocks)


def piece_rows(blocks, place, width):
    return pl.BlockSpec(
        (BLK, width), lambda i, *_: (jnp.clip(i - place * blocks, 0, blocks - 1), 0)
    )


def attend(lengths, me, order, blocks, pad_row, queries, keys, values, needs=()):
    count, width = queries.shape
    heads = width // HEAD
    return launch(
        functools.partial(attend_kernel, lengths.shape[0], order, blocks),
        needs,
        (lengths, me,),
        (blocks * len(order),),
        [
                whole(1, count),
                pl.BlockSpec(
                    (BLK, width), lambda i, l_ref, me_ref: (block_of(order, blocks, i, me_ref), 0)
                ),
                whole(count, width),
                whole(count, width),
            ],
        (pad_row, queries, keys, values,),
        scratch_shapes=[pltpu.VMEM((heads, BLK, 128), F32)],
        out_specs=[rows(BLK, width)] * 2,
        out_shape=[like((len(order) * blocks * BLK, width), BF16)] * 2,
        cost_estimate=cost(2 * count * count * width, 6 * count * width, count * count * heads // 6),
        name="attend",
    )


def attend_back_kernel(
    count, pieces, length_ref, me_ref, pad_ref, q_ref, k_ref, v_ref, raw_ref, gain_ref, *refs
):
    pairs = pieces // 2
    aux_refs, mixed_refs, delta_refs = (
        refs[:pairs],
        refs[pairs : 2 * pairs],
        refs[2 * pairs : 2 * pairs + pieces],
    )
    low_ref, scale_sum, dqt_ref, do_ref, inner_ref, aux_ref, key_acc, value_acc = refs[
        2 * pairs + pieces :
    ]
    step = pl.program_id(0)
    tokens, width = q_ref.shape
    heads = width // HEAD
    starts = later_starts(length_ref, count)
    lane = lax.broadcasted_iota(jnp.int32, (BLK, 128), 1)
    left = lane < HEAD
    zero = jnp.zeros((BLK, 128), BF16)
    one = jnp.ones((BLK, 128), BF16)
    sides = [left if head % 2 == 0 else ~left for head in range(heads)]
    columns = [slice(head // 2 * 128, (head // 2 + 1) * 128) for head in range(heads)]

    @pl.when(step == 0)
    def prepare():
        dqt_ref[...] = jnp.zeros_like(dqt_ref)
        scale_sum[...] = jnp.zeros_like(scale_sum)
        part = tokens // pieces
        row = lax.broadcasted_iota(jnp.int32, (128, 128), 0)
        column = lax.broadcasted_iota(jnp.int32, (128, 128), 1)
        other = jnp.where(row // HEAD != column // HEAD, 1.0, 0.0).astype(BF16)
        for place in range(pieces):
            first = jnp.bitwise_xor(me_ref[0], place) * part
            do_ref[pl.ds(pl.multiple_of(first, part), part), :] = delta_refs[place][...]
            base = place % 2 * part
            aux_ref[pl.ds(pl.multiple_of(first, part), part), :] = aux_refs[place // 2][
                base : base + part, :
            ]
            for block in range(part // BLK):
                source = slice(block * BLK, (block + 1) * BLK)
                here = pl.ds(pl.multiple_of(first + block * BLK, BLK), BLK)
                for pair in range(heads // 2):
                    tile = slice(pair * 128, (pair + 1) * 128)
                    high, low = split_low(
                        delta_refs[place][source, tile].astype(F32)
                        * mixed_refs[place // 2][
                            base + block * BLK : base + (block + 1) * BLK, tile
                        ].astype(F32)
                    )
                    high, low = split_low(-(dot_nn(high, other) + dot_nn(low, other)))
                    inner_ref[here, tile] = jnp.where(lax.rem(lane, HEAD) < HEAD // 2, high, low)

    key_rows = pl.ds(pl.multiple_of(step * BLK, BLK), BLK)
    last_key = step * BLK + BLK - 1
    end = jnp.int32(tokens)
    for start in reversed(starts):
        end = jnp.where(last_key < start, start, end)
    last = (end - 1) // BLK
    key_acc[...] = jnp.zeros_like(key_acc)
    value_acc[...] = jnp.zeros_like(value_acc)
    turned = jnp.transpose(k_ref[key_rows, :].astype(F32)).astype(BF16)
    keys, values = [], []
    for h in range(heads):
        hot = jnp.where((lax.rem(lane, HEAD // 2) == 0) & (~sides[h]), one, zero)
        for source, into in ((k_ref, keys), (v_ref, values)):
            tile = jnp.where(sides[h], source[key_rows, columns[h]], zero)
            into.append(jnp.concatenate([tile, hot], axis=1))
    key = step * BLK + lax.broadcasted_iota(jnp.int32, (BLK, 1), 0)
    padding = jnp.transpose(
        jnp.broadcast_to(pad_ref[:, key_rows].astype(F32), (128, BLK))
    )[:, :1]
    code = jnp.where(padding > 0.5, key, NEVER)

    def body(block, carry):
        here = pl.ds(pl.multiple_of(block * BLK, BLK), BLK)
        row = block * BLK + lax.broadcasted_iota(jnp.int32, (1, BLK), 1)
        mask = ((code >= seq_start(row, starts)) & (code <= row)) | (key == row)
        for h in range(heads):
            query, delta = q_ref[here, columns[h]], do_ref[here, columns[h]]
            scores = dot_nt(keys[h], jnp.concatenate([query, aux_ref[here, columns[h]]], axis=1))
            delta_probs = dot_nt(
                values[h], jnp.concatenate([delta, inner_ref[here, columns[h]]], axis=1)
            )
            probs = jnp.where(mask, jnp.exp2(scores * SCORE), 0.0)
            delta_scores = (probs * delta_probs).astype(BF16)
            value_acc[h] += dot_nn(probs.astype(BF16), delta)
            key_acc[h] += dot_nn(delta_scores, query)
            head_rows = slice(h * HEAD, (h + 1) * HEAD)
            dqt_ref[head_rows, here] += dot_nn(turned[head_rows, :], delta_scores)
        return carry

    lax.fori_loop(step, last + 1, body, 0)
    key_tiles, value_tiles = [
        [jnp.where(left, acc[2 * pair], acc[2 * pair + 1]) for pair in range(heads // 2)]
        for acc in (key_acc, value_acc)
    ]
    ones = head_matrix(width)
    gain = gain_ref[...]
    deltas = (jnp.transpose(dqt_ref[:, key_rows]), jnp.concatenate(key_tiles, axis=1))
    for place, delta in enumerate(deltas):
        here = slice(place * width, (place + 1) * width)
        raw = raw_ref[:, here]
        factor = lax.rsqrt(head_mean(raw * raw, ones) + EPSILON)
        unit = raw * factor
        delta = delta * HEAD**-0.5
        scale_sum[...] += jnp.sum(delta * unit, axis=0, keepdims=True)
        delta = gain * delta
        low_ref[:, here] = (factor * (delta - unit * head_mean(delta * unit, ones))).astype(BF16)
    low_ref[:, 2 * width :] = jnp.concatenate(value_tiles, axis=1).astype(BF16)


def attend_back(lengths, me, pad_row, queries, keys, values, raw, gain, aux_pieces, mixed_pieces, delta_pieces):
    count, width = queries.shape
    heads = width // HEAD
    pieces = len(delta_pieces)
    return pl.pallas_call(
        functools.partial(attend_back_kernel, lengths.shape[0], pieces),
        grid_spec=pltpu.PrefetchScalarGridSpec(
            num_scalar_prefetch=2,
            grid=(count // BLK,),
            in_specs=[whole(1, count)]
            + [whole(count, width)] * 3
            + [rows(BLK, 2 * width), whole(1, width)]
            + [whole(2 * count // pieces, width)] * pieces
            + [piece_spec((array, lead, 0), count // pieces, 0) for array, lead in delta_pieces],
            out_specs=[rows(BLK, 3 * width), whole(1, width)],
            scratch_shapes=[
                pltpu.VMEM((width, count), F32),
                pltpu.VMEM((count, width), BF16),
                pltpu.VMEM((count, width), BF16),
                pltpu.VMEM((count, width), BF16),
                pltpu.VMEM((heads, BLK, 128), F32),
                pltpu.VMEM((heads, BLK, 128), F32),
            ],
        ),
        out_shape=[like((count, 3 * width), BF16), like((1, width), F32)],
        compiler_params=params(),
        cost_estimate=cost(8 * count * count * width, 22 * count * width, count * count * heads // 3),
        name="attend_back",
    )(lengths, me, pad_row, queries, keys, values, raw, gain, *aux_pieces, *mixed_pieces, *[array for array, lead in delta_pieces])


def unit_of(values):
    factor = lax.rsqrt(jnp.mean(values * values, axis=1, keepdims=True) + EPSILON)
    return values * factor, factor


def unit_back(delta, unit, factor):
    return factor * (delta - unit * jnp.mean(delta * unit, axis=1, keepdims=True))


def mixer_kernel(pieces, *refs):
    mixed_refs, out_weights = refs[:pieces], refs[pieces : 2 * pieces]
    tokens_ref, alpha_ref, *low_refs, one_ref, unit_ref, unit_factor, one_factor = refs[2 * pieces :]
    branch = dot_nn(mixed_refs[0][...], out_weights[0][...])
    for mixed, weight in zip(mixed_refs[1:], out_weights[1:]):
        branch += dot_nn(mixed[...], weight[...])
    unit, factor = unit_of(branch * SCALE_MODEL)
    unit_ref[...] = unit
    unit_factor[...] = jnp.broadcast_to(factor, unit_factor.shape)
    residual = tokens_ref[...].astype(F32)
    hidden, factor = unit_of(residual + alpha_ref[...] * (unit - residual))
    one_ref[...] = hidden
    one_factor[...] = jnp.broadcast_to(factor, one_factor.shape)
    put(1, hidden.astype(BF16), *low_refs)


def mixer(mixed_pieces, out_weights, me, tokens_all, alpha):
    width = mixed_pieces[0][0].shape[-1]
    pieces = len(mixed_pieces)
    count = tokens_all.shape[0] // pieces
    depth = tokens_all.shape[1]
    blocks = count // BLK
    kernel = functools.partial(mixer_kernel, pieces)
    return pl.pallas_call(
        lambda me_ref, *refs: kernel(*refs),
        grid_spec=pltpu.PrefetchScalarGridSpec(
            num_scalar_prefetch=1,
            grid=(blocks,),
            in_specs=[piece_spec((array, lead, 0), BLK, 1) for array, lead in mixed_pieces]
            + [piece_spec((array, lead, 0), width, 0) for array, lead in out_weights]
            + [
                pl.BlockSpec((BLK, depth), lambda i, me_ref: (me_ref[0] * blocks + i, 0)),
                whole(1, depth),
            ],
            out_specs=[piece_rows(1, 0, depth), piece_rows(1, 1, depth)]
            + [rows(BLK, depth)] * 2
            + [rows(BLK, 128)] * 2,
        ),
        out_shape=[like((BLK, depth), BF16)] * 2
        + [like((count, depth), F32)] * 2
        + [like((count, 128), F32)] * 2,
        compiler_params=params(),
        cost_estimate=cost(2 * count * depth * depth, 16 * count * depth + 2 * depth * depth),
        name="mixer",
    )(me, *[p[0] for p in mixed_pieces], *[w[0] for w in out_weights], tokens_all, alpha)


def turn_kernel(pieces, carried, me_ref, *refs):
    own_ref, near_ref, far_ref, one_ref = refs[:4]
    seed_refs = refs[4 : 4 + pieces]
    pad_ref, alpha_ref = refs[4 + pieces : 6 + pieces]
    outs = refs[6 + pieces + carried :]
    pair_refs = outs[: pieces // 2]
    hidden_ref, low_ref, alpha_sum, seed, layer = outs[pieces // 2 :]
    width = seed_refs[0].shape[-1]
    starts = [
        pl.multiple_of(jnp.bitwise_xor(me_ref[0], place) * width, width) for place in range(pieces)
    ]
    for start, piece in zip(starts, seed_refs):
        seed[:, pl.ds(start, width)] = piece[...]
    branch = (own_ref[...].astype(F32) + near_ref[...].astype(F32)) + far_ref[...].astype(F32)
    unit, unit_factor = unit_of(branch)
    hidden = one_ref[...]
    alpha = alpha_ref[...]
    layer_rows, layer_factor = unit_of(hidden + alpha * (unit - hidden))
    layer[...] = layer_rows.astype(BF16)
    for offset, start in enumerate(starts):
        pair_refs[offset // 2][offset % 2] = layer[:, pl.ds(start, width)]
    delta = unit_back(seed[...].astype(F32) * pad_ref[...], layer_rows, layer_factor)
    alpha_sum[...] = jnp.sum(delta * (unit - hidden), axis=0, keepdims=True)
    hidden_ref[...] = (1.0 - alpha) * delta
    low_ref[...] = unit_back(alpha * delta, unit, unit_factor).astype(BF16)


def turn(me, half, own, near, far, hidden_one, seed_pieces, pad_rows, alpha, carry=()):
    count, depth = hidden_one.shape
    pieces = len(seed_pieces)
    width = depth // pieces
    here = pl.BlockSpec((BLK, depth), lambda i, *_: (half, 0))
    pair = pl.BlockSpec((2, BLK, width), lambda i, *_: (0, half, 0))
    return pl.pallas_call(
        functools.partial(turn_kernel, pieces, len(carry)),
        grid_spec=pltpu.PrefetchScalarGridSpec(
            num_scalar_prefetch=1,
            grid=(1,),
            in_specs=[whole(BLK, depth)] * 3
            + [here]
            + [piece_spec((array, lead, half), BLK, 0) for array, lead in seed_pieces]
            + [pl.BlockSpec((BLK, 1), lambda i, *_: (half, 0)), whole(1, depth)]
            + [pl.BlockSpec(memory_space=pl.ANY)] * len(carry),
            out_specs=[pair] * (pieces // 2) + [here, whole(BLK, depth), whole(1, depth)],
            scratch_shapes=[pltpu.VMEM((BLK, depth), BF16)] * 2,
        ),
        out_shape=[like((2, count, width), BF16)] * (pieces // 2)
        + [like((count, depth), F32), like((BLK, depth), BF16), like((1, depth), F32)],
        input_output_aliases={7 + pieces + k: k for k in range(len(carry))},
        compiler_params=params(),
        cost_estimate=cost(40 * count * depth, 20 * count * depth),
        name="turn",
    )(
        me, own, near, far, hidden_one, *[p[0] for p in seed_pieces], pad_rows, alpha, *carry
    )


def mixer_back_kernel(pieces, *refs):
    halves, (hidden_ref, one_ref, unit_ref) = (refs[:3], refs[3:6]), refs[6:9]
    one_factor, unit_factor, tokens_ref, alpha_ref = refs[9:13]
    out_weights = refs[13 : 13 + pieces]
    pair_refs = refs[13 + pieces : 13 + pieces + pieces // 2]
    low_ref, direct_ref, alpha_sum = refs[13 + pieces + pieces // 2 :]
    own, near, far = [
        jnp.where(pl.program_id(0) == 0, first[...].astype(F32), second[...].astype(F32))
        for first, second in zip(*halves)
    ]

    @pl.when(pl.program_id(0) == 0)
    def clear():
        alpha_sum[...] = jnp.zeros_like(alpha_sum)

    delta = hidden_ref[...] + ((own + near) + far)
    unit = unit_ref[...]
    alpha = alpha_ref[...]
    delta = unit_back(delta, one_ref[...], one_factor[:, :1])
    alpha_sum[...] += jnp.sum(delta * (unit - tokens_ref[...].astype(F32)), axis=0, keepdims=True)
    direct_ref[...] = (1.0 - alpha) * delta
    low = unit_back(alpha * delta, unit, unit_factor[:, :1]).astype(BF16)
    low_ref[...] = low
    for offset, weight in enumerate(out_weights):
        pair_refs[offset // 2][offset % 2] = (dot_nt(low, weight[...]) * SCALE_MODEL).astype(BF16)


def mixer_back(
    me, sums, hidden, one, unit, one_factor, unit_factor, tokens_all, alpha, out_weights
):
    count, depth = one.shape
    pieces = len(out_weights)
    width = depth // pieces
    blocks = count // BLK
    kernel = functools.partial(mixer_back_kernel, pieces)
    return pl.pallas_call(
        lambda me_ref, *refs: kernel(*refs),
        grid_spec=pltpu.PrefetchScalarGridSpec(
            num_scalar_prefetch=1,
            grid=(blocks,),
            in_specs=[whole(BLK, depth)] * 6
            + [rows(BLK, depth)] * 3
            + [rows(BLK, 128)] * 2
            + [
                pl.BlockSpec((BLK, depth), lambda i, me_ref: (me_ref[0] * blocks + i, 0)),
                whole(1, depth),
            ]
            + [piece_spec((array, lead, 0), width, 0) for array, lead in out_weights],
            out_specs=[pl.BlockSpec((2, BLK, width), lambda i, *_: (0, i, 0))] * (pieces // 2)
            + [rows(BLK, depth), rows(BLK, depth), whole(1, depth)],
        ),
        out_shape=[like((2, count, width), BF16)] * (pieces // 2)
        + [like((count, depth), BF16), like((count, depth), F32), like((1, depth), F32)],
        compiler_params=params(),
        cost_estimate=cost(2 * count * depth * depth, 28 * count * depth + 2 * depth * depth),
        name="mixer_back",
    )(
        me,
        *sums,
        hidden,
        one,
        unit,
        one_factor,
        unit_factor,
        tokens_all,
        alpha,
        *[w[0] for w in out_weights],
    )


def pick(half, first_ref, second_ref, out_ref):
    step = pl.program_id(0)

    @pl.when(step < half)
    def from_first():
        out_ref[...] = first_ref[...]

    @pl.when(step >= half)
    def from_second():
        out_ref[...] = second_ref[...]


def put(half, value, first_ref, second_ref):
    step = pl.program_id(0)

    @pl.when(step < half)
    def to_first():
        first_ref[...] = value

    @pl.when(step >= half)
    def to_second():
        second_ref[...] = value


def whole_weight(tok_ref, piece_refs, out_ref):
    if out_ref is None:
        return piece_refs[0]

    @pl.when(pl.program_id(0) == 0)
    def assemble_weight():
        place_columns(tok_ref[0], piece_refs, out_ref)

    return out_ref


def expand_kernel(count, pieces, tok_ref, *refs):
    block_refs, gain_ref, refs = refs[:count], refs[count], refs[count + 1 :]
    up_pieces, gate_pieces = refs[:pieces], refs[pieces : 2 * pieces]
    up_ref, gate_ref, mid_ref = refs[2 * pieces : 2 * pieces + 3]
    hidden_ref = refs[-1]
    outs = refs[2 * pieces + 3 : -1] or (None, None)
    up_w = whole_weight(tok_ref, up_pieces, outs[0])
    gate_w = whole_weight(tok_ref, gate_pieces, outs[1])
    for place, block_ref in enumerate(block_refs):

        @pl.when(pl.program_id(0) == place)
        def take(block_ref=block_ref):
            hidden_ref[...] = block_ref[...]

    hidden = hidden_ref[...]
    up = dot_nt(hidden, up_w[...]) * SCALE_MODEL
    gate = dot_nt(hidden, gate_w[...]) * SCALE_MODEL
    up_ref[...] = up.astype(BF16)
    gate_ref[...] = gate.astype(BF16)
    scaled = gain_ref[1:2, :] * gate
    mid_ref[...] = (gain_ref[0:1, :] * up * scaled * jax.nn.sigmoid(scaled)).astype(BF16)


def expand(tok, blocks_in, up_pieces, gate_pieces, gains):
    depth = blocks_in[0].shape[1]
    hidden = gains.shape[1]
    count = len(blocks_in)
    pieces = len(up_pieces)
    outs = 2 if pieces > 1 else 0
    return pl.pallas_call(
        functools.partial(expand_kernel, count, pieces),
        grid_spec=pltpu.PrefetchScalarGridSpec(
            num_scalar_prefetch=1,
            grid=(count,),
            in_specs=[whole(BLK, depth)] * count
            + [whole(2, hidden)]
            + [piece_spec(piece, hidden, 0) for piece in (*up_pieces, *gate_pieces)],
            out_specs=[rows(BLK, hidden)] * 3 + [whole(hidden, depth)] * outs,
            scratch_shapes=[pltpu.VMEM((BLK, depth), BF16)],
        ),
        out_shape=[like((count * BLK, hidden), BF16)] * 3 + [like((hidden, depth), BF16)] * outs,
        compiler_params=params(),
        cost_estimate=cost(4 * count * BLK * depth * hidden, 4 * depth * hidden),
        name="expand",
    )(tok, *blocks_in, gains, *[piece[0] for piece in (*up_pieces, *gate_pieces)])


def contract_kernel(half, pieces, tok_ref, mid_ref, *refs):
    first_ref, second_ref = refs[pieces : pieces + 2]
    outs = refs[pieces + 2 :] or (None,)
    down_w = whole_weight(tok_ref, refs[:pieces], outs[0])
    put(half, (dot_nn(mid_ref[...], down_w[...]) * SCALE_HIDDEN).astype(BF16), first_ref, second_ref)


def contract(tok, middle, first_block, down_pieces, depth, needs=()):
    hidden = middle.shape[1]
    count, half = 2 * BLK, 1
    pieces = len(down_pieces)
    outs = 1 if pieces > 1 else 0
    return launch(
        functools.partial(contract_kernel, half, pieces),
        needs,
        (tok,),
        (2 * half,),
        [pl.BlockSpec((BLK, hidden), lambda i, *_: (first_block + i, 0))] + [piece_spec(piece, hidden, 0) for piece in down_pieces],
        (middle, *[piece[0] for piece in down_pieces],),
        out_specs=[piece_rows(half, 0, depth), piece_rows(half, 1, depth)]
            + [whole(hidden, depth)] * outs,
        out_shape=[like((count // 2, depth), BF16)] * 2 + [like((hidden, depth), BF16)] * outs,
        cost_estimate=cost(
            2 * count * depth * hidden, 2 * count * (depth + hidden) + 2 * depth * hidden
        ),
        name="contract",
    )


def gated_back_kernel(
    half,
    first_ref,
    second_ref,
    up_ref,
    gate_ref,
    up_w,
    gate_w,
    down_w,
    gain_ref,
    both_ref,
    first_out,
    second_out,
    unit_ref,
    delta_ref,
):
    @pl.when(pl.program_id(0) == 0)
    def clear():
        unit_ref[...] = jnp.zeros_like(unit_ref)

    pick(half, first_ref, second_ref, delta_ref)
    delta_middle = dot_nt(delta_ref[...], down_w[...]) * SCALE_HIDDEN
    up = up_ref[...].astype(F32)
    gate = gate_ref[...].astype(F32)
    scaled = gain_ref[1:2, :] * gate
    sigmoid = jax.nn.sigmoid(scaled)
    shared = delta_middle * sigmoid
    delta_up = shared * scaled
    delta_gate = shared * (gain_ref[0:1, :] * up) * (1.0 + scaled * (1.0 - sigmoid))
    unit_ref[0:1, :] += jnp.sum(delta_up * up, axis=0, keepdims=True)
    unit_ref[1:2, :] += jnp.sum(delta_gate * gate, axis=0, keepdims=True)
    up_low = (gain_ref[0:1, :] * delta_up).astype(BF16)
    gate_low = (gain_ref[1:2, :] * delta_gate).astype(BF16)
    both_ref[:, : up_low.shape[1]] = up_low
    both_ref[:, up_low.shape[1] :] = gate_low
    total = (dot_nn(up_low, up_w[...]) + dot_nn(gate_low, gate_w[...])) * SCALE_MODEL
    put(half, total.astype(BF16), first_out, second_out)


def gated_back(first, second, up, gate, first_block, up_w, gate_w, down_w, gains):
    count, depth = first.shape
    hidden = up_w.shape[0]
    half = count // BLK
    return pl.pallas_call(
        functools.partial(gated_back_kernel, half),
        grid=(2 * half,),
        in_specs=[piece_rows(half, 0, depth), piece_rows(half, 1, depth)]
        + [pl.BlockSpec((BLK, hidden), lambda i, *_: (first_block + i, 0))] * 2
        + [whole(hidden, depth)] * 3
        + [whole(2, hidden)],
        out_specs=[rows(BLK, 2 * hidden)]
        + [piece_rows(half, 0, depth), piece_rows(half, 1, depth), whole(2, hidden)],
        scratch_shapes=[pltpu.VMEM((BLK, depth), BF16)],
        out_shape=[like((2 * count, 2 * hidden), BF16)]
        + [like((count, depth), BF16)] * 2
        + [like((2, hidden), F32)],
        compiler_params=params(),
        cost_estimate=cost(
            12 * count * depth * hidden,
            8 * count * (depth + hidden) + 6 * depth * hidden,
            2 * count * hidden,
        ),
        name="gated_back",
    )(first, second, up, gate, up_w, gate_w, down_w, gains)


def part_columns(tok_ref, total, part_refs):
    width = part_refs[0].shape[2]
    for offset in range(8):
        start = pl.multiple_of(jnp.bitwise_xor(tok_ref[0], offset) * width, width)
        place = offset % 2 * 2 + offset // 2 % 2
        value = total[:, pl.ds(start, width)].astype(BF16)
        if place < 3 or len(part_refs) == 4:
            part_refs[place][offset // 4] = value
        else:
            half = pl.num_programs(0) // 2

            @pl.when(pl.program_id(0) < half)
            def first_half(value=value, lead=offset // 4):
                part_refs[3][lead] = value

            @pl.when(pl.program_id(0) >= half)
            def second_half(value=value, lead=offset // 4):
                part_refs[4][lead] = value


def weight_grad_kernel(lefts, rights, scale, steps, outs, tok_ref, *refs):
    left_refs, right_refs = refs[:lefts], refs[lefts : lefts + rights]
    fold_refs, part_refs = refs[lefts + rights : -outs - 1], refs[-outs - 1 : -1]
    total = refs[-1]

    @pl.when(pl.program_id(0) < steps)
    def product():
        acc, lefts_in = None, []
        for ref in left_refs:
            count = right_refs[0].shape[0]
            lefts_in += [ref[k * count : (k + 1) * count, :] for k in range(ref.shape[0] // count)]
        for left, right in zip(lefts_in, right_refs):
            term = lax.dot_general(
                left, right[...], (((0,), (0,)), ((), ())), preferred_element_type=F32
            )
            acc = term if acc is None else acc + term
        total[...] = acc * scale

    if fold_refs:

        @pl.when(pl.program_id(0) >= steps)
        def fold():
            own, near, far = [ref[...].astype(F32) for ref in fold_refs]
            total[...] = (own + near) + far

    part_columns(tok_ref, total, part_refs)


def weight_grad(tok, groups, lefts, rights, scale, folds=(), halves=False, needs=()):
    height = lefts[0].shape[1]
    depth = rights[0].shape[1]
    count = sum(left.shape[0] for left in lefts)
    part = depth // groups
    steps = height // BLK
    out = pl.BlockSpec((groups // 4, BLK, part), lambda i, *_: (0, i, 0))
    total_height = height + (BLK if folds else 0)
    outs, heights = [out] * 4, [total_height] * 4
    if halves:
        half = steps // 2
        outs[3:] = [
            pl.BlockSpec((groups // 4, BLK, part), lambda i, *_: (0, jnp.minimum(i, half - 1), 0)),
            pl.BlockSpec((groups // 4, BLK, part), lambda i, *_: (0, jnp.maximum(i - half, 0), 0)),
        ]
        heights[3:] = [height // 2] * 2
    return launch(
        functools.partial(
            weight_grad_kernel, len(lefts), len(rights), scale, steps, len(outs)
        ),
        needs,
        (tok,),
        (total_height // BLK,),
        [
                pl.BlockSpec((left.shape[0], BLK), lambda i, *_: (0, jnp.minimum(i, steps - 1)))
                for left in lefts
            ]
            + [whole(*right.shape) for right in rights]
            + [piece_spec((array, lead, 0), BLK, 0) for array, lead in folds],
        (*lefts, *rights, *[array for array, lead in folds],),
        scratch_shapes=[pltpu.VMEM((BLK, depth), F32)],
        out_specs=outs,
        out_shape=[like((groups // 4, tall, part), BF16) for tall in heights],
        cost_estimate=cost(
            2 * count * height * depth, 2 * count * (height + depth) + 2 * height * depth
        ),
        name="weight_grad",
    )


def out_grad_kernel(pieces, *refs):
    right, pair_refs = refs[pieces], refs[pieces + 1 :]
    for offset, left in enumerate(refs[:pieces]):
        total = lax.dot_general(
            left[...], right[...], (((0,), (0,)), ((), ())), preferred_element_type=F32
        )
        pair_refs[offset // 2][offset % 2] = (total * SCALE_MODEL).astype(BF16)


def out_grad(lefts, right):
    width = lefts[0][0].shape[-1]
    count, depth = right.shape
    pieces = len(lefts)
    return pl.pallas_call(
        functools.partial(out_grad_kernel, pieces),
        grid=(1,),
        in_specs=[piece_spec((array, lead, 0), count, 0) for array, lead in lefts]
        + [whole(count, depth)],
        out_specs=[whole(2, width, depth)] * (pieces // 2),
        out_shape=[like((2, width, depth), BF16)] * (pieces // 2),
        compiler_params=params(),
        cost_estimate=cost(2 * count * depth * depth, 4 * count * depth + 2 * depth * depth),
        name="out_grad",
    )(*[p[0] for p in lefts], right)


def project_back_kernel(pieces, me_ref, low_ref, w_ref, direct_ref, *refs):
    part_refs, total = refs[:pieces], refs[pieces]
    step = pl.program_id(0)
    total[...] = dot_nn(low_ref[...], w_ref[...]) * SCALE_MODEL
    own_blocks = direct_ref.shape[0] // BLK

    @pl.when(step // own_blocks == me_ref[0])
    def add_direct():
        start = pl.multiple_of(lax.rem(step, own_blocks) * BLK, BLK)
        total[...] += direct_ref[pl.ds(start, BLK), :]

    part = total.shape[1] // pieces
    for place, out in enumerate(part_refs):
        start = pl.multiple_of(jnp.bitwise_xor(me_ref[0], place) * part, part)
        out[...] = total[:, pl.ds(start, part)].astype(BF16)


def project_back(me, pieces, low, weight, direct, needs=()):
    count = low.shape[0]
    depth = weight.shape[1]
    part = depth // pieces
    return launch(
        functools.partial(project_back_kernel, pieces),
        needs,
        (me,),
        (count // BLK,),
        [rows(BLK, low.shape[1]), whole(*weight.shape), whole(*direct.shape)],
        (low, weight, direct),
        scratch_shapes=[pltpu.VMEM((BLK, depth), F32)],
        out_specs=[rows(BLK, part)] * pieces,
        out_shape=[like((count, part), BF16)] * pieces,
        cost_estimate=cost(2 * count * low.shape[1] * depth, 2 * count * depth),
        name="project_back",
    )


def merge_kernel(keep_ref, first_ref, second_ref, out_ref):
    step, half = pl.program_id(0), pl.num_programs(0) // 2

    @pl.when(step < half)
    def add_first():
        out_ref[...] = (keep_ref[...].astype(F32) + first_ref[...].astype(F32)).astype(BF16)

    @pl.when(step >= half)
    def add_second():
        out_ref[...] = (keep_ref[...].astype(F32) + second_ref[...].astype(F32)).astype(BF16)


def merge(keep, first, second):
    pieces, height, part = keep.shape
    block = (pieces, height // 4, part)
    return pl.pallas_call(
        merge_kernel,
        grid=(4,),
        in_specs=[
            pl.BlockSpec(block, lambda i: (0, i, 0)),
            pl.BlockSpec(block, lambda i: (0, jnp.minimum(i, 1), 0)),
            pl.BlockSpec(block, lambda i: (0, jnp.maximum(i - 2, 0), 0)),
        ],
        out_specs=pl.BlockSpec(block, lambda i: (0, i, 0)),
        out_shape=like(keep.shape, BF16),
        compiler_params=params(),
        cost_estimate=cost(0, 6 * pieces * height * part),
        name="merge",
    )(keep, first, second)


def trade(value, axis, offset):
    size = lax.axis_size(axis)
    return lax.ppermute(value, axis, [(i, i ^ offset) for i in range(size)])


def sum_four(value, axis, first, second):
    one, two, three = [trade(value, axis, o) for o in (first, second, first ^ second)]
    return (value + one) + (two + three)


def sum_over(value, axis):
    if lax.axis_size(axis) == 4:
        return sum_four(value, axis, 1, 2)
    if lax.axis_size(axis) == 8:
        return sum_four(value + trade(value, axis, 1), axis, 2, 4)
    offset = 1
    while offset < lax.axis_size(axis):
        value = value + trade(value, axis, offset)
        offset *= 2
    return value


def join(*values):
    return lax.optimization_barrier(values)


def stack(*values):
    return jnp.concatenate([v if v.ndim == 3 else v[None] for v in values], axis=0)


def add_low(*values):
    total = values[0].astype(F32)
    for value in values[1:]:
        total = total + value.astype(F32)
    return total


def plain_sum(left, right, scale):
    total = jnp.einsum("tr,td->rd", left, right, preferred_element_type=F32) * scale
    return lax.psum_scatter(total.astype(BF16), "tok", scatter_dimension=1, tiled=True).astype(F32)


def moment_update(weights, gradient, moment, square, fix_first, fix_second):
    moment_next = BETA_ONE * moment + (1.0 - BETA_ONE) * gradient
    square_next = BETA_TWO * square + (1.0 - BETA_TWO) * gradient * gradient
    stepped = weights - LEARN_RATE * (moment_next / fix_first) / (
        jnp.sqrt(square_next / fix_second) + ADAM_EPSILON
    )
    return (stepped, moment_next, square_next)


def local(
    inputs,
    cotangent,
    lengths,
    pad_mask,
    attention_weights,
    gated_weights,
    model_gains,
    unit_gains,
    attention_moment,
    attention_square,
    gated_moment,
    gated_square,
    model_moment,
    model_square,
    unit_moment,
    unit_square,
):
    token_count, width = inputs.shape
    parts = lax.axis_size("dim")
    hidden_here = gated_weights.shape[1]
    own_count = token_count // parts
    place = lax.axis_index("dim")
    me = place.astype(jnp.int32).reshape(1)
    tok = lax.axis_index("tok").astype(jnp.int32).reshape(1)
    groups = lax.axis_size("tok")
    by_pieces = groups == 8 and (D // groups) % 128 == 0
    blocks = own_count // BLK
    length_row = lengths[0]

    def token_rows(value, offset):
        return lax.dynamic_slice_in_dim(value, (place ^ offset) * own_count, own_count, 0)

    ao = attention_weights.reshape(4 * width, -1).astype(BF16)
    gated_low = gated_weights.reshape(3 * hidden_here, -1).astype(BF16)
    both_own = gated_weights[:2].reshape(2 * hidden_here, -1).astype(BF16)
    down_own = gated_weights[2].astype(BF16)
    score_gain = model_gains[:1]
    pad_row = pad_mask[None, :]
    pad_rows = token_rows(pad_mask, 0).astype(F32)[:, None]

    x_far = trade(inputs, "dim", 2)
    seed_rows = [token_rows(cotangent, r) for r in range(parts)]
    seed_send = stack(*seed_rows[2:])
    alphas = lax.dynamic_update_slice(
        jnp.zeros((2, D), F32), model_gains[1:], (0, place * width)
    )
    alpha_near = trade(alphas, "dim", 1)
    if by_pieces:
        ao_by = {0: ao, 4: trade(ao, "tok", 4), 2: trade(ao, "tok", 2), 1: trade(ao, "tok", 1)}
        ao_by[6] = trade(ao_by[4], "tok", 2)
        ao_by[5] = trade(ao_by[4], "tok", 1)
        ao_by[3] = trade(ao_by[2], "tok", 1)
        x_far, ao_by, both_own, seed_send, alphas, alpha_near = join(
            x_far, ao_by, both_own, seed_send, alphas, alpha_near
        )
        ao_by[7] = trade(ao_by[6], "tok", 1)
        by = {0: both_own, 2: trade(both_own, "tok", 2), 4: trade(both_own, "tok", 4)}
    else:
        gather = functools.partial(lax.all_gather, axis_name="tok", axis=1, tiled=True)
        in_pieces = [(gather(ao[: 3 * width]), None, 0)]
        out_weight, up_w, gate_w, down_w = [
            gather(shard)
            for shard in (ao[3 * width :], both_own[:hidden_here], both_own[hidden_here:], down_own)
        ]
        up_pieces, gate_pieces, down_pieces = [[(w, None, 0)] for w in (up_w, gate_w, down_w)]
    x_near = trade(inputs, "dim", 1)
    x_corner = trade(x_far, "dim", 1)
    token_pieces = [inputs, x_near, x_far, x_corner]
    if by_pieces:
        token_pieces, ao_by, gated_low, down_own, seed_send, alphas = join(
            token_pieces, ao_by, gated_low, down_own, seed_send, alphas
        )
        in_pieces = [(ao_by[offset], None, 0) for offset in range(8)]
        by[1] = trade(gated_low, "tok", 1)
    seed_far = trade(seed_send, "dim", 2)
    tokens_all, raw, queries, keys, values, weight_in = project(
        me, tok, token_pieces, in_pieces, score_gain
    )
    queries, seed_far = join(queries, seed_far)

    queries, seed_far, alpha_near = join(queries, seed_far, alpha_near)
    alphas = alphas + alpha_near
    alpha_far = trade(alphas, "dim", 2)
    if by_pieces:
        queries, by[1], by[2], by[4], ao_by, down_own = join(
            queries, by[1], by[2], by[4], ao_by, down_own
        )
        by[3] = trade(by[2], "tok", 1)
        by[6] = trade(by[4], "tok", 2)
        out_weight = assemble(
            tok, [(ao_by[o], None, 3 * width // BLK) for o in range(8)], width, (queries,)
        )
    out_across = trade(out_weight, "dim", 2)
    far_mixed, far_aux = attend(
        length_row, me, (2, 3), blocks, pad_row, queries, keys, values, (out_weight,)
    )
    far_mixed, alpha_far, out_across = join(far_mixed, alpha_far, out_across)
    alphas = alphas + alpha_far
    alpha_mixer, alpha_gated = alphas[:1], alphas[1:]
    if by_pieces:
        far_mixed, by[3], by[6], down_own = join(far_mixed, by[3], by[6], down_own)
        by[5] = trade(by[4], "tok", 1)
        down_by = {0: down_own, 2: trade(down_own, "tok", 2), 4: trade(down_own, "tok", 4)}
    far_came = trade(far_mixed, "dim", 2)
    out_pair = trade(stack(out_weight, out_across), "dim", 1)
    near_mixed, near_aux = attend(
        length_row, me, (0, 1), blocks, pad_row, queries, keys, values, (far_mixed,)
    )
    near_mixed, far_came, out_pair = join(near_mixed, far_came, out_pair)
    if by_pieces:
        near_mixed, by[5], by[6], down_by = join(near_mixed, by[5], by[6], down_by)
    pair_came = trade(stack(near_mixed[own_count:], far_came[own_count:]), "dim", 1)
    out_weights = [(out_weight, None), (out_pair, 0), (out_across, None), (out_pair, 1)]
    mixed_pieces = [(near_mixed, None), (pair_came, 0), (far_came, None), (pair_came, 1)]
    low_a, low_b, hidden_one, mixer_unit, mixer_factor, one_factor = mixer(
        mixed_pieces, out_weights, me, tokens_all, alpha_mixer
    )

    far_a = trade(low_a, "dim", 2)
    near_a = trade(low_a, "dim", 1)
    near_b = trade(low_b, "dim", 1)
    if by_pieces:
        near_a, near_b, by[6], down_by = join(near_a, near_b, by[6], down_by)
        by[7] = trade(by[6], "tok", 1)
        down_by[1] = by[1]
        down_by[6] = trade(down_by[4], "tok", 2)
        near_a, far_a, by[7], down_by = join(near_a, far_a, by[7], down_by)
        down_by[3] = trade(down_by[2], "tok", 1)
        down_by[5] = trade(down_by[4], "tok", 1)
        up_pieces, gate_pieces = [[(by[o], None, k) for o in range(8)] for k in range(2)]
    near_a, far_a, low_b = join(near_a, far_a, low_b)
    far_b = trade(low_b, "dim", 2)
    corner_a = trade(far_a, "dim", 1)
    up_one, gate_one, mid_one, *assembled = expand(
        tok, [low_a, near_a, low_b, near_b], up_pieces, gate_pieces, unit_gains
    )
    if by_pieces:
        up_w, gate_w = assembled
        up_pieces, gate_pieces = [(up_w, None, 0)], [(gate_w, None, 0)]
        mid_one, down_by, corner_a = join(mid_one, down_by, corner_a)
        down_by[7] = trade(down_by[6], "tok", 1)
    seed_pair = trade(stack(seed_rows[1], seed_far[1]), "dim", 1)
    seed_pieces = [(seed_rows[0], None), (seed_pair, 0), (seed_far, 0), (seed_pair, 1)]
    up_a, gate_a, mid_a = expand(tok, [far_a, corner_a], up_pieces, gate_pieces, unit_gains)
    mid_a, far_b, seed_pair = join(mid_a, far_b, seed_pair)
    seed_pieces = [(seed_rows[0], None), (seed_pair, 0), (seed_far, 0), (seed_pair, 1)]
    corner_b = trade(far_b, "dim", 1)
    if by_pieces:
        mid_a, down_by = join(mid_a, down_by)
        down_pieces = [(down_by[o], None, 2 if o == 1 else 0) for o in range(8)]
        *parts_a, down_w = contract(tok, mid_a, 0, down_pieces, D)
        down_pieces = [(down_w, None, 0)]
    else:
        parts_a = contract(tok, mid_a, 0, down_pieces, D)
    came = trade(parts_a[1], "dim", 1)
    up_b, gate_b, mid_b = expand(tok, [far_b, corner_b], up_pieces, gate_pieces, unit_gains)
    mid_b, came = join(mid_b, came)
    across = add_low(parts_a[0], came).astype(BF16)
    across_a = trade(across, "dim", 2)
    parts_b = contract(tok, mid_b, 0, down_pieces, D, (across,))
    came = trade(parts_b[1], "dim", 1)
    own_a, pair_a = contract(tok, mid_one, 0, down_pieces, D, (parts_b[0],))
    own_a, came, parts_b, pair_a = join(own_a, came, parts_b, pair_a)
    across = add_low(parts_b[0], came).astype(BF16)
    pair_a = trade(pair_a, "dim", 1)
    own_b, pair_b = contract(tok, mid_one, 2, down_pieces, D, (own_a, across))
    own_b, pair_b, across_a, across, pair_a = join(own_b, pair_b, across_a, across, pair_a)
    across_b = trade(across, "dim", 2)
    pair_b = trade(pair_b, "dim", 1)
    *carry, delta_a, sum_a = turn(
        me, 0, own_a, pair_a, across_a, hidden_one, seed_pieces, pad_rows, alpha_gated
    )

    back_weights = (up_w, gate_w, down_w, unit_gains)
    b_near_a = trade(delta_a, "dim", 1)
    both_near_a, own_one, pair_one, unit_one = gated_back(
        delta_a, b_near_a, up_one, gate_one, 0, *back_weights
    )
    own_one, across_b, pair_b, delta_a = join(own_one, across_b, pair_b, delta_a)
    b_far_a = trade(delta_a, "dim", 2)
    layer_near, layer_far, delta_hidden, delta_b, sum_b = turn(
        me, 1, own_b, pair_b, across_b, hidden_one, seed_pieces, pad_rows, alpha_gated, carry
    )
    b_near_b = trade(delta_b, "dim", 1)
    pair_one = trade(pair_one, "dim", 1)
    both_near_b, own_two, pair_two, unit_two = gated_back(
        delta_b, b_near_b, up_one, gate_one, 2, *back_weights
    )
    own_two, b_far_a, delta_b, pair_one = join(own_two, b_far_a, delta_b, pair_one)
    b_far_b = trade(delta_b, "dim", 2)
    b_corner_a = trade(b_far_a, "dim", 1)
    pair_two = trade(pair_two, "dim", 1)
    both_far_a, back_across_a, corner, unit_three = gated_back(
        b_far_a, b_corner_a, up_a, gate_a, 0, *back_weights
    )
    corner, pair_two = join(corner, pair_two)
    corner = trade(corner, "dim", 1)
    back_across_a, b_far_b = join(back_across_a, b_far_b)
    b_corner_b = trade(b_far_b, "dim", 1)
    across = add_low(back_across_a, corner).astype(BF16)
    across_one = trade(across, "dim", 2)
    both_far_b, back_across_b, corner, unit_four = gated_back(
        b_far_b, b_corner_b, up_b, gate_b, 0, *back_weights
    )
    back_across_b, across_one = join(back_across_b, across_one)
    corner = trade(corner, "dim", 1)
    across = add_low(back_across_b, corner).astype(BF16)
    across_two = trade(across, "dim", 2)
    back_sums = [own_one, pair_one, across_one, own_two, pair_two, across_two]
    h_pieces = [low_a, near_a, low_b, near_b, far_a, corner_a, far_b, corner_b]
    b_pieces = [delta_a, b_near_a, delta_b, b_near_b, b_far_a, b_corner_a, b_far_b, b_corner_b]
    middles = [mid_one, mid_a, mid_b]
    both_pieces = [both_near_a, both_near_b, both_far_a, both_far_b]
    unit_sums = (unit_one + unit_two) + (unit_three + unit_four)
    sum_gated = sum_a + sum_b
    if by_pieces:
        down_parts = weight_grad(tok, groups, middles, b_pieces, SCALE_HIDDEN, needs=(across,))
        down_odd = trade(down_parts[3], "tok", 1)
        both_parts = weight_grad(
            tok,
            groups,
            both_pieces,
            h_pieces,
            SCALE_MODEL,
            halves=True,
            needs=(down_parts[0],),
        )
        back_sums, both_parts, down_odd = join(back_sums, both_parts, down_odd)
        up_odd = trade(both_parts[3], "tok", 1)
        down_low = add_low(down_parts[1], down_odd).astype(BF16)
        down_near = trade(down_low, "tok", 2)
    else:
        down_grad = plain_sum(
            jnp.concatenate(middles, axis=0), jnp.concatenate(b_pieces, axis=0), SCALE_HIDDEN
        )
        both_grad = plain_sum(
            jnp.concatenate(both_pieces, axis=0), jnp.concatenate(h_pieces, axis=0), SCALE_MODEL
        )

    delta_near, delta_far, mixer_low, delta_direct, sum_mixer = mixer_back(
        me,
        back_sums,
        delta_hidden,
        hidden_one,
        mixer_unit,
        one_factor,
        mixer_factor,
        tokens_all,
        alpha_mixer,
        out_weights,
    )
    if by_pieces:
        delta_far, mixer_low, up_odd, down_near = join(delta_far, mixer_low, up_odd, down_near)
        gate_odd = trade(both_parts[4], "tok", 1)
    delta_came = trade(delta_far, "dim", 2)
    out_near_grad, out_far_grad = out_grad(mixed_pieces, mixer_low)
    alpha_sums = jnp.concatenate([sum_mixer, sum_gated], axis=0)
    alpha_near = trade(alpha_sums, "dim", 1)
    out_pair = trade(stack(out_near_grad[1], out_far_grad[1]), "dim", 1)
    delta_pair = trade(stack(delta_near[1], delta_came[1]), "dim", 1)
    delta_came, delta_pair, out_near_grad, out_far_grad, out_pair, alpha_near, layer_far = join(
        delta_came, delta_pair, out_near_grad, out_far_grad, out_pair, alpha_near, layer_far
    )
    alpha_sums = alpha_sums + alpha_near
    if by_pieces:
        delta_came, gate_odd = join(delta_came, gate_odd)
        both_low = merge(both_parts[1], up_odd, gate_odd)
        both_near = trade(both_low, "tok", 2)
        both_even = trade(both_parts[2], "tok", 1)
        down_even = trade(down_parts[2], "tok", 1)
    layer_came = trade(layer_far, "dim", 2)
    out_far_sum = trade(add_low(out_far_grad[0], out_pair[1]).astype(BF16), "dim", 2)
    delta_pieces = [(delta_near, 0), (delta_pair, 0), (delta_came, 0), (delta_pair, 1)]
    delta_project, scale_sum = attend_back(
        length_row,
        me,
        pad_row,
        queries,
        keys,
        values,
        raw,
        score_gain,
        [near_aux, far_aux],
        [near_mixed, far_mixed],
        delta_pieces,
    )
    delta_project, alpha_sums, out_far_sum, layer_came = join(
        delta_project, alpha_sums, out_far_sum, layer_came
    )
    alpha_far = trade(alpha_sums, "dim", 2)
    if by_pieces:
        delta_project, both_near, both_even, down_even = join(
            delta_project, both_near, both_even, down_even
        )
        down_low = add_low(down_parts[0][1], down_even[1], down_near[1]).astype(BF16)
        down_last = trade(down_low, "tok", 4)
        up_low, gate_low = [
            add_low(
                *[value[1, k * hidden_here : (k + 1) * hidden_here] for value in (both_parts[0], both_even, both_near)]
            ).astype(BF16)
            for k in range(2)
        ]
        in_parts = weight_grad(
            tok,
            groups,
            (delta_project,),
            (tokens_all,),
            SCALE_MODEL,
            ((out_near_grad, 0), (out_pair, 0), (out_far_sum, None)),
            needs=(up_low, gate_low, down_low),
        )
        in_parts, alpha_far, layer_near, down_last, up_low, gate_low = join(
            in_parts, alpha_far, layer_near, down_last, up_low, gate_low
        )
        up_last = trade(up_low, "tok", 4)
        in_odd = trade(in_parts[3], "tok", 1)
    alpha_sums = lax.dynamic_slice_in_dim(alpha_sums + alpha_far, place * width, width, 1)
    input_parts = project_back(
        me, parts, delta_project, weight_in, delta_direct, (in_parts[3],) if by_pieces else ()
    )
    corner = trade(input_parts[3], "dim", 1)
    across = add_low(input_parts[2], corner).astype(BF16)
    far = trade(across, "dim", 2)
    near = trade(input_parts[1], "dim", 1)
    gains_sum = jnp.concatenate(
        [scale_sum.reshape(-1), alpha_sums.reshape(-1), unit_sums.reshape(-1)]
    )
    if by_pieces:
        in_odd, in_parts, across, up_last, gate_low = join(
            in_odd, in_parts, across, up_last, gate_low
        )
        in_low = add_low(in_parts[1], in_odd).astype(BF16)
        in_near = trade(in_low, "tok", 2)
        in_even = trade(in_parts[2], "tok", 1)
        gate_last = trade(gate_low, "tok", 4)
        near, gate_last, in_near, in_even = join(near, gate_last, in_near, in_even)
        in_low = add_low(in_parts[0][1], in_even[1], in_near[1]).astype(BF16)
        in_last = trade(in_low, "tok", 4)
    layer_pair = trade(stack(layer_near[1], layer_came[1]), "dim", 1)
    layer_pieces = [layer_near[0], layer_pair[0], layer_came[0], layer_pair[1]]
    layer_out = jnp.zeros((token_count, width), BF16)
    for r, piece in enumerate(layer_pieces):
        layer_out = lax.dynamic_update_slice(layer_out, piece, ((place ^ r) * own_count, 0))
    input_gradient = add_low(input_parts[0], near, far)
    if by_pieces:
        down_grad = add_low(down_parts[0][0], down_even[0], down_near[0], down_last)
        both_last = jnp.concatenate([up_last, gate_last], axis=0)
        both_grad = add_low(both_parts[0][0], both_even[0], both_near[0], both_last)
    gated_grad = jnp.concatenate([both_grad, down_grad], axis=0).reshape(3, hidden_here, -1)
    fix_first = 1.0 - BETA_ONE**STEP
    fix_second = 1.0 - BETA_TWO**STEP
    gated_stepped, moment_gated, square_gated = moment_update(
        gated_weights, gated_grad, gated_moment, gated_square, fix_first, fix_second
    )
    gated_row_sums = jnp.sum(gated_stepped * gated_stepped, axis=2)
    gated_square_sum = jnp.sum(gated_grad * gated_grad)
    if by_pieces:
        in_last, gated_row_sums, gated_square_sum, input_gradient, layer_out = join(
            in_last, gated_row_sums, gated_square_sum, input_gradient, layer_out
        )
        in_total = add_low(in_parts[0][0], in_even[0], in_near[0], in_last)
        attention_grad = in_total.reshape(4, width, -1)
    else:
        out_total = lax.psum_scatter(
            add_low(out_near_grad[0], out_pair[0], out_far_sum).astype(BF16),
            "tok",
            scatter_dimension=1,
            tiled=True,
        ).astype(F32)
        in_total = plain_sum(delta_project, tokens_all, SCALE_MODEL)
        attention_grad = jnp.concatenate([in_total, out_total], axis=0).reshape(4, width, -1)

    attention_stepped, moment_attention, square_attention = moment_update(
        attention_weights, attention_grad, attention_moment, attention_square, fix_first, fix_second
    )
    sums = sum_over(
        jnp.concatenate(
            [
                jnp.sum(attention_stepped * attention_stepped, axis=2).reshape(-1),
                gated_row_sums.reshape(-1),
                gains_sum,
                (jnp.sum(attention_grad * attention_grad) + gated_square_sum).reshape(1),
            ]
        ),
        "tok",
    )
    ends = [4 * width, 4 * width + 3 * hidden_here, 7 * width + 3 * hidden_here]
    model_grad = sums[ends[1] : ends[2]].reshape(3, width)
    unit_grad = sums[ends[2] : -1].reshape(2, hidden_here)
    model_next, moment_model, square_model = moment_update(
        model_gains, model_grad, model_moment, model_square, fix_first, fix_second
    )
    unit_next, moment_unit, square_unit = moment_update(
        unit_gains, unit_grad, unit_moment, unit_square, fix_first, fix_second
    )
    square_sum = sums[-1:] + jnp.sum(model_grad * model_grad) + jnp.sum(unit_grad * unit_grad)
    totals = sum_over(jnp.concatenate([square_sum, jnp.sum(model_next[1:], axis=1)]), "dim")
    attention_rows = sums[: ends[0]].reshape(4, width, 1)
    gated_rows = sums[ends[0] : ends[1]].reshape(3, hidden_here, 1)
    attention_next = attention_stepped * lax.rsqrt(attention_rows / D + EPSILON)
    gated_next = gated_stepped * lax.rsqrt(gated_rows / D + EPSILON)
    gradient_norm = jnp.sqrt(totals[:1])
    mean_alpha = totals[1:] / D
    return (
        layer_out,
        input_gradient,
        attention_next,
        attention_next.astype(BF16),
        moment_attention,
        square_attention,
        gated_next,
        gated_next.astype(BF16),
        moment_gated,
        square_gated,
        model_next,
        moment_model,
        square_model,
        unit_next,
        moment_unit,
        square_unit,
        gradient_norm,
        mean_alpha,
    )


def solution(mesh):
    tokens = P("tok", "dim")
    weights = P(None, "dim", "tok")
    gains = P(None, "dim")
    in_specs = (tokens, tokens, P("tok", None), P("tok"), weights, weights, gains, gains)
    in_specs += (weights,) * 4 + (gains,) * 4
    out_specs = (tokens, tokens) + (weights,) * 8 + (gains,) * 6 + (P(), P())
    return jax.shard_map(local, mesh=mesh, in_specs=in_specs, out_specs=out_specs, check_vma=False)
```

```python
import functools
import math

import jax
import jax.numpy as jnp
from jax import lax
from jax.experimental import pallas as pl
from jax.experimental.pallas import tpu as pltpu
from jax.sharding import PartitionSpec as P

D = 1024
HEAD = 64
FF = 4096
STEP = 4
BLK = 256

EPSILON = 1e-06
ADAM_EPSILON = 1e-08
BETA_ONE = 0.5
BETA_TWO = 0.5
LEARN_RATE = 1.5

F32 = jnp.float32
BF16 = jnp.bfloat16
SCALE_MODEL = D**-0.5
SCALE_HIDDEN = FF**-0.5
SCORE = HEAD**-0.5 * math.log2(math.e)
NEVER = 1 << 24


def dot_nt(left, right):
    return lax.dot_general(left, right, (((1,), (1,)), ((), ())), preferred_element_type=F32)


def dot_nn(left, right):
    return lax.dot_general(left, right, (((1,), (0,)), ((), ())), preferred_element_type=F32)


def split_low(values):
    high = values.astype(BF16)
    return high, (values - high.astype(F32)).astype(BF16)


def params():
    return pltpu.CompilerParams(vmem_limit_bytes=60 << 20)


def cost(flops, traffic, transcendentals=0):
    return pl.CostEstimate(
        flops=int(flops) // 64, bytes_accessed=int(traffic) // 64, transcendentals=int(transcendentals) // 64
    )


def like(shape, dtype):
    return jax.ShapeDtypeStruct(shape, dtype)


def whole(*shape):
    return pl.BlockSpec(shape, lambda *_: (0,) * len(shape))


def rows(count, width):
    return pl.BlockSpec((count, width), lambda i, *_: (i, 0))


def launch(kernel, needs, scalars, grid, in_specs, args, scratch_shapes=(), **options):
    taken = len(scalars) + len(args)

    def body(*refs):
        kernel(*refs[:taken], *refs[taken + len(needs) :])

    return pl.pallas_call(
        body,
        grid_spec=pltpu.PrefetchScalarGridSpec(
            num_scalar_prefetch=len(scalars),
            grid=grid,
            in_specs=[*in_specs] + [pl.BlockSpec(memory_space=pl.ANY)] * len(needs),
            out_specs=options.pop("out_specs"),
            scratch_shapes=scratch_shapes,
        ),
        compiler_params=params(),
        **options,
    )(*scalars, *args, *needs)


def head_matrix(width):
    row = lax.broadcasted_iota(jnp.int32, (width, width), 0)
    column = lax.broadcasted_iota(jnp.int32, (width, width), 1)
    return jnp.where(row // HEAD == column // HEAD, 1.0, 0.0).astype(BF16)


def head_mean(values, ones):
    return dot_nn(values.astype(BF16), ones) * (1.0 / HEAD)


def head_mean_fine(values, ones):
    high, low = split_low(values)
    return (dot_nn(high, ones) + dot_nn(low, ones)) * (1.0 / HEAD)


def project_kernel(pieces, me_ref, tok_ref, *refs):
    piece_refs = refs[:pieces]
    weight_refs = refs[pieces:-7]
    gain_ref, all_ref, raw_ref, q_ref, k_ref, v_ref, w_ref = refs[-7:]
    width = piece_refs[0].shape[1]
    if len(weight_refs) == 1:
        weight = weight_refs[0]
    else:
        weight = w_ref

        @pl.when(pl.program_id(0) == 0)
        def assemble_weight():
            place_columns(tok_ref[0], weight_refs, w_ref)

    place_columns(me_ref[0], piece_refs, all_ref)
    projected = dot_nt(all_ref[...], weight[...]) * SCALE_MODEL
    if weight is not w_ref:
        w_ref[...] = weight[...]
    raw_ref[...] = projected[:, : 2 * width]
    ones = head_matrix(width)
    for place, out in enumerate((q_ref, k_ref)):
        values = projected[:, place * width : (place + 1) * width]
        factor = lax.rsqrt(head_mean_fine(values * values, ones) + EPSILON)
        out[...] = (values * factor * gain_ref[...]).astype(BF16)
    v_ref[...] = projected[:, 2 * width :].astype(BF16)


def place_columns(index, piece_refs, out_ref):
    width = piece_refs[0].shape[1]
    for offset, piece in enumerate(piece_refs):
        start = pl.multiple_of(jnp.bitwise_xor(index, offset) * width, width)
        out_ref[:, pl.ds(start, width)] = piece[...]


def piece_spec(piece, height, step):
    array, lead, block = piece
    width = array.shape[-1]
    if lead is None:
        return pl.BlockSpec((height, width), lambda i, *_: (block + step * i, 0))
    return pl.BlockSpec((None, height, width), lambda i, *_: (lead, block + step * i, 0))


def project(me, tok, pieces, weights, gain):
    count, width = pieces[0].shape
    depth = width * len(pieces)
    return pl.pallas_call(
        functools.partial(project_kernel, len(pieces)),
        grid_spec=pltpu.PrefetchScalarGridSpec(
            num_scalar_prefetch=2,
            grid=(count // BLK,),
            in_specs=[rows(BLK, width)] * len(pieces)
            + [piece_spec(weight, 3 * width, 0) for weight in weights]
            + [whole(1, width)],
            out_specs=[rows(BLK, depth), rows(BLK, 2 * width)]
            + [rows(BLK, width)] * 3
            + [whole(3 * width, depth)],
        ),
        out_shape=[like((count, depth), BF16), like((count, 2 * width), F32)]
        + [like((count, width), BF16)] * 3
        + [like((3 * width, depth), BF16)],
        compiler_params=params(),
        cost_estimate=cost(6 * count * width * depth, count * (4 * depth + 14 * width)),
        name="project",
    )(me, tok, *pieces, *[weight[0] for weight in weights], gain)


def assemble_kernel(tok_ref, *refs):
    place_columns(tok_ref[0], refs[:-1], refs[-1])


def assemble(tok, pieces, count, needs=()):
    width = pieces[0][0].shape[-1]
    depth = width * len(pieces)
    return launch(
        assemble_kernel,
        needs,
        (tok,),
        (count // BLK,),
        [piece_spec(piece, BLK, 1) for piece in pieces],
        (*[piece[0] for piece in pieces],),
        out_specs=rows(BLK, depth),
        out_shape=like((count, depth), BF16),
        cost_estimate=cost(0, 4 * count * depth),
        name="assemble",
    )


def seq_start(place, starts):
    found = jnp.zeros_like(place)
    for start in starts:
        found = jnp.where(place >= start, start, found)
    return found


def later_starts(length_ref, count):
    starts, total = [], jnp.int32(0)
    for position in range(count - 1):
        total = total + length_ref[position]
        starts.append(total)
    return starts


def attend_kernel(count, order, blocks, length_ref, me_ref, pad_ref, q_ref, k_ref, v_ref, *refs):
    mixed_ref, aux_ref, acc_ref = refs
    grid_step = pl.program_id(0)
    step = block_of(order, blocks, grid_step, me_ref)
    first_row = step * BLK
    starts = later_starts(length_ref, count)
    first = seq_start(first_row, starts) // BLK
    lane = lax.broadcasted_iota(jnp.int32, (BLK, 128), 1)
    left = lane < HEAD
    heads = q_ref.shape[1] // HEAD
    zero = jnp.zeros((BLK, 128), BF16)
    one = jnp.ones((BLK, 128), BF16)
    sides = [left if head % 2 == 0 else ~left for head in range(heads)]
    columns = [slice(head // 2 * 128, (head // 2 + 1) * 128) for head in range(heads)]
    queries = [jnp.where(sides[h], q_ref[:, columns[h]], zero) for h in range(heads)]
    acc_ref[...] = jnp.zeros_like(acc_ref)
    row = first_row + lax.broadcasted_iota(jnp.int32, (BLK, 1), 0)
    row_start = seq_start(row, starts)

    def body(block, carry):
        key_rows = pl.ds(pl.multiple_of(block * BLK, BLK), BLK)
        key = block * BLK + lax.broadcasted_iota(jnp.int32, (1, BLK), 1)
        code = jnp.where(pad_ref[:, key_rows] == 1, key, NEVER)
        mask = ((code >= row_start) & (code <= row)) | (key == row)
        for h in range(heads):
            value = jnp.where(sides[h], v_ref[key_rows, columns[h]], one)
            scores = dot_nt(queries[h], k_ref[key_rows, columns[h]])
            powers = jnp.where(mask, jnp.exp2(scores * SCORE), 0.0).astype(BF16)
            acc_ref[h] += dot_nn(powers, value)
        return carry

    lax.fori_loop(first, step + 1, body, 0)
    for pair in range(heads // 2):
        tile = slice(pair * 128, (pair + 1) * 128)
        even, odd = acc_ref[2 * pair], acc_ref[2 * pair + 1]
        total = jnp.where(left, odd, even)
        mixed = jnp.where(left, even, odd)
        mixed_ref[:, tile] = (mixed / pltpu.roll(total, HEAD, 1)).astype(BF16)
        high, low = split_low(jnp.log2(total) * (-1.0 / SCORE))
        aux_ref[:, tile] = jnp.where(lax.rem(lane, HEAD) < HEAD // 2, high, low)


def block_of(order, blocks, grid_step, me_ref):
    offset = order[0] + grid_step // blocks
    return jnp.bitwise_xor(me_ref[0], offset) * blocks + lax.rem(grid_step, blocks)


def piece_rows(blocks, place, width):
    return pl.BlockSpec(
        (BLK, width), lambda i, *_: (jnp.clip(i - place * blocks, 0, blocks - 1), 0)
    )


def attend(lengths, me, order, blocks, pad_row, queries, keys, values, needs=()):
    count, width = queries.shape
    heads = width // HEAD
    return launch(
        functools.partial(attend_kernel, lengths.shape[0], order, blocks),
        needs,
        (lengths, me,),
        (blocks * len(order),),
        [
                whole(1, count),
                pl.BlockSpec(
                    (BLK, width), lambda i, l_ref, me_ref: (block_of(order, blocks, i, me_ref), 0)
                ),
                whole(count, width),
                whole(count, width),
            ],
        (pad_row, queries, keys, values,),
        scratch_shapes=[pltpu.VMEM((heads, BLK, 128), F32)],
        out_specs=[rows(BLK, width)] * 2,
        out_shape=[like((len(order) * blocks * BLK, width), BF16)] * 2,
        cost_estimate=cost(2 * count * count * width, 6 * count * width, count * count * heads // 6),
        name="attend",
    )


def attend_back_kernel(
    count, pieces, length_ref, me_ref, pad_ref, q_ref, k_ref, v_ref, raw_ref, gain_ref, *refs
):
    pairs = pieces // 2
    aux_refs, mixed_refs, delta_refs = (
        refs[:pairs],
        refs[pairs : 2 * pairs],
        refs[2 * pairs : 2 * pairs + pieces],
    )
    low_ref, scale_sum, dqt_ref, do_ref, inner_ref, aux_ref, key_acc, value_acc = refs[
        2 * pairs + pieces :
    ]
    step = pl.program_id(0)
    tokens, width = q_ref.shape
    heads = width // HEAD
    starts = later_starts(length_ref, count)
    lane = lax.broadcasted_iota(jnp.int32, (BLK, 128), 1)
    left = lane < HEAD
    zero = jnp.zeros((BLK, 128), BF16)
    one = jnp.ones((BLK, 128), BF16)
    sides = [left if head % 2 == 0 else ~left for head in range(heads)]
    columns = [slice(head // 2 * 128, (head // 2 + 1) * 128) for head in range(heads)]

    @pl.when(step == 0)
    def prepare():
        dqt_ref[...] = jnp.zeros_like(dqt_ref)
        scale_sum[...] = jnp.zeros_like(scale_sum)
        part = tokens // pieces
        row = lax.broadcasted_iota(jnp.int32, (128, 128), 0)
        column = lax.broadcasted_iota(jnp.int32, (128, 128), 1)
        other = jnp.where(row // HEAD != column // HEAD, 1.0, 0.0).astype(BF16)
        for place in range(pieces):
            first = jnp.bitwise_xor(me_ref[0], place) * part
            do_ref[pl.ds(pl.multiple_of(first, part), part), :] = delta_refs[place][...]
            base = place % 2 * part
            aux_ref[pl.ds(pl.multiple_of(first, part), part), :] = aux_refs[place // 2][
                base : base + part, :
            ]
            for block in range(part // BLK):
                source = slice(block * BLK, (block + 1) * BLK)
                here = pl.ds(pl.multiple_of(first + block * BLK, BLK), BLK)
                for pair in range(heads // 2):
                    tile = slice(pair * 128, (pair + 1) * 128)
                    high, low = split_low(
                        delta_refs[place][source, tile].astype(F32)
                        * mixed_refs[place // 2][
                            base + block * BLK : base + (block + 1) * BLK, tile
                        ].astype(F32)
                    )
                    high, low = split_low(-(dot_nn(high, other) + dot_nn(low, other)))
                    inner_ref[here, tile] = jnp.where(lax.rem(lane, HEAD) < HEAD // 2, high, low)

    key_rows = pl.ds(pl.multiple_of(step * BLK, BLK), BLK)
    last_key = step * BLK + BLK - 1
    end = jnp.int32(tokens)
    for start in reversed(starts):
        end = jnp.where(last_key < start, start, end)
    last = (end - 1) // BLK
    key_acc[...] = jnp.zeros_like(key_acc)
    value_acc[...] = jnp.zeros_like(value_acc)
    turned = jnp.transpose(k_ref[key_rows, :].astype(F32)).astype(BF16)
    keys, values = [], []
    for h in range(heads):
        hot = jnp.where((lax.rem(lane, HEAD // 2) == 0) & (~sides[h]), one, zero)
        for source, into in ((k_ref, keys), (v_ref, values)):
            tile = jnp.where(sides[h], source[key_rows, columns[h]], zero)
            into.append(jnp.concatenate([tile, hot], axis=1))
    key = step * BLK + lax.broadcasted_iota(jnp.int32, (BLK, 1), 0)
    padding = jnp.transpose(
        jnp.broadcast_to(pad_ref[:, key_rows].astype(F32), (128, BLK))
    )[:, :1]
    code = jnp.where(padding > 0.5, key, NEVER)

    def body(block, carry):
        here = pl.ds(pl.multiple_of(block * BLK, BLK), BLK)
        row = block * BLK + lax.broadcasted_iota(jnp.int32, (1, BLK), 1)
        mask = ((code >= seq_start(row, starts)) & (code <= row)) | (key == row)
        for h in range(heads):
            query, delta = q_ref[here, columns[h]], do_ref[here, columns[h]]
            scores = dot_nt(keys[h], jnp.concatenate([query, aux_ref[here, columns[h]]], axis=1))
            delta_probs = dot_nt(
                values[h], jnp.concatenate([delta, inner_ref[here, columns[h]]], axis=1)
            )
            probs = jnp.where(mask, jnp.exp2(scores * SCORE), 0.0)
            delta_scores = (probs * delta_probs).astype(BF16)
            value_acc[h] += dot_nn(probs.astype(BF16), delta)
            key_acc[h] += dot_nn(delta_scores, query)
            head_rows = slice(h * HEAD, (h + 1) * HEAD)
            dqt_ref[head_rows, here] += dot_nn(turned[head_rows, :], delta_scores)
        return carry

    lax.fori_loop(step, last + 1, body, 0)
    key_tiles, value_tiles = [
        [jnp.where(left, acc[2 * pair], acc[2 * pair + 1]) for pair in range(heads // 2)]
        for acc in (key_acc, value_acc)
    ]
    ones = head_matrix(width)
    gain = gain_ref[...]
    deltas = (jnp.transpose(dqt_ref[:, key_rows]), jnp.concatenate(key_tiles, axis=1))
    for place, delta in enumerate(deltas):
        here = slice(place * width, (place + 1) * width)
        raw = raw_ref[:, here]
        factor = lax.rsqrt(head_mean(raw * raw, ones) + EPSILON)
        unit = raw * factor
        delta = delta * HEAD**-0.5
        scale_sum[...] += jnp.sum(delta * unit, axis=0, keepdims=True)
        delta = gain * delta
        low_ref[:, here] = (factor * (delta - unit * head_mean(delta * unit, ones))).astype(BF16)
    low_ref[:, 2 * width :] = jnp.concatenate(value_tiles, axis=1).astype(BF16)


def attend_back(lengths, me, pad_row, queries, keys, values, raw, gain, aux_pieces, mixed_pieces, delta_pieces):
    count, width = queries.shape
    heads = width // HEAD
    pieces = len(delta_pieces)
    return pl.pallas_call(
        functools.partial(attend_back_kernel, lengths.shape[0], pieces),
        grid_spec=pltpu.PrefetchScalarGridSpec(
            num_scalar_prefetch=2,
            grid=(count // BLK,),
            in_specs=[whole(1, count)]
            + [whole(count, width)] * 3
            + [rows(BLK, 2 * width), whole(1, width)]
            + [whole(2 * count // pieces, width)] * pieces
            + [piece_spec((array, lead, 0), count // pieces, 0) for array, lead in delta_pieces],
            out_specs=[rows(BLK, 3 * width), whole(1, width)],
            scratch_shapes=[
                pltpu.VMEM((width, count), F32),
                pltpu.VMEM((count, width), BF16),
                pltpu.VMEM((count, width), BF16),
                pltpu.VMEM((count, width), BF16),
                pltpu.VMEM((heads, BLK, 128), F32),
                pltpu.VMEM((heads, BLK, 128), F32),
            ],
        ),
        out_shape=[like((count, 3 * width), BF16), like((1, width), F32)],
        compiler_params=params(),
        cost_estimate=cost(8 * count * count * width, 22 * count * width, count * count * heads // 3),
        name="attend_back",
    )(lengths, me, pad_row, queries, keys, values, raw, gain, *aux_pieces, *mixed_pieces, *[array for array, lead in delta_pieces])


def unit_of(values):
    factor = lax.rsqrt(jnp.mean(values * values, axis=1, keepdims=True) + EPSILON)
    return values * factor, factor


def unit_back(delta, unit, factor):
    return factor * (delta - unit * jnp.mean(delta * unit, axis=1, keepdims=True))


def mixer_kernel(pieces, *refs):
    mixed_refs, out_weights = refs[:pieces], refs[pieces : 2 * pieces]
    tokens_ref, alpha_ref, *low_refs, one_ref, unit_ref, unit_factor, one_factor = refs[2 * pieces :]
    branch = dot_nn(mixed_refs[0][...], out_weights[0][...])
    for mixed, weight in zip(mixed_refs[1:], out_weights[1:]):
        branch += dot_nn(mixed[...], weight[...])
    unit, factor = unit_of(branch * SCALE_MODEL)
    unit_ref[...] = unit
    unit_factor[...] = jnp.broadcast_to(factor, unit_factor.shape)
    residual = tokens_ref[...].astype(F32)
    hidden, factor = unit_of(residual + alpha_ref[...] * (unit - residual))
    one_ref[...] = hidden
    one_factor[...] = jnp.broadcast_to(factor, one_factor.shape)
    put(1, hidden.astype(BF16), *low_refs)


def mixer(mixed_pieces, out_weights, me, tokens_all, alpha):
    width = mixed_pieces[0][0].shape[-1]
    pieces = len(mixed_pieces)
    count = tokens_all.shape[0] // pieces
    depth = tokens_all.shape[1]
    blocks = count // BLK
    kernel = functools.partial(mixer_kernel, pieces)
    return pl.pallas_call(
        lambda me_ref, *refs: kernel(*refs),
        grid_spec=pltpu.PrefetchScalarGridSpec(
            num_scalar_prefetch=1,
            grid=(blocks,),
            in_specs=[piece_spec((array, lead, 0), BLK, 1) for array, lead in mixed_pieces]
            + [piece_spec((array, lead, 0), width, 0) for array, lead in out_weights]
            + [
                pl.BlockSpec((BLK, depth), lambda i, me_ref: (me_ref[0] * blocks + i, 0)),
                whole(1, depth),
            ],
            out_specs=[piece_rows(1, 0, depth), piece_rows(1, 1, depth)]
            + [rows(BLK, depth)] * 2
            + [rows(BLK, 128)] * 2,
        ),
        out_shape=[like((BLK, depth), BF16)] * 2
        + [like((count, depth), F32)] * 2
        + [like((count, 128), F32)] * 2,
        compiler_params=params(),
        cost_estimate=cost(2 * count * depth * depth, 16 * count * depth + 2 * depth * depth),
        name="mixer",
    )(me, *[p[0] for p in mixed_pieces], *[w[0] for w in out_weights], tokens_all, alpha)


def turn_kernel(pieces, carried, me_ref, *refs):
    own_ref, near_ref, far_ref, one_ref = refs[:4]
    seed_refs = refs[4 : 4 + pieces]
    pad_ref, alpha_ref = refs[4 + pieces : 6 + pieces]
    outs = refs[6 + pieces + carried :]
    pair_refs = outs[: pieces // 2]
    hidden_ref, low_ref, alpha_sum, seed, layer = outs[pieces // 2 :]
    width = seed_refs[0].shape[-1]
    starts = [
        pl.multiple_of(jnp.bitwise_xor(me_ref[0], place) * width, width) for place in range(pieces)
    ]
    for start, piece in zip(starts, seed_refs):
        seed[:, pl.ds(start, width)] = piece[...]
    branch = (own_ref[...].astype(F32) + near_ref[...].astype(F32)) + far_ref[...].astype(F32)
    unit, unit_factor = unit_of(branch)
    hidden = one_ref[...]
    alpha = alpha_ref[...]
    layer_rows, layer_factor = unit_of(hidden + alpha * (unit - hidden))
    layer[...] = layer_rows.astype(BF16)
    for offset, start in enumerate(starts):
        pair_refs[offset // 2][offset % 2] = layer[:, pl.ds(start, width)]
    delta = unit_back(seed[...].astype(F32) * pad_ref[...], layer_rows, layer_factor)
    alpha_sum[...] = jnp.sum(delta * (unit - hidden), axis=0, keepdims=True)
    hidden_ref[...] = (1.0 - alpha) * delta
    low_ref[...] = unit_back(alpha * delta, unit, unit_factor).astype(BF16)


def turn(me, half, own, near, far, hidden_one, seed_pieces, pad_rows, alpha, carry=()):
    count, depth = hidden_one.shape
    pieces = len(seed_pieces)
    width = depth // pieces
    here = pl.BlockSpec((BLK, depth), lambda i, *_: (half, 0))
    pair = pl.BlockSpec((2, BLK, width), lambda i, *_: (0, half, 0))
    return pl.pallas_call(
        functools.partial(turn_kernel, pieces, len(carry)),
        grid_spec=pltpu.PrefetchScalarGridSpec(
            num_scalar_prefetch=1,
            grid=(1,),
            in_specs=[whole(BLK, depth)] * 3
            + [here]
            + [piece_spec((array, lead, half), BLK, 0) for array, lead in seed_pieces]
            + [pl.BlockSpec((BLK, 1), lambda i, *_: (half, 0)), whole(1, depth)]
            + [pl.BlockSpec(memory_space=pl.ANY)] * len(carry),
            out_specs=[pair] * (pieces // 2) + [here, whole(BLK, depth), whole(1, depth)],
            scratch_shapes=[pltpu.VMEM((BLK, depth), BF16)] * 2,
        ),
        out_shape=[like((2, count, width), BF16)] * (pieces // 2)
        + [like((count, depth), F32), like((BLK, depth), BF16), like((1, depth), F32)],
        input_output_aliases={7 + pieces + k: k for k in range(len(carry))},
        compiler_params=params(),
        cost_estimate=cost(40 * count * depth, 20 * count * depth),
        name="turn",
    )(
        me, own, near, far, hidden_one, *[p[0] for p in seed_pieces], pad_rows, alpha, *carry
    )


def mixer_back_kernel(pieces, *refs):
    halves, (hidden_ref, one_ref, unit_ref) = (refs[:6:2], refs[1:6:2]), refs[6:9]
    one_factor, unit_factor, tokens_ref, alpha_ref = refs[9:13]
    out_weights = refs[13 : 13 + pieces]
    pair_refs = refs[13 + pieces : 13 + pieces + pieces // 2]
    low_ref, direct_ref, alpha_sum = refs[13 + pieces + pieces // 2 :]
    own, near, far = [
        jnp.where(pl.program_id(0) < pl.num_programs(0) // 2, first[...].astype(F32), second[...].astype(F32))
        for first, second in zip(*halves)
    ]

    @pl.when(pl.program_id(0) == 0)
    def clear():
        alpha_sum[...] = jnp.zeros_like(alpha_sum)

    delta = hidden_ref[...] + ((own + near) + far)
    unit = unit_ref[...]
    alpha = alpha_ref[...]
    delta = unit_back(delta, one_ref[...], one_factor[:, :1])
    alpha_sum[...] += jnp.sum(delta * (unit - tokens_ref[...].astype(F32)), axis=0, keepdims=True)
    direct_ref[...] = (1.0 - alpha) * delta
    low = unit_back(alpha * delta, unit, unit_factor[:, :1]).astype(BF16)
    low_ref[...] = low
    for offset, weight in enumerate(out_weights):
        pair_refs[offset // 2][offset % 2] = (dot_nt(low, weight[...]) * SCALE_MODEL).astype(BF16)


def mixer_back(
    me, sums, hidden, one, unit, one_factor, unit_factor, tokens_all, alpha, out_weights
):
    count, depth = one.shape
    pieces = len(out_weights)
    width = depth // pieces
    block = BLK
    blocks = count // block
    half = blocks // 2
    kernel = functools.partial(mixer_back_kernel, pieces)
    return pl.pallas_call(
        lambda me_ref, *refs: kernel(*refs),
        grid_spec=pltpu.PrefetchScalarGridSpec(
            num_scalar_prefetch=1,
            grid=(blocks,),
            in_specs=[
                pl.BlockSpec((block, depth), lambda i, *_: (jnp.minimum(i, half - 1), 0)),
                pl.BlockSpec((block, depth), lambda i, *_: (jnp.maximum(i - half, 0), 0)),
            ]
            * 3
            + [rows(block, depth)] * 3
            + [rows(block, 128)] * 2
            + [
                pl.BlockSpec((block, depth), lambda i, me_ref: (me_ref[0] * blocks + i, 0)),
                whole(1, depth),
            ]
            + [piece_spec((array, lead, 0), width, 0) for array, lead in out_weights],
            out_specs=[pl.BlockSpec((2, block, width), lambda i, *_: (0, i, 0))] * (pieces // 2)
            + [rows(block, depth), rows(block, depth), whole(1, depth)],
        ),
        out_shape=[like((2, count, width), BF16)] * (pieces // 2)
        + [like((count, depth), BF16), like((count, depth), F32), like((1, depth), F32)],
        compiler_params=params(),
        cost_estimate=cost(2 * count * depth * depth, 28 * count * depth + 2 * depth * depth),
        name="mixer_back",
    )(
        me,
        *[value for pair in zip(sums[:3], sums[3:]) for value in pair],
        hidden,
        one,
        unit,
        one_factor,
        unit_factor,
        tokens_all,
        alpha,
        *[w[0] for w in out_weights],
    )


def pick(half, first_ref, second_ref, out_ref):
    step = pl.program_id(0)

    @pl.when(step < half)
    def from_first():
        out_ref[...] = first_ref[...]

    @pl.when(step >= half)
    def from_second():
        out_ref[...] = second_ref[...]


def put(half, value, first_ref, second_ref):
    step = pl.program_id(0)

    @pl.when(step < half)
    def to_first():
        first_ref[...] = value

    @pl.when(step >= half)
    def to_second():
        second_ref[...] = value


def whole_weight(tok_ref, piece_refs, out_ref):
    if out_ref is None:
        return piece_refs[0]

    @pl.when(pl.program_id(0) == 0)
    def assemble_weight():
        place_columns(tok_ref[0], piece_refs, out_ref)

    return out_ref


def expand_kernel(count, pieces, tok_ref, *refs):
    block_refs, gain_ref, refs = refs[:count], refs[count], refs[count + 1 :]
    up_pieces, gate_pieces = refs[:pieces], refs[pieces : 2 * pieces]
    up_ref, gate_ref, mid_ref = refs[2 * pieces : 2 * pieces + 3]
    hidden_ref = refs[-1]
    outs = refs[2 * pieces + 3 : -1] or (None, None)
    up_w = whole_weight(tok_ref, up_pieces, outs[0])
    gate_w = whole_weight(tok_ref, gate_pieces, outs[1])
    for place, block_ref in enumerate(block_refs):

        @pl.when(pl.program_id(0) == place)
        def take(block_ref=block_ref):
            hidden_ref[...] = block_ref[...]

    hidden = hidden_ref[...]
    up = dot_nt(hidden, up_w[...]) * SCALE_MODEL
    gate = dot_nt(hidden, gate_w[...]) * SCALE_MODEL
    up_ref[...] = up.astype(BF16)
    gate_ref[...] = gate.astype(BF16)
    scaled = gain_ref[1:2, :] * gate
    mid_ref[...] = (gain_ref[0:1, :] * up * scaled * jax.nn.sigmoid(scaled)).astype(BF16)


def expand(tok, blocks_in, up_pieces, gate_pieces, gains):
    depth = blocks_in[0].shape[1]
    hidden = gains.shape[1]
    count = len(blocks_in)
    pieces = len(up_pieces)
    outs = 2 if pieces > 1 else 0
    return pl.pallas_call(
        functools.partial(expand_kernel, count, pieces),
        grid_spec=pltpu.PrefetchScalarGridSpec(
            num_scalar_prefetch=1,
            grid=(count,),
            in_specs=[whole(BLK, depth)] * count
            + [whole(2, hidden)]
            + [piece_spec(piece, hidden, 0) for piece in (*up_pieces, *gate_pieces)],
            out_specs=[rows(BLK, hidden)] * 3 + [whole(hidden, depth)] * outs,
            scratch_shapes=[pltpu.VMEM((BLK, depth), BF16)],
        ),
        out_shape=[like((count * BLK, hidden), BF16)] * 3 + [like((hidden, depth), BF16)] * outs,
        compiler_params=params(),
        cost_estimate=cost(4 * count * BLK * depth * hidden, 4 * depth * hidden),
        name="expand",
    )(tok, *blocks_in, gains, *[piece[0] for piece in (*up_pieces, *gate_pieces)])


def contract_kernel(half, pieces, tok_ref, mid_ref, *refs):
    first_ref, second_ref = refs[pieces : pieces + 2]
    outs = refs[pieces + 2 :] or (None,)
    down_w = whole_weight(tok_ref, refs[:pieces], outs[0])
    put(half, (dot_nn(mid_ref[...], down_w[...]) * SCALE_HIDDEN).astype(BF16), first_ref, second_ref)


def contract(tok, middle, first_block, down_pieces, depth, needs=()):
    hidden = middle.shape[1]
    count, half = 2 * BLK, 1
    pieces = len(down_pieces)
    outs = 1 if pieces > 1 else 0
    return launch(
        functools.partial(contract_kernel, half, pieces),
        needs,
        (tok,),
        (2 * half,),
        [pl.BlockSpec((BLK, hidden), lambda i, *_: (first_block + i, 0))] + [piece_spec(piece, hidden, 0) for piece in down_pieces],
        (middle, *[piece[0] for piece in down_pieces],),
        out_specs=[piece_rows(half, 0, depth), piece_rows(half, 1, depth)]
            + [whole(hidden, depth)] * outs,
        out_shape=[like((count // 2, depth), BF16)] * 2 + [like((hidden, depth), BF16)] * outs,
        cost_estimate=cost(
            2 * count * depth * hidden, 2 * count * (depth + hidden) + 2 * depth * hidden
        ),
        name="contract",
    )


def gated_back_kernel(
    half,
    first_ref,
    second_ref,
    up_ref,
    gate_ref,
    up_w,
    gate_w,
    down_w,
    gain_ref,
    both_ref,
    first_out,
    second_out,
    unit_ref,
    delta_ref,
):
    @pl.when(pl.program_id(0) == 0)
    def clear():
        unit_ref[...] = jnp.zeros_like(unit_ref)

    pick(half, first_ref, second_ref, delta_ref)
    delta_middle = dot_nt(delta_ref[...], down_w[...]) * SCALE_HIDDEN
    up = up_ref[...].astype(F32)
    gate = gate_ref[...].astype(F32)
    scaled = gain_ref[1:2, :] * gate
    sigmoid = jax.nn.sigmoid(scaled)
    shared = delta_middle * sigmoid
    delta_up = shared * scaled
    delta_gate = shared * (gain_ref[0:1, :] * up) * (1.0 + scaled * (1.0 - sigmoid))
    unit_ref[0:1, :] += jnp.sum(delta_up * up, axis=0, keepdims=True)
    unit_ref[1:2, :] += jnp.sum(delta_gate * gate, axis=0, keepdims=True)
    up_low = (gain_ref[0:1, :] * delta_up).astype(BF16)
    gate_low = (gain_ref[1:2, :] * delta_gate).astype(BF16)
    both_ref[:, : up_low.shape[1]] = up_low
    both_ref[:, up_low.shape[1] :] = gate_low
    total = (dot_nn(up_low, up_w[...]) + dot_nn(gate_low, gate_w[...])) * SCALE_MODEL
    put(half, total.astype(BF16), first_out, second_out)


def gated_back(first, second, up, gate, first_block, up_w, gate_w, down_w, gains):
    count, depth = first.shape
    hidden = up_w.shape[0]
    half = count // BLK
    return pl.pallas_call(
        functools.partial(gated_back_kernel, half),
        grid=(2 * half,),
        in_specs=[piece_rows(half, 0, depth), piece_rows(half, 1, depth)]
        + [pl.BlockSpec((BLK, hidden), lambda i, *_: (first_block + i, 0))] * 2
        + [whole(hidden, depth)] * 3
        + [whole(2, hidden)],
        out_specs=[rows(BLK, 2 * hidden)]
        + [piece_rows(half, 0, depth), piece_rows(half, 1, depth), whole(2, hidden)],
        scratch_shapes=[pltpu.VMEM((BLK, depth), BF16)],
        out_shape=[like((2 * count, 2 * hidden), BF16)]
        + [like((count, depth), BF16)] * 2
        + [like((2, hidden), F32)],
        compiler_params=params(),
        cost_estimate=cost(
            12 * count * depth * hidden,
            8 * count * (depth + hidden) + 6 * depth * hidden,
            2 * count * hidden,
        ),
        name="gated_back",
    )(first, second, up, gate, up_w, gate_w, down_w, gains)


def part_columns(tok_ref, total, part_refs):
    width = part_refs[0].shape[2]
    in_halves = len(part_refs) == 6
    for offset in range(8):
        start = pl.multiple_of(jnp.bitwise_xor(tok_ref[0], offset) * width, width)
        value = total[:, pl.ds(start, width)].astype(BF16)
        sent, odd, lead = offset % 2, offset // 2 % 2, offset // 4
        if not in_halves:
            part_refs[2 * sent + odd][lead] = value
        elif not odd:
            part_refs[3 * sent][lead] = value
        else:
            half = pl.num_programs(0) // 2

            @pl.when(pl.program_id(0) < half)
            def first_half(value=value, into=part_refs[3 * sent + 1], lead=lead):
                into[lead] = value

            @pl.when(pl.program_id(0) >= half)
            def second_half(value=value, into=part_refs[3 * sent + 2], lead=lead):
                into[lead] = value


def weight_grad_kernel(lefts, rights, scale, steps, outs, tok_ref, *refs):
    left_refs, right_refs = refs[:lefts], refs[lefts : lefts + rights]
    fold_refs, part_refs = refs[lefts + rights : -outs - 1], refs[-outs - 1 : -1]
    total = refs[-1]

    @pl.when(pl.program_id(0) < steps)
    def product():
        acc, lefts_in = None, []
        for ref in left_refs:
            count = right_refs[0].shape[0]
            lefts_in += [ref[k * count : (k + 1) * count, :] for k in range(ref.shape[0] // count)]
        for left, right in zip(lefts_in, right_refs):
            term = lax.dot_general(
                left, right[...], (((0,), (0,)), ((), ())), preferred_element_type=F32
            )
            acc = term if acc is None else acc + term
        total[...] = acc * scale

    if fold_refs:

        @pl.when(pl.program_id(0) >= steps)
        def fold():
            own, near, far = [ref[...].astype(F32) for ref in fold_refs]
            total[...] = (own + near) + far

    part_columns(tok_ref, total, part_refs)


def weight_grad(tok, groups, lefts, rights, scale, folds=(), halves=False, needs=()):
    height = lefts[0].shape[1]
    depth = rights[0].shape[1]
    count = sum(left.shape[0] for left in lefts)
    part = depth // groups
    steps = height // BLK
    out = pl.BlockSpec((groups // 4, BLK, part), lambda i, *_: (0, i, 0))
    total_height = height + (BLK if folds else 0)
    outs, heights = [out] * 4, [total_height] * 4
    if halves:
        half = steps // 2
        odd = [
            pl.BlockSpec((groups // 4, BLK, part), lambda i, *_: (0, jnp.minimum(i, half - 1), 0)),
            pl.BlockSpec((groups // 4, BLK, part), lambda i, *_: (0, jnp.maximum(i - half, 0), 0)),
        ]
        outs = [out, *odd] * 2
        heights = [height, height // 2, height // 2] * 2
    return launch(
        functools.partial(
            weight_grad_kernel, len(lefts), len(rights), scale, steps, len(outs)
        ),
        needs,
        (tok,),
        (total_height // BLK,),
        [
                pl.BlockSpec((left.shape[0], BLK), lambda i, *_: (0, jnp.minimum(i, steps - 1)))
                for left in lefts
            ]
            + [whole(*right.shape) for right in rights]
            + [piece_spec((array, lead, 0), BLK, 0) for array, lead in folds],
        (*lefts, *rights, *[array for array, lead in folds],),
        scratch_shapes=[pltpu.VMEM((BLK, depth), F32)],
        out_specs=outs,
        out_shape=[like((groups // 4, tall, part), BF16) for tall in heights],
        cost_estimate=cost(
            2 * count * height * depth, 2 * count * (height + depth) + 2 * height * depth
        ),
        name="weight_grad",
    )


def out_grad_kernel(pieces, *refs):
    right, pair_refs = refs[pieces], refs[pieces + 1 :]
    for offset, left in enumerate(refs[:pieces]):
        total = lax.dot_general(
            left[...], right[...], (((0,), (0,)), ((), ())), preferred_element_type=F32
        )
        pair_refs[offset // 2][offset % 2] = (total * SCALE_MODEL).astype(BF16)


def out_grad(lefts, right):
    width = lefts[0][0].shape[-1]
    count, depth = right.shape
    pieces = len(lefts)
    return pl.pallas_call(
        functools.partial(out_grad_kernel, pieces),
        grid=(1,),
        in_specs=[piece_spec((array, lead, 0), count, 0) for array, lead in lefts]
        + [whole(count, depth)],
        out_specs=[whole(2, width, depth)] * (pieces // 2),
        out_shape=[like((2, width, depth), BF16)] * (pieces // 2),
        compiler_params=params(),
        cost_estimate=cost(2 * count * depth * depth, 4 * count * depth + 2 * depth * depth),
        name="out_grad",
    )(*[p[0] for p in lefts], right)


def project_back_kernel(pieces, me_ref, low_ref, w_ref, direct_ref, *refs):
    part_refs, total = refs[:pieces], refs[pieces]
    step = pl.program_id(0)
    total[...] = dot_nn(low_ref[...], w_ref[...]) * SCALE_MODEL
    own_blocks = direct_ref.shape[0] // BLK

    @pl.when(step // own_blocks == me_ref[0])
    def add_direct():
        start = pl.multiple_of(lax.rem(step, own_blocks) * BLK, BLK)
        total[...] += direct_ref[pl.ds(start, BLK), :]

    part = total.shape[1] // pieces
    for place, out in enumerate(part_refs):
        start = pl.multiple_of(jnp.bitwise_xor(me_ref[0], place) * part, part)
        out[...] = total[:, pl.ds(start, part)].astype(BF16)


def project_back(me, pieces, low, weight, direct, needs=()):
    count = low.shape[0]
    depth = weight.shape[1]
    part = depth // pieces
    return launch(
        functools.partial(project_back_kernel, pieces),
        needs,
        (me,),
        (count // BLK,),
        [rows(BLK, low.shape[1]), whole(*weight.shape), whole(*direct.shape)],
        (low, weight, direct),
        scratch_shapes=[pltpu.VMEM((BLK, depth), F32)],
        out_specs=[rows(BLK, part)] * pieces,
        out_shape=[like((count, part), BF16)] * pieces,
        cost_estimate=cost(2 * count * low.shape[1] * depth, 2 * count * depth),
        name="project_back",
    )


def trade(value, axis, offset):
    size = lax.axis_size(axis)
    return lax.ppermute(value, axis, [(i, i ^ offset) for i in range(size)])


def sum_four(value, axis, first, second):
    one, two, three = [trade(value, axis, o) for o in (first, second, first ^ second)]
    return (value + one) + (two + three)


def sum_over(value, axis):
    if lax.axis_size(axis) == 4:
        return sum_four(value, axis, 1, 2)
    if lax.axis_size(axis) == 8:
        return sum_four(value + trade(value, axis, 1), axis, 2, 4)
    offset = 1
    while offset < lax.axis_size(axis):
        value = value + trade(value, axis, offset)
        offset *= 2
    return value


def join(*values):
    return lax.optimization_barrier(values)


def stack(*values):
    return jnp.concatenate([v if v.ndim == 3 else v[None] for v in values], axis=0)


def add_low(*values):
    total = values[0].astype(F32)
    for value in values[1:]:
        total = total + value.astype(F32)
    return total


def plain_sum(left, right, scale):
    total = jnp.einsum("tr,td->rd", left, right, preferred_element_type=F32) * scale
    return lax.psum_scatter(total.astype(BF16), "tok", scatter_dimension=1, tiled=True).astype(F32)


def moment_update(weights, gradient, moment, square, fix_first, fix_second):
    moment_next = BETA_ONE * moment + (1.0 - BETA_ONE) * gradient
    square_next = BETA_TWO * square + (1.0 - BETA_TWO) * gradient * gradient
    stepped = weights - LEARN_RATE * (moment_next / fix_first) / (
        jnp.sqrt(square_next / fix_second) + ADAM_EPSILON
    )
    return (stepped, moment_next, square_next)


def local(
    inputs,
    cotangent,
    lengths,
    pad_mask,
    attention_weights,
    gated_weights,
    model_gains,
    unit_gains,
    attention_moment,
    attention_square,
    gated_moment,
    gated_square,
    model_moment,
    model_square,
    unit_moment,
    unit_square,
):
    token_count, width = inputs.shape
    parts = lax.axis_size("dim")
    hidden_here = gated_weights.shape[1]
    own_count = token_count // parts
    place = lax.axis_index("dim")
    me = place.astype(jnp.int32).reshape(1)
    tok = lax.axis_index("tok").astype(jnp.int32).reshape(1)
    groups = lax.axis_size("tok")
    by_pieces = groups == 8 and (D // groups) % 128 == 0
    blocks = own_count // BLK
    length_row = lengths[0]

    def token_rows(value, offset):
        return lax.dynamic_slice_in_dim(value, (place ^ offset) * own_count, own_count, 0)

    ao = attention_weights.reshape(4 * width, -1).astype(BF16)
    gated_low = gated_weights.reshape(3 * hidden_here, -1).astype(BF16)
    both_own = gated_weights[:2].reshape(2 * hidden_here, -1).astype(BF16)
    down_own = gated_weights[2].astype(BF16)
    score_gain = model_gains[:1]
    pad_row = pad_mask[None, :]
    pad_rows = token_rows(pad_mask, 0).astype(F32)[:, None]

    x_far = trade(inputs, "dim", 2)
    seed_rows = [token_rows(cotangent, r) for r in range(parts)]
    seed_send = stack(*seed_rows[2:])
    alphas = lax.dynamic_update_slice(
        jnp.zeros((2, D), F32), model_gains[1:], (0, place * width)
    )
    alpha_near = trade(alphas, "dim", 1)
    if by_pieces:
        ao_by = {0: ao, 4: trade(ao, "tok", 4), 2: trade(ao, "tok", 2), 1: trade(ao, "tok", 1)}
        ao_by[6] = trade(ao_by[4], "tok", 2)
        ao_by[5] = trade(ao_by[4], "tok", 1)
        ao_by[3] = trade(ao_by[2], "tok", 1)
        x_far, ao_by, both_own, seed_send, alphas, alpha_near = join(
            x_far, ao_by, both_own, seed_send, alphas, alpha_near
        )
        ao_by[7] = trade(ao_by[6], "tok", 1)
        by = {0: both_own, 2: trade(both_own, "tok", 2), 4: trade(both_own, "tok", 4)}
    else:
        gather = functools.partial(lax.all_gather, axis_name="tok", axis=1, tiled=True)
        in_pieces = [(gather(ao[: 3 * width]), None, 0)]
        out_weight, up_w, gate_w, down_w = [
            gather(shard)
            for shard in (ao[3 * width :], both_own[:hidden_here], both_own[hidden_here:], down_own)
        ]
        up_pieces, gate_pieces, down_pieces = [[(w, None, 0)] for w in (up_w, gate_w, down_w)]
    x_near = trade(inputs, "dim", 1)
    x_corner = trade(x_far, "dim", 1)
    token_pieces = [inputs, x_near, x_far, x_corner]
    if by_pieces:
        token_pieces, ao_by, gated_low, down_own, seed_send, alphas = join(
            token_pieces, ao_by, gated_low, down_own, seed_send, alphas
        )
        in_pieces = [(ao_by[offset], None, 0) for offset in range(8)]
        by[1] = trade(gated_low, "tok", 1)
    seed_far = trade(seed_send, "dim", 2)
    tokens_all, raw, queries, keys, values, weight_in = project(
        me, tok, token_pieces, in_pieces, score_gain
    )
    queries, seed_far = join(queries, seed_far)

    queries, seed_far, alpha_near = join(queries, seed_far, alpha_near)
    alphas = alphas + alpha_near
    alpha_far = trade(alphas, "dim", 2)
    if by_pieces:
        queries, by[1], by[2], by[4], ao_by, down_own = join(
            queries, by[1], by[2], by[4], ao_by, down_own
        )
        by[3] = trade(by[2], "tok", 1)
        by[6] = trade(by[4], "tok", 2)
        out_weight = assemble(
            tok, [(ao_by[o], None, 3 * width // BLK) for o in range(8)], width, (queries,)
        )
    out_across = trade(out_weight, "dim", 2)
    far_mixed, far_aux = attend(
        length_row, me, (2, 3), blocks, pad_row, queries, keys, values, (out_weight,)
    )
    far_mixed, alpha_far, out_across = join(far_mixed, alpha_far, out_across)
    alphas = alphas + alpha_far
    alpha_mixer, alpha_gated = alphas[:1], alphas[1:]
    if by_pieces:
        far_mixed, by[3], by[6], down_own = join(far_mixed, by[3], by[6], down_own)
        by[5] = trade(by[4], "tok", 1)
        down_by = {0: down_own, 2: trade(down_own, "tok", 2), 4: trade(down_own, "tok", 4)}
    far_came = trade(far_mixed, "dim", 2)
    out_pair = trade(stack(out_weight, out_across), "dim", 1)
    near_mixed, near_aux = attend(
        length_row, me, (0, 1), blocks, pad_row, queries, keys, values, (far_mixed,)
    )
    near_mixed, far_came, out_pair = join(near_mixed, far_came, out_pair)
    if by_pieces:
        near_mixed, by[5], by[6], down_by = join(near_mixed, by[5], by[6], down_by)
    pair_came = trade(stack(near_mixed[own_count:], far_came[own_count:]), "dim", 1)
    out_weights = [(out_weight, None), (out_pair, 0), (out_across, None), (out_pair, 1)]
    mixed_pieces = [(near_mixed, None), (pair_came, 0), (far_came, None), (pair_came, 1)]
    low_a, low_b, hidden_one, mixer_unit, mixer_factor, one_factor = mixer(
        mixed_pieces, out_weights, me, tokens_all, alpha_mixer
    )

    far_a = trade(low_a, "dim", 2)
    near_a = trade(low_a, "dim", 1)
    near_b = trade(low_b, "dim", 1)
    if by_pieces:
        near_a, near_b, by[6], down_by = join(near_a, near_b, by[6], down_by)
        by[7] = trade(by[6], "tok", 1)
        down_by[1] = by[1]
        down_by[6] = trade(down_by[4], "tok", 2)
        near_a, far_a, by[7], down_by = join(near_a, far_a, by[7], down_by)
        down_by[3] = trade(down_by[2], "tok", 1)
        down_by[5] = trade(down_by[4], "tok", 1)
        up_pieces, gate_pieces = [[(by[o], None, k) for o in range(8)] for k in range(2)]
    near_a, far_a, low_b = join(near_a, far_a, low_b)
    far_b = trade(low_b, "dim", 2)
    corner_a = trade(far_a, "dim", 1)
    up_one, gate_one, mid_one, *assembled = expand(
        tok, [low_a, near_a, low_b, near_b], up_pieces, gate_pieces, unit_gains
    )
    if by_pieces:
        up_w, gate_w = assembled
        up_pieces, gate_pieces = [(up_w, None, 0)], [(gate_w, None, 0)]
        mid_one, down_by, corner_a = join(mid_one, down_by, corner_a)
        down_by[7] = trade(down_by[6], "tok", 1)
    seed_pair = trade(stack(seed_rows[1], seed_far[1]), "dim", 1)
    seed_pieces = [(seed_rows[0], None), (seed_pair, 0), (seed_far, 0), (seed_pair, 1)]
    up_a, gate_a, mid_a = expand(tok, [far_a, corner_a], up_pieces, gate_pieces, unit_gains)
    mid_a, far_b, seed_pair = join(mid_a, far_b, seed_pair)
    seed_pieces = [(seed_rows[0], None), (seed_pair, 0), (seed_far, 0), (seed_pair, 1)]
    corner_b = trade(far_b, "dim", 1)
    if by_pieces:
        mid_a, down_by = join(mid_a, down_by)
        down_pieces = [(down_by[o], None, 2 if o == 1 else 0) for o in range(8)]
        *parts_a, down_w = contract(tok, mid_a, 0, down_pieces, D)
        down_pieces = [(down_w, None, 0)]
    else:
        parts_a = contract(tok, mid_a, 0, down_pieces, D)
    came = trade(parts_a[1], "dim", 1)
    up_b, gate_b, mid_b = expand(tok, [far_b, corner_b], up_pieces, gate_pieces, unit_gains)
    mid_b, came = join(mid_b, came)
    across = add_low(parts_a[0], came).astype(BF16)
    across_a = trade(across, "dim", 2)
    parts_b = contract(tok, mid_b, 0, down_pieces, D, (across,))
    came = trade(parts_b[1], "dim", 1)
    own_a, pair_a = contract(tok, mid_one, 0, down_pieces, D, (parts_b[0],))
    own_a, came, parts_b, pair_a, across_a = join(own_a, came, parts_b, pair_a, across_a)
    across = add_low(parts_b[0], came).astype(BF16)
    across_b = trade(across, "dim", 2)
    pair_a = trade(pair_a, "dim", 1)
    own_b, pair_b = contract(tok, mid_one, 2, down_pieces, D, (own_a, across))
    own_b, pair_b, pair_a = join(own_b, pair_b, pair_a)
    *carry, delta_a, sum_a = turn(
        me, 0, own_a, pair_a, across_a, hidden_one, seed_pieces, pad_rows, alpha_gated
    )
    pair_b = trade(pair_b, "dim", 1)
    delta_a, across_b, pair_b, carry = join(delta_a, across_b, pair_b, carry)

    back_weights = (up_w, gate_w, down_w, unit_gains)
    b_far_a = trade(delta_a, "dim", 2)
    b_near_a = trade(delta_a, "dim", 1)
    layer_near, layer_far, delta_hidden, delta_b, sum_b = turn(
        me, 1, own_b, pair_b, across_b, hidden_one, seed_pieces, pad_rows, alpha_gated, carry
    )
    delta_b, b_near_a = join(delta_b, b_near_a)
    both_near_a, own_one, pair_one, unit_one = gated_back(
        delta_a, b_near_a, up_one, gate_one, 0, *back_weights
    )
    b_near_b = trade(delta_b, "dim", 1)
    own_one, b_far_a, delta_b, pair_one, b_near_b = join(own_one, b_far_a, delta_b, pair_one, b_near_b)
    b_far_b = trade(delta_b, "dim", 2)
    b_corner_a = trade(b_far_a, "dim", 1)
    pair_one = trade(pair_one, "dim", 1)
    both_near_b, own_two, pair_two, unit_two = gated_back(
        delta_b, b_near_b, up_one, gate_one, 2, *back_weights
    )
    own_two, b_corner_a, pair_one, pair_two, b_far_b = join(
        own_two, b_corner_a, pair_one, pair_two, b_far_b
    )
    pair_two = trade(pair_two, "dim", 1)
    b_corner_b = trade(b_far_b, "dim", 1)
    both_far_a, back_across_a, corner, unit_three = gated_back(
        b_far_a, b_corner_a, up_a, gate_a, 0, *back_weights
    )
    corner, pair_two, b_corner_b = join(corner, pair_two, b_corner_b)
    corner = trade(corner, "dim", 1)
    across = add_low(back_across_a, corner).astype(BF16)
    across, b_corner_b = join(across, b_corner_b)
    across_one = trade(across, "dim", 2)
    both_far_b, back_across_b, corner, unit_four = gated_back(
        b_far_b, b_corner_b, up_b, gate_b, 0, *back_weights
    )
    back_across_b, across_one = join(back_across_b, across_one)
    corner = trade(corner, "dim", 1)
    across = add_low(back_across_b, corner).astype(BF16)
    across_two = trade(across, "dim", 2)
    back_sums = [own_one, pair_one, across_one, own_two, pair_two, across_two]
    h_pieces = [low_a, near_a, low_b, near_b, far_a, corner_a, far_b, corner_b]
    b_pieces = [delta_a, b_near_a, delta_b, b_near_b, b_far_a, b_corner_a, b_far_b, b_corner_b]
    middles = [mid_one, mid_a, mid_b]
    both_pieces = [both_near_a, both_near_b, both_far_a, both_far_b]
    unit_sums = (unit_one + unit_two) + (unit_three + unit_four)
    sum_gated = sum_a + sum_b
    if by_pieces:
        down_parts = weight_grad(tok, groups, middles, b_pieces, SCALE_HIDDEN, needs=(across,))
        down_odd = trade(down_parts[3], "tok", 1)
        both_parts = weight_grad(
            tok,
            groups,
            both_pieces,
            h_pieces,
            SCALE_MODEL,
            halves=True,
            needs=(down_parts[0],),
        )
        back_sums, both_parts, down_odd = join(back_sums, both_parts, down_odd)
        both_even, up_odd, gate_odd, *both_send = both_parts
        up_came = trade(both_send[1], "tok", 1)
        down_low = add_low(down_parts[1], down_odd).astype(BF16)
        down_near = trade(down_low, "tok", 2)
    else:
        down_grad = plain_sum(
            jnp.concatenate(middles, axis=0), jnp.concatenate(b_pieces, axis=0), SCALE_HIDDEN
        )
        both_grad = plain_sum(
            jnp.concatenate(both_pieces, axis=0), jnp.concatenate(h_pieces, axis=0), SCALE_MODEL
        )

    delta_near, delta_far, mixer_low, delta_direct, sum_mixer = mixer_back(
        me,
        back_sums,
        delta_hidden,
        hidden_one,
        mixer_unit,
        one_factor,
        mixer_factor,
        tokens_all,
        alpha_mixer,
        out_weights,
    )
    if by_pieces:
        delta_far, mixer_low, up_came, down_near = join(delta_far, mixer_low, up_came, down_near)
        gate_came = trade(both_send[2], "tok", 1)
        up_near = trade(add_low(up_odd, up_came).astype(BF16), "tok", 2)
    delta_came = trade(delta_far, "dim", 2)
    out_near_grad, out_far_grad = out_grad(mixed_pieces, mixer_low)
    alpha_sums = jnp.concatenate([sum_mixer, sum_gated], axis=0)
    alpha_near = trade(alpha_sums, "dim", 1)
    delta_came, out_near_grad, out_far_grad, alpha_near, layer_far = join(
        delta_came, out_near_grad, out_far_grad, alpha_near, layer_far
    )
    if by_pieces:
        delta_came, gate_came, up_near = join(delta_came, gate_came, up_near)
    delta_pair = trade(stack(delta_near[1], delta_came[1]), "dim", 1)
    out_pair = trade(stack(out_near_grad[1], out_far_grad[1]), "dim", 1)
    alpha_sums = alpha_sums + alpha_near
    delta_pair, out_pair = join(delta_pair, out_pair)
    if by_pieces:
        gate_near = trade(add_low(gate_odd, gate_came).astype(BF16), "tok", 2)
        both_even_came = trade(both_send[0], "tok", 1)
        down_even = trade(down_parts[2], "tok", 1)
    layer_came = trade(layer_far, "dim", 2)
    out_far_sum = trade(add_low(out_far_grad[0], out_pair[1]).astype(BF16), "dim", 2)
    delta_pieces = [(delta_near, 0), (delta_pair, 0), (delta_came, 0), (delta_pair, 1)]
    delta_project, scale_sum = attend_back(
        length_row,
        me,
        pad_row,
        queries,
        keys,
        values,
        raw,
        score_gain,
        [near_aux, far_aux],
        [near_mixed, far_mixed],
        delta_pieces,
    )
    delta_project, alpha_sums, out_far_sum, layer_came = join(
        delta_project, alpha_sums, out_far_sum, layer_came
    )
    alpha_far = trade(alpha_sums, "dim", 2)
    if by_pieces:
        delta_project, gate_near, both_even_came, down_even = join(
            delta_project, gate_near, both_even_came, down_even
        )
        down_low = add_low(down_parts[0][1], down_even[1], down_near[1]).astype(BF16)
        down_last = trade(down_low, "tok", 4)
        up_low, gate_low = [
            add_low(
                *[value[1, k * hidden_here : (k + 1) * hidden_here] for value in (both_even, both_even_came)],
                near[1],
            ).astype(BF16)
            for k, near in enumerate((up_near, gate_near))
        ]
        in_parts = weight_grad(
            tok,
            groups,
            (delta_project,),
            (tokens_all,),
            SCALE_MODEL,
            ((out_near_grad, 0), (out_pair, 0), (out_far_sum, None)),
            needs=(up_low, gate_low, down_low),
        )
        in_parts, alpha_far, layer_near, down_last, up_low, gate_low = join(
            in_parts, alpha_far, layer_near, down_last, up_low, gate_low
        )
        up_last = trade(up_low, "tok", 4)
        in_odd = trade(in_parts[3], "tok", 1)
    alpha_sums = lax.dynamic_slice_in_dim(alpha_sums + alpha_far, place * width, width, 1)
    gains_sum = jnp.concatenate(
        [scale_sum.reshape(-1), alpha_sums.reshape(-1), unit_sums.reshape(-1)]
    )
    input_parts = project_back(
        me, parts, delta_project, weight_in, delta_direct, (in_parts[3],) if by_pieces else ()
    )
    if by_pieces:
        input_parts, in_odd, in_parts, up_last, gate_low = join(
            input_parts, in_odd, in_parts, up_last, gate_low
        )
        in_low = add_low(in_parts[1], in_odd).astype(BF16)
        in_near = trade(in_low, "tok", 2)
        in_even = trade(in_parts[2], "tok", 1)
        gate_last = trade(gate_low, "tok", 4)
    corner = trade(input_parts[3], "dim", 1)
    near = trade(input_parts[1], "dim", 1)
    half = token_count // 2
    across = [
        add_low(input_parts[2][k * half : (k + 1) * half], corner[k * half : (k + 1) * half])
        for k in range(2)
    ]
    far_one = trade(across[0].astype(BF16), "dim", 2)
    across_two = across[1].astype(BF16)
    if by_pieces:
        far_one, near, across_two, gate_last, in_near, in_even = join(
            far_one, near, across_two, gate_last, in_near, in_even
        )
    far_two = trade(across_two, "dim", 2)
    layer_pair = trade(stack(layer_near[1], layer_came[1]), "dim", 1)
    layer_pieces = [layer_near[0], layer_pair[0], layer_came[0], layer_pair[1]]
    layer_out = jnp.zeros((token_count, width), BF16)
    for r, piece in enumerate(layer_pieces):
        layer_out = lax.dynamic_update_slice(layer_out, piece, ((place ^ r) * own_count, 0))
    if by_pieces:
        in_low = add_low(in_parts[0][1], in_even[1], in_near[1]).astype(BF16)
        in_last = trade(in_low, "tok", 4)
        down_grad = add_low(down_parts[0][0], down_even[0], down_near[0], down_last)
        up_grad, gate_grad = [
            add_low(
                *[value[0, k * hidden_here : (k + 1) * hidden_here] for value in (both_even, both_even_came)],
                near_sum[0],
                last,
            )
            for k, (near_sum, last) in enumerate(((up_near, up_last), (gate_near, gate_last)))
        ]
        both_grad = jnp.concatenate([up_grad, gate_grad], axis=0)
    gated_grad = jnp.concatenate([both_grad, down_grad], axis=0).reshape(3, hidden_here, -1)
    fix_first = 1.0 - BETA_ONE**STEP
    fix_second = 1.0 - BETA_TWO**STEP
    gated_stepped, moment_gated, square_gated = moment_update(
        gated_weights, gated_grad, gated_moment, gated_square, fix_first, fix_second
    )
    gated_row_sums = jnp.sum(gated_stepped * gated_stepped, axis=2)
    gated_square_sum = jnp.sum(gated_grad * gated_grad)
    if by_pieces:
        in_last, gated_row_sums, gated_square_sum, layer_out, far_two = join(
            in_last, gated_row_sums, gated_square_sum, layer_out, far_two
        )
        in_total = add_low(in_parts[0][0], in_even[0], in_near[0], in_last)
        attention_grad = in_total.reshape(4, width, -1)
    else:
        out_total = lax.psum_scatter(
            add_low(out_near_grad[0], out_pair[0], out_far_sum).astype(BF16),
            "tok",
            scatter_dimension=1,
            tiled=True,
        ).astype(F32)
        in_total = plain_sum(delta_project, tokens_all, SCALE_MODEL)
        attention_grad = jnp.concatenate([in_total, out_total], axis=0).reshape(4, width, -1)

    input_gradient = add_low(input_parts[0], near, jnp.concatenate([far_one, far_two], axis=0))

    attention_stepped, moment_attention, square_attention = moment_update(
        attention_weights, attention_grad, attention_moment, attention_square, fix_first, fix_second
    )
    sums = sum_over(
        jnp.concatenate(
            [
                jnp.sum(attention_stepped * attention_stepped, axis=2).reshape(-1),
                gated_row_sums.reshape(-1),
                gains_sum,
                (jnp.sum(attention_grad * attention_grad) + gated_square_sum).reshape(1),
            ]
        ),
        "tok",
    )
    ends = [4 * width, 4 * width + 3 * hidden_here, 7 * width + 3 * hidden_here]
    model_grad = sums[ends[1] : ends[2]].reshape(3, width)
    unit_grad = sums[ends[2] : -1].reshape(2, hidden_here)
    model_next, moment_model, square_model = moment_update(
        model_gains, model_grad, model_moment, model_square, fix_first, fix_second
    )
    unit_next, moment_unit, square_unit = moment_update(
        unit_gains, unit_grad, unit_moment, unit_square, fix_first, fix_second
    )
    square_sum = sums[-1:] + jnp.sum(model_grad * model_grad) + jnp.sum(unit_grad * unit_grad)
    totals = sum_over(jnp.concatenate([square_sum, jnp.sum(model_next[1:], axis=1)]), "dim")
    attention_rows = sums[: ends[0]].reshape(4, width, 1)
    gated_rows = sums[ends[0] : ends[1]].reshape(3, hidden_here, 1)
    attention_next = attention_stepped * lax.rsqrt(attention_rows / D + EPSILON)
    gated_next = gated_stepped * lax.rsqrt(gated_rows / D + EPSILON)
    gradient_norm = jnp.sqrt(totals[:1])
    mean_alpha = totals[1:] / D
    return (
        layer_out,
        input_gradient,
        attention_next,
        attention_next.astype(BF16),
        moment_attention,
        square_attention,
        gated_next,
        gated_next.astype(BF16),
        moment_gated,
        square_gated,
        model_next,
        moment_model,
        square_model,
        unit_next,
        moment_unit,
        square_unit,
        gradient_norm,
        mean_alpha,
    )


def solution(mesh):
    tokens = P("tok", "dim")
    weights = P(None, "dim", "tok")
    gains = P(None, "dim")
    in_specs = (tokens, tokens, P("tok", None), P("tok"), weights, weights, gains, gains)
    in_specs += (weights,) * 4 + (gains,) * 4
    out_specs = (tokens, tokens) + (weights,) * 8 + (gains,) * 6 + (P(), P())
    return jax.shard_map(local, mesh=mesh, in_specs=in_specs, out_specs=out_specs, check_vma=False)
```

```python
import functools
import math

import jax
import jax.numpy as jnp
from jax import lax
from jax.experimental import pallas as pl
from jax.experimental.pallas import tpu as pltpu
from jax.sharding import PartitionSpec as P

D = 1024
HEAD = 64
FF = 4096
STEP = 4
BLK = 256

EPSILON = 1e-06
ADAM_EPSILON = 1e-08
BETA_ONE = 0.5
BETA_TWO = 0.5
LEARN_RATE = 1.5

F32 = jnp.float32
BF16 = jnp.bfloat16
SCALE_MODEL = D**-0.5
SCALE_HIDDEN = FF**-0.5
SCORE = HEAD**-0.5 * math.log2(math.e)
NEVER = 1 << 24


def dot_nt(left, right):
    return lax.dot_general(left, right, (((1,), (1,)), ((), ())), preferred_element_type=F32)


def dot_nn(left, right):
    return lax.dot_general(left, right, (((1,), (0,)), ((), ())), preferred_element_type=F32)


def split_low(values):
    high = values.astype(BF16)
    return high, (values - high.astype(F32)).astype(BF16)


def params():
    return pltpu.CompilerParams(vmem_limit_bytes=60 << 20)


def cost(flops, traffic, transcendentals=0):
    return pl.CostEstimate(
        flops=int(flops) // 64, bytes_accessed=int(traffic) // 64, transcendentals=int(transcendentals) // 64
    )


def like(shape, dtype):
    return jax.ShapeDtypeStruct(shape, dtype)


def whole(*shape):
    return pl.BlockSpec(shape, lambda *_: (0,) * len(shape))


def rows(count, width):
    return pl.BlockSpec((count, width), lambda i, *_: (i, 0))


def launch(kernel, needs, scalars, grid, in_specs, args, scratch_shapes=(), **options):
    taken = len(scalars) + len(args)

    def body(*refs):
        kernel(*refs[:taken], *refs[taken + len(needs) :])

    return pl.pallas_call(
        body,
        grid_spec=pltpu.PrefetchScalarGridSpec(
            num_scalar_prefetch=len(scalars),
            grid=grid,
            in_specs=[*in_specs] + [pl.BlockSpec(memory_space=pl.ANY)] * len(needs),
            out_specs=options.pop("out_specs"),
            scratch_shapes=scratch_shapes,
        ),
        compiler_params=params(),
        **options,
    )(*scalars, *args, *needs)


def head_matrix(width):
    row = lax.broadcasted_iota(jnp.int32, (width, width), 0)
    column = lax.broadcasted_iota(jnp.int32, (width, width), 1)
    return jnp.where(row // HEAD == column // HEAD, 1.0, 0.0).astype(BF16)


def head_mean(values, ones):
    return dot_nn(values.astype(BF16), ones) * (1.0 / HEAD)


def head_mean_fine(values, ones):
    high, low = split_low(values)
    return (dot_nn(high, ones) + dot_nn(low, ones)) * (1.0 / HEAD)


def project_kernel(pieces, me_ref, tok_ref, *refs):
    piece_refs = refs[:pieces]
    weight_refs = refs[pieces:-7]
    gain_ref, all_ref, raw_ref, q_ref, k_ref, v_ref, w_ref = refs[-7:]
    width = piece_refs[0].shape[1]
    if len(weight_refs) == 1:
        weight = weight_refs[0]
    else:
        weight = w_ref

        @pl.when(pl.program_id(0) == 0)
        def assemble_weight():
            place_columns(tok_ref[0], weight_refs, w_ref)

    place_columns(me_ref[0], piece_refs, all_ref)
    projected = dot_nt(all_ref[...], weight[...]) * SCALE_MODEL
    if weight is not w_ref:
        w_ref[...] = weight[...]
    raw_ref[...] = projected[:, : 2 * width]
    ones = head_matrix(width)
    for place, out in enumerate((q_ref, k_ref)):
        values = projected[:, place * width : (place + 1) * width]
        factor = lax.rsqrt(head_mean_fine(values * values, ones) + EPSILON)
        out[...] = (values * factor * gain_ref[...]).astype(BF16)
    v_ref[...] = projected[:, 2 * width :].astype(BF16)


def place_columns(index, piece_refs, out_ref):
    width = piece_refs[0].shape[1]
    for offset, piece in enumerate(piece_refs):
        start = pl.multiple_of(jnp.bitwise_xor(index, offset) * width, width)
        out_ref[:, pl.ds(start, width)] = piece[...]


def piece_spec(piece, height, step):
    array, lead, block = piece
    width = array.shape[-1]
    if lead is None:
        return pl.BlockSpec((height, width), lambda i, *_: (block + step * i, 0))
    return pl.BlockSpec((None, height, width), lambda i, *_: (lead, block + step * i, 0))


def project(me, tok, pieces, weights, gain):
    count, width = pieces[0].shape
    depth = width * len(pieces)
    return pl.pallas_call(
        functools.partial(project_kernel, len(pieces)),
        grid_spec=pltpu.PrefetchScalarGridSpec(
            num_scalar_prefetch=2,
            grid=(count // BLK,),
            in_specs=[rows(BLK, width)] * len(pieces)
            + [piece_spec(weight, 3 * width, 0) for weight in weights]
            + [whole(1, width)],
            out_specs=[rows(BLK, depth), rows(BLK, 2 * width)]
            + [rows(BLK, width)] * 3
            + [whole(3 * width, depth)],
        ),
        out_shape=[like((count, depth), BF16), like((count, 2 * width), F32)]
        + [like((count, width), BF16)] * 3
        + [like((3 * width, depth), BF16)],
        compiler_params=params(),
        cost_estimate=cost(6 * count * width * depth, count * (4 * depth + 14 * width)),
        name="project",
    )(me, tok, *pieces, *[weight[0] for weight in weights], gain)


def assemble_kernel(tok_ref, *refs):
    place_columns(tok_ref[0], refs[:-1], refs[-1])


def assemble(tok, pieces, count, needs=()):
    width = pieces[0][0].shape[-1]
    depth = width * len(pieces)
    return launch(
        assemble_kernel,
        needs,
        (tok,),
        (count // BLK,),
        [piece_spec(piece, BLK, 1) for piece in pieces],
        (*[piece[0] for piece in pieces],),
        out_specs=rows(BLK, depth),
        out_shape=like((count, depth), BF16),
        cost_estimate=cost(0, 4 * count * depth),
        name="assemble",
    )


def seq_start(place, starts):
    found = jnp.zeros_like(place)
    for start in starts:
        found = jnp.where(place >= start, start, found)
    return found


def later_starts(length_ref, count):
    starts, total = [], jnp.int32(0)
    for position in range(count - 1):
        total = total + length_ref[position]
        starts.append(total)
    return starts


def attend_kernel(count, order, blocks, length_ref, me_ref, pad_ref, q_ref, k_ref, v_ref, *refs):
    mixed_ref, aux_ref, acc_ref = refs
    grid_step = pl.program_id(0)
    step = block_of(order, blocks, grid_step, me_ref)
    first_row = step * BLK
    starts = later_starts(length_ref, count)
    first = seq_start(first_row, starts) // BLK
    lane = lax.broadcasted_iota(jnp.int32, (BLK, 128), 1)
    left = lane < HEAD
    heads = q_ref.shape[1] // HEAD
    zero = jnp.zeros((BLK, 128), BF16)
    one = jnp.ones((BLK, 128), BF16)
    sides = [left if head % 2 == 0 else ~left for head in range(heads)]
    columns = [slice(head // 2 * 128, (head // 2 + 1) * 128) for head in range(heads)]
    queries = [jnp.where(sides[h], q_ref[:, columns[h]], zero) for h in range(heads)]
    acc_ref[...] = jnp.zeros_like(acc_ref)
    row = first_row + lax.broadcasted_iota(jnp.int32, (BLK, 1), 0)
    row_start = seq_start(row, starts)

    def body(block, carry):
        key_rows = pl.ds(pl.multiple_of(block * BLK, BLK), BLK)
        key = block * BLK + lax.broadcasted_iota(jnp.int32, (1, BLK), 1)
        code = jnp.where(pad_ref[:, key_rows] == 1, key, NEVER)
        mask = ((code >= row_start) & (code <= row)) | (key == row)
        for h in range(heads):
            value = jnp.where(sides[h], v_ref[key_rows, columns[h]], one)
            scores = dot_nt(queries[h], k_ref[key_rows, columns[h]])
            powers = jnp.where(mask, jnp.exp2(scores * SCORE), 0.0).astype(BF16)
            acc_ref[h] += dot_nn(powers, value)
        return carry

    lax.fori_loop(first, step + 1, body, 0)
    for pair in range(heads // 2):
        tile = slice(pair * 128, (pair + 1) * 128)
        even, odd = acc_ref[2 * pair], acc_ref[2 * pair + 1]
        total = jnp.where(left, odd, even)
        mixed = jnp.where(left, even, odd)
        mixed_ref[:, tile] = (mixed / pltpu.roll(total, HEAD, 1)).astype(BF16)
        high, low = split_low(jnp.log2(total) * (-1.0 / SCORE))
        aux_ref[:, tile] = jnp.where(lax.rem(lane, HEAD) < HEAD // 2, high, low)


def block_of(order, blocks, grid_step, me_ref):
    offset = order[0] + grid_step // blocks
    return jnp.bitwise_xor(me_ref[0], offset) * blocks + lax.rem(grid_step, blocks)


def piece_rows(blocks, place, width):
    return pl.BlockSpec(
        (BLK, width), lambda i, *_: (jnp.clip(i - place * blocks, 0, blocks - 1), 0)
    )


def attend(lengths, me, order, blocks, pad_row, queries, keys, values, needs=()):
    count, width = queries.shape
    heads = width // HEAD
    return launch(
        functools.partial(attend_kernel, lengths.shape[0], order, blocks),
        needs,
        (lengths, me,),
        (blocks * len(order),),
        [
                whole(1, count),
                pl.BlockSpec(
                    (BLK, width), lambda i, l_ref, me_ref: (block_of(order, blocks, i, me_ref), 0)
                ),
                whole(count, width),
                whole(count, width),
            ],
        (pad_row, queries, keys, values,),
        scratch_shapes=[pltpu.VMEM((heads, BLK, 128), F32)],
        out_specs=[rows(BLK, width)] * 2,
        out_shape=[like((len(order) * blocks * BLK, width), BF16)] * 2,
        cost_estimate=cost(2 * count * count * width, 6 * count * width, count * count * heads // 6),
        name="attend",
    )


def attend_back_kernel(
    count, pieces, length_ref, me_ref, pad_ref, q_ref, k_ref, v_ref, raw_ref, gain_ref, *refs
):
    pairs = pieces // 2
    aux_refs, mixed_refs, delta_refs = (
        refs[:pairs],
        refs[pairs : 2 * pairs],
        refs[2 * pairs : 2 * pairs + pieces],
    )
    low_ref, scale_sum, dqt_ref, do_ref, inner_ref, aux_ref, key_acc, value_acc = refs[
        2 * pairs + pieces :
    ]
    step = pl.program_id(0)
    tokens, width = q_ref.shape
    heads = width // HEAD
    starts = later_starts(length_ref, count)
    lane = lax.broadcasted_iota(jnp.int32, (BLK, 128), 1)
    left = lane < HEAD
    zero = jnp.zeros((BLK, 128), BF16)
    one = jnp.ones((BLK, 128), BF16)
    sides = [left if head % 2 == 0 else ~left for head in range(heads)]
    columns = [slice(head // 2 * 128, (head // 2 + 1) * 128) for head in range(heads)]

    @pl.when(step == 0)
    def prepare():
        dqt_ref[...] = jnp.zeros_like(dqt_ref)
        scale_sum[...] = jnp.zeros_like(scale_sum)
        part = tokens // pieces
        row = lax.broadcasted_iota(jnp.int32, (128, 128), 0)
        column = lax.broadcasted_iota(jnp.int32, (128, 128), 1)
        other = jnp.where(row // HEAD != column // HEAD, 1.0, 0.0).astype(BF16)
        for place in range(pieces):
            first = jnp.bitwise_xor(me_ref[0], place) * part
            do_ref[pl.ds(pl.multiple_of(first, part), part), :] = delta_refs[place][...]
            base = place % 2 * part
            aux_ref[pl.ds(pl.multiple_of(first, part), part), :] = aux_refs[place // 2][
                base : base + part, :
            ]
            for block in range(part // BLK):
                source = slice(block * BLK, (block + 1) * BLK)
                here = pl.ds(pl.multiple_of(first + block * BLK, BLK), BLK)
                for pair in range(heads // 2):
                    tile = slice(pair * 128, (pair + 1) * 128)
                    high, low = split_low(
                        delta_refs[place][source, tile].astype(F32)
                        * mixed_refs[place // 2][
                            base + block * BLK : base + (block + 1) * BLK, tile
                        ].astype(F32)
                    )
                    high, low = split_low(-(dot_nn(high, other) + dot_nn(low, other)))
                    inner_ref[here, tile] = jnp.where(lax.rem(lane, HEAD) < HEAD // 2, high, low)

    key_rows = pl.ds(pl.multiple_of(step * BLK, BLK), BLK)
    last_key = step * BLK + BLK - 1
    end = jnp.int32(tokens)
    for start in reversed(starts):
        end = jnp.where(last_key < start, start, end)
    last = (end - 1) // BLK
    key_acc[...] = jnp.zeros_like(key_acc)
    value_acc[...] = jnp.zeros_like(value_acc)
    turned = jnp.transpose(k_ref[key_rows, :].astype(F32)).astype(BF16)
    keys, values = [], []
    for h in range(heads):
        hot = jnp.where((lax.rem(lane, HEAD // 2) == 0) & (~sides[h]), one, zero)
        for source, into in ((k_ref, keys), (v_ref, values)):
            tile = jnp.where(sides[h], source[key_rows, columns[h]], zero)
            into.append(jnp.concatenate([tile, hot], axis=1))
    key = step * BLK + lax.broadcasted_iota(jnp.int32, (BLK, 1), 0)
    padding = jnp.transpose(
        jnp.broadcast_to(pad_ref[:, key_rows].astype(F32), (128, BLK))
    )[:, :1]
    code = jnp.where(padding > 0.5, key, NEVER)

    def body(block, carry):
        here = pl.ds(pl.multiple_of(block * BLK, BLK), BLK)
        row = block * BLK + lax.broadcasted_iota(jnp.int32, (1, BLK), 1)
        mask = ((code >= seq_start(row, starts)) & (code <= row)) | (key == row)
        for h in range(heads):
            query, delta = q_ref[here, columns[h]], do_ref[here, columns[h]]
            scores = dot_nt(keys[h], jnp.concatenate([query, aux_ref[here, columns[h]]], axis=1))
            delta_probs = dot_nt(
                values[h], jnp.concatenate([delta, inner_ref[here, columns[h]]], axis=1)
            )
            probs = jnp.where(mask, jnp.exp2(scores * SCORE), 0.0)
            delta_scores = (probs * delta_probs).astype(BF16)
            value_acc[h] += dot_nn(probs.astype(BF16), delta)
            key_acc[h] += dot_nn(delta_scores, query)
            head_rows = slice(h * HEAD, (h + 1) * HEAD)
            dqt_ref[head_rows, here] += dot_nn(turned[head_rows, :], delta_scores)
        return carry

    lax.fori_loop(step, last + 1, body, 0)
    key_tiles, value_tiles = [
        [jnp.where(left, acc[2 * pair], acc[2 * pair + 1]) for pair in range(heads // 2)]
        for acc in (key_acc, value_acc)
    ]
    ones = head_matrix(width)
    gain = gain_ref[...]
    deltas = (jnp.transpose(dqt_ref[:, key_rows]), jnp.concatenate(key_tiles, axis=1))
    for place, delta in enumerate(deltas):
        here = slice(place * width, (place + 1) * width)
        raw = raw_ref[:, here]
        factor = lax.rsqrt(head_mean(raw * raw, ones) + EPSILON)
        unit = raw * factor
        delta = delta * HEAD**-0.5
        scale_sum[...] += jnp.sum(delta * unit, axis=0, keepdims=True)
        delta = gain * delta
        low_ref[:, here] = (factor * (delta - unit * head_mean(delta * unit, ones))).astype(BF16)
    low_ref[:, 2 * width :] = jnp.concatenate(value_tiles, axis=1).astype(BF16)


def attend_back(lengths, me, pad_row, queries, keys, values, raw, gain, aux_pieces, mixed_pieces, delta_pieces):
    count, width = queries.shape
    heads = width // HEAD
    pieces = len(delta_pieces)
    return pl.pallas_call(
        functools.partial(attend_back_kernel, lengths.shape[0], pieces),
        grid_spec=pltpu.PrefetchScalarGridSpec(
            num_scalar_prefetch=2,
            grid=(count // BLK,),
            in_specs=[whole(1, count)]
            + [whole(count, width)] * 3
            + [rows(BLK, 2 * width), whole(1, width)]
            + [whole(2 * count // pieces, width)] * pieces
            + [piece_spec((array, lead, 0), count // pieces, 0) for array, lead in delta_pieces],
            out_specs=[rows(BLK, 3 * width), whole(1, width)],
            scratch_shapes=[
                pltpu.VMEM((width, count), F32),
                pltpu.VMEM((count, width), BF16),
                pltpu.VMEM((count, width), BF16),
                pltpu.VMEM((count, width), BF16),
                pltpu.VMEM((heads, BLK, 128), F32),
                pltpu.VMEM((heads, BLK, 128), F32),
            ],
        ),
        out_shape=[like((count, 3 * width), BF16), like((1, width), F32)],
        compiler_params=params(),
        cost_estimate=cost(8 * count * count * width, 22 * count * width, count * count * heads // 3),
        name="attend_back",
    )(lengths, me, pad_row, queries, keys, values, raw, gain, *aux_pieces, *mixed_pieces, *[array for array, lead in delta_pieces])


def unit_of(values):
    factor = lax.rsqrt(jnp.mean(values * values, axis=1, keepdims=True) + EPSILON)
    return values * factor, factor


def unit_back(delta, unit, factor):
    return factor * (delta - unit * jnp.mean(delta * unit, axis=1, keepdims=True))


def mixer_kernel(pieces, *refs):
    mixed_refs, out_weights = refs[:pieces], refs[pieces : 2 * pieces]
    tokens_ref, alpha_ref, *low_refs, one_ref, unit_ref, unit_factor, one_factor = refs[2 * pieces :]
    branch = dot_nn(mixed_refs[0][...], out_weights[0][...])
    for mixed, weight in zip(mixed_refs[1:], out_weights[1:]):
        branch += dot_nn(mixed[...], weight[...])
    unit, factor = unit_of(branch * SCALE_MODEL)
    unit_ref[...] = unit
    unit_factor[...] = jnp.broadcast_to(factor, unit_factor.shape)
    residual = tokens_ref[...].astype(F32)
    hidden, factor = unit_of(residual + alpha_ref[...] * (unit - residual))
    one_ref[...] = hidden
    one_factor[...] = jnp.broadcast_to(factor, one_factor.shape)
    put(1, hidden.astype(BF16), *low_refs)


def mixer(mixed_pieces, out_weights, me, tokens_all, alpha):
    width = mixed_pieces[0][0].shape[-1]
    pieces = len(mixed_pieces)
    count = tokens_all.shape[0] // pieces
    depth = tokens_all.shape[1]
    blocks = count // BLK
    kernel = functools.partial(mixer_kernel, pieces)
    return pl.pallas_call(
        lambda me_ref, *refs: kernel(*refs),
        grid_spec=pltpu.PrefetchScalarGridSpec(
            num_scalar_prefetch=1,
            grid=(blocks,),
            in_specs=[piece_spec((array, lead, 0), BLK, 1) for array, lead in mixed_pieces]
            + [piece_spec((array, lead, 0), width, 0) for array, lead in out_weights]
            + [
                pl.BlockSpec((BLK, depth), lambda i, me_ref: (me_ref[0] * blocks + i, 0)),
                whole(1, depth),
            ],
            out_specs=[piece_rows(1, 0, depth), piece_rows(1, 1, depth)]
            + [rows(BLK, depth)] * 2
            + [rows(BLK, 128)] * 2,
        ),
        out_shape=[like((BLK, depth), BF16)] * 2
        + [like((count, depth), F32)] * 2
        + [like((count, 128), F32)] * 2,
        compiler_params=params(),
        cost_estimate=cost(2 * count * depth * depth, 16 * count * depth + 2 * depth * depth),
        name="mixer",
    )(me, *[p[0] for p in mixed_pieces], *[w[0] for w in out_weights], tokens_all, alpha)


def turn_kernel(pieces, carried, me_ref, *refs):
    own_ref, near_ref, far_ref, one_ref = refs[:4]
    seed_refs = refs[4 : 4 + pieces]
    pad_ref, alpha_ref = refs[4 + pieces : 6 + pieces]
    outs = refs[6 + pieces + carried :]
    pair_refs = outs[: pieces // 2]
    hidden_ref, low_ref, alpha_sum, seed, layer = outs[pieces // 2 :]
    width = seed_refs[0].shape[-1]
    starts = [
        pl.multiple_of(jnp.bitwise_xor(me_ref[0], place) * width, width) for place in range(pieces)
    ]
    for start, piece in zip(starts, seed_refs):
        seed[:, pl.ds(start, width)] = piece[...]
    branch = (own_ref[...].astype(F32) + near_ref[...].astype(F32)) + far_ref[...].astype(F32)
    unit, unit_factor = unit_of(branch)
    hidden = one_ref[...]
    alpha = alpha_ref[...]
    layer_rows, layer_factor = unit_of(hidden + alpha * (unit - hidden))
    layer[...] = layer_rows.astype(BF16)
    for offset, start in enumerate(starts):
        pair_refs[offset // 2][offset % 2] = layer[:, pl.ds(start, width)]
    delta = unit_back(seed[...].astype(F32) * pad_ref[...], layer_rows, layer_factor)
    alpha_sum[...] = jnp.sum(delta * (unit - hidden), axis=0, keepdims=True)
    hidden_ref[...] = (1.0 - alpha) * delta
    low_ref[...] = unit_back(alpha * delta, unit, unit_factor).astype(BF16)


def turn(me, half, own, near, far, hidden_one, seed_pieces, pad_rows, alpha, carry=()):
    count, depth = hidden_one.shape
    pieces = len(seed_pieces)
    width = depth // pieces
    here = pl.BlockSpec((BLK, depth), lambda i, *_: (half, 0))
    pair = pl.BlockSpec((2, BLK, width), lambda i, *_: (0, half, 0))
    return pl.pallas_call(
        functools.partial(turn_kernel, pieces, len(carry)),
        grid_spec=pltpu.PrefetchScalarGridSpec(
            num_scalar_prefetch=1,
            grid=(1,),
            in_specs=[whole(BLK, depth)] * 3
            + [here]
            + [piece_spec((array, lead, half), BLK, 0) for array, lead in seed_pieces]
            + [pl.BlockSpec((BLK, 1), lambda i, *_: (half, 0)), whole(1, depth)]
            + [pl.BlockSpec(memory_space=pl.ANY)] * len(carry),
            out_specs=[pair] * (pieces // 2) + [here, whole(BLK, depth), whole(1, depth)],
            scratch_shapes=[pltpu.VMEM((BLK, depth), BF16)] * 2,
        ),
        out_shape=[like((2, count, width), BF16)] * (pieces // 2)
        + [like((count, depth), F32), like((BLK, depth), BF16), like((1, depth), F32)],
        input_output_aliases={7 + pieces + k: k for k in range(len(carry))},
        compiler_params=params(),
        cost_estimate=cost(40 * count * depth, 20 * count * depth),
        name="turn",
    )(
        me, own, near, far, hidden_one, *[p[0] for p in seed_pieces], pad_rows, alpha, *carry
    )


def mixer_back_kernel(pieces, *refs):
    halves, (hidden_ref, one_ref, unit_ref) = (refs[:6:2], refs[1:6:2]), refs[6:9]
    one_factor, unit_factor, tokens_ref, alpha_ref = refs[9:13]
    out_weights = refs[13 : 13 + pieces]
    pair_refs = refs[13 + pieces : 13 + pieces + pieces // 2]
    low_ref, direct_ref, alpha_sum = refs[13 + pieces + pieces // 2 :]
    own, near, far = [
        jnp.where(pl.program_id(0) < pl.num_programs(0) // 2, first[...].astype(F32), second[...].astype(F32))
        for first, second in zip(*halves)
    ]

    @pl.when(pl.program_id(0) == 0)
    def clear():
        alpha_sum[...] = jnp.zeros_like(alpha_sum)

    delta = hidden_ref[...] + ((own + near) + far)
    unit = unit_ref[...]
    alpha = alpha_ref[...]
    delta = unit_back(delta, one_ref[...], one_factor[:, :1])
    alpha_sum[...] += jnp.sum(delta * (unit - tokens_ref[...].astype(F32)), axis=0, keepdims=True)
    direct_ref[...] = (1.0 - alpha) * delta
    low = unit_back(alpha * delta, unit, unit_factor[:, :1]).astype(BF16)
    low_ref[...] = low
    for offset, weight in enumerate(out_weights):
        pair_refs[offset // 2][offset % 2] = (dot_nt(low, weight[...]) * SCALE_MODEL).astype(BF16)


def mixer_back(
    me, sums, hidden, one, unit, one_factor, unit_factor, tokens_all, alpha, out_weights
):
    count, depth = one.shape
    pieces = len(out_weights)
    width = depth // pieces
    block = BLK
    blocks = count // block
    half = blocks // 2
    kernel = functools.partial(mixer_back_kernel, pieces)
    return pl.pallas_call(
        lambda me_ref, *refs: kernel(*refs),
        grid_spec=pltpu.PrefetchScalarGridSpec(
            num_scalar_prefetch=1,
            grid=(blocks,),
            in_specs=[
                pl.BlockSpec((block, depth), lambda i, *_: (jnp.minimum(i, half - 1), 0)),
                pl.BlockSpec((block, depth), lambda i, *_: (jnp.maximum(i - half, 0), 0)),
            ]
            * 3
            + [rows(block, depth)] * 3
            + [rows(block, 128)] * 2
            + [
                pl.BlockSpec((block, depth), lambda i, me_ref: (me_ref[0] * blocks + i, 0)),
                whole(1, depth),
            ]
            + [piece_spec((array, lead, 0), width, 0) for array, lead in out_weights],
            out_specs=[pl.BlockSpec((2, block, width), lambda i, *_: (0, i, 0))] * (pieces // 2)
            + [rows(block, depth), rows(block, depth), whole(1, depth)],
        ),
        out_shape=[like((2, count, width), BF16)] * (pieces // 2)
        + [like((count, depth), BF16), like((count, depth), F32), like((1, depth), F32)],
        compiler_params=params(),
        cost_estimate=cost(2 * count * depth * depth, 28 * count * depth + 2 * depth * depth),
        name="mixer_back",
    )(
        me,
        *[value for pair in zip(sums[:3], sums[3:]) for value in pair],
        hidden,
        one,
        unit,
        one_factor,
        unit_factor,
        tokens_all,
        alpha,
        *[w[0] for w in out_weights],
    )


def pick(half, first_ref, second_ref, out_ref):
    step = pl.program_id(0)

    @pl.when(step < half)
    def from_first():
        out_ref[...] = first_ref[...]

    @pl.when(step >= half)
    def from_second():
        out_ref[...] = second_ref[...]


def put(half, value, first_ref, second_ref):
    step = pl.program_id(0)

    @pl.when(step < half)
    def to_first():
        first_ref[...] = value

    @pl.when(step >= half)
    def to_second():
        second_ref[...] = value


def whole_weight(tok_ref, piece_refs, out_ref):
    if out_ref is None:
        return piece_refs[0]

    @pl.when(pl.program_id(0) == 0)
    def assemble_weight():
        place_columns(tok_ref[0], piece_refs, out_ref)

    return out_ref


def expand_kernel(count, pieces, tok_ref, *refs):
    block_refs, gain_ref, refs = refs[:count], refs[count], refs[count + 1 :]
    up_pieces, gate_pieces = refs[:pieces], refs[pieces : 2 * pieces]
    up_ref, gate_ref, mid_ref = refs[2 * pieces : 2 * pieces + 3]
    hidden_ref = refs[-1]
    outs = refs[2 * pieces + 3 : -1] or (None, None)
    up_w = whole_weight(tok_ref, up_pieces, outs[0])
    gate_w = whole_weight(tok_ref, gate_pieces, outs[1])
    for place, block_ref in enumerate(block_refs):

        @pl.when(pl.program_id(0) == place)
        def take(block_ref=block_ref):
            hidden_ref[...] = block_ref[...]

    hidden = hidden_ref[...]
    up = dot_nt(hidden, up_w[...]) * SCALE_MODEL
    gate = dot_nt(hidden, gate_w[...]) * SCALE_MODEL
    up_ref[...] = up.astype(BF16)
    gate_ref[...] = gate.astype(BF16)
    scaled = gain_ref[1:2, :] * gate
    mid_ref[...] = (gain_ref[0:1, :] * up * scaled * jax.nn.sigmoid(scaled)).astype(BF16)


def expand(tok, blocks_in, up_pieces, gate_pieces, gains):
    depth = blocks_in[0].shape[1]
    hidden = gains.shape[1]
    count = len(blocks_in)
    pieces = len(up_pieces)
    outs = 2 if pieces > 1 else 0
    return pl.pallas_call(
        functools.partial(expand_kernel, count, pieces),
        grid_spec=pltpu.PrefetchScalarGridSpec(
            num_scalar_prefetch=1,
            grid=(count,),
            in_specs=[whole(BLK, depth)] * count
            + [whole(2, hidden)]
            + [piece_spec(piece, hidden, 0) for piece in (*up_pieces, *gate_pieces)],
            out_specs=[rows(BLK, hidden)] * 3 + [whole(hidden, depth)] * outs,
            scratch_shapes=[pltpu.VMEM((BLK, depth), BF16)],
        ),
        out_shape=[like((count * BLK, hidden), BF16)] * 3 + [like((hidden, depth), BF16)] * outs,
        compiler_params=params(),
        cost_estimate=cost(4 * count * BLK * depth * hidden, 4 * depth * hidden),
        name="expand",
    )(tok, *blocks_in, gains, *[piece[0] for piece in (*up_pieces, *gate_pieces)])


def contract_kernel(pieces, tok_ref, mid_ref, *refs):
    first_ref, second_ref = refs[pieces : pieces + 2]
    outs = refs[pieces + 2 :] or (None,)
    down_w = whole_weight(tok_ref, refs[:pieces], outs[0])
    total = (dot_nn(mid_ref[...], down_w[...]) * SCALE_HIDDEN).astype(BF16)
    first_ref[...] = total[:BLK]
    second_ref[...] = total[BLK:]


def contract(tok, middle, first_block, down_pieces, depth, needs=()):
    hidden = middle.shape[1]
    count = 2 * BLK
    pieces = len(down_pieces)
    outs = 1 if pieces > 1 else 0
    return launch(
        functools.partial(contract_kernel, pieces),
        needs,
        (tok,),
        (1,),
        [pl.BlockSpec((2 * BLK, hidden), lambda i, *_: (first_block // 2, 0))] + [piece_spec(piece, hidden, 0) for piece in down_pieces],
        (middle, *[piece[0] for piece in down_pieces],),
        out_specs=[whole(BLK, depth), whole(BLK, depth)]
            + [whole(hidden, depth)] * outs,
        out_shape=[like((count // 2, depth), BF16)] * 2 + [like((hidden, depth), BF16)] * outs,
        cost_estimate=cost(
            2 * count * depth * hidden, 2 * count * (depth + hidden) + 2 * depth * hidden
        ),
        name="contract",
    )


def gated_back_kernel(
    up_from,
    gate_from,
    down_from,
    first_ref,
    second_ref,
    up_ref,
    gate_ref,
    gain_ref,
    both_ref,
    first_out,
    second_out,
    unit_ref,
    delta_ref,
    down_w,
    up_w,
    gate_w,
    arrived,
):
    copies = [
        pltpu.make_async_copy(source, into, arrived.at[k])
        for k, (source, into) in enumerate(
            ((down_from, down_w), (up_from, up_w), (gate_from, gate_w))
        )
    ]
    for copy in copies:
        copy.start()
    count = first_ref.shape[0]
    delta_ref[:count, :] = first_ref[...]
    delta_ref[count:, :] = second_ref[...]
    copies[0].wait()
    hidden = up_w.shape[0]
    part = hidden // 2
    total = None
    for start in range(0, hidden, part):
        here = slice(start, start + part)
        delta_middle = dot_nt(delta_ref[...], down_w[here, :]) * SCALE_HIDDEN
        up = up_ref[:, here].astype(F32)
        gate = gate_ref[:, here].astype(F32)
        scaled = gain_ref[1:2, here] * gate
        sigmoid = jax.nn.sigmoid(scaled)
        shared = delta_middle * sigmoid
        delta_up = shared * scaled
        delta_gate = shared * (gain_ref[0:1, here] * up) * (1.0 + scaled * (1.0 - sigmoid))
        unit_ref[0:1, here] = jnp.sum(delta_up * up, axis=0, keepdims=True)
        unit_ref[1:2, here] = jnp.sum(delta_gate * gate, axis=0, keepdims=True)
        up_low = (gain_ref[0:1, here] * delta_up).astype(BF16)
        gate_low = (gain_ref[1:2, here] * delta_gate).astype(BF16)
        both_ref[:, here] = up_low
        both_ref[:, hidden + start : hidden + start + part] = gate_low
        if start == 0:
            copies[1].wait()
            copies[2].wait()
        term = dot_nn(up_low, up_w[here, :]) + dot_nn(gate_low, gate_w[here, :])
        total = term if total is None else total + term
    total = total * SCALE_MODEL
    first_out[...] = total[:count].astype(BF16)
    second_out[...] = total[count:].astype(BF16)


def gated_back(first, second, up, gate, first_block, up_w, gate_w, down_w, gains):
    count, depth = first.shape
    hidden = up_w.shape[0]
    here = pl.BlockSpec((2 * count, hidden), lambda i: (first_block * BLK // (2 * count), 0))
    return pl.pallas_call(
        gated_back_kernel,
        grid=(1,),
        in_specs=[pl.BlockSpec(memory_space=pl.ANY)] * 3
        + [whole(count, depth)] * 2
        + [here, here, whole(2, hidden)],
        out_specs=[whole(2 * count, 2 * hidden)] + [whole(count, depth)] * 2 + [whole(2, hidden)],
        scratch_shapes=[pltpu.VMEM((2 * count, depth), BF16)]
        + [pltpu.VMEM((hidden, depth), BF16)] * 3
        + [pltpu.SemaphoreType.DMA((3,))],
        out_shape=[like((2 * count, 2 * hidden), BF16)]
        + [like((count, depth), BF16)] * 2
        + [like((2, hidden), F32)],
        compiler_params=params(),
        cost_estimate=cost(
            12 * count * depth * hidden,
            8 * count * (depth + hidden) + 6 * depth * hidden,
            2 * count * hidden,
        ),
        name="gated_back",
    )(up_w, gate_w, down_w, first, second, up, gate, gains)


def part_columns(tok_ref, total, part_refs):
    width = part_refs[0].shape[2]
    in_halves = len(part_refs) == 6
    for offset in range(8):
        start = pl.multiple_of(jnp.bitwise_xor(tok_ref[0], offset) * width, width)
        value = total[:, pl.ds(start, width)].astype(BF16)
        sent, odd, lead = offset % 2, offset // 2 % 2, offset // 4
        if not in_halves:
            part_refs[2 * sent + odd][lead] = value
        elif not odd:
            part_refs[3 * sent][lead] = value
        else:
            half = pl.num_programs(0) // 2

            @pl.when(pl.program_id(0) < half)
            def first_half(value=value, into=part_refs[3 * sent + 1], lead=lead):
                into[lead] = value

            @pl.when(pl.program_id(0) >= half)
            def second_half(value=value, into=part_refs[3 * sent + 2], lead=lead):
                into[lead] = value


def weight_grad_kernel(lefts, rights, scale, steps, outs, tok_ref, *refs):
    left_refs, right_refs = refs[:lefts], refs[lefts : lefts + rights]
    fold_refs, part_refs = refs[lefts + rights : -outs - 1], refs[-outs - 1 : -1]
    total = refs[-1]

    @pl.when(pl.program_id(0) < steps)
    def product():
        acc, lefts_in = None, []
        for ref in left_refs:
            count = right_refs[0].shape[0]
            lefts_in += [ref[k * count : (k + 1) * count, :] for k in range(ref.shape[0] // count)]
        for left, right in zip(lefts_in, right_refs):
            term = lax.dot_general(
                left, right[...], (((0,), (0,)), ((), ())), preferred_element_type=F32
            )
            acc = term if acc is None else acc + term
        total[...] = acc * scale

    if fold_refs:

        @pl.when(pl.program_id(0) >= steps)
        def fold():
            own, near, far = [ref[...].astype(F32) for ref in fold_refs]
            total[...] = (own + near) + far

    part_columns(tok_ref, total, part_refs)


def weight_grad(tok, groups, lefts, rights, scale, folds=(), halves=False, needs=()):
    height = lefts[0].shape[1]
    depth = rights[0].shape[1]
    count = sum(left.shape[0] for left in lefts)
    part = depth // groups
    steps = height // BLK
    out = pl.BlockSpec((groups // 4, BLK, part), lambda i, *_: (0, i, 0))
    total_height = height + (BLK if folds else 0)
    outs, heights = [out] * 4, [total_height] * 4
    if halves:
        half = steps // 2
        odd = [
            pl.BlockSpec((groups // 4, BLK, part), lambda i, *_: (0, jnp.minimum(i, half - 1), 0)),
            pl.BlockSpec((groups // 4, BLK, part), lambda i, *_: (0, jnp.maximum(i - half, 0), 0)),
        ]
        outs = [out, *odd] * 2
        heights = [height, height // 2, height // 2] * 2
    return launch(
        functools.partial(
            weight_grad_kernel, len(lefts), len(rights), scale, steps, len(outs)
        ),
        needs,
        (tok,),
        (total_height // BLK,),
        [
                pl.BlockSpec((left.shape[0], BLK), lambda i, *_: (0, jnp.minimum(i, steps - 1)))
                for left in lefts
            ]
            + [whole(*right.shape) for right in rights]
            + [piece_spec((array, lead, 0), BLK, 0) for array, lead in folds],
        (*lefts, *rights, *[array for array, lead in folds],),
        scratch_shapes=[pltpu.VMEM((BLK, depth), F32)],
        out_specs=outs,
        out_shape=[like((groups // 4, tall, part), BF16) for tall in heights],
        cost_estimate=cost(
            2 * count * height * depth, 2 * count * (height + depth) + 2 * height * depth
        ),
        name="weight_grad",
    )


def out_grad_kernel(pieces, *refs):
    right, pair_refs = refs[pieces], refs[pieces + 1 :]
    for offset, left in enumerate(refs[:pieces]):
        total = lax.dot_general(
            left[...], right[...], (((0,), (0,)), ((), ())), preferred_element_type=F32
        )
        pair_refs[offset // 2][offset % 2] = (total * SCALE_MODEL).astype(BF16)


def out_grad(lefts, right):
    width = lefts[0][0].shape[-1]
    count, depth = right.shape
    pieces = len(lefts)
    return pl.pallas_call(
        functools.partial(out_grad_kernel, pieces),
        grid=(1,),
        in_specs=[piece_spec((array, lead, 0), count, 0) for array, lead in lefts]
        + [whole(count, depth)],
        out_specs=[whole(2, width, depth)] * (pieces // 2),
        out_shape=[like((2, width, depth), BF16)] * (pieces // 2),
        compiler_params=params(),
        cost_estimate=cost(2 * count * depth * depth, 4 * count * depth + 2 * depth * depth),
        name="out_grad",
    )(*[p[0] for p in lefts], right)


def project_back_kernel(pieces, me_ref, low_ref, w_ref, direct_ref, *refs):
    part_refs, total = refs[:pieces], refs[pieces]
    step = pl.program_id(0)
    total[...] = dot_nn(low_ref[...], w_ref[...]) * SCALE_MODEL
    own_blocks = direct_ref.shape[0] // BLK

    @pl.when(step // own_blocks == me_ref[0])
    def add_direct():
        start = pl.multiple_of(lax.rem(step, own_blocks) * BLK, BLK)
        total[...] += direct_ref[pl.ds(start, BLK), :]

    part = total.shape[1] // pieces
    for place, out in enumerate(part_refs):
        start = pl.multiple_of(jnp.bitwise_xor(me_ref[0], place) * part, part)
        out[...] = total[:, pl.ds(start, part)].astype(BF16)


def project_back(me, pieces, low, weight, direct, needs=()):
    count = low.shape[0]
    depth = weight.shape[1]
    part = depth // pieces
    return launch(
        functools.partial(project_back_kernel, pieces),
        needs,
        (me,),
        (count // BLK,),
        [rows(BLK, low.shape[1]), whole(*weight.shape), whole(*direct.shape)],
        (low, weight, direct),
        scratch_shapes=[pltpu.VMEM((BLK, depth), F32)],
        out_specs=[rows(BLK, part)] * pieces,
        out_shape=[like((count, part), BF16)] * pieces,
        cost_estimate=cost(2 * count * low.shape[1] * depth, 2 * count * depth),
        name="project_back",
    )


def trade(value, axis, offset):
    size = lax.axis_size(axis)
    return lax.ppermute(value, axis, [(i, i ^ offset) for i in range(size)])


def sum_four(value, axis, first, second):
    one, two, three = [trade(value, axis, o) for o in (first, second, first ^ second)]
    return (value + one) + (two + three)


def sum_over(value, axis):
    if lax.axis_size(axis) == 4:
        return sum_four(value, axis, 1, 2)
    if lax.axis_size(axis) == 8:
        return sum_four(value + trade(value, axis, 1), axis, 2, 4)
    offset = 1
    while offset < lax.axis_size(axis):
        value = value + trade(value, axis, offset)
        offset *= 2
    return value


def join(*values):
    return lax.optimization_barrier(values)


def stack(*values):
    return jnp.concatenate([v if v.ndim == 3 else v[None] for v in values], axis=0)


def add_low(*values):
    total = values[0].astype(F32)
    for value in values[1:]:
        total = total + value.astype(F32)
    return total


def plain_sum(left, right, scale):
    total = jnp.einsum("tr,td->rd", left, right, preferred_element_type=F32) * scale
    return lax.psum_scatter(total.astype(BF16), "tok", scatter_dimension=1, tiled=True).astype(F32)


def moment_update(weights, gradient, moment, square, fix_first, fix_second):
    moment_next = BETA_ONE * moment + (1.0 - BETA_ONE) * gradient
    square_next = BETA_TWO * square + (1.0 - BETA_TWO) * gradient * gradient
    stepped = weights - LEARN_RATE * (moment_next / fix_first) / (
        jnp.sqrt(square_next / fix_second) + ADAM_EPSILON
    )
    return (stepped, moment_next, square_next)


def local(
    inputs,
    cotangent,
    lengths,
    pad_mask,
    attention_weights,
    gated_weights,
    model_gains,
    unit_gains,
    attention_moment,
    attention_square,
    gated_moment,
    gated_square,
    model_moment,
    model_square,
    unit_moment,
    unit_square,
):
    token_count, width = inputs.shape
    parts = lax.axis_size("dim")
    hidden_here = gated_weights.shape[1]
    own_count = token_count // parts
    place = lax.axis_index("dim")
    me = place.astype(jnp.int32).reshape(1)
    tok = lax.axis_index("tok").astype(jnp.int32).reshape(1)
    groups = lax.axis_size("tok")
    by_pieces = groups == 8 and (D // groups) % 128 == 0
    blocks = own_count // BLK
    length_row = lengths[0]

    def token_rows(value, offset):
        return lax.dynamic_slice_in_dim(value, (place ^ offset) * own_count, own_count, 0)

    ao = attention_weights.reshape(4 * width, -1).astype(BF16)
    gated_low = gated_weights.reshape(3 * hidden_here, -1).astype(BF16)
    both_own = gated_weights[:2].reshape(2 * hidden_here, -1).astype(BF16)
    down_own = gated_weights[2].astype(BF16)
    score_gain = model_gains[:1]
    pad_row = pad_mask[None, :]
    pad_rows = token_rows(pad_mask, 0).astype(F32)[:, None]

    x_far = trade(inputs, "dim", 2)
    seed_rows = [token_rows(cotangent, r) for r in range(parts)]
    seed_send = stack(*seed_rows[2:])
    alphas = lax.dynamic_update_slice(
        jnp.zeros((2, D), F32), model_gains[1:], (0, place * width)
    )
    alpha_near = trade(alphas, "dim", 1)
    if by_pieces:
        ao_by = {0: ao, 4: trade(ao, "tok", 4), 2: trade(ao, "tok", 2), 1: trade(ao, "tok", 1)}
        ao_by[6] = trade(ao_by[4], "tok", 2)
        ao_by[5] = trade(ao_by[4], "tok", 1)
        ao_by[3] = trade(ao_by[2], "tok", 1)
        x_far, ao_by, both_own, seed_send, alphas, alpha_near = join(
            x_far, ao_by, both_own, seed_send, alphas, alpha_near
        )
        ao_by[7] = trade(ao_by[6], "tok", 1)
        by = {0: both_own, 2: trade(both_own, "tok", 2), 4: trade(both_own, "tok", 4)}
    else:
        gather = functools.partial(lax.all_gather, axis_name="tok", axis=1, tiled=True)
        in_pieces = [(gather(ao[: 3 * width]), None, 0)]
        out_weight, up_w, gate_w, down_w = [
            gather(shard)
            for shard in (ao[3 * width :], both_own[:hidden_here], both_own[hidden_here:], down_own)
        ]
        up_pieces, gate_pieces, down_pieces = [[(w, None, 0)] for w in (up_w, gate_w, down_w)]
    x_near = trade(inputs, "dim", 1)
    x_corner = trade(x_far, "dim", 1)
    token_pieces = [inputs, x_near, x_far, x_corner]
    if by_pieces:
        token_pieces, ao_by, gated_low, down_own, seed_send, alphas = join(
            token_pieces, ao_by, gated_low, down_own, seed_send, alphas
        )
        in_pieces = [(ao_by[offset], None, 0) for offset in range(8)]
        by[1] = trade(gated_low, "tok", 1)
    seed_far = trade(seed_send, "dim", 2)
    tokens_all, raw, queries, keys, values, weight_in = project(
        me, tok, token_pieces, in_pieces, score_gain
    )
    queries, seed_far = join(queries, seed_far)

    queries, seed_far, alpha_near = join(queries, seed_far, alpha_near)
    alphas = alphas + alpha_near
    alpha_far = trade(alphas, "dim", 2)
    if by_pieces:
        queries, ao_by = join(queries, ao_by)
        out_weight = assemble(
            tok, [(ao_by[o], None, 3 * width // BLK) for o in range(8)], width, (queries,)
        )
        out_weight, by[1], by[2], by[4], down_own = join(
            out_weight, by[1], by[2], by[4], down_own
        )
        by[3] = trade(by[2], "tok", 1)
        by[6] = trade(by[4], "tok", 2)
    out_across = trade(out_weight, "dim", 2)
    far_mixed, far_aux = attend(
        length_row, me, (2, 3), blocks, pad_row, queries, keys, values, (out_weight,)
    )
    far_mixed, alpha_far, out_across = join(far_mixed, alpha_far, out_across)
    alphas = alphas + alpha_far
    alpha_mixer, alpha_gated = alphas[:1], alphas[1:]
    if by_pieces:
        far_mixed, by[3], by[6], down_own = join(far_mixed, by[3], by[6], down_own)
        by[5] = trade(by[4], "tok", 1)
        down_by = {0: down_own, 2: trade(down_own, "tok", 2), 4: trade(down_own, "tok", 4)}
    far_came = trade(far_mixed, "dim", 2)
    out_pair = trade(stack(out_weight, out_across), "dim", 1)
    near_mixed, near_aux = attend(
        length_row, me, (0, 1), blocks, pad_row, queries, keys, values, (far_mixed,)
    )
    near_mixed, far_came, out_pair = join(near_mixed, far_came, out_pair)
    if by_pieces:
        near_mixed, by[5], by[6], down_by = join(near_mixed, by[5], by[6], down_by)
    pair_came = trade(stack(near_mixed[own_count:], far_came[own_count:]), "dim", 1)
    out_weights = [(out_weight, None), (out_pair, 0), (out_across, None), (out_pair, 1)]
    mixed_pieces = [(near_mixed, None), (pair_came, 0), (far_came, None), (pair_came, 1)]
    low_a, low_b, hidden_one, mixer_unit, mixer_factor, one_factor = mixer(
        mixed_pieces, out_weights, me, tokens_all, alpha_mixer
    )

    far_a = trade(low_a, "dim", 2)
    near_a = trade(low_a, "dim", 1)
    near_b = trade(low_b, "dim", 1)
    if by_pieces:
        near_a, near_b, by[6], down_by = join(near_a, near_b, by[6], down_by)
        by[7] = trade(by[6], "tok", 1)
        down_by[1] = by[1]
        down_by[6] = trade(down_by[4], "tok", 2)
        near_a, far_a, by[7], down_by = join(near_a, far_a, by[7], down_by)
        down_by[3] = trade(down_by[2], "tok", 1)
        down_by[5] = trade(down_by[4], "tok", 1)
        up_pieces, gate_pieces = [[(by[o], None, k) for o in range(8)] for k in range(2)]
    near_a, far_a, low_b = join(near_a, far_a, low_b)
    far_b = trade(low_b, "dim", 2)
    corner_a = trade(far_a, "dim", 1)
    up_one, gate_one, mid_one, *assembled = expand(
        tok, [low_a, near_a, low_b, near_b], up_pieces, gate_pieces, unit_gains
    )
    if by_pieces:
        up_w, gate_w = assembled
        up_pieces, gate_pieces = [(up_w, None, 0)], [(gate_w, None, 0)]
        mid_one, down_by, corner_a = join(mid_one, down_by, corner_a)
        down_by[7] = trade(down_by[6], "tok", 1)
    seed_pair = trade(stack(seed_rows[1], seed_far[1]), "dim", 1)
    seed_pieces = [(seed_rows[0], None), (seed_pair, 0), (seed_far, 0), (seed_pair, 1)]
    up_a, gate_a, mid_a = expand(tok, [far_a, corner_a], up_pieces, gate_pieces, unit_gains)
    mid_a, far_b, seed_pair = join(mid_a, far_b, seed_pair)
    seed_pieces = [(seed_rows[0], None), (seed_pair, 0), (seed_far, 0), (seed_pair, 1)]
    corner_b = trade(far_b, "dim", 1)
    if by_pieces:
        mid_a, down_by = join(mid_a, down_by)
        down_pieces = [(down_by[o], None, 2 if o == 1 else 0) for o in range(8)]
        *parts_a, down_w = contract(tok, mid_a, 0, down_pieces, D)
        down_pieces = [(down_w, None, 0)]
    else:
        parts_a = contract(tok, mid_a, 0, down_pieces, D)
    came = trade(parts_a[1], "dim", 1)
    up_b, gate_b, mid_b = expand(tok, [far_b, corner_b], up_pieces, gate_pieces, unit_gains)
    mid_b, came = join(mid_b, came)
    across = add_low(parts_a[0], came).astype(BF16)
    across_a = trade(across, "dim", 2)
    parts_b = contract(tok, mid_b, 0, down_pieces, D, (across,))
    came = trade(parts_b[1], "dim", 1)
    own_a, pair_a = contract(tok, mid_one, 0, down_pieces, D, (parts_b[0],))
    own_a, came, parts_b, pair_a, across_a = join(own_a, came, parts_b, pair_a, across_a)
    across = add_low(parts_b[0], came).astype(BF16)
    across_b = trade(across, "dim", 2)
    pair_a = trade(pair_a, "dim", 1)
    own_b, pair_b = contract(tok, mid_one, 2, down_pieces, D, (own_a, across))
    own_b, pair_b, pair_a = join(own_b, pair_b, pair_a)
    *carry, delta_a, sum_a = turn(
        me, 0, own_a, pair_a, across_a, hidden_one, seed_pieces, pad_rows, alpha_gated
    )
    pair_b = trade(pair_b, "dim", 1)
    delta_a, across_b, pair_b, carry = join(delta_a, across_b, pair_b, carry)

    back_weights = (up_w, gate_w, down_w, unit_gains)
    b_far_a = trade(delta_a, "dim", 2)
    b_near_a = trade(delta_a, "dim", 1)
    layer_near, layer_far, delta_hidden, delta_b, sum_b = turn(
        me, 1, own_b, pair_b, across_b, hidden_one, seed_pieces, pad_rows, alpha_gated, carry
    )
    delta_b, b_near_a = join(delta_b, b_near_a)
    both_near_a, own_one, pair_one, unit_one = gated_back(
        delta_a, b_near_a, up_one, gate_one, 0, *back_weights
    )
    b_near_b = trade(delta_b, "dim", 1)
    own_one, b_far_a, delta_b, pair_one, b_near_b = join(own_one, b_far_a, delta_b, pair_one, b_near_b)
    b_far_b = trade(delta_b, "dim", 2)
    b_corner_a = trade(b_far_a, "dim", 1)
    pair_one = trade(pair_one, "dim", 1)
    both_near_b, own_two, pair_two, unit_two = gated_back(
        delta_b, b_near_b, up_one, gate_one, 2, *back_weights
    )
    own_two, b_corner_a, pair_one, pair_two, b_far_b = join(
        own_two, b_corner_a, pair_one, pair_two, b_far_b
    )
    pair_two = trade(pair_two, "dim", 1)
    b_corner_b = trade(b_far_b, "dim", 1)
    both_far_a, back_across_a, corner, unit_three = gated_back(
        b_far_a, b_corner_a, up_a, gate_a, 0, *back_weights
    )
    corner, pair_two, b_corner_b = join(corner, pair_two, b_corner_b)
    corner = trade(corner, "dim", 1)
    across = add_low(back_across_a, corner).astype(BF16)
    across, b_corner_b = join(across, b_corner_b)
    across_one = trade(across, "dim", 2)
    both_far_b, back_across_b, corner, unit_four = gated_back(
        b_far_b, b_corner_b, up_b, gate_b, 0, *back_weights
    )
    back_across_b, across_one = join(back_across_b, across_one)
    corner = trade(corner, "dim", 1)
    across = add_low(back_across_b, corner).astype(BF16)
    across_two = trade(across, "dim", 2)
    back_sums = [own_one, pair_one, across_one, own_two, pair_two, across_two]
    h_pieces = [low_a, near_a, low_b, near_b, far_a, corner_a, far_b, corner_b]
    b_pieces = [delta_a, b_near_a, delta_b, b_near_b, b_far_a, b_corner_a, b_far_b, b_corner_b]
    middles = [mid_one, mid_a, mid_b]
    both_pieces = [both_near_a, both_near_b, both_far_a, both_far_b]
    unit_sums = (unit_one + unit_two) + (unit_three + unit_four)
    sum_gated = sum_a + sum_b
    if by_pieces:
        down_parts = weight_grad(tok, groups, middles, b_pieces, SCALE_HIDDEN, needs=(across,))
        down_odd = trade(down_parts[3], "tok", 1)
        both_parts = weight_grad(
            tok,
            groups,
            both_pieces,
            h_pieces,
            SCALE_MODEL,
            halves=True,
            needs=(down_parts[0],),
        )
        back_sums, both_parts, down_odd = join(back_sums, both_parts, down_odd)
        both_even, up_odd, gate_odd, *both_send = both_parts
        up_came = trade(both_send[1], "tok", 1)
        down_low = add_low(down_parts[1], down_odd).astype(BF16)
        down_near = trade(down_low, "tok", 2)
    else:
        down_grad = plain_sum(
            jnp.concatenate(middles, axis=0), jnp.concatenate(b_pieces, axis=0), SCALE_HIDDEN
        )
        both_grad = plain_sum(
            jnp.concatenate(both_pieces, axis=0), jnp.concatenate(h_pieces, axis=0), SCALE_MODEL
        )

    delta_near, delta_far, mixer_low, delta_direct, sum_mixer = mixer_back(
        me,
        back_sums,
        delta_hidden,
        hidden_one,
        mixer_unit,
        one_factor,
        mixer_factor,
        tokens_all,
        alpha_mixer,
        out_weights,
    )
    if by_pieces:
        delta_far, mixer_low, up_came, down_near = join(delta_far, mixer_low, up_came, down_near)
        gate_came = trade(both_send[2], "tok", 1)
        up_near = trade(add_low(up_odd, up_came).astype(BF16), "tok", 2)
    delta_came = trade(delta_far, "dim", 2)
    out_near_grad, out_far_grad = out_grad(mixed_pieces, mixer_low)
    alpha_sums = jnp.concatenate([sum_mixer, sum_gated], axis=0)
    alpha_near = trade(alpha_sums, "dim", 1)
    delta_came, out_near_grad, out_far_grad, alpha_near, layer_far = join(
        delta_came, out_near_grad, out_far_grad, alpha_near, layer_far
    )
    if by_pieces:
        delta_came, gate_came, up_near = join(delta_came, gate_came, up_near)
    delta_pair = trade(stack(delta_near[1], delta_came[1]), "dim", 1)
    out_pair = trade(stack(out_near_grad[1], out_far_grad[1]), "dim", 1)
    alpha_sums = alpha_sums + alpha_near
    delta_pair, out_pair = join(delta_pair, out_pair)
    if by_pieces:
        gate_near = trade(add_low(gate_odd, gate_came).astype(BF16), "tok", 2)
        both_even_came = trade(both_send[0], "tok", 1)
        down_even = trade(down_parts[2], "tok", 1)
    layer_came = trade(layer_far, "dim", 2)
    out_far_sum = trade(add_low(out_far_grad[0], out_pair[1]).astype(BF16), "dim", 2)
    delta_pieces = [(delta_near, 0), (delta_pair, 0), (delta_came, 0), (delta_pair, 1)]
    delta_project, scale_sum = attend_back(
        length_row,
        me,
        pad_row,
        queries,
        keys,
        values,
        raw,
        score_gain,
        [near_aux, far_aux],
        [near_mixed, far_mixed],
        delta_pieces,
    )
    delta_project, alpha_sums, out_far_sum, layer_came = join(
        delta_project, alpha_sums, out_far_sum, layer_came
    )
    alpha_far = trade(alpha_sums, "dim", 2)
    if by_pieces:
        delta_project, gate_near, both_even_came, down_even = join(
            delta_project, gate_near, both_even_came, down_even
        )
        down_low = add_low(down_parts[0][1], down_even[1], down_near[1]).astype(BF16)
        down_last = trade(down_low, "tok", 4)
        up_low, gate_low = [
            add_low(
                *[value[1, k * hidden_here : (k + 1) * hidden_here] for value in (both_even, both_even_came)],
                near[1],
            ).astype(BF16)
            for k, near in enumerate((up_near, gate_near))
        ]
        in_parts = weight_grad(
            tok,
            groups,
            (delta_project,),
            (tokens_all,),
            SCALE_MODEL,
            ((out_near_grad, 0), (out_pair, 0), (out_far_sum, None)),
            needs=(up_low, gate_low, down_low),
        )
        in_parts, alpha_far, layer_near, down_last, up_low, gate_low = join(
            in_parts, alpha_far, layer_near, down_last, up_low, gate_low
        )
        up_last = trade(up_low, "tok", 4)
        in_odd = trade(in_parts[3], "tok", 1)
    alpha_sums = lax.dynamic_slice_in_dim(alpha_sums + alpha_far, place * width, width, 1)
    gains_sum = jnp.concatenate(
        [scale_sum.reshape(-1), alpha_sums.reshape(-1), unit_sums.reshape(-1)]
    )
    input_parts = project_back(
        me, parts, delta_project, weight_in, delta_direct, (in_parts[3],) if by_pieces else ()
    )
    if by_pieces:
        input_parts, in_odd, in_parts, up_last, gate_low = join(
            input_parts, in_odd, in_parts, up_last, gate_low
        )
        in_low = add_low(in_parts[1], in_odd).astype(BF16)
        in_near = trade(in_low, "tok", 2)
        in_even = trade(in_parts[2], "tok", 1)
        gate_last = trade(gate_low, "tok", 4)
    corner = trade(input_parts[3], "dim", 1)
    near = trade(input_parts[1], "dim", 1)
    half = token_count // 2
    across = [
        add_low(input_parts[2][k * half : (k + 1) * half], corner[k * half : (k + 1) * half])
        for k in range(2)
    ]
    far_one = trade(across[0].astype(BF16), "dim", 2)
    across_two = across[1].astype(BF16)
    if by_pieces:
        far_one, near, across_two, gate_last, in_near, in_even = join(
            far_one, near, across_two, gate_last, in_near, in_even
        )
    far_two = trade(across_two, "dim", 2)
    layer_pair = trade(stack(layer_near[1], layer_came[1]), "dim", 1)
    layer_pieces = [layer_near[0], layer_pair[0], layer_came[0], layer_pair[1]]
    layer_out = jnp.zeros((token_count, width), BF16)
    for r, piece in enumerate(layer_pieces):
        layer_out = lax.dynamic_update_slice(layer_out, piece, ((place ^ r) * own_count, 0))
    if by_pieces:
        in_low = add_low(in_parts[0][1], in_even[1], in_near[1]).astype(BF16)
        in_last = trade(in_low, "tok", 4)
        down_grad = add_low(down_parts[0][0], down_even[0], down_near[0], down_last)
        up_grad, gate_grad = [
            add_low(
                *[value[0, k * hidden_here : (k + 1) * hidden_here] for value in (both_even, both_even_came)],
                near_sum[0],
                last,
            )
            for k, (near_sum, last) in enumerate(((up_near, up_last), (gate_near, gate_last)))
        ]
        both_grad = jnp.concatenate([up_grad, gate_grad], axis=0)
    gated_grad = jnp.concatenate([both_grad, down_grad], axis=0).reshape(3, hidden_here, -1)
    fix_first = 1.0 - BETA_ONE**STEP
    fix_second = 1.0 - BETA_TWO**STEP
    gated_stepped, moment_gated, square_gated = moment_update(
        gated_weights, gated_grad, gated_moment, gated_square, fix_first, fix_second
    )
    gated_row_sums = jnp.sum(gated_stepped * gated_stepped, axis=2)
    gated_square_sum = jnp.sum(gated_grad * gated_grad)
    if by_pieces:
        in_last, gated_row_sums, gated_square_sum, layer_out, far_two = join(
            in_last, gated_row_sums, gated_square_sum, layer_out, far_two
        )
        in_total = add_low(in_parts[0][0], in_even[0], in_near[0], in_last)
        attention_grad = in_total.reshape(4, width, -1)
    else:
        out_total = lax.psum_scatter(
            add_low(out_near_grad[0], out_pair[0], out_far_sum).astype(BF16),
            "tok",
            scatter_dimension=1,
            tiled=True,
        ).astype(F32)
        in_total = plain_sum(delta_project, tokens_all, SCALE_MODEL)
        attention_grad = jnp.concatenate([in_total, out_total], axis=0).reshape(4, width, -1)

    input_gradient = add_low(input_parts[0], near, jnp.concatenate([far_one, far_two], axis=0))

    attention_stepped, moment_attention, square_attention = moment_update(
        attention_weights, attention_grad, attention_moment, attention_square, fix_first, fix_second
    )
    sums = sum_over(
        jnp.concatenate(
            [
                jnp.sum(attention_stepped * attention_stepped, axis=2).reshape(-1),
                gated_row_sums.reshape(-1),
                gains_sum,
                (jnp.sum(attention_grad * attention_grad) + gated_square_sum).reshape(1),
            ]
        ),
        "tok",
    )
    ends = [4 * width, 4 * width + 3 * hidden_here, 7 * width + 3 * hidden_here]
    model_grad = sums[ends[1] : ends[2]].reshape(3, width)
    unit_grad = sums[ends[2] : -1].reshape(2, hidden_here)
    model_next, moment_model, square_model = moment_update(
        model_gains, model_grad, model_moment, model_square, fix_first, fix_second
    )
    unit_next, moment_unit, square_unit = moment_update(
        unit_gains, unit_grad, unit_moment, unit_square, fix_first, fix_second
    )
    square_sum = sums[-1:] + jnp.sum(model_grad * model_grad) + jnp.sum(unit_grad * unit_grad)
    totals = sum_over(jnp.concatenate([square_sum, jnp.sum(model_next[1:], axis=1)]), "dim")
    attention_rows = sums[: ends[0]].reshape(4, width, 1)
    gated_rows = sums[ends[0] : ends[1]].reshape(3, hidden_here, 1)
    attention_next = attention_stepped * lax.rsqrt(attention_rows / D + EPSILON)
    gated_next = gated_stepped * lax.rsqrt(gated_rows / D + EPSILON)
    gradient_norm = jnp.sqrt(totals[:1])
    mean_alpha = totals[1:] / D
    return (
        layer_out,
        input_gradient,
        attention_next,
        attention_next.astype(BF16),
        moment_attention,
        square_attention,
        gated_next,
        gated_next.astype(BF16),
        moment_gated,
        square_gated,
        model_next,
        moment_model,
        square_model,
        unit_next,
        moment_unit,
        square_unit,
        gradient_norm,
        mean_alpha,
    )


def solution(mesh):
    tokens = P("tok", "dim")
    weights = P(None, "dim", "tok")
    gains = P(None, "dim")
    in_specs = (tokens, tokens, P("tok", None), P("tok"), weights, weights, gains, gains)
    in_specs += (weights,) * 4 + (gains,) * 4
    out_specs = (tokens, tokens) + (weights,) * 8 + (gains,) * 6 + (P(), P())
    return jax.shard_map(local, mesh=mesh, in_specs=in_specs, out_specs=out_specs, check_vma=False)
```

```python
import functools
import math

import jax
import jax.numpy as jnp
from jax import lax
from jax.experimental import pallas as pl
from jax.experimental.pallas import tpu as pltpu
from jax.sharding import PartitionSpec as P

D = 1024
HEAD = 64
FF = 4096
STEP = 4
BLK = 256

EPSILON = 1e-06
ADAM_EPSILON = 1e-08
BETA_ONE = 0.5
BETA_TWO = 0.5
LEARN_RATE = 1.5

F32 = jnp.float32
BF16 = jnp.bfloat16
SCALE_MODEL = D**-0.5
SCALE_HIDDEN = FF**-0.5
SCORE = HEAD**-0.5 * math.log2(math.e)
NEVER = 1 << 24


def dot_nt(left, right):
    return lax.dot_general(left, right, (((1,), (1,)), ((), ())), preferred_element_type=F32)


def dot_nn(left, right):
    return lax.dot_general(left, right, (((1,), (0,)), ((), ())), preferred_element_type=F32)


def split_low(values):
    high = values.astype(BF16)
    return high, (values - high.astype(F32)).astype(BF16)


def params():
    return pltpu.CompilerParams(vmem_limit_bytes=60 << 20)


def cost(flops, traffic, transcendentals=0):
    return pl.CostEstimate(
        flops=int(flops) // 64, bytes_accessed=int(traffic) // 64, transcendentals=int(transcendentals) // 64
    )


def like(shape, dtype):
    return jax.ShapeDtypeStruct(shape, dtype)


def whole(*shape):
    return pl.BlockSpec(shape, lambda *_: (0,) * len(shape))


def rows(count, width):
    return pl.BlockSpec((count, width), lambda i, *_: (i, 0))


def launch(kernel, needs, scalars, grid, in_specs, args, scratch_shapes=(), **options):
    taken = len(scalars) + len(args)

    def body(*refs):
        kernel(*refs[:taken], *refs[taken + len(needs) :])

    return pl.pallas_call(
        body,
        grid_spec=pltpu.PrefetchScalarGridSpec(
            num_scalar_prefetch=len(scalars),
            grid=grid,
            in_specs=[*in_specs] + [pl.BlockSpec(memory_space=pl.ANY)] * len(needs),
            out_specs=options.pop("out_specs"),
            scratch_shapes=scratch_shapes,
        ),
        compiler_params=params(),
        **options,
    )(*scalars, *args, *needs)


def head_matrix(width):
    row = lax.broadcasted_iota(jnp.int32, (width, width), 0)
    column = lax.broadcasted_iota(jnp.int32, (width, width), 1)
    return jnp.where(row // HEAD == column // HEAD, 1.0, 0.0).astype(BF16)


def head_mean(values, ones):
    return dot_nn(values.astype(BF16), ones) * (1.0 / HEAD)


def head_mean_fine(values, ones):
    high, low = split_low(values)
    return (dot_nn(high, ones) + dot_nn(low, ones)) * (1.0 / HEAD)


def project_kernel(pieces, me_ref, tok_ref, *refs):
    piece_refs = refs[:pieces]
    weight_refs = refs[pieces:-7]
    gain_ref, all_ref, raw_ref, q_ref, k_ref, v_ref, w_ref = refs[-7:]
    width = piece_refs[0].shape[1]
    if len(weight_refs) == 1:
        weight = weight_refs[0]
    else:
        weight = w_ref

        @pl.when(pl.program_id(0) == 0)
        def assemble_weight():
            place_columns(tok_ref[0], weight_refs, w_ref)

    place_columns(me_ref[0], piece_refs, all_ref)
    projected = dot_nt(all_ref[...], weight[...]) * SCALE_MODEL
    if weight is not w_ref:
        w_ref[...] = weight[...]
    raw_ref[...] = projected[:, : 2 * width]
    ones = head_matrix(width)
    for place, out in enumerate((q_ref, k_ref)):
        values = projected[:, place * width : (place + 1) * width]
        factor = lax.rsqrt(head_mean_fine(values * values, ones) + EPSILON)
        out[...] = (values * factor * gain_ref[...]).astype(BF16)
    v_ref[...] = projected[:, 2 * width :].astype(BF16)


def place_columns(index, piece_refs, out_ref):
    width = piece_refs[0].shape[1]
    for offset, piece in enumerate(piece_refs):
        start = pl.multiple_of(jnp.bitwise_xor(index, offset) * width, width)
        out_ref[:, pl.ds(start, width)] = piece[...]


def piece_spec(piece, height, step):
    array, lead, block = piece
    width = array.shape[-1]
    if lead is None:
        return pl.BlockSpec((height, width), lambda i, *_: (block + step * i, 0))
    return pl.BlockSpec((None, height, width), lambda i, *_: (lead, block + step * i, 0))


def project(me, tok, pieces, weights, gain):
    count, width = pieces[0].shape
    depth = width * len(pieces)
    return pl.pallas_call(
        functools.partial(project_kernel, len(pieces)),
        grid_spec=pltpu.PrefetchScalarGridSpec(
            num_scalar_prefetch=2,
            grid=(count // BLK,),
            in_specs=[rows(BLK, width)] * len(pieces)
            + [piece_spec(weight, 3 * width, 0) for weight in weights]
            + [whole(1, width)],
            out_specs=[rows(BLK, depth), rows(BLK, 2 * width)]
            + [rows(BLK, width)] * 3
            + [whole(3 * width, depth)],
        ),
        out_shape=[like((count, depth), BF16), like((count, 2 * width), F32)]
        + [like((count, width), BF16)] * 3
        + [like((3 * width, depth), BF16)],
        compiler_params=params(),
        cost_estimate=cost(6 * count * width * depth, count * (4 * depth + 14 * width)),
        name="project",
    )(me, tok, *pieces, *[weight[0] for weight in weights], gain)


def assemble_kernel(tok_ref, *refs):
    place_columns(tok_ref[0], refs[:-1], refs[-1])


def assemble(tok, pieces, count, needs=()):
    width = pieces[0][0].shape[-1]
    depth = width * len(pieces)
    return launch(
        assemble_kernel,
        needs,
        (tok,),
        (count // BLK,),
        [piece_spec(piece, BLK, 1) for piece in pieces],
        (*[piece[0] for piece in pieces],),
        out_specs=rows(BLK, depth),
        out_shape=like((count, depth), BF16),
        cost_estimate=cost(0, 4 * count * depth),
        name="assemble",
    )


def seq_start(place, starts):
    found = jnp.zeros_like(place)
    for start in starts:
        found = jnp.where(place >= start, start, found)
    return found


def later_starts(length_ref, count):
    starts, total = [], jnp.int32(0)
    for position in range(count - 1):
        total = total + length_ref[position]
        starts.append(total)
    return starts


def attend_kernel(count, order, blocks, length_ref, me_ref, pad_ref, q_ref, k_ref, v_ref, *refs):
    mixed_ref, aux_ref, acc_ref = refs
    grid_step = pl.program_id(0)
    step = block_of(order, blocks, grid_step, me_ref)
    first_row = step * BLK
    starts = later_starts(length_ref, count)
    first = seq_start(first_row, starts) // BLK
    lane = lax.broadcasted_iota(jnp.int32, (BLK, 128), 1)
    left = lane < HEAD
    heads = q_ref.shape[1] // HEAD
    zero = jnp.zeros((BLK, 128), BF16)
    one = jnp.ones((BLK, 128), BF16)
    sides = [left if head % 2 == 0 else ~left for head in range(heads)]
    columns = [slice(head // 2 * 128, (head // 2 + 1) * 128) for head in range(heads)]
    queries = [jnp.where(sides[h], q_ref[:, columns[h]], zero) for h in range(heads)]
    acc_ref[...] = jnp.zeros_like(acc_ref)
    row = first_row + lax.broadcasted_iota(jnp.int32, (BLK, 1), 0)
    row_start = seq_start(row, starts)

    def body(block, carry):
        key_rows = pl.ds(pl.multiple_of(block * BLK, BLK), BLK)
        key = block * BLK + lax.broadcasted_iota(jnp.int32, (1, BLK), 1)
        code = jnp.where(pad_ref[:, key_rows] == 1, key, NEVER)
        mask = ((code >= row_start) & (code <= row)) | (key == row)
        for h in range(heads):
            value = jnp.where(sides[h], v_ref[key_rows, columns[h]], one)
            scores = dot_nt(queries[h], k_ref[key_rows, columns[h]])
            powers = jnp.where(mask, jnp.exp2(scores * SCORE), 0.0).astype(BF16)
            acc_ref[h] += dot_nn(powers, value)
        return carry

    lax.fori_loop(first, step + 1, body, 0)
    for pair in range(heads // 2):
        tile = slice(pair * 128, (pair + 1) * 128)
        even, odd = acc_ref[2 * pair], acc_ref[2 * pair + 1]
        total = jnp.where(left, odd, even)
        mixed = jnp.where(left, even, odd)
        mixed_ref[:, tile] = (mixed / pltpu.roll(total, HEAD, 1)).astype(BF16)
        high, low = split_low(jnp.log2(total) * (-1.0 / SCORE))
        aux_ref[:, tile] = jnp.where(lax.rem(lane, HEAD) < HEAD // 2, high, low)


def block_of(order, blocks, grid_step, me_ref):
    offset = order[0] + grid_step // blocks
    return jnp.bitwise_xor(me_ref[0], offset) * blocks + lax.rem(grid_step, blocks)


def piece_rows(blocks, place, width):
    return pl.BlockSpec(
        (BLK, width), lambda i, *_: (jnp.clip(i - place * blocks, 0, blocks - 1), 0)
    )


def attend(lengths, me, order, blocks, pad_row, queries, keys, values, needs=()):
    count, width = queries.shape
    heads = width // HEAD
    return launch(
        functools.partial(attend_kernel, lengths.shape[0], order, blocks),
        needs,
        (lengths, me,),
        (blocks * len(order),),
        [
                whole(1, count),
                pl.BlockSpec(
                    (BLK, width), lambda i, l_ref, me_ref: (block_of(order, blocks, i, me_ref), 0)
                ),
                whole(count, width),
                whole(count, width),
            ],
        (pad_row, queries, keys, values,),
        scratch_shapes=[pltpu.VMEM((heads, BLK, 128), F32)],
        out_specs=[rows(BLK, width)] * 2,
        out_shape=[like((len(order) * blocks * BLK, width), BF16)] * 2,
        cost_estimate=cost(2 * count * count * width, 6 * count * width, count * count * heads // 6),
        name="attend",
    )


def attend_back_kernel(
    count, pieces, length_ref, me_ref, pad_ref, q_ref, k_ref, v_ref, raw_ref, gain_ref, *refs
):
    pairs = pieces // 2
    aux_refs, mixed_refs, delta_refs = (
        refs[:pairs],
        refs[pairs : 2 * pairs],
        refs[2 * pairs : 2 * pairs + pieces],
    )
    low_ref, scale_sum, dqt_ref, do_ref, inner_ref, aux_ref, key_acc, value_acc = refs[
        2 * pairs + pieces :
    ]
    step = pl.program_id(0)
    tokens, width = q_ref.shape
    heads = width // HEAD
    starts = later_starts(length_ref, count)
    lane = lax.broadcasted_iota(jnp.int32, (BLK, 128), 1)
    left = lane < HEAD
    zero = jnp.zeros((BLK, 128), BF16)
    one = jnp.ones((BLK, 128), BF16)
    sides = [left if head % 2 == 0 else ~left for head in range(heads)]
    columns = [slice(head // 2 * 128, (head // 2 + 1) * 128) for head in range(heads)]

    @pl.when(step == 0)
    def prepare():
        dqt_ref[...] = jnp.zeros_like(dqt_ref)
        scale_sum[...] = jnp.zeros_like(scale_sum)
        part = tokens // pieces
        row = lax.broadcasted_iota(jnp.int32, (128, 128), 0)
        column = lax.broadcasted_iota(jnp.int32, (128, 128), 1)
        other = jnp.where(row // HEAD != column // HEAD, 1.0, 0.0).astype(BF16)
        for place in range(pieces):
            first = jnp.bitwise_xor(me_ref[0], place) * part
            do_ref[pl.ds(pl.multiple_of(first, part), part), :] = delta_refs[place][...]
            base = place % 2 * part
            aux_ref[pl.ds(pl.multiple_of(first, part), part), :] = aux_refs[place // 2][
                base : base + part, :
            ]
            for block in range(part // BLK):
                source = slice(block * BLK, (block + 1) * BLK)
                here = pl.ds(pl.multiple_of(first + block * BLK, BLK), BLK)
                for pair in range(heads // 2):
                    tile = slice(pair * 128, (pair + 1) * 128)
                    high, low = split_low(
                        delta_refs[place][source, tile].astype(F32)
                        * mixed_refs[place // 2][
                            base + block * BLK : base + (block + 1) * BLK, tile
                        ].astype(F32)
                    )
                    high, low = split_low(-(dot_nn(high, other) + dot_nn(low, other)))
                    inner_ref[here, tile] = jnp.where(lax.rem(lane, HEAD) < HEAD // 2, high, low)

    key_rows = pl.ds(pl.multiple_of(step * BLK, BLK), BLK)
    last_key = step * BLK + BLK - 1
    end = jnp.int32(tokens)
    for start in reversed(starts):
        end = jnp.where(last_key < start, start, end)
    last = (end - 1) // BLK
    key_acc[...] = jnp.zeros_like(key_acc)
    value_acc[...] = jnp.zeros_like(value_acc)
    turned = jnp.transpose(k_ref[key_rows, :].astype(F32)).astype(BF16)
    keys, values = [], []
    for h in range(heads):
        hot = jnp.where((lax.rem(lane, HEAD // 2) == 0) & (~sides[h]), one, zero)
        for source, into in ((k_ref, keys), (v_ref, values)):
            tile = jnp.where(sides[h], source[key_rows, columns[h]], zero)
            into.append(jnp.concatenate([tile, hot], axis=1))
    key = step * BLK + lax.broadcasted_iota(jnp.int32, (BLK, 1), 0)
    padding = jnp.transpose(
        jnp.broadcast_to(pad_ref[:, key_rows].astype(F32), (128, BLK))
    )[:, :1]
    code = jnp.where(padding > 0.5, key, NEVER)

    def body(block, carry):
        here = pl.ds(pl.multiple_of(block * BLK, BLK), BLK)
        row = block * BLK + lax.broadcasted_iota(jnp.int32, (1, BLK), 1)
        mask = ((code >= seq_start(row, starts)) & (code <= row)) | (key == row)
        for h in range(heads):
            query, delta = q_ref[here, columns[h]], do_ref[here, columns[h]]
            scores = dot_nt(keys[h], jnp.concatenate([query, aux_ref[here, columns[h]]], axis=1))
            delta_probs = dot_nt(
                values[h], jnp.concatenate([delta, inner_ref[here, columns[h]]], axis=1)
            )
            probs = jnp.where(mask, jnp.exp2(scores * SCORE), 0.0)
            delta_scores = (probs * delta_probs).astype(BF16)
            value_acc[h] += dot_nn(probs.astype(BF16), delta)
            key_acc[h] += dot_nn(delta_scores, query)
            head_rows = slice(h * HEAD, (h + 1) * HEAD)
            dqt_ref[head_rows, here] += dot_nn(turned[head_rows, :], delta_scores)
        return carry

    lax.fori_loop(step, last + 1, body, 0)
    key_tiles, value_tiles = [
        [jnp.where(left, acc[2 * pair], acc[2 * pair + 1]) for pair in range(heads // 2)]
        for acc in (key_acc, value_acc)
    ]
    ones = head_matrix(width)
    gain = gain_ref[...]
    deltas = (jnp.transpose(dqt_ref[:, key_rows]), jnp.concatenate(key_tiles, axis=1))
    for place, delta in enumerate(deltas):
        here = slice(place * width, (place + 1) * width)
        raw = raw_ref[:, here]
        factor = lax.rsqrt(head_mean(raw * raw, ones) + EPSILON)
        unit = raw * factor
        delta = delta * HEAD**-0.5
        scale_sum[...] += jnp.sum(delta * unit, axis=0, keepdims=True)
        delta = gain * delta
        low_ref[:, here] = (factor * (delta - unit * head_mean(delta * unit, ones))).astype(BF16)
    low_ref[:, 2 * width :] = jnp.concatenate(value_tiles, axis=1).astype(BF16)


def attend_back(lengths, me, pad_row, queries, keys, values, raw, gain, aux_pieces, mixed_pieces, delta_pieces):
    count, width = queries.shape
    heads = width // HEAD
    pieces = len(delta_pieces)
    return pl.pallas_call(
        functools.partial(attend_back_kernel, lengths.shape[0], pieces),
        grid_spec=pltpu.PrefetchScalarGridSpec(
            num_scalar_prefetch=2,
            grid=(count // BLK,),
            in_specs=[whole(1, count)]
            + [whole(count, width)] * 3
            + [rows(BLK, 2 * width), whole(1, width)]
            + [whole(2 * count // pieces, width)] * pieces
            + [piece_spec((array, lead, 0), count // pieces, 0) for array, lead in delta_pieces],
            out_specs=[rows(BLK, 3 * width), whole(1, width)],
            scratch_shapes=[
                pltpu.VMEM((width, count), F32),
                pltpu.VMEM((count, width), BF16),
                pltpu.VMEM((count, width), BF16),
                pltpu.VMEM((count, width), BF16),
                pltpu.VMEM((heads, BLK, 128), F32),
                pltpu.VMEM((heads, BLK, 128), F32),
            ],
        ),
        out_shape=[like((count, 3 * width), BF16), like((1, width), F32)],
        compiler_params=params(),
        cost_estimate=cost(8 * count * count * width, 22 * count * width, count * count * heads // 3),
        name="attend_back",
    )(lengths, me, pad_row, queries, keys, values, raw, gain, *aux_pieces, *mixed_pieces, *[array for array, lead in delta_pieces])


def unit_of(values):
    factor = lax.rsqrt(jnp.mean(values * values, axis=1, keepdims=True) + EPSILON)
    return values * factor, factor


def unit_back(delta, unit, factor):
    return factor * (delta - unit * jnp.mean(delta * unit, axis=1, keepdims=True))


def mixer_kernel(pieces, *refs):
    mixed_refs, out_weights = refs[:pieces], refs[pieces : 2 * pieces]
    tokens_ref, alpha_ref, *low_refs, one_ref, unit_ref, unit_factor, one_factor = refs[2 * pieces :]
    branch = dot_nn(mixed_refs[0][...], out_weights[0][...])
    for mixed, weight in zip(mixed_refs[1:], out_weights[1:]):
        branch += dot_nn(mixed[...], weight[...])
    unit, factor = unit_of(branch * SCALE_MODEL)
    unit_ref[...] = unit
    unit_factor[...] = jnp.broadcast_to(factor, unit_factor.shape)
    residual = tokens_ref[...].astype(F32)
    hidden, factor = unit_of(residual + alpha_ref[...] * (unit - residual))
    one_ref[...] = hidden
    one_factor[...] = jnp.broadcast_to(factor, one_factor.shape)
    put(1, hidden.astype(BF16), *low_refs)


def mixer(mixed_pieces, out_weights, me, tokens_all, alpha):
    width = mixed_pieces[0][0].shape[-1]
    pieces = len(mixed_pieces)
    count = tokens_all.shape[0] // pieces
    depth = tokens_all.shape[1]
    blocks = count // BLK
    kernel = functools.partial(mixer_kernel, pieces)
    return pl.pallas_call(
        lambda me_ref, *refs: kernel(*refs),
        grid_spec=pltpu.PrefetchScalarGridSpec(
            num_scalar_prefetch=1,
            grid=(blocks,),
            in_specs=[piece_spec((array, lead, 0), BLK, 1) for array, lead in mixed_pieces]
            + [piece_spec((array, lead, 0), width, 0) for array, lead in out_weights]
            + [
                pl.BlockSpec((BLK, depth), lambda i, me_ref: (me_ref[0] * blocks + i, 0)),
                whole(1, depth),
            ],
            out_specs=[piece_rows(1, 0, depth), piece_rows(1, 1, depth)]
            + [rows(BLK, depth)] * 2
            + [rows(BLK, 128)] * 2,
        ),
        out_shape=[like((BLK, depth), BF16)] * 2
        + [like((count, depth), F32)] * 2
        + [like((count, 128), F32)] * 2,
        compiler_params=params(),
        cost_estimate=cost(2 * count * depth * depth, 16 * count * depth + 2 * depth * depth),
        name="mixer",
    )(me, *[p[0] for p in mixed_pieces], *[w[0] for w in out_weights], tokens_all, alpha)


def turn_kernel(pieces, carried, me_ref, *refs):
    own_ref, near_ref, far_ref, one_ref = refs[:4]
    seed_refs = refs[4 : 4 + pieces]
    pad_ref, alpha_ref = refs[4 + pieces : 6 + pieces]
    outs = refs[6 + pieces + carried :]
    pair_refs = outs[: pieces // 2]
    hidden_ref, low_ref, alpha_sum, seed, layer = outs[pieces // 2 :]
    width = seed_refs[0].shape[-1]
    starts = [
        pl.multiple_of(jnp.bitwise_xor(me_ref[0], place) * width, width) for place in range(pieces)
    ]
    for start, piece in zip(starts, seed_refs):
        seed[:, pl.ds(start, width)] = piece[...]
    branch = (own_ref[...].astype(F32) + near_ref[...].astype(F32)) + far_ref[...].astype(F32)
    unit, unit_factor = unit_of(branch)
    hidden = one_ref[...]
    alpha = alpha_ref[...]
    layer_rows, layer_factor = unit_of(hidden + alpha * (unit - hidden))
    layer[...] = layer_rows.astype(BF16)
    for offset, start in enumerate(starts):
        pair_refs[offset // 2][offset % 2] = layer[:, pl.ds(start, width)]
    delta = unit_back(seed[...].astype(F32) * pad_ref[...], layer_rows, layer_factor)
    alpha_sum[...] = jnp.sum(delta * (unit - hidden), axis=0, keepdims=True)
    hidden_ref[...] = (1.0 - alpha) * delta
    low_ref[...] = unit_back(alpha * delta, unit, unit_factor).astype(BF16)


def turn(me, half, own, near, far, hidden_one, seed_pieces, pad_rows, alpha, carry=()):
    count, depth = hidden_one.shape
    pieces = len(seed_pieces)
    width = depth // pieces
    here = pl.BlockSpec((BLK, depth), lambda i, *_: (half, 0))
    pair = pl.BlockSpec((2, BLK, width), lambda i, *_: (0, half, 0))
    return pl.pallas_call(
        functools.partial(turn_kernel, pieces, len(carry)),
        grid_spec=pltpu.PrefetchScalarGridSpec(
            num_scalar_prefetch=1,
            grid=(1,),
            in_specs=[whole(BLK, depth)] * 3
            + [here]
            + [piece_spec((array, lead, half), BLK, 0) for array, lead in seed_pieces]
            + [pl.BlockSpec((BLK, 1), lambda i, *_: (half, 0)), whole(1, depth)]
            + [pl.BlockSpec(memory_space=pl.ANY)] * len(carry),
            out_specs=[pair] * (pieces // 2) + [here, whole(BLK, depth), whole(1, depth)],
            scratch_shapes=[pltpu.VMEM((BLK, depth), BF16)] * 2,
        ),
        out_shape=[like((2, count, width), BF16)] * (pieces // 2)
        + [like((count, depth), F32), like((BLK, depth), BF16), like((1, depth), F32)],
        input_output_aliases={7 + pieces + k: k for k in range(len(carry))},
        compiler_params=params(),
        cost_estimate=cost(40 * count * depth, 20 * count * depth),
        name="turn",
    )(
        me, own, near, far, hidden_one, *[p[0] for p in seed_pieces], pad_rows, alpha, *carry
    )


def mixer_back_kernel(pieces, *refs):
    halves, (hidden_ref, one_ref, unit_ref) = (refs[:6:2], refs[1:6:2]), refs[6:9]
    one_factor, unit_factor, tokens_ref, alpha_ref = refs[9:13]
    out_weights = refs[13 : 13 + pieces]
    pair_refs = refs[13 + pieces : 13 + pieces + pieces // 2]
    low_ref, direct_ref, alpha_sum = refs[13 + pieces + pieces // 2 :]
    own, near, far = [
        jnp.where(pl.program_id(0) < pl.num_programs(0) // 2, first[...].astype(F32), second[...].astype(F32))
        for first, second in zip(*halves)
    ]

    @pl.when(pl.program_id(0) == 0)
    def clear():
        alpha_sum[...] = jnp.zeros_like(alpha_sum)

    delta = hidden_ref[...] + ((own + near) + far)
    unit = unit_ref[...]
    alpha = alpha_ref[...]
    delta = unit_back(delta, one_ref[...], one_factor[:, :1])
    alpha_sum[...] += jnp.sum(delta * (unit - tokens_ref[...].astype(F32)), axis=0, keepdims=True)
    direct_ref[...] = (1.0 - alpha) * delta
    low = unit_back(alpha * delta, unit, unit_factor[:, :1]).astype(BF16)
    low_ref[...] = low
    for offset, weight in enumerate(out_weights):
        pair_refs[offset // 2][offset % 2] = (dot_nt(low, weight[...]) * SCALE_MODEL).astype(BF16)


def mixer_back(
    me, sums, hidden, one, unit, one_factor, unit_factor, tokens_all, alpha, out_weights
):
    count, depth = one.shape
    pieces = len(out_weights)
    width = depth // pieces
    block = BLK
    blocks = count // block
    half = blocks // 2
    kernel = functools.partial(mixer_back_kernel, pieces)
    return pl.pallas_call(
        lambda me_ref, *refs: kernel(*refs),
        grid_spec=pltpu.PrefetchScalarGridSpec(
            num_scalar_prefetch=1,
            grid=(blocks,),
            in_specs=[
                pl.BlockSpec((block, depth), lambda i, *_: (jnp.minimum(i, half - 1), 0)),
                pl.BlockSpec((block, depth), lambda i, *_: (jnp.maximum(i - half, 0), 0)),
            ]
            * 3
            + [rows(block, depth)] * 3
            + [rows(block, 128)] * 2
            + [
                pl.BlockSpec((block, depth), lambda i, me_ref: (me_ref[0] * blocks + i, 0)),
                whole(1, depth),
            ]
            + [piece_spec((array, lead, 0), width, 0) for array, lead in out_weights],
            out_specs=[pl.BlockSpec((2, block, width), lambda i, *_: (0, i, 0))] * (pieces // 2)
            + [rows(block, depth), rows(block, depth), whole(1, depth)],
        ),
        out_shape=[like((2, count, width), BF16)] * (pieces // 2)
        + [like((count, depth), BF16), like((count, depth), F32), like((1, depth), F32)],
        compiler_params=params(),
        cost_estimate=cost(2 * count * depth * depth, 28 * count * depth + 2 * depth * depth),
        name="mixer_back",
    )(
        me,
        *[value for pair in zip(sums[:3], sums[3:]) for value in pair],
        hidden,
        one,
        unit,
        one_factor,
        unit_factor,
        tokens_all,
        alpha,
        *[w[0] for w in out_weights],
    )


def pick(half, first_ref, second_ref, out_ref):
    step = pl.program_id(0)

    @pl.when(step < half)
    def from_first():
        out_ref[...] = first_ref[...]

    @pl.when(step >= half)
    def from_second():
        out_ref[...] = second_ref[...]


def put(half, value, first_ref, second_ref):
    step = pl.program_id(0)

    @pl.when(step < half)
    def to_first():
        first_ref[...] = value

    @pl.when(step >= half)
    def to_second():
        second_ref[...] = value


def whole_weight(tok_ref, piece_refs, out_ref):
    if out_ref is None:
        return piece_refs[0]

    @pl.when(pl.program_id(0) == 0)
    def assemble_weight():
        place_columns(tok_ref[0], piece_refs, out_ref)

    return out_ref


def expand_kernel(count, pieces, tok_ref, *refs):
    block_refs, gain_ref, refs = refs[:count], refs[count], refs[count + 1 :]
    up_pieces, gate_pieces = refs[:pieces], refs[pieces : 2 * pieces]
    up_ref, gate_ref, mid_ref = refs[2 * pieces : 2 * pieces + 3]
    hidden_ref = refs[-1]
    outs = refs[2 * pieces + 3 : -1] or (None, None)
    up_w = whole_weight(tok_ref, up_pieces, outs[0])
    gate_w = whole_weight(tok_ref, gate_pieces, outs[1])
    for place, block_ref in enumerate(block_refs):

        @pl.when(pl.program_id(0) == place)
        def take(block_ref=block_ref):
            hidden_ref[...] = block_ref[...]

    hidden = hidden_ref[...]
    up = dot_nt(hidden, up_w[...]) * SCALE_MODEL
    gate = dot_nt(hidden, gate_w[...]) * SCALE_MODEL
    up_ref[...] = up.astype(BF16)
    gate_ref[...] = gate.astype(BF16)
    scaled = gain_ref[1:2, :] * gate
    mid_ref[...] = (gain_ref[0:1, :] * up * scaled * jax.nn.sigmoid(scaled)).astype(BF16)


def expand(tok, blocks_in, up_pieces, gate_pieces, gains):
    depth = blocks_in[0].shape[1]
    hidden = gains.shape[1]
    count = len(blocks_in)
    pieces = len(up_pieces)
    outs = 2 if pieces > 1 else 0
    return pl.pallas_call(
        functools.partial(expand_kernel, count, pieces),
        grid_spec=pltpu.PrefetchScalarGridSpec(
            num_scalar_prefetch=1,
            grid=(count,),
            in_specs=[whole(BLK, depth)] * count
            + [whole(2, hidden)]
            + [piece_spec(piece, hidden, 0) for piece in (*up_pieces, *gate_pieces)],
            out_specs=[rows(BLK, hidden)] * 3 + [whole(hidden, depth)] * outs,
            scratch_shapes=[pltpu.VMEM((BLK, depth), BF16)],
        ),
        out_shape=[like((count * BLK, hidden), BF16)] * 3 + [like((hidden, depth), BF16)] * outs,
        compiler_params=params(),
        cost_estimate=cost(4 * count * BLK * depth * hidden, 4 * depth * hidden),
        name="expand",
    )(tok, *blocks_in, gains, *[piece[0] for piece in (*up_pieces, *gate_pieces)])


def contract_kernel(pieces, tok_ref, mid_ref, *refs):
    first_ref, second_ref = refs[pieces : pieces + 2]
    outs = refs[pieces + 2 :] or (None,)
    down_w = whole_weight(tok_ref, refs[:pieces], outs[0])
    total = (dot_nn(mid_ref[...], down_w[...]) * SCALE_HIDDEN).astype(BF16)
    first_ref[...] = total[:BLK]
    second_ref[...] = total[BLK:]


def contract(tok, middle, first_block, down_pieces, depth, needs=()):
    hidden = middle.shape[1]
    count = 2 * BLK
    pieces = len(down_pieces)
    outs = 1 if pieces > 1 else 0
    return launch(
        functools.partial(contract_kernel, pieces),
        needs,
        (tok,),
        (1,),
        [pl.BlockSpec((2 * BLK, hidden), lambda i, *_: (first_block // 2, 0))] + [piece_spec(piece, hidden, 0) for piece in down_pieces],
        (middle, *[piece[0] for piece in down_pieces],),
        out_specs=[whole(BLK, depth), whole(BLK, depth)]
            + [whole(hidden, depth)] * outs,
        out_shape=[like((count // 2, depth), BF16)] * 2 + [like((hidden, depth), BF16)] * outs,
        cost_estimate=cost(
            2 * count * depth * hidden, 2 * count * (depth + hidden) + 2 * depth * hidden
        ),
        name="contract",
    )


def gated_back_kernel(
    up_from,
    gate_from,
    down_from,
    first_ref,
    second_ref,
    up_ref,
    gate_ref,
    gain_ref,
    both_ref,
    first_out,
    second_out,
    unit_ref,
    delta_ref,
    down_w,
    up_w,
    gate_w,
    arrived,
):
    copies = [
        pltpu.make_async_copy(source, into, arrived.at[k])
        for k, (source, into) in enumerate(
            ((down_from, down_w), (up_from, up_w), (gate_from, gate_w))
        )
    ]
    for copy in copies:
        copy.start()
    count = first_ref.shape[0]
    delta_ref[:count, :] = first_ref[...]
    delta_ref[count:, :] = second_ref[...]
    copies[0].wait()
    hidden = up_w.shape[0]
    part = hidden // 2
    total = None
    for start in range(0, hidden, part):
        here = slice(start, start + part)
        delta_middle = dot_nt(delta_ref[...], down_w[here, :]) * SCALE_HIDDEN
        up = up_ref[:, here].astype(F32)
        gate = gate_ref[:, here].astype(F32)
        scaled = gain_ref[1:2, here] * gate
        sigmoid = jax.nn.sigmoid(scaled)
        shared = delta_middle * sigmoid
        delta_up = shared * scaled
        delta_gate = shared * (gain_ref[0:1, here] * up) * (1.0 + scaled * (1.0 - sigmoid))
        unit_ref[0:1, here] = jnp.sum(delta_up * up, axis=0, keepdims=True)
        unit_ref[1:2, here] = jnp.sum(delta_gate * gate, axis=0, keepdims=True)
        up_low = (gain_ref[0:1, here] * delta_up).astype(BF16)
        gate_low = (gain_ref[1:2, here] * delta_gate).astype(BF16)
        both_ref[:, here] = up_low
        both_ref[:, hidden + start : hidden + start + part] = gate_low
        if start == 0:
            copies[1].wait()
            copies[2].wait()
        term = dot_nn(up_low, up_w[here, :]) + dot_nn(gate_low, gate_w[here, :])
        total = term if total is None else total + term
    total = total * SCALE_MODEL
    first_out[...] = total[:count].astype(BF16)
    second_out[...] = total[count:].astype(BF16)


def gated_back(first, second, up, gate, first_block, up_w, gate_w, down_w, gains):
    count, depth = first.shape
    hidden = up_w.shape[0]
    here = pl.BlockSpec((2 * count, hidden), lambda i: (first_block * BLK // (2 * count), 0))
    return pl.pallas_call(
        gated_back_kernel,
        grid=(1,),
        in_specs=[pl.BlockSpec(memory_space=pl.ANY)] * 3
        + [whole(count, depth)] * 2
        + [here, here, whole(2, hidden)],
        out_specs=[whole(2 * count, 2 * hidden)] + [whole(count, depth)] * 2 + [whole(2, hidden)],
        scratch_shapes=[pltpu.VMEM((2 * count, depth), BF16)]
        + [pltpu.VMEM((hidden, depth), BF16)] * 3
        + [pltpu.SemaphoreType.DMA((3,))],
        out_shape=[like((2 * count, 2 * hidden), BF16)]
        + [like((count, depth), BF16)] * 2
        + [like((2, hidden), F32)],
        compiler_params=params(),
        cost_estimate=cost(
            12 * count * depth * hidden,
            8 * count * (depth + hidden) + 6 * depth * hidden,
            2 * count * hidden,
        ),
        name="gated_back",
    )(up_w, gate_w, down_w, first, second, up, gate, gains)


def part_columns(tok_ref, total, part_refs):
    width = part_refs[0].shape[2]
    in_halves = len(part_refs) == 5
    for offset in range(8):
        start = pl.multiple_of(jnp.bitwise_xor(tok_ref[0], offset) * width, width)
        value = total[:, pl.ds(start, width)].astype(BF16)
        sent, odd, lead = offset % 2, offset // 2 % 2, offset // 4
        if not in_halves or not sent:
            part_refs[2 * sent + odd][lead] = value
        elif odd:
            part_refs[4][lead] = value
        else:
            half = pl.num_programs(0) // 2

            @pl.when(pl.program_id(0) < half)
            def first_half(value=value, into=part_refs[2], lead=lead):
                into[lead] = value

            @pl.when(pl.program_id(0) >= half)
            def second_half(value=value, into=part_refs[3], lead=lead):
                into[lead] = value


def weight_grad_kernel(lefts, rights, scale, steps, outs, tok_ref, *refs):
    left_refs, right_refs = refs[:lefts], refs[lefts : lefts + rights]
    fold_refs, part_refs = refs[lefts + rights : -outs - 1], refs[-outs - 1 : -1]
    total = refs[-1]

    @pl.when(pl.program_id(0) < steps)
    def product():
        acc, lefts_in = None, []
        for ref in left_refs:
            count = right_refs[0].shape[0]
            lefts_in += [ref[k * count : (k + 1) * count, :] for k in range(ref.shape[0] // count)]
        for left, right in zip(lefts_in, right_refs):
            term = lax.dot_general(
                left, right[...], (((0,), (0,)), ((), ())), preferred_element_type=F32
            )
            acc = term if acc is None else acc + term
        total[...] = acc * scale

    if fold_refs:

        @pl.when(pl.program_id(0) >= steps)
        def fold():
            own, near, far = [ref[...].astype(F32) for ref in fold_refs]
            total[...] = (own + near) + far

    part_columns(tok_ref, total, part_refs)


def weight_grad(tok, groups, lefts, rights, scale, folds=(), halves=False, needs=()):
    height = lefts[0].shape[1]
    depth = rights[0].shape[1]
    count = sum(left.shape[0] for left in lefts)
    part = depth // groups
    steps = height // BLK
    out = pl.BlockSpec((groups // 4, BLK, part), lambda i, *_: (0, i, 0))
    total_height = height + (BLK if folds else 0)
    outs, heights = [out] * 4, [total_height] * 4
    if halves:
        half = steps // 2
        even = [
            pl.BlockSpec((groups // 4, BLK, part), lambda i, *_: (0, jnp.minimum(i, half - 1), 0)),
            pl.BlockSpec((groups // 4, BLK, part), lambda i, *_: (0, jnp.maximum(i - half, 0), 0)),
        ]
        outs = [out, out, *even, out]
        heights = [height, height, height // 2, height // 2, height]
    return launch(
        functools.partial(
            weight_grad_kernel, len(lefts), len(rights), scale, steps, len(outs)
        ),
        needs,
        (tok,),
        (total_height // BLK,),
        [
                pl.BlockSpec((left.shape[0], BLK), lambda i, *_: (0, jnp.minimum(i, steps - 1)))
                for left in lefts
            ]
            + [whole(*right.shape) for right in rights]
            + [piece_spec((array, lead, 0), BLK, 0) for array, lead in folds],
        (*lefts, *rights, *[array for array, lead in folds],),
        scratch_shapes=[pltpu.VMEM((BLK, depth), F32)],
        out_specs=outs,
        out_shape=[like((groups // 4, tall, part), BF16) for tall in heights],
        cost_estimate=cost(
            2 * count * height * depth, 2 * count * (height + depth) + 2 * height * depth
        ),
        name="weight_grad",
    )


def out_grad_kernel(pieces, *refs):
    right, pair_refs = refs[pieces], refs[pieces + 1 :]
    for offset, left in enumerate(refs[:pieces]):
        total = lax.dot_general(
            left[...], right[...], (((0,), (0,)), ((), ())), preferred_element_type=F32
        )
        pair_refs[offset // 2][offset % 2] = (total * SCALE_MODEL).astype(BF16)


def out_grad(lefts, right):
    width = lefts[0][0].shape[-1]
    count, depth = right.shape
    pieces = len(lefts)
    return pl.pallas_call(
        functools.partial(out_grad_kernel, pieces),
        grid=(1,),
        in_specs=[piece_spec((array, lead, 0), count, 0) for array, lead in lefts]
        + [whole(count, depth)],
        out_specs=[whole(2, width, depth)] * (pieces // 2),
        out_shape=[like((2, width, depth), BF16)] * (pieces // 2),
        compiler_params=params(),
        cost_estimate=cost(2 * count * depth * depth, 4 * count * depth + 2 * depth * depth),
        name="out_grad",
    )(*[p[0] for p in lefts], right)


def project_back_kernel(pieces, me_ref, low_ref, w_ref, direct_ref, *refs):
    part_refs, total = refs[:pieces], refs[pieces]
    step = pl.program_id(0)
    total[...] = dot_nn(low_ref[...], w_ref[...]) * SCALE_MODEL
    own_blocks = direct_ref.shape[0] // BLK

    @pl.when(step // own_blocks == me_ref[0])
    def add_direct():
        start = pl.multiple_of(lax.rem(step, own_blocks) * BLK, BLK)
        total[...] += direct_ref[pl.ds(start, BLK), :]

    part = total.shape[1] // pieces
    for place, out in enumerate(part_refs):
        start = pl.multiple_of(jnp.bitwise_xor(me_ref[0], place) * part, part)
        out[...] = total[:, pl.ds(start, part)].astype(BF16)


def project_back(me, pieces, low, weight, direct, needs=()):
    count = low.shape[0]
    depth = weight.shape[1]
    part = depth // pieces
    return launch(
        functools.partial(project_back_kernel, pieces),
        needs,
        (me,),
        (count // BLK,),
        [rows(BLK, low.shape[1]), whole(*weight.shape), whole(*direct.shape)],
        (low, weight, direct),
        scratch_shapes=[pltpu.VMEM((BLK, depth), F32)],
        out_specs=[rows(BLK, part)] * pieces,
        out_shape=[like((count, part), BF16)] * pieces,
        cost_estimate=cost(2 * count * low.shape[1] * depth, 2 * count * depth),
        name="project_back",
    )


def trade(value, axis, offset):
    size = lax.axis_size(axis)
    return lax.ppermute(value, axis, [(i, i ^ offset) for i in range(size)])


def sum_four(value, axis, first, second):
    one, two, three = [trade(value, axis, o) for o in (first, second, first ^ second)]
    return (value + one) + (two + three)


def sum_over(value, axis):
    if lax.axis_size(axis) == 4:
        return sum_four(value, axis, 1, 2)
    if lax.axis_size(axis) == 8:
        return sum_four(value + trade(value, axis, 1), axis, 2, 4)
    offset = 1
    while offset < lax.axis_size(axis):
        value = value + trade(value, axis, offset)
        offset *= 2
    return value


def join(*values):
    return lax.optimization_barrier(values)


def stack(*values):
    return jnp.concatenate([v if v.ndim == 3 else v[None] for v in values], axis=0)


def add_low(*values):
    total = values[0].astype(F32)
    for value in values[1:]:
        total = total + value.astype(F32)
    return total


def plain_sum(left, right, scale):
    total = jnp.einsum("tr,td->rd", left, right, preferred_element_type=F32) * scale
    return lax.psum_scatter(total.astype(BF16), "tok", scatter_dimension=1, tiled=True).astype(F32)


def moment_update(weights, gradient, moment, square, fix_first, fix_second):
    moment_next = BETA_ONE * moment + (1.0 - BETA_ONE) * gradient
    square_next = BETA_TWO * square + (1.0 - BETA_TWO) * gradient * gradient
    stepped = weights - LEARN_RATE * (moment_next / fix_first) / (
        jnp.sqrt(square_next / fix_second) + ADAM_EPSILON
    )
    return (stepped, moment_next, square_next)


def local(
    inputs,
    cotangent,
    lengths,
    pad_mask,
    attention_weights,
    gated_weights,
    model_gains,
    unit_gains,
    attention_moment,
    attention_square,
    gated_moment,
    gated_square,
    model_moment,
    model_square,
    unit_moment,
    unit_square,
):
    token_count, width = inputs.shape
    parts = lax.axis_size("dim")
    hidden_here = gated_weights.shape[1]
    own_count = token_count // parts
    place = lax.axis_index("dim")
    me = place.astype(jnp.int32).reshape(1)
    tok = lax.axis_index("tok").astype(jnp.int32).reshape(1)
    groups = lax.axis_size("tok")
    by_pieces = groups == 8 and (D // groups) % 128 == 0
    blocks = own_count // BLK
    length_row = lengths[0]

    def token_rows(value, offset):
        return lax.dynamic_slice_in_dim(value, (place ^ offset) * own_count, own_count, 0)

    ao = attention_weights.reshape(4 * width, -1).astype(BF16)
    gated_low = gated_weights.reshape(3 * hidden_here, -1).astype(BF16)
    both_own = gated_weights[:2].reshape(2 * hidden_here, -1).astype(BF16)
    down_own = gated_weights[2].astype(BF16)
    score_gain = model_gains[:1]
    pad_row = pad_mask[None, :]
    pad_rows = token_rows(pad_mask, 0).astype(F32)[:, None]

    x_far = trade(inputs, "dim", 2)
    seed_rows = [token_rows(cotangent, r) for r in range(parts)]
    seed_send = stack(*seed_rows[2:])
    alphas = lax.dynamic_update_slice(
        jnp.zeros((2, D), F32), model_gains[1:], (0, place * width)
    )
    alpha_near = trade(alphas, "dim", 1)
    if by_pieces:
        ao_by = {0: ao, 4: trade(ao, "tok", 4), 2: trade(ao, "tok", 2), 1: trade(ao, "tok", 1)}
        ao_by[6] = trade(ao_by[4], "tok", 2)
        ao_by[5] = trade(ao_by[4], "tok", 1)
        ao_by[3] = trade(ao_by[2], "tok", 1)
        x_far, ao_by, both_own, seed_send, alphas, alpha_near = join(
            x_far, ao_by, both_own, seed_send, alphas, alpha_near
        )
        ao_by[7] = trade(ao_by[6], "tok", 1)
        by = {0: both_own, 2: trade(both_own, "tok", 2), 4: trade(both_own, "tok", 4)}
    else:
        gather = functools.partial(lax.all_gather, axis_name="tok", axis=1, tiled=True)
        in_pieces = [(gather(ao[: 3 * width]), None, 0)]
        out_weight, up_w, gate_w, down_w = [
            gather(shard)
            for shard in (ao[3 * width :], both_own[:hidden_here], both_own[hidden_here:], down_own)
        ]
        up_pieces, gate_pieces, down_pieces = [[(w, None, 0)] for w in (up_w, gate_w, down_w)]
    x_near = trade(inputs, "dim", 1)
    x_corner = trade(x_far, "dim", 1)
    token_pieces = [inputs, x_near, x_far, x_corner]
    if by_pieces:
        token_pieces, ao_by, gated_low, down_own, seed_send, alphas = join(
            token_pieces, ao_by, gated_low, down_own, seed_send, alphas
        )
        in_pieces = [(ao_by[offset], None, 0) for offset in range(8)]
        by[1] = trade(gated_low, "tok", 1)
    seed_far = trade(seed_send, "dim", 2)
    tokens_all, raw, queries, keys, values, weight_in = project(
        me, tok, token_pieces, in_pieces, score_gain
    )
    queries, seed_far = join(queries, seed_far)

    queries, seed_far, alpha_near = join(queries, seed_far, alpha_near)
    alphas = alphas + alpha_near
    alpha_far = trade(alphas, "dim", 2)
    if by_pieces:
        queries, ao_by = join(queries, ao_by)
        out_weight = assemble(
            tok, [(ao_by[o], None, 3 * width // BLK) for o in range(8)], width, (queries,)
        )
        out_weight, by[1], by[2], by[4], down_own = join(
            out_weight, by[1], by[2], by[4], down_own
        )
        by[3] = trade(by[2], "tok", 1)
        by[6] = trade(by[4], "tok", 2)
    out_across = trade(out_weight, "dim", 2)
    far_mixed, far_aux = attend(
        length_row, me, (2, 3), blocks, pad_row, queries, keys, values, (out_weight,)
    )
    far_mixed, alpha_far, out_across = join(far_mixed, alpha_far, out_across)
    alphas = alphas + alpha_far
    alpha_mixer, alpha_gated = alphas[:1], alphas[1:]
    if by_pieces:
        far_mixed, by[3], by[6], down_own = join(far_mixed, by[3], by[6], down_own)
        by[5] = trade(by[4], "tok", 1)
        down_by = {0: down_own, 2: trade(down_own, "tok", 2), 4: trade(down_own, "tok", 4)}
    far_came = trade(far_mixed, "dim", 2)
    out_pair = trade(stack(out_weight, out_across), "dim", 1)
    near_mixed, near_aux = attend(
        length_row, me, (0, 1), blocks, pad_row, queries, keys, values, (far_mixed,)
    )
    near_mixed, far_came, out_pair = join(near_mixed, far_came, out_pair)
    if by_pieces:
        near_mixed, by[5], by[6], down_by = join(near_mixed, by[5], by[6], down_by)
    pair_came = trade(stack(near_mixed[own_count:], far_came[own_count:]), "dim", 1)
    out_weights = [(out_weight, None), (out_pair, 0), (out_across, None), (out_pair, 1)]
    mixed_pieces = [(near_mixed, None), (pair_came, 0), (far_came, None), (pair_came, 1)]
    low_a, low_b, hidden_one, mixer_unit, mixer_factor, one_factor = mixer(
        mixed_pieces, out_weights, me, tokens_all, alpha_mixer
    )

    far_a = trade(low_a, "dim", 2)
    near_a = trade(low_a, "dim", 1)
    near_b = trade(low_b, "dim", 1)
    if by_pieces:
        near_a, near_b, by[6], down_by = join(near_a, near_b, by[6], down_by)
        by[7] = trade(by[6], "tok", 1)
        down_by[1] = by[1]
        down_by[6] = trade(down_by[4], "tok", 2)
        near_a, far_a, by[7], down_by = join(near_a, far_a, by[7], down_by)
        down_by[3] = trade(down_by[2], "tok", 1)
        down_by[5] = trade(down_by[4], "tok", 1)
        up_pieces, gate_pieces = [[(by[o], None, k) for o in range(8)] for k in range(2)]
    near_a, far_a, low_b = join(near_a, far_a, low_b)
    far_b = trade(low_b, "dim", 2)
    corner_a = trade(far_a, "dim", 1)
    up_one, gate_one, mid_one, *assembled = expand(
        tok, [low_a, near_a, low_b, near_b], up_pieces, gate_pieces, unit_gains
    )
    if by_pieces:
        up_w, gate_w = assembled
        up_pieces, gate_pieces = [(up_w, None, 0)], [(gate_w, None, 0)]
        mid_one, down_by, corner_a = join(mid_one, down_by, corner_a)
        down_by[7] = trade(down_by[6], "tok", 1)
    seed_pair = trade(stack(seed_rows[1], seed_far[1]), "dim", 1)
    seed_pieces = [(seed_rows[0], None), (seed_pair, 0), (seed_far, 0), (seed_pair, 1)]
    up_a, gate_a, mid_a = expand(tok, [far_a, corner_a], up_pieces, gate_pieces, unit_gains)
    mid_a, far_b, seed_pair = join(mid_a, far_b, seed_pair)
    seed_pieces = [(seed_rows[0], None), (seed_pair, 0), (seed_far, 0), (seed_pair, 1)]
    corner_b = trade(far_b, "dim", 1)
    if by_pieces:
        mid_a, down_by = join(mid_a, down_by)
        down_pieces = [(down_by[o], None, 2 if o == 1 else 0) for o in range(8)]
        *parts_a, down_w = contract(tok, mid_a, 0, down_pieces, D)
        down_pieces = [(down_w, None, 0)]
    else:
        parts_a = contract(tok, mid_a, 0, down_pieces, D)
    came = trade(parts_a[1], "dim", 1)
    up_b, gate_b, mid_b = expand(tok, [far_b, corner_b], up_pieces, gate_pieces, unit_gains)
    mid_b, came = join(mid_b, came)
    across = add_low(parts_a[0], came).astype(BF16)
    across_a = trade(across, "dim", 2)
    parts_b = contract(tok, mid_b, 0, down_pieces, D, (across,))
    came = trade(parts_b[1], "dim", 1)
    own_a, pair_a = contract(tok, mid_one, 0, down_pieces, D, (parts_b[0],))
    own_a, came, parts_b, pair_a, across_a = join(own_a, came, parts_b, pair_a, across_a)
    across = add_low(parts_b[0], came).astype(BF16)
    across_b = trade(across, "dim", 2)
    pair_a = trade(pair_a, "dim", 1)
    own_b, pair_b = contract(tok, mid_one, 2, down_pieces, D, (own_a, across))
    own_b, pair_b, pair_a = join(own_b, pair_b, pair_a)
    *carry, delta_a, sum_a = turn(
        me, 0, own_a, pair_a, across_a, hidden_one, seed_pieces, pad_rows, alpha_gated
    )
    pair_b = trade(pair_b, "dim", 1)
    delta_a, across_b, pair_b, carry = join(delta_a, across_b, pair_b, carry)

    back_weights = (up_w, gate_w, down_w, unit_gains)
    b_far_a = trade(delta_a, "dim", 2)
    b_near_a = trade(delta_a, "dim", 1)
    layer_near, layer_far, delta_hidden, delta_b, sum_b = turn(
        me, 1, own_b, pair_b, across_b, hidden_one, seed_pieces, pad_rows, alpha_gated, carry
    )
    delta_b, b_near_a = join(delta_b, b_near_a)
    both_near_a, own_one, pair_one, unit_one = gated_back(
        delta_a, b_near_a, up_one, gate_one, 0, *back_weights
    )
    b_near_b = trade(delta_b, "dim", 1)
    own_one, b_far_a, delta_b, pair_one, b_near_b = join(own_one, b_far_a, delta_b, pair_one, b_near_b)
    b_far_b = trade(delta_b, "dim", 2)
    b_corner_a = trade(b_far_a, "dim", 1)
    pair_one = trade(pair_one, "dim", 1)
    both_near_b, own_two, pair_two, unit_two = gated_back(
        delta_b, b_near_b, up_one, gate_one, 2, *back_weights
    )
    own_two, b_corner_a, pair_one, pair_two, b_far_b = join(
        own_two, b_corner_a, pair_one, pair_two, b_far_b
    )
    pair_two = trade(pair_two, "dim", 1)
    b_corner_b = trade(b_far_b, "dim", 1)
    both_far_a, back_across_a, corner, unit_three = gated_back(
        b_far_a, b_corner_a, up_a, gate_a, 0, *back_weights
    )
    corner, pair_two, b_corner_b = join(corner, pair_two, b_corner_b)
    corner = trade(corner, "dim", 1)
    across = add_low(back_across_a, corner).astype(BF16)
    across, b_corner_b = join(across, b_corner_b)
    across_one = trade(across, "dim", 2)
    both_far_b, back_across_b, corner, unit_four = gated_back(
        b_far_b, b_corner_b, up_b, gate_b, 0, *back_weights
    )
    back_across_b, across_one = join(back_across_b, across_one)
    corner = trade(corner, "dim", 1)
    across = add_low(back_across_b, corner).astype(BF16)
    across_two = trade(across, "dim", 2)
    back_sums = [own_one, pair_one, across_one, own_two, pair_two, across_two]
    h_pieces = [low_a, near_a, low_b, near_b, far_a, corner_a, far_b, corner_b]
    b_pieces = [delta_a, b_near_a, delta_b, b_near_b, b_far_a, b_corner_a, b_far_b, b_corner_b]
    middles = [mid_one, mid_a, mid_b]
    both_pieces = [both_near_a, both_near_b, both_far_a, both_far_b]
    unit_sums = (unit_one + unit_two) + (unit_three + unit_four)
    sum_gated = sum_a + sum_b
    if by_pieces:
        down_parts = weight_grad(tok, groups, middles, b_pieces, SCALE_HIDDEN, needs=(across,))
        back_sums, down_parts, both_pieces, h_pieces = join(
            back_sums, down_parts, both_pieces, h_pieces
        )
        down_odd = trade(down_parts[3], "tok", 1)
    else:
        down_grad = plain_sum(
            jnp.concatenate(middles, axis=0), jnp.concatenate(b_pieces, axis=0), SCALE_HIDDEN
        )
        both_grad = plain_sum(
            jnp.concatenate(both_pieces, axis=0), jnp.concatenate(h_pieces, axis=0), SCALE_MODEL
        )

    delta_near, delta_far, mixer_low, delta_direct, sum_mixer = mixer_back(
        me,
        back_sums,
        delta_hidden,
        hidden_one,
        mixer_unit,
        one_factor,
        mixer_factor,
        tokens_all,
        alpha_mixer,
        out_weights,
    )
    if by_pieces:
        delta_far, mixer_low, down_odd, both_pieces = join(
            delta_far, mixer_low, down_odd, both_pieces
        )
        down_near = trade(add_low(down_parts[1], down_odd).astype(BF16), "tok", 2)
        down_even = trade(down_parts[2], "tok", 1)
        both_parts = weight_grad(
            tok, groups, both_pieces, h_pieces, SCALE_MODEL, halves=True, needs=(delta_far,)
        )
    delta_came = trade(delta_far, "dim", 2)
    out_near_grad, out_far_grad = out_grad(mixed_pieces, mixer_low)
    alpha_sums = jnp.concatenate([sum_mixer, sum_gated], axis=0)
    alpha_near = trade(alpha_sums, "dim", 1)
    if by_pieces:
        delta_came, out_near_grad, out_far_grad, both_parts, alpha_near, layer_far = join(
            delta_came, out_near_grad, out_far_grad, both_parts, alpha_near, layer_far
        )
        delta_came, down_near, down_even = join(delta_came, down_near, down_even)
    delta_pair = trade(stack(delta_near[1], delta_came[1]), "dim", 1)
    out_pair = trade(stack(out_near_grad[1], out_far_grad[1]), "dim", 1)
    alpha_sums = alpha_sums + alpha_near
    delta_pair, out_pair = join(delta_pair, out_pair)
    if by_pieces:
        both_even, both_odd, *even_send, odd_send = both_parts
        odd_came = trade(odd_send, "tok", 1)
        up_even = trade(even_send[0], "tok", 1)
        down_low = add_low(down_parts[0][1], down_even[1], down_near[1]).astype(BF16)
        down_last = trade(down_low, "tok", 4)
    layer_came = trade(layer_far, "dim", 2)
    out_far_sum = trade(add_low(out_far_grad[0], out_pair[1]).astype(BF16), "dim", 2)
    delta_pieces = [(delta_near, 0), (delta_pair, 0), (delta_came, 0), (delta_pair, 1)]
    delta_project, scale_sum = attend_back(
        length_row,
        me,
        pad_row,
        queries,
        keys,
        values,
        raw,
        score_gain,
        [near_aux, far_aux],
        [near_mixed, far_mixed],
        delta_pieces,
    )
    delta_project, alpha_sums, out_far_sum, layer_came = join(
        delta_project, alpha_sums, out_far_sum, layer_came
    )
    alpha_far = trade(alpha_sums, "dim", 2)
    if by_pieces:
        delta_project, odd_came, up_even, down_last = join(
            delta_project, odd_came, up_even, down_last
        )
        gate_even = trade(even_send[1], "tok", 1)
        halves = [slice(k * hidden_here, (k + 1) * hidden_here) for k in range(2)]
        up_odd, gate_odd = [
            add_low(both_odd[:, here], odd_came[:, here]).astype(BF16) for here in halves
        ]
        up_near = trade(up_odd, "tok", 2)
        in_parts = weight_grad(
            tok,
            groups,
            (delta_project,),
            (tokens_all,),
            SCALE_MODEL,
            ((out_near_grad, 0), (out_pair, 0), (out_far_sum, None)),
            needs=(up_odd, gate_odd),
        )
        in_parts, alpha_far, layer_near, up_near, gate_even, gate_odd = join(
            in_parts, alpha_far, layer_near, up_near, gate_even, gate_odd
        )
        in_odd = trade(in_parts[3], "tok", 1)
        gate_near = trade(gate_odd, "tok", 2)
        up_low = add_low(both_even[1, halves[0]], up_even[1], up_near[1]).astype(BF16)
        up_last = trade(up_low, "tok", 4)
    alpha_sums = lax.dynamic_slice_in_dim(alpha_sums + alpha_far, place * width, width, 1)
    gains_sum = jnp.concatenate(
        [scale_sum.reshape(-1), alpha_sums.reshape(-1), unit_sums.reshape(-1)]
    )
    input_parts = project_back(
        me, parts, delta_project, weight_in, delta_direct, (in_parts[3],) if by_pieces else ()
    )
    if by_pieces:
        input_parts, in_odd, in_parts, up_last, gate_near = join(
            input_parts, in_odd, in_parts, up_last, gate_near
        )
        gate_low = add_low(both_even[1, halves[1]], gate_even[1], gate_near[1]).astype(BF16)
        in_low = add_low(in_parts[1], in_odd).astype(BF16)
        in_near = trade(in_low, "tok", 2)
        in_even = trade(in_parts[2], "tok", 1)
        gate_last = trade(gate_low, "tok", 4)
    corner = trade(input_parts[3], "dim", 1)
    near = trade(input_parts[1], "dim", 1)
    half = token_count // 2
    across = [
        add_low(input_parts[2][k * half : (k + 1) * half], corner[k * half : (k + 1) * half])
        for k in range(2)
    ]
    far_one = trade(across[0].astype(BF16), "dim", 2)
    across_two = across[1].astype(BF16)
    if by_pieces:
        far_one, near, across_two, gate_last, in_near, in_even = join(
            far_one, near, across_two, gate_last, in_near, in_even
        )
    far_two = trade(across_two, "dim", 2)
    layer_pair = trade(stack(layer_near[1], layer_came[1]), "dim", 1)
    layer_pieces = [layer_near[0], layer_pair[0], layer_came[0], layer_pair[1]]
    layer_out = jnp.zeros((token_count, width), BF16)
    for r, piece in enumerate(layer_pieces):
        layer_out = lax.dynamic_update_slice(layer_out, piece, ((place ^ r) * own_count, 0))
    if by_pieces:
        in_low = add_low(in_parts[0][1], in_even[1], in_near[1]).astype(BF16)
        in_last = trade(in_low, "tok", 4)
        down_grad = add_low(down_parts[0][0], down_even[0], down_near[0], down_last)
        up_grad = add_low(both_even[0, halves[0]], up_even[0], up_near[0], up_last)
        gate_grad = add_low(both_even[0, halves[1]], gate_even[0], gate_near[0], gate_last)
        both_grad = jnp.concatenate([up_grad, gate_grad], axis=0)
    gated_grad = jnp.concatenate([both_grad, down_grad], axis=0).reshape(3, hidden_here, -1)
    fix_first = 1.0 - BETA_ONE**STEP
    fix_second = 1.0 - BETA_TWO**STEP
    gated_stepped, moment_gated, square_gated = moment_update(
        gated_weights, gated_grad, gated_moment, gated_square, fix_first, fix_second
    )
    gated_row_sums = jnp.sum(gated_stepped * gated_stepped, axis=2)
    gated_square_sum = jnp.sum(gated_grad * gated_grad)
    if by_pieces:
        in_last, gated_row_sums, gated_square_sum, layer_out, far_two = join(
            in_last, gated_row_sums, gated_square_sum, layer_out, far_two
        )
        in_total = add_low(in_parts[0][0], in_even[0], in_near[0], in_last)
        attention_grad = in_total.reshape(4, width, -1)
    else:
        out_total = lax.psum_scatter(
            add_low(out_near_grad[0], out_pair[0], out_far_sum).astype(BF16),
            "tok",
            scatter_dimension=1,
            tiled=True,
        ).astype(F32)
        in_total = plain_sum(delta_project, tokens_all, SCALE_MODEL)
        attention_grad = jnp.concatenate([in_total, out_total], axis=0).reshape(4, width, -1)

    input_gradient = add_low(input_parts[0], near, jnp.concatenate([far_one, far_two], axis=0))

    attention_stepped, moment_attention, square_attention = moment_update(
        attention_weights, attention_grad, attention_moment, attention_square, fix_first, fix_second
    )
    sums = sum_over(
        jnp.concatenate(
            [
                jnp.sum(attention_stepped * attention_stepped, axis=2).reshape(-1),
                gated_row_sums.reshape(-1),
                gains_sum,
                (jnp.sum(attention_grad * attention_grad) + gated_square_sum).reshape(1),
            ]
        ),
        "tok",
    )
    ends = [4 * width, 4 * width + 3 * hidden_here, 7 * width + 3 * hidden_here]
    model_grad = sums[ends[1] : ends[2]].reshape(3, width)
    unit_grad = sums[ends[2] : -1].reshape(2, hidden_here)
    model_next, moment_model, square_model = moment_update(
        model_gains, model_grad, model_moment, model_square, fix_first, fix_second
    )
    unit_next, moment_unit, square_unit = moment_update(
        unit_gains, unit_grad, unit_moment, unit_square, fix_first, fix_second
    )
    square_sum = sums[-1:] + jnp.sum(model_grad * model_grad) + jnp.sum(unit_grad * unit_grad)
    totals = sum_over(jnp.concatenate([square_sum, jnp.sum(model_next[1:], axis=1)]), "dim")
    attention_rows = sums[: ends[0]].reshape(4, width, 1)
    gated_rows = sums[ends[0] : ends[1]].reshape(3, hidden_here, 1)
    attention_next = attention_stepped * lax.rsqrt(attention_rows / D + EPSILON)
    gated_next = gated_stepped * lax.rsqrt(gated_rows / D + EPSILON)
    gradient_norm = jnp.sqrt(totals[:1])
    mean_alpha = totals[1:] / D
    return (
        layer_out,
        input_gradient,
        attention_next,
        attention_next.astype(BF16),
        moment_attention,
        square_attention,
        gated_next,
        gated_next.astype(BF16),
        moment_gated,
        square_gated,
        model_next,
        moment_model,
        square_model,
        unit_next,
        moment_unit,
        square_unit,
        gradient_norm,
        mean_alpha,
    )


def solution(mesh):
    tokens = P("tok", "dim")
    weights = P(None, "dim", "tok")
    gains = P(None, "dim")
    in_specs = (tokens, tokens, P("tok", None), P("tok"), weights, weights, gains, gains)
    in_specs += (weights,) * 4 + (gains,) * 4
    out_specs = (tokens, tokens) + (weights,) * 8 + (gains,) * 6 + (P(), P())
    return jax.shard_map(local, mesh=mesh, in_specs=in_specs, out_specs=out_specs, check_vma=False)
```

```python
import functools
import math

import jax
import jax.numpy as jnp
from jax import lax
from jax.experimental import pallas as pl
from jax.experimental.pallas import tpu as pltpu
from jax.sharding import PartitionSpec as P

D = 1024
HEAD = 64
FF = 4096
STEP = 4
BLK = 256

EPSILON = 1e-06
ADAM_EPSILON = 1e-08
BETA_ONE = 0.5
BETA_TWO = 0.5
LEARN_RATE = 1.5

F32 = jnp.float32
BF16 = jnp.bfloat16
SCALE_MODEL = D**-0.5
SCALE_HIDDEN = FF**-0.5
SCORE = HEAD**-0.5 * math.log2(math.e)
NEVER = 1 << 24


def dot_nt(left, right):
    return lax.dot_general(left, right, (((1,), (1,)), ((), ())), preferred_element_type=F32)


def dot_nn(left, right):
    return lax.dot_general(left, right, (((1,), (0,)), ((), ())), preferred_element_type=F32)


def split_low(values):
    high = values.astype(BF16)
    return high, (values - high.astype(F32)).astype(BF16)


def params():
    return pltpu.CompilerParams(vmem_limit_bytes=60 << 20)


def cost(flops, traffic, transcendentals=0):
    return pl.CostEstimate(
        flops=int(flops) // 64, bytes_accessed=int(traffic) // 64, transcendentals=int(transcendentals) // 64
    )


def like(shape, dtype):
    return jax.ShapeDtypeStruct(shape, dtype)


def whole(*shape):
    return pl.BlockSpec(shape, lambda *_: (0,) * len(shape))


def rows(count, width):
    return pl.BlockSpec((count, width), lambda i, *_: (i, 0))


def launch(kernel, needs, scalars, grid, in_specs, args, scratch_shapes=(), **options):
    taken = len(scalars) + len(args)

    def body(*refs):
        kernel(*refs[:taken], *refs[taken + len(needs) :])

    return pl.pallas_call(
        body,
        grid_spec=pltpu.PrefetchScalarGridSpec(
            num_scalar_prefetch=len(scalars),
            grid=grid,
            in_specs=[*in_specs] + [pl.BlockSpec(memory_space=pl.ANY)] * len(needs),
            out_specs=options.pop("out_specs"),
            scratch_shapes=scratch_shapes,
        ),
        compiler_params=params(),
        **options,
    )(*scalars, *args, *needs)


def head_matrix(width):
    row = lax.broadcasted_iota(jnp.int32, (width, width), 0)
    column = lax.broadcasted_iota(jnp.int32, (width, width), 1)
    return jnp.where(row // HEAD == column // HEAD, 1.0, 0.0).astype(BF16)


def head_mean(values, ones):
    return dot_nn(values.astype(BF16), ones) * (1.0 / HEAD)


def head_mean_fine(values, ones):
    high, low = split_low(values)
    return (dot_nn(high, ones) + dot_nn(low, ones)) * (1.0 / HEAD)


def project_kernel(pieces, me_ref, tok_ref, *refs):
    piece_refs = refs[:pieces]
    weight_refs = refs[pieces:-7]
    gain_ref, all_ref, raw_ref, q_ref, k_ref, v_ref, w_ref = refs[-7:]
    width = piece_refs[0].shape[1]
    if len(weight_refs) == 1:
        weight = weight_refs[0]
    else:
        weight = w_ref

        @pl.when(pl.program_id(0) == 0)
        def assemble_weight():
            place_columns(tok_ref[0], weight_refs, w_ref)

    place_columns(me_ref[0], piece_refs, all_ref)
    projected = dot_nt(all_ref[...], weight[...]) * SCALE_MODEL
    if weight is not w_ref:
        w_ref[...] = weight[...]
    raw_ref[...] = projected[:, : 2 * width]
    ones = head_matrix(width)
    for place, out in enumerate((q_ref, k_ref)):
        values = projected[:, place * width : (place + 1) * width]
        factor = lax.rsqrt(head_mean_fine(values * values, ones) + EPSILON)
        out[...] = (values * factor * gain_ref[...]).astype(BF16)
    v_ref[...] = projected[:, 2 * width :].astype(BF16)


def place_columns(index, piece_refs, out_ref):
    width = piece_refs[0].shape[1]
    for offset, piece in enumerate(piece_refs):
        start = pl.multiple_of(jnp.bitwise_xor(index, offset) * width, width)
        out_ref[:, pl.ds(start, width)] = piece[...]


def piece_spec(piece, height, step):
    array, lead, block = piece
    width = array.shape[-1]
    if lead is None:
        return pl.BlockSpec((height, width), lambda i, *_: (block + step * i, 0))
    return pl.BlockSpec((None, height, width), lambda i, *_: (lead, block + step * i, 0))


def project(me, tok, pieces, weights, gain):
    count, width = pieces[0].shape
    depth = width * len(pieces)
    return pl.pallas_call(
        functools.partial(project_kernel, len(pieces)),
        grid_spec=pltpu.PrefetchScalarGridSpec(
            num_scalar_prefetch=2,
            grid=(count // BLK,),
            in_specs=[rows(BLK, width)] * len(pieces)
            + [piece_spec(weight, 3 * width, 0) for weight in weights]
            + [whole(1, width)],
            out_specs=[rows(BLK, depth), rows(BLK, 2 * width)]
            + [rows(BLK, width)] * 3
            + [whole(3 * width, depth)],
        ),
        out_shape=[like((count, depth), BF16), like((count, 2 * width), F32)]
        + [like((count, width), BF16)] * 3
        + [like((3 * width, depth), BF16)],
        compiler_params=params(),
        cost_estimate=cost(6 * count * width * depth, count * (4 * depth + 14 * width)),
        name="project",
    )(me, tok, *pieces, *[weight[0] for weight in weights], gain)


def assemble_kernel(tok_ref, *refs):
    place_columns(tok_ref[0], refs[:-1], refs[-1])


def assemble(tok, pieces, count, needs=()):
    width = pieces[0][0].shape[-1]
    depth = width * len(pieces)
    return launch(
        assemble_kernel,
        needs,
        (tok,),
        (count // BLK,),
        [piece_spec(piece, BLK, 1) for piece in pieces],
        (*[piece[0] for piece in pieces],),
        out_specs=rows(BLK, depth),
        out_shape=like((count, depth), BF16),
        cost_estimate=cost(0, 4 * count * depth),
        name="assemble",
    )


def seq_start(place, starts):
    found = jnp.zeros_like(place)
    for start in starts:
        found = jnp.where(place >= start, start, found)
    return found


def later_starts(length_ref, count):
    starts, total = [], jnp.int32(0)
    for position in range(count - 1):
        total = total + length_ref[position]
        starts.append(total)
    return starts


def attend_kernel(count, order, blocks, length_ref, me_ref, pad_ref, q_ref, k_ref, v_ref, *refs):
    mixed_ref, aux_ref, acc_ref = refs
    grid_step = pl.program_id(0)
    step = block_of(order, blocks, grid_step, me_ref)
    first_row = step * BLK
    starts = later_starts(length_ref, count)
    first = seq_start(first_row, starts) // BLK
    lane = lax.broadcasted_iota(jnp.int32, (BLK, 128), 1)
    left = lane < HEAD
    heads = q_ref.shape[1] // HEAD
    zero = jnp.zeros((BLK, 128), BF16)
    one = jnp.ones((BLK, 128), BF16)
    sides = [left if head % 2 == 0 else ~left for head in range(heads)]
    columns = [slice(head // 2 * 128, (head // 2 + 1) * 128) for head in range(heads)]
    queries = [jnp.where(sides[h], q_ref[:, columns[h]], zero) for h in range(heads)]
    acc_ref[...] = jnp.zeros_like(acc_ref)
    row = first_row + lax.broadcasted_iota(jnp.int32, (BLK, 1), 0)
    row_start = seq_start(row, starts)

    def body(block, carry):
        key_rows = pl.ds(pl.multiple_of(block * BLK, BLK), BLK)
        key = block * BLK + lax.broadcasted_iota(jnp.int32, (1, BLK), 1)
        code = jnp.where(pad_ref[:, key_rows] == 1, key, NEVER)
        mask = ((code >= row_start) & (code <= row)) | (key == row)
        for h in range(heads):
            value = jnp.where(sides[h], v_ref[key_rows, columns[h]], one)
            scores = dot_nt(queries[h], k_ref[key_rows, columns[h]])
            powers = jnp.where(mask, jnp.exp2(scores * SCORE), 0.0).astype(BF16)
            acc_ref[h] += dot_nn(powers, value)
        return carry

    lax.fori_loop(first, step + 1, body, 0)
    for pair in range(heads // 2):
        tile = slice(pair * 128, (pair + 1) * 128)
        even, odd = acc_ref[2 * pair], acc_ref[2 * pair + 1]
        total = jnp.where(left, odd, even)
        mixed = jnp.where(left, even, odd)
        mixed_ref[:, tile] = (mixed / pltpu.roll(total, HEAD, 1)).astype(BF16)
        high, low = split_low(jnp.log2(total) * (-1.0 / SCORE))
        aux_ref[:, tile] = jnp.where(lax.rem(lane, HEAD) < HEAD // 2, high, low)


def block_of(order, blocks, grid_step, me_ref):
    offset = order[0] + grid_step // blocks
    return jnp.bitwise_xor(me_ref[0], offset) * blocks + lax.rem(grid_step, blocks)


def piece_rows(blocks, place, width):
    return pl.BlockSpec(
        (BLK, width), lambda i, *_: (jnp.clip(i - place * blocks, 0, blocks - 1), 0)
    )


def attend(lengths, me, order, blocks, pad_row, queries, keys, values, needs=()):
    count, width = queries.shape
    heads = width // HEAD
    return launch(
        functools.partial(attend_kernel, lengths.shape[0], order, blocks),
        needs,
        (lengths, me,),
        (blocks * len(order),),
        [
                whole(1, count),
                pl.BlockSpec(
                    (BLK, width), lambda i, l_ref, me_ref: (block_of(order, blocks, i, me_ref), 0)
                ),
                whole(count, width),
                whole(count, width),
            ],
        (pad_row, queries, keys, values,),
        scratch_shapes=[pltpu.VMEM((heads, BLK, 128), F32)],
        out_specs=[rows(BLK, width)] * 2,
        out_shape=[like((len(order) * blocks * BLK, width), BF16)] * 2,
        cost_estimate=cost(2 * count * count * width, 6 * count * width, count * count * heads // 6),
        name="attend",
    )


def attend_back_kernel(
    count, pieces, length_ref, me_ref, pad_ref, q_ref, k_ref, v_ref, raw_ref, gain_ref, *refs
):
    pairs = pieces // 2
    aux_refs, mixed_refs, delta_refs = (
        refs[:pairs],
        refs[pairs : 2 * pairs],
        refs[2 * pairs : 2 * pairs + pieces],
    )
    low_ref, scale_sum, dqt_ref, do_ref, inner_ref, aux_ref, key_acc, value_acc = refs[
        2 * pairs + pieces :
    ]
    step = pl.program_id(0)
    tokens, width = q_ref.shape
    heads = width // HEAD
    starts = later_starts(length_ref, count)
    lane = lax.broadcasted_iota(jnp.int32, (BLK, 128), 1)
    left = lane < HEAD
    zero = jnp.zeros((BLK, 128), BF16)
    one = jnp.ones((BLK, 128), BF16)
    sides = [left if head % 2 == 0 else ~left for head in range(heads)]
    columns = [slice(head // 2 * 128, (head // 2 + 1) * 128) for head in range(heads)]

    @pl.when(step == 0)
    def prepare():
        dqt_ref[...] = jnp.zeros_like(dqt_ref)
        scale_sum[...] = jnp.zeros_like(scale_sum)
        part = tokens // pieces
        row = lax.broadcasted_iota(jnp.int32, (128, 128), 0)
        column = lax.broadcasted_iota(jnp.int32, (128, 128), 1)
        other = jnp.where(row // HEAD != column // HEAD, 1.0, 0.0).astype(BF16)
        for place in range(pieces):
            first = jnp.bitwise_xor(me_ref[0], place) * part
            do_ref[pl.ds(pl.multiple_of(first, part), part), :] = delta_refs[place][...]
            base = place % 2 * part
            aux_ref[pl.ds(pl.multiple_of(first, part), part), :] = aux_refs[place // 2][
                base : base + part, :
            ]
            for block in range(part // BLK):
                source = slice(block * BLK, (block + 1) * BLK)
                here = pl.ds(pl.multiple_of(first + block * BLK, BLK), BLK)
                for pair in range(heads // 2):
                    tile = slice(pair * 128, (pair + 1) * 128)
                    high, low = split_low(
                        delta_refs[place][source, tile].astype(F32)
                        * mixed_refs[place // 2][
                            base + block * BLK : base + (block + 1) * BLK, tile
                        ].astype(F32)
                    )
                    high, low = split_low(-(dot_nn(high, other) + dot_nn(low, other)))
                    inner_ref[here, tile] = jnp.where(lax.rem(lane, HEAD) < HEAD // 2, high, low)

    key_rows = pl.ds(pl.multiple_of(step * BLK, BLK), BLK)
    last_key = step * BLK + BLK - 1
    end = jnp.int32(tokens)
    for start in reversed(starts):
        end = jnp.where(last_key < start, start, end)
    last = (end - 1) // BLK
    key_acc[...] = jnp.zeros_like(key_acc)
    value_acc[...] = jnp.zeros_like(value_acc)
    turned = jnp.transpose(k_ref[key_rows, :].astype(F32)).astype(BF16)
    keys, values = [], []
    for h in range(heads):
        hot = jnp.where((lax.rem(lane, HEAD // 2) == 0) & (~sides[h]), one, zero)
        for source, into in ((k_ref, keys), (v_ref, values)):
            tile = jnp.where(sides[h], source[key_rows, columns[h]], zero)
            into.append(jnp.concatenate([tile, hot], axis=1))
    key = step * BLK + lax.broadcasted_iota(jnp.int32, (BLK, 1), 0)
    padding = jnp.transpose(
        jnp.broadcast_to(pad_ref[:, key_rows].astype(F32), (128, BLK))
    )[:, :1]
    code = jnp.where(padding > 0.5, key, NEVER)

    def body(block, carry):
        here = pl.ds(pl.multiple_of(block * BLK, BLK), BLK)
        row = block * BLK + lax.broadcasted_iota(jnp.int32, (1, BLK), 1)
        mask = ((code >= seq_start(row, starts)) & (code <= row)) | (key == row)
        for h in range(heads):
            query, delta = q_ref[here, columns[h]], do_ref[here, columns[h]]
            scores = dot_nt(keys[h], jnp.concatenate([query, aux_ref[here, columns[h]]], axis=1))
            delta_probs = dot_nt(
                values[h], jnp.concatenate([delta, inner_ref[here, columns[h]]], axis=1)
            )
            probs = jnp.where(mask, jnp.exp2(scores * SCORE), 0.0)
            delta_scores = (probs * delta_probs).astype(BF16)
            value_acc[h] += dot_nn(probs.astype(BF16), delta)
            key_acc[h] += dot_nn(delta_scores, query)
            head_rows = slice(h * HEAD, (h + 1) * HEAD)
            dqt_ref[head_rows, here] += dot_nn(turned[head_rows, :], delta_scores)
        return carry

    lax.fori_loop(step, last + 1, body, 0)
    key_tiles, value_tiles = [
        [jnp.where(left, acc[2 * pair], acc[2 * pair + 1]) for pair in range(heads // 2)]
        for acc in (key_acc, value_acc)
    ]
    ones = head_matrix(width)
    gain = gain_ref[...]
    deltas = (jnp.transpose(dqt_ref[:, key_rows]), jnp.concatenate(key_tiles, axis=1))
    for place, delta in enumerate(deltas):
        here = slice(place * width, (place + 1) * width)
        raw = raw_ref[:, here]
        factor = lax.rsqrt(head_mean(raw * raw, ones) + EPSILON)
        unit = raw * factor
        delta = delta * HEAD**-0.5
        scale_sum[...] += jnp.sum(delta * unit, axis=0, keepdims=True)
        delta = gain * delta
        low_ref[:, here] = (factor * (delta - unit * head_mean(delta * unit, ones))).astype(BF16)
    low_ref[:, 2 * width :] = jnp.concatenate(value_tiles, axis=1).astype(BF16)


def attend_back(lengths, me, pad_row, queries, keys, values, raw, gain, aux_pieces, mixed_pieces, delta_pieces):
    count, width = queries.shape
    heads = width // HEAD
    pieces = len(delta_pieces)
    return pl.pallas_call(
        functools.partial(attend_back_kernel, lengths.shape[0], pieces),
        grid_spec=pltpu.PrefetchScalarGridSpec(
            num_scalar_prefetch=2,
            grid=(count // BLK,),
            in_specs=[whole(1, count)]
            + [whole(count, width)] * 3
            + [rows(BLK, 2 * width), whole(1, width)]
            + [whole(2 * count // pieces, width)] * pieces
            + [piece_spec((array, lead, 0), count // pieces, 0) for array, lead in delta_pieces],
            out_specs=[rows(BLK, 3 * width), whole(1, width)],
            scratch_shapes=[
                pltpu.VMEM((width, count), F32),
                pltpu.VMEM((count, width), BF16),
                pltpu.VMEM((count, width), BF16),
                pltpu.VMEM((count, width), BF16),
                pltpu.VMEM((heads, BLK, 128), F32),
                pltpu.VMEM((heads, BLK, 128), F32),
            ],
        ),
        out_shape=[like((count, 3 * width), BF16), like((1, width), F32)],
        compiler_params=params(),
        cost_estimate=cost(8 * count * count * width, 22 * count * width, count * count * heads // 3),
        name="attend_back",
    )(lengths, me, pad_row, queries, keys, values, raw, gain, *aux_pieces, *mixed_pieces, *[array for array, lead in delta_pieces])


def unit_of(values):
    factor = lax.rsqrt(jnp.mean(values * values, axis=1, keepdims=True) + EPSILON)
    return values * factor, factor


def unit_back(delta, unit, factor):
    return factor * (delta - unit * jnp.mean(delta * unit, axis=1, keepdims=True))


def mixer_kernel(pieces, *refs):
    mixed_refs, out_weights = refs[:pieces], refs[pieces : 2 * pieces]
    tokens_ref, alpha_ref, *low_refs, one_ref, unit_ref, unit_factor, one_factor = refs[2 * pieces :]
    branch = dot_nn(mixed_refs[0][...], out_weights[0][...])
    for mixed, weight in zip(mixed_refs[1:], out_weights[1:]):
        branch += dot_nn(mixed[...], weight[...])
    unit, factor = unit_of(branch * SCALE_MODEL)
    unit_ref[...] = unit
    unit_factor[...] = jnp.broadcast_to(factor, unit_factor.shape)
    residual = tokens_ref[...].astype(F32)
    hidden, factor = unit_of(residual + alpha_ref[...] * (unit - residual))
    one_ref[...] = hidden
    one_factor[...] = jnp.broadcast_to(factor, one_factor.shape)
    put(1, hidden.astype(BF16), *low_refs)


def mixer(mixed_pieces, out_weights, me, tokens_all, alpha):
    width = mixed_pieces[0][0].shape[-1]
    pieces = len(mixed_pieces)
    count = tokens_all.shape[0] // pieces
    depth = tokens_all.shape[1]
    blocks = count // BLK
    kernel = functools.partial(mixer_kernel, pieces)
    return pl.pallas_call(
        lambda me_ref, *refs: kernel(*refs),
        grid_spec=pltpu.PrefetchScalarGridSpec(
            num_scalar_prefetch=1,
            grid=(blocks,),
            in_specs=[piece_spec((array, lead, 0), BLK, 1) for array, lead in mixed_pieces]
            + [piece_spec((array, lead, 0), width, 0) for array, lead in out_weights]
            + [
                pl.BlockSpec((BLK, depth), lambda i, me_ref: (me_ref[0] * blocks + i, 0)),
                whole(1, depth),
            ],
            out_specs=[piece_rows(1, 0, depth), piece_rows(1, 1, depth)]
            + [rows(BLK, depth)] * 2
            + [rows(BLK, 128)] * 2,
        ),
        out_shape=[like((BLK, depth), BF16)] * 2
        + [like((count, depth), F32)] * 2
        + [like((count, 128), F32)] * 2,
        compiler_params=params(),
        cost_estimate=cost(2 * count * depth * depth, 16 * count * depth + 2 * depth * depth),
        name="mixer",
    )(me, *[p[0] for p in mixed_pieces], *[w[0] for w in out_weights], tokens_all, alpha)


def turn_kernel(pieces, carried, me_ref, *refs):
    own_ref, near_ref, far_ref, one_ref = refs[:4]
    seed_refs = refs[4 : 4 + pieces]
    pad_ref, alpha_ref = refs[4 + pieces : 6 + pieces]
    outs = refs[6 + pieces + carried :]
    pair_refs = outs[: pieces // 2]
    hidden_ref, low_ref, alpha_sum, seed, layer = outs[pieces // 2 :]
    width = seed_refs[0].shape[-1]
    starts = [
        pl.multiple_of(jnp.bitwise_xor(me_ref[0], place) * width, width) for place in range(pieces)
    ]
    for start, piece in zip(starts, seed_refs):
        seed[:, pl.ds(start, width)] = piece[...]
    branch = (own_ref[...].astype(F32) + near_ref[...].astype(F32)) + far_ref[...].astype(F32)
    unit, unit_factor = unit_of(branch)
    hidden = one_ref[...]
    alpha = alpha_ref[...]
    layer_rows, layer_factor = unit_of(hidden + alpha * (unit - hidden))
    layer[...] = layer_rows.astype(BF16)
    for offset, start in enumerate(starts):
        pair_refs[offset // 2][offset % 2] = layer[:, pl.ds(start, width)]
    delta = unit_back(seed[...].astype(F32) * pad_ref[...], layer_rows, layer_factor)
    alpha_sum[...] = jnp.sum(delta * (unit - hidden), axis=0, keepdims=True)
    hidden_ref[...] = (1.0 - alpha) * delta
    low_ref[...] = unit_back(alpha * delta, unit, unit_factor).astype(BF16)


def turn(me, half, own, near, far, hidden_one, seed_pieces, pad_rows, alpha, carry=()):
    count, depth = hidden_one.shape
    pieces = len(seed_pieces)
    width = depth // pieces
    here = pl.BlockSpec((BLK, depth), lambda i, *_: (half, 0))
    pair = pl.BlockSpec((2, BLK, width), lambda i, *_: (0, half, 0))
    return pl.pallas_call(
        functools.partial(turn_kernel, pieces, len(carry)),
        grid_spec=pltpu.PrefetchScalarGridSpec(
            num_scalar_prefetch=1,
            grid=(1,),
            in_specs=[whole(BLK, depth)] * 3
            + [here]
            + [piece_spec((array, lead, half), BLK, 0) for array, lead in seed_pieces]
            + [pl.BlockSpec((BLK, 1), lambda i, *_: (half, 0)), whole(1, depth)]
            + [pl.BlockSpec(memory_space=pl.ANY)] * len(carry),
            out_specs=[pair] * (pieces // 2) + [here, whole(BLK, depth), whole(1, depth)],
            scratch_shapes=[pltpu.VMEM((BLK, depth), BF16)] * 2,
        ),
        out_shape=[like((2, count, width), BF16)] * (pieces // 2)
        + [like((count, depth), F32), like((BLK, depth), BF16), like((1, depth), F32)],
        input_output_aliases={7 + pieces + k: k for k in range(len(carry))},
        compiler_params=params(),
        cost_estimate=cost(40 * count * depth, 20 * count * depth),
        name="turn",
    )(
        me, own, near, far, hidden_one, *[p[0] for p in seed_pieces], pad_rows, alpha, *carry
    )


def mixer_back_kernel(pieces, *refs):
    halves, (hidden_ref, one_ref, unit_ref) = (refs[:6:2], refs[1:6:2]), refs[6:9]
    one_factor, unit_factor, tokens_ref, alpha_ref = refs[9:13]
    out_weights = refs[13 : 13 + pieces]
    pair_refs = refs[13 + pieces : 13 + pieces + pieces // 2]
    low_ref, direct_ref, alpha_sum = refs[13 + pieces + pieces // 2 :]
    own, near, far = [
        jnp.where(pl.program_id(0) < pl.num_programs(0) // 2, first[...].astype(F32), second[...].astype(F32))
        for first, second in zip(*halves)
    ]

    @pl.when(pl.program_id(0) == 0)
    def clear():
        alpha_sum[...] = jnp.zeros_like(alpha_sum)

    delta = hidden_ref[...] + ((own + near) + far)
    unit = unit_ref[...]
    alpha = alpha_ref[...]
    delta = unit_back(delta, one_ref[...], one_factor[:, :1])
    alpha_sum[...] += jnp.sum(delta * (unit - tokens_ref[...].astype(F32)), axis=0, keepdims=True)
    direct_ref[...] = (1.0 - alpha) * delta
    low = unit_back(alpha * delta, unit, unit_factor[:, :1]).astype(BF16)
    low_ref[...] = low
    for offset, weight in enumerate(out_weights):
        pair_refs[offset // 2][offset % 2] = (dot_nt(low, weight[...]) * SCALE_MODEL).astype(BF16)


def mixer_back(
    me, sums, hidden, one, unit, one_factor, unit_factor, tokens_all, alpha, out_weights
):
    count, depth = one.shape
    pieces = len(out_weights)
    width = depth // pieces
    block = BLK
    blocks = count // block
    half = blocks // 2
    kernel = functools.partial(mixer_back_kernel, pieces)
    return pl.pallas_call(
        lambda me_ref, *refs: kernel(*refs),
        grid_spec=pltpu.PrefetchScalarGridSpec(
            num_scalar_prefetch=1,
            grid=(blocks,),
            in_specs=[
                pl.BlockSpec((block, depth), lambda i, *_: (jnp.minimum(i, half - 1), 0)),
                pl.BlockSpec((block, depth), lambda i, *_: (jnp.maximum(i - half, 0), 0)),
            ]
            * 3
            + [rows(block, depth)] * 3
            + [rows(block, 128)] * 2
            + [
                pl.BlockSpec((block, depth), lambda i, me_ref: (me_ref[0] * blocks + i, 0)),
                whole(1, depth),
            ]
            + [piece_spec((array, lead, 0), width, 0) for array, lead in out_weights],
            out_specs=[pl.BlockSpec((2, block, width), lambda i, *_: (0, i, 0))] * (pieces // 2)
            + [rows(block, depth), rows(block, depth), whole(1, depth)],
        ),
        out_shape=[like((2, count, width), BF16)] * (pieces // 2)
        + [like((count, depth), BF16), like((count, depth), F32), like((1, depth), F32)],
        compiler_params=params(),
        cost_estimate=cost(2 * count * depth * depth, 28 * count * depth + 2 * depth * depth),
        name="mixer_back",
    )(
        me,
        *[value for pair in zip(sums[:3], sums[3:]) for value in pair],
        hidden,
        one,
        unit,
        one_factor,
        unit_factor,
        tokens_all,
        alpha,
        *[w[0] for w in out_weights],
    )


def pick(half, first_ref, second_ref, out_ref):
    step = pl.program_id(0)

    @pl.when(step < half)
    def from_first():
        out_ref[...] = first_ref[...]

    @pl.when(step >= half)
    def from_second():
        out_ref[...] = second_ref[...]


def put(half, value, first_ref, second_ref):
    step = pl.program_id(0)

    @pl.when(step < half)
    def to_first():
        first_ref[...] = value

    @pl.when(step >= half)
    def to_second():
        second_ref[...] = value


def whole_weight(tok_ref, piece_refs, out_ref):
    if out_ref is None:
        return piece_refs[0]

    @pl.when(pl.program_id(0) == 0)
    def assemble_weight():
        place_columns(tok_ref[0], piece_refs, out_ref)

    return out_ref


def expand_kernel(count, pieces, tok_ref, *refs):
    block_refs, gain_ref, refs = refs[:count], refs[count], refs[count + 1 :]
    up_pieces, gate_pieces = refs[:pieces], refs[pieces : 2 * pieces]
    up_ref, gate_ref, mid_ref = refs[2 * pieces : 2 * pieces + 3]
    hidden_ref = refs[-1]
    outs = refs[2 * pieces + 3 : -1] or (None, None)
    up_w = whole_weight(tok_ref, up_pieces, outs[0])
    gate_w = whole_weight(tok_ref, gate_pieces, outs[1])
    for place, block_ref in enumerate(block_refs):

        @pl.when(pl.program_id(0) == place)
        def take(block_ref=block_ref):
            hidden_ref[...] = block_ref[...]

    hidden = hidden_ref[...]
    up = dot_nt(hidden, up_w[...]) * SCALE_MODEL
    gate = dot_nt(hidden, gate_w[...]) * SCALE_MODEL
    up_ref[...] = up.astype(BF16)
    gate_ref[...] = gate.astype(BF16)
    scaled = gain_ref[1:2, :] * gate
    mid_ref[...] = (gain_ref[0:1, :] * up * scaled * jax.nn.sigmoid(scaled)).astype(BF16)


def expand(tok, blocks_in, up_pieces, gate_pieces, gains):
    depth = blocks_in[0].shape[1]
    hidden = gains.shape[1]
    count = len(blocks_in)
    pieces = len(up_pieces)
    outs = 2 if pieces > 1 else 0
    return pl.pallas_call(
        functools.partial(expand_kernel, count, pieces),
        grid_spec=pltpu.PrefetchScalarGridSpec(
            num_scalar_prefetch=1,
            grid=(count,),
            in_specs=[whole(BLK, depth)] * count
            + [whole(2, hidden)]
            + [piece_spec(piece, hidden, 0) for piece in (*up_pieces, *gate_pieces)],
            out_specs=[rows(BLK, hidden)] * 3 + [whole(hidden, depth)] * outs,
            scratch_shapes=[pltpu.VMEM((BLK, depth), BF16)],
        ),
        out_shape=[like((count * BLK, hidden), BF16)] * 3 + [like((hidden, depth), BF16)] * outs,
        compiler_params=params(),
        cost_estimate=cost(4 * count * BLK * depth * hidden, 4 * depth * hidden),
        name="expand",
    )(tok, *blocks_in, gains, *[piece[0] for piece in (*up_pieces, *gate_pieces)])


def contract_kernel(pieces, tok_ref, mid_ref, *refs):
    first_ref, second_ref = refs[pieces : pieces + 2]
    outs = refs[pieces + 2 :] or (None,)
    down_w = whole_weight(tok_ref, refs[:pieces], outs[0])
    total = (dot_nn(mid_ref[...], down_w[...]) * SCALE_HIDDEN).astype(BF16)
    first_ref[...] = total[:BLK]
    second_ref[...] = total[BLK:]


def contract(tok, middle, first_block, down_pieces, depth, needs=()):
    hidden = middle.shape[1]
    count = 2 * BLK
    pieces = len(down_pieces)
    outs = 1 if pieces > 1 else 0
    return launch(
        functools.partial(contract_kernel, pieces),
        needs,
        (tok,),
        (1,),
        [pl.BlockSpec((2 * BLK, hidden), lambda i, *_: (first_block // 2, 0))] + [piece_spec(piece, hidden, 0) for piece in down_pieces],
        (middle, *[piece[0] for piece in down_pieces],),
        out_specs=[whole(BLK, depth), whole(BLK, depth)]
            + [whole(hidden, depth)] * outs,
        out_shape=[like((count // 2, depth), BF16)] * 2 + [like((hidden, depth), BF16)] * outs,
        cost_estimate=cost(
            2 * count * depth * hidden, 2 * count * (depth + hidden) + 2 * depth * hidden
        ),
        name="contract",
    )


def gated_back_kernel(
    up_from,
    gate_from,
    down_from,
    first_ref,
    second_ref,
    up_ref,
    gate_ref,
    gain_ref,
    both_ref,
    first_out,
    second_out,
    unit_ref,
    delta_ref,
    down_w,
    up_w,
    gate_w,
    arrived,
):
    copies = [
        pltpu.make_async_copy(source, into, arrived.at[k])
        for k, (source, into) in enumerate(
            ((down_from, down_w), (up_from, up_w), (gate_from, gate_w))
        )
    ]
    for copy in copies:
        copy.start()
    count = first_ref.shape[0]
    delta_ref[:count, :] = first_ref[...]
    delta_ref[count:, :] = second_ref[...]
    copies[0].wait()
    hidden = up_w.shape[0]
    part = hidden // 2
    total = None
    for start in range(0, hidden, part):
        here = slice(start, start + part)
        delta_middle = dot_nt(delta_ref[...], down_w[here, :]) * SCALE_HIDDEN
        up = up_ref[:, here].astype(F32)
        gate = gate_ref[:, here].astype(F32)
        scaled = gain_ref[1:2, here] * gate
        sigmoid = jax.nn.sigmoid(scaled)
        shared = delta_middle * sigmoid
        delta_up = shared * scaled
        delta_gate = shared * (gain_ref[0:1, here] * up) * (1.0 + scaled * (1.0 - sigmoid))
        unit_ref[0:1, here] = jnp.sum(delta_up * up, axis=0, keepdims=True)
        unit_ref[1:2, here] = jnp.sum(delta_gate * gate, axis=0, keepdims=True)
        up_low = (gain_ref[0:1, here] * delta_up).astype(BF16)
        gate_low = (gain_ref[1:2, here] * delta_gate).astype(BF16)
        both_ref[:, here] = up_low
        both_ref[:, hidden + start : hidden + start + part] = gate_low
        if start == 0:
            copies[1].wait()
            copies[2].wait()
        term = dot_nn(up_low, up_w[here, :]) + dot_nn(gate_low, gate_w[here, :])
        total = term if total is None else total + term
    total = total * SCALE_MODEL
    first_out[...] = total[:count].astype(BF16)
    second_out[...] = total[count:].astype(BF16)


def gated_back(first, second, up, gate, first_block, up_w, gate_w, down_w, gains):
    count, depth = first.shape
    hidden = up_w.shape[0]
    here = pl.BlockSpec((2 * count, hidden), lambda i: (first_block * BLK // (2 * count), 0))
    return pl.pallas_call(
        gated_back_kernel,
        grid=(1,),
        in_specs=[pl.BlockSpec(memory_space=pl.ANY)] * 3
        + [whole(count, depth)] * 2
        + [here, here, whole(2, hidden)],
        out_specs=[whole(2 * count, 2 * hidden)] + [whole(count, depth)] * 2 + [whole(2, hidden)],
        scratch_shapes=[pltpu.VMEM((2 * count, depth), BF16)]
        + [pltpu.VMEM((hidden, depth), BF16)] * 3
        + [pltpu.SemaphoreType.DMA((3,))],
        out_shape=[like((2 * count, 2 * hidden), BF16)]
        + [like((count, depth), BF16)] * 2
        + [like((2, hidden), F32)],
        compiler_params=params(),
        cost_estimate=cost(
            12 * count * depth * hidden,
            8 * count * (depth + hidden) + 6 * depth * hidden,
            2 * count * hidden,
        ),
        name="gated_back",
    )(up_w, gate_w, down_w, first, second, up, gate, gains)


def part_columns(tok_ref, total, part_refs):
    width = part_refs[0].shape[2]
    in_halves = len(part_refs) == 5
    for offset in range(8):
        start = pl.multiple_of(jnp.bitwise_xor(tok_ref[0], offset) * width, width)
        value = total[:, pl.ds(start, width)].astype(BF16)
        sent, odd, lead = offset % 2, offset // 2 % 2, offset // 4
        if not in_halves or not sent:
            part_refs[2 * sent + odd][lead] = value
        elif odd:
            part_refs[4][lead] = value
        else:
            half = pl.num_programs(0) // 2

            @pl.when(pl.program_id(0) < half)
            def first_half(value=value, into=part_refs[2], lead=lead):
                into[lead] = value

            @pl.when(pl.program_id(0) >= half)
            def second_half(value=value, into=part_refs[3], lead=lead):
                into[lead] = value


def weight_grad_kernel(lefts, rights, scale, steps, outs, tok_ref, *refs):
    left_refs, right_refs = refs[:lefts], refs[lefts : lefts + rights]
    fold_refs, part_refs = refs[lefts + rights : -outs - 1], refs[-outs - 1 : -1]
    total = refs[-1]

    @pl.when(pl.program_id(0) < steps)
    def product():
        acc, lefts_in = None, []
        for ref in left_refs:
            count = right_refs[0].shape[0]
            lefts_in += [ref[k * count : (k + 1) * count, :] for k in range(ref.shape[0] // count)]
        for left, right in zip(lefts_in, right_refs):
            term = lax.dot_general(
                left, right[...], (((0,), (0,)), ((), ())), preferred_element_type=F32
            )
            acc = term if acc is None else acc + term
        total[...] = acc * scale

    if fold_refs:

        @pl.when(pl.program_id(0) >= steps)
        def fold():
            own, near, far = [ref[...].astype(F32) for ref in fold_refs]
            total[...] = (own + near) + far

    part_columns(tok_ref, total, part_refs)


def weight_grad(tok, groups, lefts, rights, scale, folds=(), halves=False, needs=()):
    height = lefts[0].shape[1]
    depth = rights[0].shape[1]
    count = sum(left.shape[0] for left in lefts)
    part = depth // groups
    steps = height // BLK
    out = pl.BlockSpec((groups // 4, BLK, part), lambda i, *_: (0, i, 0))
    total_height = height + (BLK if folds else 0)
    outs, heights = [out] * 4, [total_height] * 4
    if halves:
        half = steps // 2
        even = [
            pl.BlockSpec((groups // 4, BLK, part), lambda i, *_: (0, jnp.minimum(i, half - 1), 0)),
            pl.BlockSpec((groups // 4, BLK, part), lambda i, *_: (0, jnp.maximum(i - half, 0), 0)),
        ]
        outs = [out, out, *even, out]
        heights = [height, height, height // 2, height // 2, height]
    return launch(
        functools.partial(
            weight_grad_kernel, len(lefts), len(rights), scale, steps, len(outs)
        ),
        needs,
        (tok,),
        (total_height // BLK,),
        [
                pl.BlockSpec((left.shape[0], BLK), lambda i, *_: (0, jnp.minimum(i, steps - 1)))
                for left in lefts
            ]
            + [whole(*right.shape) for right in rights]
            + [piece_spec((array, lead, 0), BLK, 0) for array, lead in folds],
        (*lefts, *rights, *[array for array, lead in folds],),
        scratch_shapes=[pltpu.VMEM((BLK, depth), F32)],
        out_specs=outs,
        out_shape=[like((groups // 4, tall, part), BF16) for tall in heights],
        cost_estimate=cost(
            2 * count * height * depth, 2 * count * (height + depth) + 2 * height * depth
        ),
        name="weight_grad",
    )


def out_grad_kernel(pieces, *refs):
    right, pair_refs = refs[pieces], refs[pieces + 1 :]
    for offset, left in enumerate(refs[:pieces]):
        total = lax.dot_general(
            left[...], right[...], (((0,), (0,)), ((), ())), preferred_element_type=F32
        )
        pair_refs[offset // 2][offset % 2] = (total * SCALE_MODEL).astype(BF16)


def out_grad(lefts, right):
    width = lefts[0][0].shape[-1]
    count, depth = right.shape
    pieces = len(lefts)
    return pl.pallas_call(
        functools.partial(out_grad_kernel, pieces),
        grid=(1,),
        in_specs=[piece_spec((array, lead, 0), count, 0) for array, lead in lefts]
        + [whole(count, depth)],
        out_specs=[whole(2, width, depth)] * (pieces // 2),
        out_shape=[like((2, width, depth), BF16)] * (pieces // 2),
        compiler_params=params(),
        cost_estimate=cost(2 * count * depth * depth, 4 * count * depth + 2 * depth * depth),
        name="out_grad",
    )(*[p[0] for p in lefts], right)


def project_back_kernel(pieces, me_ref, low_ref, w_ref, direct_ref, *refs):
    part_refs, total = refs[:pieces], refs[pieces]
    step = pl.program_id(0)
    total[...] = dot_nn(low_ref[...], w_ref[...]) * SCALE_MODEL
    own_blocks = direct_ref.shape[0] // BLK

    @pl.when(step // own_blocks == me_ref[0])
    def add_direct():
        start = pl.multiple_of(lax.rem(step, own_blocks) * BLK, BLK)
        total[...] += direct_ref[pl.ds(start, BLK), :]

    part = total.shape[1] // pieces
    for place, out in enumerate(part_refs):
        start = pl.multiple_of(jnp.bitwise_xor(me_ref[0], place) * part, part)
        out[...] = total[:, pl.ds(start, part)].astype(BF16)


def project_back(me, pieces, low, weight, direct, needs=()):
    count = low.shape[0]
    depth = weight.shape[1]
    part = depth // pieces
    return launch(
        functools.partial(project_back_kernel, pieces),
        needs,
        (me,),
        (count // BLK,),
        [rows(BLK, low.shape[1]), whole(*weight.shape), whole(*direct.shape)],
        (low, weight, direct),
        scratch_shapes=[pltpu.VMEM((BLK, depth), F32)],
        out_specs=[rows(BLK, part)] * pieces,
        out_shape=[like((count, part), BF16)] * pieces,
        cost_estimate=cost(2 * count * low.shape[1] * depth, 2 * count * depth),
        name="project_back",
    )


def trade(value, axis, offset):
    size = lax.axis_size(axis)
    return lax.ppermute(value, axis, [(i, i ^ offset) for i in range(size)])


def sum_four(value, axis, first, second):
    one, two, three = [trade(value, axis, o) for o in (first, second, first ^ second)]
    return (value + one) + (two + three)


def sum_over(value, axis):
    if lax.axis_size(axis) == 4:
        return sum_four(value, axis, 1, 2)
    if lax.axis_size(axis) == 8:
        return sum_four(value + trade(value, axis, 1), axis, 2, 4)
    offset = 1
    while offset < lax.axis_size(axis):
        value = value + trade(value, axis, offset)
        offset *= 2
    return value


def join(*values):
    return lax.optimization_barrier(values)


def stack(*values):
    return jnp.concatenate([v if v.ndim == 3 else v[None] for v in values], axis=0)


def add_low(*values):
    total = values[0].astype(F32)
    for value in values[1:]:
        total = total + value.astype(F32)
    return total


def plain_sum(left, right, scale):
    total = jnp.einsum("tr,td->rd", left, right, preferred_element_type=F32) * scale
    return lax.psum_scatter(total.astype(BF16), "tok", scatter_dimension=1, tiled=True).astype(F32)


def moment_update(weights, gradient, moment, square, fix_first, fix_second):
    moment_next = BETA_ONE * moment + (1.0 - BETA_ONE) * gradient
    square_next = BETA_TWO * square + (1.0 - BETA_TWO) * gradient * gradient
    stepped = weights - LEARN_RATE * (moment_next / fix_first) / (
        jnp.sqrt(square_next / fix_second) + ADAM_EPSILON
    )
    return (stepped, moment_next, square_next)


def local(
    inputs,
    cotangent,
    lengths,
    pad_mask,
    attention_weights,
    gated_weights,
    model_gains,
    unit_gains,
    attention_moment,
    attention_square,
    gated_moment,
    gated_square,
    model_moment,
    model_square,
    unit_moment,
    unit_square,
):
    token_count, width = inputs.shape
    parts = lax.axis_size("dim")
    hidden_here = gated_weights.shape[1]
    own_count = token_count // parts
    place = lax.axis_index("dim")
    me = place.astype(jnp.int32).reshape(1)
    tok = lax.axis_index("tok").astype(jnp.int32).reshape(1)
    groups = lax.axis_size("tok")
    by_pieces = groups == 8 and (D // groups) % 128 == 0
    blocks = own_count // BLK
    length_row = lengths[0]

    def token_rows(value, offset):
        return lax.dynamic_slice_in_dim(value, (place ^ offset) * own_count, own_count, 0)

    ao = attention_weights.reshape(4 * width, -1).astype(BF16)
    gated_low = gated_weights.reshape(3 * hidden_here, -1).astype(BF16)
    both_own = gated_weights[:2].reshape(2 * hidden_here, -1).astype(BF16)
    down_own = gated_weights[2].astype(BF16)
    score_gain = model_gains[:1]
    pad_row = pad_mask[None, :]
    pad_rows = token_rows(pad_mask, 0).astype(F32)[:, None]

    x_far = trade(inputs, "dim", 2)
    seed_rows = [token_rows(cotangent, r) for r in range(parts)]
    seed_send = stack(*seed_rows[2:])
    alphas = lax.dynamic_update_slice(
        jnp.zeros((2, D), F32), model_gains[1:], (0, place * width)
    )
    alpha_near = trade(alphas, "dim", 1)
    if by_pieces:
        ao_by = {0: ao, 4: trade(ao, "tok", 4), 2: trade(ao, "tok", 2), 1: trade(ao, "tok", 1)}
        ao_by[6] = trade(ao_by[4], "tok", 2)
        ao_by[5] = trade(ao_by[4], "tok", 1)
        ao_by[3] = trade(ao_by[2], "tok", 1)
        x_far, ao_by, both_own, seed_send, alphas, alpha_near = join(
            x_far, ao_by, both_own, seed_send, alphas, alpha_near
        )
        ao_by[7] = trade(ao_by[6], "tok", 1)
        by = {0: both_own, 2: trade(both_own, "tok", 2), 4: trade(both_own, "tok", 4)}
    else:
        gather = functools.partial(lax.all_gather, axis_name="tok", axis=1, tiled=True)
        in_pieces = [(gather(ao[: 3 * width]), None, 0)]
        out_weight, up_w, gate_w, down_w = [
            gather(shard)
            for shard in (ao[3 * width :], both_own[:hidden_here], both_own[hidden_here:], down_own)
        ]
        up_pieces, gate_pieces, down_pieces = [[(w, None, 0)] for w in (up_w, gate_w, down_w)]
    x_near = trade(inputs, "dim", 1)
    x_corner = trade(x_far, "dim", 1)
    token_pieces = [inputs, x_near, x_far, x_corner]
    if by_pieces:
        token_pieces, ao_by, gated_low, down_own, seed_send, alphas = join(
            token_pieces, ao_by, gated_low, down_own, seed_send, alphas
        )
        in_pieces = [(ao_by[offset], None, 0) for offset in range(8)]
        by[1] = trade(gated_low, "tok", 1)
    seed_far = trade(seed_send, "dim", 2)
    tokens_all, raw, queries, keys, values, weight_in = project(
        me, tok, token_pieces, in_pieces, score_gain
    )
    queries, seed_far = join(queries, seed_far)

    queries, seed_far, alpha_near = join(queries, seed_far, alpha_near)
    alphas = alphas + alpha_near
    alpha_far = trade(alphas, "dim", 2)
    if by_pieces:
        queries, ao_by = join(queries, ao_by)
        out_weight = assemble(
            tok, [(ao_by[o], None, 3 * width // BLK) for o in range(8)], width, (queries,)
        )
        out_weight, by[1], by[2], by[4], down_own = join(
            out_weight, by[1], by[2], by[4], down_own
        )
        by[3] = trade(by[2], "tok", 1)
        by[6] = trade(by[4], "tok", 2)
    out_across = trade(out_weight, "dim", 2)
    far_mixed, far_aux = attend(
        length_row, me, (2, 3), blocks, pad_row, queries, keys, values, (out_weight,)
    )
    far_mixed, alpha_far, out_across = join(far_mixed, alpha_far, out_across)
    alphas = alphas + alpha_far
    alpha_mixer, alpha_gated = alphas[:1], alphas[1:]
    if by_pieces:
        far_mixed, by[3], by[6], down_own = join(far_mixed, by[3], by[6], down_own)
        by[5] = trade(by[4], "tok", 1)
        down_by = {0: down_own, 2: trade(down_own, "tok", 2), 4: trade(down_own, "tok", 4)}
    far_came = trade(far_mixed, "dim", 2)
    out_pair = trade(stack(out_weight, out_across), "dim", 1)
    near_mixed, near_aux = attend(
        length_row, me, (0, 1), blocks, pad_row, queries, keys, values, (far_mixed,)
    )
    near_mixed, far_came, out_pair = join(near_mixed, far_came, out_pair)
    if by_pieces:
        near_mixed, by[5], by[6], down_by = join(near_mixed, by[5], by[6], down_by)
    pair_came = trade(stack(near_mixed[own_count:], far_came[own_count:]), "dim", 1)
    out_weights = [(out_weight, None), (out_pair, 0), (out_across, None), (out_pair, 1)]
    mixed_pieces = [(near_mixed, None), (pair_came, 0), (far_came, None), (pair_came, 1)]
    low_a, low_b, hidden_one, mixer_unit, mixer_factor, one_factor = mixer(
        mixed_pieces, out_weights, me, tokens_all, alpha_mixer
    )

    far_a = trade(low_a, "dim", 2)
    near_a = trade(low_a, "dim", 1)
    near_b = trade(low_b, "dim", 1)
    if by_pieces:
        near_a, near_b, by[6], down_by = join(near_a, near_b, by[6], down_by)
        by[7] = trade(by[6], "tok", 1)
        down_by[1] = by[1]
        down_by[6] = trade(down_by[4], "tok", 2)
        near_a, far_a, by[7], down_by = join(near_a, far_a, by[7], down_by)
        down_by[3] = trade(down_by[2], "tok", 1)
        down_by[5] = trade(down_by[4], "tok", 1)
        up_pieces, gate_pieces = [[(by[o], None, k) for o in range(8)] for k in range(2)]
    near_a, far_a, low_b = join(near_a, far_a, low_b)
    far_b = trade(low_b, "dim", 2)
    corner_a = trade(far_a, "dim", 1)
    up_one, gate_one, mid_one, *assembled = expand(
        tok, [low_a, near_a, low_b, near_b], up_pieces, gate_pieces, unit_gains
    )
    if by_pieces:
        up_w, gate_w = assembled
        up_pieces, gate_pieces = [(up_w, None, 0)], [(gate_w, None, 0)]
        mid_one, down_by, corner_a = join(mid_one, down_by, corner_a)
        down_by[7] = trade(down_by[6], "tok", 1)
    seed_pair = trade(stack(seed_rows[1], seed_far[1]), "dim", 1)
    seed_pieces = [(seed_rows[0], None), (seed_pair, 0), (seed_far, 0), (seed_pair, 1)]
    up_a, gate_a, mid_a = expand(tok, [far_a, corner_a], up_pieces, gate_pieces, unit_gains)
    mid_a, far_b, seed_pair = join(mid_a, far_b, seed_pair)
    seed_pieces = [(seed_rows[0], None), (seed_pair, 0), (seed_far, 0), (seed_pair, 1)]
    corner_b = trade(far_b, "dim", 1)
    if by_pieces:
        mid_a, down_by = join(mid_a, down_by)
        down_pieces = [(down_by[o], None, 2 if o == 1 else 0) for o in range(8)]
        *parts_a, down_w = contract(tok, mid_a, 0, down_pieces, D)
        down_pieces = [(down_w, None, 0)]
    else:
        parts_a = contract(tok, mid_a, 0, down_pieces, D)
    came = trade(parts_a[1], "dim", 1)
    up_b, gate_b, mid_b = expand(tok, [far_b, corner_b], up_pieces, gate_pieces, unit_gains)
    mid_b, came = join(mid_b, came)
    across = add_low(parts_a[0], came).astype(BF16)
    across_a = trade(across, "dim", 2)
    parts_b = contract(tok, mid_b, 0, down_pieces, D, (across,))
    came = trade(parts_b[1], "dim", 1)
    own_a, pair_a = contract(tok, mid_one, 0, down_pieces, D, (parts_b[0],))
    own_a, came, parts_b, pair_a, across_a = join(own_a, came, parts_b, pair_a, across_a)
    across = add_low(parts_b[0], came).astype(BF16)
    across_b = trade(across, "dim", 2)
    pair_a = trade(pair_a, "dim", 1)
    own_b, pair_b = contract(tok, mid_one, 2, down_pieces, D, (own_a, across))
    own_b, pair_b, pair_a = join(own_b, pair_b, pair_a)
    *carry, delta_a, sum_a = turn(
        me, 0, own_a, pair_a, across_a, hidden_one, seed_pieces, pad_rows, alpha_gated
    )
    pair_b = trade(pair_b, "dim", 1)
    delta_a, across_b, pair_b, carry = join(delta_a, across_b, pair_b, carry)

    back_weights = (up_w, gate_w, down_w, unit_gains)
    b_far_a = trade(delta_a, "dim", 2)
    b_near_a = trade(delta_a, "dim", 1)
    layer_near, layer_far, delta_hidden, delta_b, sum_b = turn(
        me, 1, own_b, pair_b, across_b, hidden_one, seed_pieces, pad_rows, alpha_gated, carry
    )
    delta_b, b_near_a = join(delta_b, b_near_a)
    both_near_a, own_one, pair_one, unit_one = gated_back(
        delta_a, b_near_a, up_one, gate_one, 0, *back_weights
    )
    b_near_b = trade(delta_b, "dim", 1)
    own_one, b_far_a, delta_b, pair_one, b_near_b = join(own_one, b_far_a, delta_b, pair_one, b_near_b)
    b_far_b = trade(delta_b, "dim", 2)
    b_corner_a = trade(b_far_a, "dim", 1)
    pair_one = trade(pair_one, "dim", 1)
    both_near_b, own_two, pair_two, unit_two = gated_back(
        delta_b, b_near_b, up_one, gate_one, 2, *back_weights
    )
    own_two, b_corner_a, pair_one, pair_two, b_far_b = join(
        own_two, b_corner_a, pair_one, pair_two, b_far_b
    )
    pair_two = trade(pair_two, "dim", 1)
    b_corner_b = trade(b_far_b, "dim", 1)
    both_far_a, back_across_a, corner, unit_three = gated_back(
        b_far_a, b_corner_a, up_a, gate_a, 0, *back_weights
    )
    corner, pair_two, b_corner_b = join(corner, pair_two, b_corner_b)
    corner = trade(corner, "dim", 1)
    across = add_low(back_across_a, corner).astype(BF16)
    across, b_corner_b = join(across, b_corner_b)
    across_one = trade(across, "dim", 2)
    both_far_b, back_across_b, corner, unit_four = gated_back(
        b_far_b, b_corner_b, up_b, gate_b, 0, *back_weights
    )
    back_across_b, across_one = join(back_across_b, across_one)
    corner = trade(corner, "dim", 1)
    across = add_low(back_across_b, corner).astype(BF16)
    across_two = trade(across, "dim", 2)
    back_sums = [own_one, pair_one, across_one, own_two, pair_two, across_two]
    h_pieces = [low_a, near_a, low_b, near_b, far_a, corner_a, far_b, corner_b]
    b_pieces = [delta_a, b_near_a, delta_b, b_near_b, b_far_a, b_corner_a, b_far_b, b_corner_b]
    middles = [mid_one, mid_a, mid_b]
    both_pieces = [both_near_a, both_near_b, both_far_a, both_far_b]
    unit_sums = (unit_one + unit_two) + (unit_three + unit_four)
    sum_gated = sum_a + sum_b
    if by_pieces:
        down_parts = weight_grad(tok, groups, middles, b_pieces, SCALE_HIDDEN, needs=(across,))
        back_sums, down_parts, both_pieces, h_pieces = join(
            back_sums, down_parts, both_pieces, h_pieces
        )
        down_odd = trade(down_parts[3], "tok", 1)
    else:
        down_grad = plain_sum(
            jnp.concatenate(middles, axis=0), jnp.concatenate(b_pieces, axis=0), SCALE_HIDDEN
        )
        both_grad = plain_sum(
            jnp.concatenate(both_pieces, axis=0), jnp.concatenate(h_pieces, axis=0), SCALE_MODEL
        )

    delta_near, delta_far, mixer_low, delta_direct, sum_mixer = mixer_back(
        me,
        back_sums,
        delta_hidden,
        hidden_one,
        mixer_unit,
        one_factor,
        mixer_factor,
        tokens_all,
        alpha_mixer,
        out_weights,
    )
    if by_pieces:
        delta_far, mixer_low, down_odd, both_pieces = join(
            delta_far, mixer_low, down_odd, both_pieces
        )
        down_near = trade(add_low(down_parts[1], down_odd).astype(BF16), "tok", 2)
        down_even = trade(down_parts[2], "tok", 1)
        both_parts = weight_grad(
            tok, groups, both_pieces, h_pieces, SCALE_MODEL, halves=True, needs=(delta_far,)
        )
    delta_came = trade(delta_far, "dim", 2)
    out_near_grad, out_far_grad = out_grad(mixed_pieces, mixer_low)
    alpha_sums = jnp.concatenate([sum_mixer, sum_gated], axis=0)
    if by_pieces:
        delta_came, out_near_grad, out_far_grad, both_parts, layer_far = join(
            delta_came, out_near_grad, out_far_grad, both_parts, layer_far
        )
        delta_came, down_near, down_even = join(delta_came, down_near, down_even)
    delta_pair = trade(stack(delta_near[1], delta_came[1]), "dim", 1)
    out_pair = trade(stack(out_near_grad[1], out_far_grad[1]), "dim", 1)
    delta_pair, out_pair = join(delta_pair, out_pair)
    if by_pieces:
        both_even, both_odd, *even_send, odd_send = both_parts
        odd_came = trade(odd_send, "tok", 1)
        up_even = trade(even_send[0], "tok", 1)
        down_low = add_low(down_parts[0][1], down_even[1], down_near[1]).astype(BF16)
        down_last = trade(down_low, "tok", 4)
    layer_came = trade(layer_far, "dim", 2)
    out_far_sum = trade(add_low(out_far_grad[0], out_pair[1]).astype(BF16), "dim", 2)
    delta_pieces = [(delta_near, 0), (delta_pair, 0), (delta_came, 0), (delta_pair, 1)]
    delta_project, scale_sum = attend_back(
        length_row,
        me,
        pad_row,
        queries,
        keys,
        values,
        raw,
        score_gain,
        [near_aux, far_aux],
        [near_mixed, far_mixed],
        delta_pieces,
    )
    delta_project, alpha_sums, out_far_sum, layer_came = join(
        delta_project, alpha_sums, out_far_sum, layer_came
    )
    alpha_near = trade(alpha_sums, "dim", 1)
    if by_pieces:
        delta_project, odd_came, up_even, down_last = join(
            delta_project, odd_came, up_even, down_last
        )
        gate_even = trade(even_send[1], "tok", 1)
        halves = [slice(k * hidden_here, (k + 1) * hidden_here) for k in range(2)]
        up_odd, gate_odd = [
            add_low(both_odd[:, here], odd_came[:, here]).astype(BF16) for here in halves
        ]
        up_near = trade(up_odd, "tok", 2)
        in_parts = weight_grad(
            tok,
            groups,
            (delta_project,),
            (tokens_all,),
            SCALE_MODEL,
            ((out_near_grad, 0), (out_pair, 0), (out_far_sum, None)),
            needs=(up_odd, gate_odd),
        )
        in_parts, alpha_near, layer_near, up_near, gate_even, gate_odd = join(
            in_parts, alpha_near, layer_near, up_near, gate_even, gate_odd
        )
        in_odd = trade(in_parts[3], "tok", 1)
        gate_near = trade(gate_odd, "tok", 2)
        up_low = add_low(both_even[1, halves[0]], up_even[1], up_near[1]).astype(BF16)
        up_last = trade(up_low, "tok", 4)
    alpha_sums = alpha_sums + alpha_near
    alpha_far = trade(alpha_sums, "dim", 2)
    input_parts = project_back(
        me, parts, delta_project, weight_in, delta_direct, (in_parts[3],) if by_pieces else ()
    )
    if by_pieces:
        input_parts, in_odd, in_parts, up_last, gate_near, alpha_far = join(
            input_parts, in_odd, in_parts, up_last, gate_near, alpha_far
        )
        gate_low = add_low(both_even[1, halves[1]], gate_even[1], gate_near[1]).astype(BF16)
        in_low = add_low(in_parts[1], in_odd).astype(BF16)
        in_near = trade(in_low, "tok", 2)
        in_even = trade(in_parts[2], "tok", 1)
        gate_last = trade(gate_low, "tok", 4)
    alpha_sums = lax.dynamic_slice_in_dim(alpha_sums + alpha_far, place * width, width, 1)
    gains_sum = jnp.concatenate(
        [scale_sum.reshape(-1), alpha_sums.reshape(-1), unit_sums.reshape(-1)]
    )
    corner = trade(input_parts[3], "dim", 1)
    near = trade(input_parts[1], "dim", 1)
    half = token_count // 2
    across = [
        add_low(input_parts[2][k * half : (k + 1) * half], corner[k * half : (k + 1) * half])
        for k in range(2)
    ]
    far_one = trade(across[0].astype(BF16), "dim", 2)
    across_two = across[1].astype(BF16)
    if by_pieces:
        far_one, near, across_two, gate_last, in_near, in_even = join(
            far_one, near, across_two, gate_last, in_near, in_even
        )
    far_two = trade(across_two, "dim", 2)
    layer_pair = trade(stack(layer_near[1], layer_came[1]), "dim", 1)
    layer_pieces = [layer_near[0], layer_pair[0], layer_came[0], layer_pair[1]]
    layer_out = jnp.zeros((token_count, width), BF16)
    for r, piece in enumerate(layer_pieces):
        layer_out = lax.dynamic_update_slice(layer_out, piece, ((place ^ r) * own_count, 0))
    if by_pieces:
        in_low = add_low(in_parts[0][1], in_even[1], in_near[1]).astype(BF16)
        in_last = trade(in_low, "tok", 4)
        down_grad = add_low(down_parts[0][0], down_even[0], down_near[0], down_last)
        up_grad = add_low(both_even[0, halves[0]], up_even[0], up_near[0], up_last)
        gate_grad = add_low(both_even[0, halves[1]], gate_even[0], gate_near[0], gate_last)
        both_grad = jnp.concatenate([up_grad, gate_grad], axis=0)
    gated_grad = jnp.concatenate([both_grad, down_grad], axis=0).reshape(3, hidden_here, -1)
    fix_first = 1.0 - BETA_ONE**STEP
    fix_second = 1.0 - BETA_TWO**STEP
    gated_stepped, moment_gated, square_gated = moment_update(
        gated_weights, gated_grad, gated_moment, gated_square, fix_first, fix_second
    )
    gated_row_sums = jnp.sum(gated_stepped * gated_stepped, axis=2)
    gated_square_sum = jnp.sum(gated_grad * gated_grad)
    if by_pieces:
        in_last, gated_row_sums, gated_square_sum, layer_out, far_two = join(
            in_last, gated_row_sums, gated_square_sum, layer_out, far_two
        )
        in_total = add_low(in_parts[0][0], in_even[0], in_near[0], in_last)
        attention_grad = in_total.reshape(4, width, -1)
    else:
        out_total = lax.psum_scatter(
            add_low(out_near_grad[0], out_pair[0], out_far_sum).astype(BF16),
            "tok",
            scatter_dimension=1,
            tiled=True,
        ).astype(F32)
        in_total = plain_sum(delta_project, tokens_all, SCALE_MODEL)
        attention_grad = jnp.concatenate([in_total, out_total], axis=0).reshape(4, width, -1)

    input_gradient = add_low(input_parts[0], near, jnp.concatenate([far_one, far_two], axis=0))

    attention_stepped, moment_attention, square_attention = moment_update(
        attention_weights, attention_grad, attention_moment, attention_square, fix_first, fix_second
    )
    sums = sum_over(
        jnp.concatenate(
            [
                jnp.sum(attention_stepped * attention_stepped, axis=2).reshape(-1),
                gated_row_sums.reshape(-1),
                gains_sum,
                (jnp.sum(attention_grad * attention_grad) + gated_square_sum).reshape(1),
            ]
        ),
        "tok",
    )
    ends = [4 * width, 4 * width + 3 * hidden_here, 7 * width + 3 * hidden_here]
    model_grad = sums[ends[1] : ends[2]].reshape(3, width)
    unit_grad = sums[ends[2] : -1].reshape(2, hidden_here)
    model_next, moment_model, square_model = moment_update(
        model_gains, model_grad, model_moment, model_square, fix_first, fix_second
    )
    unit_next, moment_unit, square_unit = moment_update(
        unit_gains, unit_grad, unit_moment, unit_square, fix_first, fix_second
    )
    square_sum = sums[-1:] + jnp.sum(model_grad * model_grad) + jnp.sum(unit_grad * unit_grad)
    totals = sum_over(jnp.concatenate([square_sum, jnp.sum(model_next[1:], axis=1)]), "dim")
    attention_rows = sums[: ends[0]].reshape(4, width, 1)
    gated_rows = sums[ends[0] : ends[1]].reshape(3, hidden_here, 1)
    attention_next = attention_stepped * lax.rsqrt(attention_rows / D + EPSILON)
    gated_next = gated_stepped * lax.rsqrt(gated_rows / D + EPSILON)
    gradient_norm = jnp.sqrt(totals[:1])
    mean_alpha = totals[1:] / D
    return (
        layer_out,
        input_gradient,
        attention_next,
        attention_next.astype(BF16),
        moment_attention,
        square_attention,
        gated_next,
        gated_next.astype(BF16),
        moment_gated,
        square_gated,
        model_next,
        moment_model,
        square_model,
        unit_next,
        moment_unit,
        square_unit,
        gradient_norm,
        mean_alpha,
    )


def solution(mesh):
    tokens = P("tok", "dim")
    weights = P(None, "dim", "tok")
    gains = P(None, "dim")
    in_specs = (tokens, tokens, P("tok", None), P("tok"), weights, weights, gains, gains)
    in_specs += (weights,) * 4 + (gains,) * 4
    out_specs = (tokens, tokens) + (weights,) * 8 + (gains,) * 6 + (P(), P())
    return jax.shard_map(local, mesh=mesh, in_specs=in_specs, out_specs=out_specs, check_vma=False)
```
